32 devices in a mesh: dp: 16 (over z, y, x), seq: 2 (over core).
Axes of the slice: x: 2, y: 2, z: 4, core: 2. Of those that a mesh axis runs over, the one named last changes fastest.
Arguments:
- inputs: bfloat16 [16, 256, 1024], P('dp', 'seq'), may hold values from -6 to 6
- segments: int32 [16, 256], P('dp', 'seq'), may hold values from 0 to 2, as said below
- cotangent: bfloat16 [16, 256, 1024], P('dp', 'seq'), may hold values from -6 to 6
- ln1_gain: bfloat16 [1024], P(('dp', 'seq')), may hold values from 0.5 to 1.5
- w_qkv: bfloat16 [3145728], P(('dp', 'seq')), may hold values from -0.1875 to 0.1875
- w_attn_out: bfloat16 [1048576], P(('dp', 'seq')), may hold values from -1 to 1
- ln2_gain: bfloat16 [1024], P(('dp', 'seq')), may hold values from 0.5 to 1.5
- w_in: bfloat16 [5373952], P(('dp', 'seq')), may hold values from -0.1875 to 0.1875
- w_mlp_out: bfloat16 [2686976], P(('dp', 'seq')), may hold values from -0.125 to 0.125
Outputs:
- output: bfloat16 [16, 256, 1024], P('dp', 'seq')
- input_grad: float32 [16, 256, 1024], P('dp', 'seq')
- ln1_gain_grad: float32 [1024], P(('dp', 'seq'))
- w_qkv_grad: float32 [3145728], P(('dp', 'seq'))
- w_attn_out_grad: float32 [1048576], P(('dp', 'seq'))
- ln2_gain_grad: float32 [1024], P(('dp', 'seq'))
- w_in_grad: float32 [5373952], P(('dp', 'seq'))
- w_mlp_out_grad: float32 [2686976], P(('dp', 'seq'))
The draws below stay inside these ranges and needn't reach their ends.
Inputs may be any that keep to these rules, and one draw needn't show every extreme that they name: `segments`: along a packed sequence the numbers never fall, and 0, 1 and 2 all occur in each.
All inputs are finite; a program needn't handle non-finite values.
Results may differ from the reference program's by a relative error of at most 0.022.
Values may be sent and summed in bfloat16 or wider, within the bound.
A program may use at most 192 MiB of HBM per device.

```python
import jax
import jax.numpy as jnp
from jax import lax

D = 1024
HEADS = 16
HD = 64
FF = 2624
TOK_DEV = 128
SEQ_LEN = 256
SEQS = 16


def draw_segments(key, part):
    key = jax.random.fold_in(key, 11)
    first_key, last_key = jax.random.split(key)
    start_doc = jax.random.randint(first_key, (SEQS, 1), TOK_DEV // 2, TOK_DEV)
    end_doc = SEQ_LEN - jax.random.randint(last_key, (SEQS, 1), TOK_DEV // 2, TOK_DEV)
    places = jnp.arange(SEQ_LEN, dtype=jnp.int32)[None, :]
    return (places >= start_doc).astype(jnp.int32) + (places >= end_doc).astype(jnp.int32)


def levels(own_key, extent, shards, smallest, largest):
    def one(axis_at, parts):
        heights = jax.random.uniform(jax.random.fold_in(jax.random.fold_in(own_key, 6), axis_at), (parts,), jnp.float32, smallest / len(shards), largest / len(shards))
        return jnp.repeat(jnp.exp(heights), extent[axis_at] // parts).reshape((-1,) + (1,) * (len(extent) - axis_at - 1))

    factor_of = one(*shards[0])
    for cut in shards[1:]:
        factor_of = factor_of * one(*cut)
    return factor_of


def normal_values(rng, extent, deviation, reach, cuts=(), held_as=jnp.bfloat16):
    values = deviation * jax.random.normal(rng, extent, jnp.float32)
    if cuts:
        values = values * levels(rng, extent, cuts, -0.22, 0.18)
    return jnp.clip(values, -reach, reach).astype(held_as)


def setup_inputs(seed: int = 0) -> dict:
    splits = jax.random.split(jax.random.key(seed), 10)
    inputs = normal_values(splits[0], (SEQS, SEQ_LEN, D), 1.0, 6.0, ((0, 16), (1, 2)))
    segments = draw_segments(jax.random.fold_in(splits[9], 71), 0)
    cotangent = normal_values(splits[2], (SEQS, SEQ_LEN, D), 1.0, 6.0, ((0, 16), (1, 2)))
    ln1_gain = jnp.clip(1.0 + 0.1 * jax.random.normal(splits[3], (D,), jnp.float32), 0.5, 1.5).astype(jnp.bfloat16)
    w_qkv = normal_values(splits[4], (3 * D * D,), D ** -0.5, 0.1875, ((0, 32),))
    w_attn_out = normal_values(splits[5], (D * D,), (max(1, 9 * D // SEQ_LEN)) ** -0.5, 1.0, ((0, 32),))
    ln2_gain = jnp.clip(1.0 + 0.1 * jax.random.normal(splits[6], (D,), jnp.float32), 0.5, 1.5).astype(jnp.bfloat16)
    w_in = normal_values(splits[7], (2 * D * FF,), D ** -0.5, 0.1875, ((0, 32),))
    w_mlp_out = normal_values(splits[8], (FF * D,), FF ** -0.5, 0.125, ((0, 32),))
    return dict(inputs=inputs, segments=segments, cotangent=cotangent, ln1_gain=ln1_gain, w_qkv=w_qkv, w_attn_out=w_attn_out, ln2_gain=ln2_gain, w_in=w_in, w_mlp_out=w_mlp_out)


@jax.custom_vjp
def low(v):
    return lax.optimization_barrier(v.astype(jnp.bfloat16)).astype(jnp.float32)

@jax.custom_vjp
def low_back(v):
    return v

def low_keep(v):
    return (low(v), None)

def low_pass(kept, grad):
    return (grad,)

def back_keep(v):
    return (v, None)

def back_low(kept, grad):
    return (low(grad),)
low.defvjp(low_keep, low_pass)
low_back.defvjp(back_keep, back_low)
EPSILON = 1e-05
ROPE_BASE = 160000.0

def rope_tables(places):
    freqs = 1.0 / ROPE_BASE ** (jnp.arange(0, HD, 2, dtype=jnp.float32) / HD)
    angles = places[:, None] * freqs[None, :]
    angles = jnp.concatenate([angles, angles], axis=1)
    return (jnp.cos(angles), jnp.sin(angles))

def rotate(values_in, cosines, sines):
    halfway = values_in.shape[-1] // 2
    turned = jnp.concatenate([-values_in[..., halfway:], values_in[..., :halfway]], axis=-1)
    return values_in * cosines[:, None, :] + turned * sines[:, None, :]

def layer_norm(values_in, gain):
    centred = values_in - lax.optimization_barrier(jnp.mean(values_in, axis=-1, keepdims=True))
    spread = lax.optimization_barrier(jnp.mean(centred * centred, axis=-1, keepdims=True))
    return centred * lax.rsqrt(spread + EPSILON) * gain

def layer(tokens_in, seg_row, gain_one, qkv_flat, proj_flat, gain_two, in_flat, down_flat):
    highest = lax.Precision.HIGHEST
    length, model_width = tokens_in.shape
    normed_one = low(layer_norm(tokens_in, gain_one))
    qkv_rows = low_back(jnp.dot(normed_one, qkv_flat.reshape(model_width, 3 * model_width), precision=highest))
    cosines, sines = rope_tables(jnp.arange(length, dtype=jnp.float32))
    query = low(rotate(qkv_rows[:, :model_width].reshape(length, HEADS, HD), cosines, sines))
    key_rot = low(rotate(qkv_rows[:, model_width:2 * model_width].reshape(length, HEADS, HD), cosines, sines))
    value_rows = low(qkv_rows[:, 2 * model_width:].reshape(length, HEADS, HD))
    block_rows = min(512, length)
    block_count = length // block_rows

    def attend(item):
        query_block, seg_block = item
        scores = low_back(jnp.einsum('qhd,khd->hqk', query_block, key_rot, precision=highest) * 0.125)
        same_doc = seg_block[:, None] == seg_row[None, :]
        scores = jnp.where(same_doc[None], scores, -1e+30)
        top_score = lax.optimization_barrier(jnp.max(scores, axis=-1, keepdims=True))
        weights = jnp.exp(scores - top_score)
        probs = weights / lax.optimization_barrier(jnp.sum(weights, axis=-1, keepdims=True))
        return jnp.einsum('hqk,khd->qhd', low(probs), value_rows, precision=highest)
    mixed = lax.map(jax.checkpoint(attend), (query.reshape(block_count, block_rows, HEADS, HD), seg_row.reshape(block_count, block_rows)))
    attended = low(low_back(mixed.reshape(length, model_width)))
    middle = tokens_in + low_back(jnp.dot(attended, proj_flat.reshape(model_width, model_width), precision=highest))
    normed_two = low(layer_norm(middle, gain_two))
    upper = low_back(jnp.dot(normed_two, in_flat.reshape(model_width, 2 * FF), precision=highest))
    hidden = low(jax.nn.gelu(upper[:, :FF], approximate=False) * upper[:, FF:])
    return middle + jnp.dot(hidden, down_flat.reshape(FF, model_width), precision=highest)

def reference(inputs, segments, cotangent, ln1_gain, w_qkv, w_attn_out, ln2_gain, w_in, w_mlp_out):
    params = tuple((p.astype(jnp.float32) for p in (ln1_gain, w_qkv, w_attn_out, ln2_gain, w_in, w_mlp_out)))

    def one_sequence(totals, item):
        tokens_in, seg_row, grad_row = item

        def forward(tokens_now, *weights):
            return layer(tokens_now, seg_row, *weights)
        result, pull = jax.vjp(forward, tokens_in.astype(jnp.float32), *params)
        grads = pull(grad_row.astype(jnp.float32))
        totals = tuple((t + g for t, g in zip(totals, grads[1:])))
        return (totals, (result.astype(jnp.bfloat16), grads[0]))
    zeros_init = tuple((jnp.zeros(p.shape, jnp.float32) for p in params))
    totals, (output, input_grad) = lax.scan(one_sequence, zeros_init, (inputs, segments, cotangent))
    return (output, input_grad, totals[0], totals[1], totals[2], totals[3], totals[4], totals[5])
```

```python
import functools
import math

import jax
import jax.numpy as jnp
from jax import lax
from jax.experimental import pallas as pl
from jax.experimental.pallas import tpu as pltpu
from jax.sharding import PartitionSpec as P

HEADS = 16
HD = 64
FF = 2624


EPSILON = 1e-05
ROPE_BASE = 160000.0


def rope_tables(places):
    freqs = 1.0 / ROPE_BASE ** (jnp.arange(0, HD, 2, dtype=jnp.float32) / HD)
    angles = places[:, None] * freqs[None, :]
    angles = jnp.concatenate([angles, angles], axis=1)
    return (jnp.cos(angles), jnp.sin(angles))


def rotate(values_in, cosines, sines):
    halfway = values_in.shape[-1] // 2
    turned = jnp.concatenate([-values_in[..., halfway:], values_in[..., :halfway]], axis=-1)
    return values_in * cosines[:, None, :] + turned * sines[:, None, :]


def rotate_back(grads_in, cosines, sines):
    halfway = grads_in.shape[-1] // 2
    scaled = grads_in * sines[:, None, :]
    turned = jnp.concatenate([scaled[..., halfway:], -scaled[..., :halfway]], axis=-1)
    return grads_in * cosines[:, None, :] + turned


def norm_forward(values_in, gain):
    centred = values_in - jnp.mean(values_in, axis=-1, keepdims=True)
    inv_spread = lax.rsqrt(jnp.mean(centred * centred, axis=-1, keepdims=True) + EPSILON)
    unit_rows = centred * inv_spread
    return (unit_rows * gain, unit_rows, inv_spread)


def norm_back(grad_rows, unit_rows, inv_spread, gain):
    gain_grad = jnp.sum(grad_rows * unit_rows, axis=0)
    scaled = grad_rows * gain
    inner_mean = jnp.mean(scaled, axis=-1, keepdims=True)
    cross_mean = jnp.mean(scaled * unit_rows, axis=-1, keepdims=True)
    return (gain_grad, inv_spread * (scaled - inner_mean - unit_rows * cross_mean))


def matmul_tn(left, right):
    return lax.dot_general(
        left, right, (((0,), (0,)), ((), ())), preferred_element_type=jnp.float32
    )


def matmul_nt(left, right):
    return lax.dot_general(
        left, right, (((1,), (1,)), ((), ())), preferred_element_type=jnp.float32
    )


def masked_scores(query, key_block, seg_query, seg_block):
    scores = (
        jnp.einsum("qhd,khd->hqk", query, key_block, preferred_element_type=jnp.float32) * 0.125
    )
    same_doc = seg_query[:, None] == seg_block[None, :]
    return jnp.where(same_doc[None], scores, -1e30)


def gated(inner, gate):
    return jax.nn.gelu(inner, approximate=False) * gate


def general_device(inputs, segments, cotangent, ln1_gain, w_qkv, w_attn_out, ln2_gain, w_in, w_mlp_out):
    tok_rows = inputs.shape[1]
    model_width = inputs.shape[2]
    seq_devices = lax.axis_size("seq")
    dp_devices = lax.axis_size("dp")
    tokens_in = inputs[0].astype(jnp.float32)
    seg_send = segments.astype(jnp.bfloat16)
    seg_query = seg_send[0]
    gathered_attn = (
        lax.all_gather(ln1_gain, ("dp", "seq"), axis=0, tiled=True),
        lax.all_gather(w_qkv, ("dp", "seq"), axis=0, tiled=True),
        lax.all_gather(w_attn_out, ("dp", "seq"), axis=0, tiled=True),
    )
    gain_one = gathered_attn[0].astype(jnp.float32)
    qkv_mat = gathered_attn[1].reshape(model_width, 3 * model_width)
    proj_mat = gathered_attn[2].reshape(model_width, model_width)
    places = (lax.axis_index("seq") * tok_rows + jnp.arange(tok_rows, dtype=jnp.int32)).astype(
        jnp.float32
    )
    cosines, sines = rope_tables(places)
    normed_one, unit_one, spread_one = norm_forward(tokens_in, gain_one)
    normed_one_low = normed_one.astype(jnp.bfloat16)
    qkv_rows = jnp.dot(normed_one_low, qkv_mat, preferred_element_type=jnp.float32)
    query = rotate(qkv_rows[:, :model_width].reshape(tok_rows, HEADS, HD), cosines, sines).astype(
        jnp.bfloat16
    )
    key_rot = rotate(
        qkv_rows[:, model_width : 2 * model_width].reshape(tok_rows, HEADS, HD), cosines, sines
    ).astype(jnp.bfloat16)
    value_rows = qkv_rows[:, 2 * model_width :].astype(jnp.bfloat16)
    key_send = key_rot.reshape(1, tok_rows, model_width)
    value_send = value_rows.reshape(1, tok_rows, model_width)
    fwd_init = (
        jnp.full((HEADS, tok_rows), -1e30, jnp.float32),
        jnp.zeros((HEADS, tok_rows), jnp.float32),
        jnp.zeros((tok_rows, HEADS, HD), jnp.float32),
    )
    key_piece = lax.all_gather(key_send, "seq", axis=1, tiled=True)
    value_piece = lax.all_gather(value_send, "seq", axis=1, tiled=True)
    seg_piece = lax.all_gather(seg_send, "seq", axis=1, tiled=True)
    span = key_piece.shape[1]
    step_rows = math.gcd(span, 512)

    def one_block(block_id, inner_state):
        top_score, total, accum = inner_state
        begin = block_id * step_rows
        key_block = lax.dynamic_slice_in_dim(key_piece[0], begin, step_rows, 0).reshape(
            step_rows, HEADS, HD
        )
        value_block = lax.dynamic_slice_in_dim(value_piece[0], begin, step_rows, 0).reshape(
            step_rows, HEADS, HD
        )
        seg_block = lax.dynamic_slice_in_dim(seg_piece[0], begin, step_rows, 0)
        scores = masked_scores(query, key_block, seg_query, seg_block)
        new_top = jnp.maximum(top_score, jnp.max(scores, axis=-1))
        fading = jnp.exp(top_score - new_top)
        weights = jnp.exp(scores - new_top[..., None])
        total = total * fading + jnp.sum(weights, axis=-1)
        accum = accum * fading.T[:, :, None] + jnp.einsum(
            "hqk,khd->qhd",
            weights.astype(jnp.bfloat16),
            value_block,
            preferred_element_type=jnp.float32,
        )
        return (new_top, total, accum)

    fwd_state = lax.fori_loop(0, span // step_rows, one_block, fwd_init)
    run_top, run_total, run_accum = fwd_state
    log_total = run_top + jnp.log(run_total)
    attended = (run_accum / run_total.T[:, :, None]).astype(jnp.bfloat16)
    attended_rows = attended.reshape(tok_rows, model_width)
    middle = tokens_in + jnp.dot(attended_rows, proj_mat, preferred_element_type=jnp.float32)
    gathered_mlp = (
        lax.all_gather(ln2_gain, ("dp", "seq"), axis=0, tiled=True),
        lax.all_gather(w_in, ("dp", "seq"), axis=0, tiled=True),
        lax.all_gather(w_mlp_out, ("dp", "seq"), axis=0, tiled=True),
    )
    gain_two = gathered_mlp[0].astype(jnp.float32)
    in_mat = gathered_mlp[1].reshape(model_width, 2 * FF)
    down_mat = gathered_mlp[2].reshape(FF, model_width)
    normed_two, unit_two, spread_two = norm_forward(middle, gain_two)
    normed_two_low = normed_two.astype(jnp.bfloat16)
    upper = jnp.dot(normed_two_low, in_mat, preferred_element_type=jnp.float32)
    inner = upper[:, :FF]
    gate = upper[:, FF:]
    hidden_low = gated(inner, gate).astype(jnp.bfloat16)
    output = (middle + jnp.dot(hidden_low, down_mat, preferred_element_type=jnp.float32)).astype(
        jnp.bfloat16
    )
    gathered_mlp = (
        lax.all_gather(ln2_gain, ("dp", "seq"), axis=0, tiled=True),
        lax.all_gather(w_in, ("dp", "seq"), axis=0, tiled=True),
        lax.all_gather(w_mlp_out, ("dp", "seq"), axis=0, tiled=True),
    )
    gain_two = gathered_mlp[0].astype(jnp.float32)
    in_mat = gathered_mlp[1].reshape(model_width, 2 * FF)
    down_mat = gathered_mlp[2].reshape(FF, model_width)
    grad_low = cotangent[0]
    grad_rows = grad_low.astype(jnp.float32)
    d_hidden = matmul_nt(grad_low, down_mat)
    grad_down = matmul_tn(hidden_low, grad_low)
    gated_value, pull = jax.vjp(gated, inner, gate)
    d_inner, d_gate = pull(d_hidden)
    d_upper_low = jnp.concatenate([d_inner, d_gate], axis=1).astype(jnp.bfloat16)
    grad_in = matmul_tn(normed_two_low, d_upper_low)
    d_normed_two = matmul_nt(d_upper_low, in_mat)
    grad_gain_two, d_middle_part = norm_back(d_normed_two, unit_two, spread_two, gain_two)
    d_middle = grad_rows + d_middle_part
    mlp_parts = tuple(
        (g.reshape(dp_devices, seq_devices, -1) for g in (grad_gain_two, grad_in, grad_down))
    )
    mlp_mid = (
        lax.psum_scatter(
            mlp_parts[0].astype(jnp.bfloat16), "seq", scatter_dimension=1, tiled=True
        ).astype(jnp.float32),
        lax.psum_scatter(
            mlp_parts[1].astype(jnp.bfloat16), "seq", scatter_dimension=1, tiled=True
        ).astype(jnp.float32),
        lax.psum_scatter(
            mlp_parts[2].astype(jnp.bfloat16), "seq", scatter_dimension=1, tiled=True
        ).astype(jnp.float32),
    )
    mlp_shards = (
        lax.psum_scatter(
            mlp_mid[0].astype(jnp.bfloat16), "dp", scatter_dimension=0, tiled=True
        ).astype(jnp.float32),
        lax.psum_scatter(
            mlp_mid[1].astype(jnp.bfloat16), "dp", scatter_dimension=0, tiled=True
        ).astype(jnp.float32),
        lax.psum_scatter(
            mlp_mid[2].astype(jnp.bfloat16), "dp", scatter_dimension=0, tiled=True
        ).astype(jnp.float32),
    )
    gathered_attn = (
        lax.all_gather(ln1_gain, ("dp", "seq"), axis=0, tiled=True),
        lax.all_gather(w_qkv, ("dp", "seq"), axis=0, tiled=True),
        lax.all_gather(w_attn_out, ("dp", "seq"), axis=0, tiled=True),
    )
    gain_one = gathered_attn[0].astype(jnp.float32)
    qkv_mat = gathered_attn[1].reshape(model_width, 3 * model_width)
    proj_mat = gathered_attn[2].reshape(model_width, model_width)
    d_branch_low = d_middle.astype(jnp.bfloat16)
    grad_proj = matmul_tn(attended_rows, d_branch_low)
    d_attended = matmul_nt(d_branch_low, proj_mat).astype(jnp.bfloat16).reshape(tok_rows, HEADS, HD)
    delta_rows = jnp.einsum(
        "qhd,qhd->hq", d_attended.astype(jnp.float32), attended.astype(jnp.float32)
    )
    back_init = (
        jnp.zeros((tok_rows, HEADS, HD), jnp.float32),
        jnp.zeros((tok_rows * seq_devices, 2 * model_width), jnp.float32),
    )
    attend_key_piece = lax.all_gather(key_send, "seq", axis=1, tiled=True)
    attend_value_piece = lax.all_gather(value_send, "seq", axis=1, tiled=True)
    attend_seg_piece = lax.all_gather(seg_send, "seq", axis=1, tiled=True)
    span = attend_key_piece.shape[1]
    attend_step_rows = math.gcd(span, 512)

    def one_block(block_id, inner_state):
        grad_query, grad_kv = inner_state
        begin = block_id * attend_step_rows
        key_block = lax.dynamic_slice_in_dim(
            attend_key_piece[0], begin, attend_step_rows, 0
        ).reshape(attend_step_rows, HEADS, HD)
        value_block = lax.dynamic_slice_in_dim(
            attend_value_piece[0], begin, attend_step_rows, 0
        ).reshape(attend_step_rows, HEADS, HD)
        seg_block = lax.dynamic_slice_in_dim(attend_seg_piece[0], begin, attend_step_rows, 0)
        scores = masked_scores(query, key_block, seg_query, seg_block)
        probs = jnp.exp(scores - log_total[..., None])
        probs_low = probs.astype(jnp.bfloat16)
        value_grad = jnp.einsum(
            "hqk,qhd->khd", probs_low, d_attended, preferred_element_type=jnp.float32
        )
        d_probs = jnp.einsum(
            "qhd,khd->hqk", d_attended, value_block, preferred_element_type=jnp.float32
        )
        d_scores = (probs * (d_probs - delta_rows[..., None])).astype(jnp.bfloat16)
        grad_query = (
            grad_query
            + jnp.einsum("hqk,khd->qhd", d_scores, key_block, preferred_element_type=jnp.float32)
            * 0.125
        )
        key_grad = (
            jnp.einsum("hqk,qhd->khd", d_scores, query, preferred_element_type=jnp.float32) * 0.125
        )
        block_grads = jnp.concatenate(
            [
                key_grad.reshape(attend_step_rows, model_width),
                value_grad.reshape(attend_step_rows, model_width),
            ],
            axis=1,
        )
        grad_kv = lax.dynamic_update_slice_in_dim(grad_kv, block_grads, begin, 0)
        return (grad_query, grad_kv)

    back_state = lax.fori_loop(0, span // attend_step_rows, one_block, back_init)
    kv_grads = lax.psum_scatter(
        back_state[1].astype(jnp.bfloat16), "seq", scatter_dimension=0, tiled=True
    ).astype(jnp.float32)
    d_query = rotate_back(back_state[0], cosines, sines).reshape(tok_rows, model_width)
    d_key = rotate_back(
        kv_grads[:, :model_width].reshape(tok_rows, HEADS, HD), cosines, sines
    ).reshape(tok_rows, model_width)
    d_qkv_low = jnp.concatenate([d_query, d_key, kv_grads[:, model_width:]], axis=1).astype(
        jnp.bfloat16
    )
    grad_qkv = matmul_tn(normed_one_low, d_qkv_low)
    d_normed_one = matmul_nt(d_qkv_low, qkv_mat)
    grad_gain_one, d_input_part = norm_back(d_normed_one, unit_one, spread_one, gain_one)
    input_grad = d_middle + d_input_part
    attn_parts = tuple(
        (g.reshape(dp_devices, seq_devices, -1) for g in (grad_gain_one, grad_qkv, grad_proj))
    )
    attn_mid = (
        lax.psum_scatter(
            attn_parts[0].astype(jnp.bfloat16), "seq", scatter_dimension=1, tiled=True
        ).astype(jnp.float32),
        lax.psum_scatter(
            attn_parts[1].astype(jnp.bfloat16), "seq", scatter_dimension=1, tiled=True
        ).astype(jnp.float32),
        lax.psum_scatter(
            attn_parts[2].astype(jnp.bfloat16), "seq", scatter_dimension=1, tiled=True
        ).astype(jnp.float32),
    )
    attn_shards = (
        lax.psum_scatter(
            attn_mid[0].astype(jnp.bfloat16), "dp", scatter_dimension=0, tiled=True
        ).astype(jnp.float32),
        lax.psum_scatter(
            attn_mid[1].astype(jnp.bfloat16), "dp", scatter_dimension=0, tiled=True
        ).astype(jnp.float32),
        lax.psum_scatter(
            attn_mid[2].astype(jnp.bfloat16), "dp", scatter_dimension=0, tiled=True
        ).astype(jnp.float32),
    )
    return (
        output.reshape(1, tok_rows, model_width),
        input_grad.reshape(1, tok_rows, model_width),
        attn_shards[0].reshape(-1),
        attn_shards[1].reshape(-1),
        attn_shards[2].reshape(-1),
        mlp_shards[0].reshape(-1),
        mlp_shards[1].reshape(-1),
        mlp_shards[2].reshape(-1),
    )


MESH_IDS = pl.DeviceIdType.MESH
TOK = 128
WIDTH = 1024
PART = FF // 32
PAD = 96
HID = 8 * PAD
QKV = 3 * 256
BF = jnp.bfloat16
F32 = jnp.float32


def dot_nn(a, b):
    return lax.dot_general(a, b, (((1,), (0,)), ((), ())), preferred_element_type=F32)


def turned(u, low_half):
    return jnp.where(low_half, pltpu.roll(u, 96, axis=1), pltpu.roll(u, 32, axis=1))


def layer_kernel(
    n_sems,
    x_ref,
    cot_in,
    seg_in,
    cos_ref,
    sin_ref,
    wq_in,
    wo_in,
    wi_in,
    wd_in,
    out_ref,
    ig_ref,
    gq_ref,
    go_ref,
    gi_ref,
    gd_ref,
    seg_buf,
    n1,
    n2,
    cot,
    db,
    wq,
    wo,
    wi,
    wd,
    unit1,
    inv1,
    unit2,
    inv2,
    middle,
    dmid,
    q_buf,
    k_buf,
    v_buf,
    probs,
    att,
    datt,
    up_a,
    up_b,
    hidden,
    d_up,
    dqkv,
    ps,
    ps_in,
    ps_far,
    ps_back,
    gq,
    go,
    gi,
    gd,
    rq1,
    rq2,
    rq3,
    ro1,
    ro2,
    ro3,
    ri1,
    ri2,
    ri3,
    rd1,
    rd2,
    rd3,
    send_sems,
    recv_sems,
):
    dp, c = lax.axis_index("dp"), lax.axis_index("seq")
    x, y, z = lax.rem(dp, 2), lax.rem(dp // 2, 2), dp // 4
    zh, zp = z // 2, lax.rem(z, 2)
    role = zp * 2 + c

    def device(X, Y, Z, C):
        return (Z * 4 + Y * 2 + X, C)

    core_dev = device(x, y, z, 1 - c)
    pair_dev = device(x, y, zh * 2 + 1 - zp, c)
    diag_dev = device(x, y, zh * 2 + 1 - zp, 1 - c)
    half_dev = device(x, y, (1 - zh) * 2 + zp, c)
    x_dev = device(1 - x, y, z, c)
    y_dev = device(x, 1 - y, z, c)

    barrier = pltpu.get_barrier_semaphore()
    for dev in (core_dev, pair_dev, diag_dev, half_dev, x_dev, y_dev):
        pl.semaphore_signal(barrier, inc=1, device_id=dev, device_id_type=MESH_IDS)
    pl.semaphore_wait(barrier, 6)

    sent = []

    def copy_to(src, dst, dev, keep=True):
        i = n_sems[0]
        n_sems[0] += 1
        cp = pltpu.make_async_remote_copy(
            src_ref=src,
            dst_ref=dst,
            send_sem=send_sems.at[i],
            recv_sem=recv_sems.at[i],
            device_id=dev,
            device_id_type=MESH_IDS,
        )
        if keep:
            sent.append(cp)
        return cp

    def go_copy(src, dst, dev):
        cp = copy_to(src, dst, dev)
        cp.start()
        return cp


    others = (
        (core_dev, zp * 2 + 1 - c),
        (pair_dev, (1 - zp) * 2 + c),
        (diag_dev, (1 - zp) * 2 + 1 - c),
    )

    def spread(own, buf):
        cps = [go_copy(own.at[r], buf.at[z, y, x, c], dev) for dev, r in others]
        buf[z, y, x, c] = own[role]
        return cps

    class Gather:
        def __init__(self, buf, kind, cols):
            self.buf, self.kind = buf, kind
            self.halves = (pl.ds(0, cols // 2), pl.ds(cols // 2, cols // 2))

        def own(self, which, cut):
            b = self.buf
            if self.kind == "rows":
                return b.at[pl.ds(2 * which, 2), y, x, :, :, cut]
            if self.kind == "down":
                return b.at[which, y, x, :, cut]
            return b.at[y, x, :, :, cut]

        def line(self, which, cut, first):
            b = self.buf
            if self.kind == "rows":
                at = pl.ds(2 * which, 2)
                return b.at[at, y, :, :, :, cut] if first == 0 else b.at[at, :, x, :, :, cut]
            if self.kind == "down":
                return b.at[which, y, :, :, cut] if first == 0 else b.at[which, :, x, :, cut]
            return b.at[y, :, :, :, cut] if first == 0 else b.at[:, x, :, :, cut]

        def same(self, ref, dev):
            return go_copy(ref, ref, dev)

        def first(self):
            self.across = [self.same(self.own(zh, cut), half_dev) for cut in self.halves]
            self.a = [
                self.same(self.own(zh, cut), dev) for cut, dev in zip(self.halves, (x_dev, y_dev))
            ]

        def second(self):
            self.b = []
            for i, dev in enumerate((y_dev, x_dev)):
                self.a[i].wait_recv()
                self.b.append(self.same(self.line(zh, self.halves[i], i), dev))

        def third(self):
            self.a2 = []
            for i, dev in enumerate((x_dev, y_dev)):
                self.across[i].wait_recv()
                self.a2.append(self.same(self.own(1 - zh, self.halves[i]), dev))

        def fourth(self):
            self.b2 = []
            for i, dev in enumerate((y_dev, x_dev)):
                self.a2[i].wait_recv()
                self.b2.append(self.same(self.line(1 - zh, self.halves[i], i), dev))

        def done(self):
            for cp in self.b + self.b2:
                cp.wait_recv()

    class GatherOut(Gather):
        def first(self):
            self.s0 = copy_to(wo_in, self.buf.at[y, x, c], core_dev, keep=False)

            @pl.when(c != zh)
            def _():
                self.s0.start()
                self.s0.wait_send()

            self.s1 = copy_to(self.buf.at[y, x], self.buf.at[y, x], half_dev, keep=False)

            @pl.when(c == zh)
            def _():
                self.buf[y, x, c] = wo_in[...]
                self.s0.wait_recv()
                self.s1.start()
                self.s1.wait_send()

        def third(self):
            @pl.when(c != zh)
            def _():
                self.s1.wait_recv()

            self.a = [
                self.same(self.own(0, cut), dev) for cut, dev in zip(self.halves, (x_dev, y_dev))
            ]

        def fourth(self):
            self.b = []
            for i, dev in enumerate((y_dev, x_dev)):
                self.a[i].wait_recv()
                self.b.append(self.same(self.line(0, self.halves[i], i), dev))

        def done(self):
            for cp in self.b:
                cp.wait_recv()


    class Share:
        def __init__(self, buf):
            self.buf = buf
            self.to_core = go_copy(buf.at[zp, c], buf.at[zp, c], core_dev)
            self.to_pair = go_copy(buf.at[zp, c], buf.at[zp, c], pair_dev)

        def forward(self):
            self.to_pair.wait_recv()
            self.fwd = go_copy(self.buf.at[1 - zp, c], self.buf.at[1 - zp, c], core_dev)

        def done(self):
            self.to_core.wait_recv()
            self.fwd.wait_recv()

    class Reduce:
        def __init__(self, i):
            self.i = i
            self.mine = go_copy(ps.at[i, :, 1 - c], ps_in.at[i], core_dev)

        def cross(self):
            i = self.i
            self.mine.wait_recv()
            ps_far[i] = (ps[i, 1 - zp, c].astype(F32) + ps_in[i, 1 - zp].astype(F32)).astype(BF)
            self.far = go_copy(ps_far.at[i], ps_back.at[i], pair_dev)

        def total(self):
            i = self.i
            near = ps[i, zp, c].astype(F32) + ps_in[i, zp].astype(F32)
            self.far.wait_recv()
            return near + ps_back[i].astype(F32)


    def add_into(pairs):
        for target, extra in pairs:
            t, e = target, extra
            t[...] = (t[...].astype(F32) + e[...].astype(F32)).astype(BF)

    class Scatter:
        def __init__(self, buf, kind, cols, r1, r2, r3):
            self.buf, self.kind, self.r1, self.r2, self.r3 = buf, kind, r1, r2, r3
            self.halves = (pl.ds(0, cols // 2), pl.ds(cols // 2, cols // 2))

        def row(self, i, at, cut):
            b = self.buf
            if self.kind == "rows":
                return b.at[:, at, :, :, :, cut] if i == 0 else b.at[:, :, at, :, :, cut]
            if self.kind == "down":
                return b.at[:, at, :, :, cut] if i == 0 else b.at[:, :, at, :, cut]
            return b.at[at, :, :, :, cut] if i == 0 else b.at[:, at, :, :, cut]

        def spot(self, Y, X, cut):
            b = self.buf
            if self.kind == "rows":
                return b.at[:, Y, X, :, :, cut]
            if self.kind == "down":
                return b.at[:, Y, X, :, cut]
            return b.at[Y, X, :, :, cut]

        def first(self):
            self.c1 = []
            for i, (at, dev) in enumerate(((1 - y, y_dev), (1 - x, x_dev))):
                self.c1.append(go_copy(self.row(i, at, self.halves[i]), self.r1.at[i], dev))

        def second(self):
            self.c2 = []
            for i, dev in enumerate((x_dev, y_dev)):
                self.c1[i].wait_recv()
                at = y if i == 0 else x
                mine = self.row(i, at, self.halves[i])
                got = self.r1.at[i]

                def body(j, carry, mine=mine, got=got):
                    add_into([(mine.at[j], got.at[j])])
                    return carry

                lax.fori_loop(0, got.shape[0], body, 0)
                there = (y, 1 - x) if i == 0 else (1 - y, x)
                self.c2.append(
                    go_copy(self.spot(*there, self.halves[i]), self.r2.at[i], dev)
                )

        def third(self):
            for i in range(2):
                self.c2[i].wait_recv()
                mine = self.spot(y, x, self.halves[i])
                got = self.r2.at[i]

                def body(j, carry, mine=mine, got=got):
                    add_into([(mine.at[j], got.at[j])])
                    return carry

                lax.fori_loop(0, got.shape[0], body, 0)
            self.over()

        def over(self):
            b = self.buf
            src = (
                b.at[pl.ds(2 * (1 - zh), 2), y, x]
                if self.kind == "rows"
                else b.at[1 - zh, y, x]
            )
            self.c3 = go_copy(src, self.r3, half_dev)

    class ScatterRows(Scatter):
        def fourth(self, out):
            self.c3.wait_recv()
            self.out = out
            for i in range(2):
                add_into([(self.buf.at[2 * zh + i, y, x], self.r3.at[i])])
            self.c4 = []
            for dev, r in others:
                src = self.buf.at[2 * zh + r // 2, y, x, lax.rem(r, 2)]
                self.c4.append(go_copy(src, out.at[role], dev))
            out[role] = self.buf[z, y, x, c]

        def done(self):
            for cp in self.c4:
                cp.wait_recv()

    class ScatterDown(Scatter):
        def fourth(self, out):
            self.c3.wait_recv()
            out[...] = self.buf[zh, y, x].astype(F32) + self.r3[...].astype(F32)

    class ScatterOut(Scatter):
        def over(self):
            self.c3 = copy_to(self.buf.at[y, x], self.r3, half_dev, keep=False)

            @pl.when(c != zh)
            def _():
                self.c3.start()
                self.c3.wait_send()

        def fourth(self, out):
            self.c4 = copy_to(self.r3.at[1 - c], out, core_dev, keep=False)

            @pl.when(c == zh)
            def _():
                self.c3.wait_recv()
                for i in range(2):
                    add_into([(self.r3.at[i], self.buf.at[y, x, i])])
                self.c4.start()
                out[...] = self.r3[c]
                self.c4.wait_send()

            @pl.when(c != zh)
            def _():
                self.c4.wait_recv()

    s_q = spread(wq_in, wq)
    seg_buf[zp, c] = seg_in[...]
    s_seg = [go_copy(seg_buf.at[zp, c], seg_buf.at[zp, c], dev) for dev, _ in others]

    tokens = x_ref[...].astype(F32)
    centred = tokens - jnp.mean(tokens, axis=-1, keepdims=True)
    inv = lax.rsqrt(jnp.mean(centred * centred, axis=-1, keepdims=True) + EPSILON)
    unit = centred * inv
    unit1[...] = unit
    inv1[...] = jnp.broadcast_to(inv, (TOK, 128))
    n1[zp, c] = unit.astype(BF)
    share_n1 = Share(n1)

    g_q = Gather(wq, "rows", QKV)
    g_i = Gather(wi, "rows", 2 * HID)
    g_d = Gather(wd, "down", WIDTH)
    g_o = GatherOut(wo, "out", WIDTH)

    for cp in s_q:
        cp.wait_recv()
    g_q.first()
    s_i = spread(wi_in, wi)
    g_o.first()
    g_q.second()
    share_n1.forward()
    g_q.third()
    for cp in s_i:
        cp.wait_recv()
    g_i.first()
    cot[zp, c] = cot_in[...]
    share_cot = Share(cot)
    g_o.third()
    g_q.fourth()
    g_o.fourth()
    wd[zh, y, x] = wd_in[...]
    share_n1.done()
    for cp in s_seg:
        cp.wait_recv()
    g_q.done()

    lanes = lax.broadcasted_iota(jnp.int32, (1, 128), 1)
    low_half = lax.rem(lanes, 64) < 32
    first_head = lanes < 64

    def qkv_step(s, carry):
        rows = n1[s].reshape(256, WIDTH)
        for part, dst in enumerate((q_buf, k_buf, v_buf)):
            for j in range(2):
                at = part * 256 + j * 128
                w = wq[:, :, :, :, :, pl.ds(at, 128)].reshape(WIDTH, 128)
                u = dot_nn(rows, w)
                if part < 2:
                    u = u * cos_ref[...] + turned(u, low_half) * sin_ref[...]
                dst[s, j] = u.astype(BF)
        return carry

    lax.fori_loop(0, 2, qkv_step, 0)
    g_i.second()
    share_cot.forward()

    def only(head, u):
        return jnp.where(first_head if head == 0 else ~first_head, u, jnp.zeros_like(u))

    def attend(i, carry):
        s, j = i // 2, lax.rem(i, 2)
        q, k, v = q_buf[s, j], k_buf[s, j], v_buf[s, j]
        seg_row = jnp.concatenate([seg_buf[s, 0, 0:1], seg_buf[s, 1, 0:1]], axis=1)
        seg_col = jnp.broadcast_to(seg_row, (128, 256)).T[:, 0:1]
        same = seg_col == seg_row
        heads = []
        for h in range(2):
            scores = matmul_nt(only(h, q), k) * 0.125
            scores = jnp.where(same, scores, -1e30)
            weights = jnp.exp(scores - jnp.max(scores, axis=-1, keepdims=True))
            p = weights * (1.0 / jnp.sum(weights, axis=-1, keepdims=True))
            probs[i, h] = p
            heads.append(dot_nn(p.astype(BF), v))
        att[s, j] = jnp.where(first_head, heads[0], heads[1]).astype(BF)
        return carry

    lax.fori_loop(0, 4, attend, 0)
    g_o.done()

    def att_rows(s):
        return jnp.concatenate([att[s, 0], att[s, 1]], axis=1)

    def branch(s, carry):
        w = wo[...].reshape(256, WIDTH)
        ps[0, s] = dot_nn(att_rows(s), w).astype(BF).reshape(2, TOK, WIDTH)
        return carry

    lax.fori_loop(0, 2, branch, 0)
    red = Reduce(0)
    red.cross()
    g_i.third()
    g_d.first()
    share_cot.done()
    mid = x_ref[...].astype(F32) + red.total()
    middle[...] = mid
    centred = mid - jnp.mean(mid, axis=-1, keepdims=True)
    inv = lax.rsqrt(jnp.mean(centred * centred, axis=-1, keepdims=True) + EPSILON)
    unit = centred * inv
    unit2[...] = unit
    inv2[...] = jnp.broadcast_to(inv, (TOK, 128))
    n2[zp, c] = unit.astype(BF)
    share_n2 = Share(n2)
    g_i.fourth()
    g_d.second()
    share_n2.forward()
    g_d.third()
    share_n2.done()
    g_i.done()
    g_d.fourth()

    def upper(j, carry):
        at = pl.multiple_of(j * 256, 256)
        for s in range(2):
            rows = n2[s].reshape(256, WIDTH)
            inner = dot_nn(rows, wi[:, :, :, :, :, pl.ds(at, 256)].reshape(WIDTH, 256))
            gate = dot_nn(
                rows,
                wi[:, :, :, :, :, pl.ds(pl.multiple_of(HID + at, 256), 256)].reshape(WIDTH, 256),
            )
            cdf = 0.5 * (1.0 + lax.erf(inner * math.sqrt(0.5)))
            slope = cdf + inner * jnp.exp(-0.5 * inner * inner) * (1.0 / math.sqrt(2 * math.pi))
            bent = inner * cdf
            up_a[s, :, pl.ds(at, 256)] = gate * slope
            up_b[s, :, pl.ds(at, 256)] = bent
            hidden[s, :, pl.ds(at, 256)] = (bent * gate).astype(BF)
        return carry

    lax.fori_loop(0, HID // 256, upper, 0)

    def down_grad(i, carry):
        lhs = hidden[:, :, pl.ds(pl.multiple_of(i * 384, 384), 384)].reshape(512, 384)
        for j in range(2):
            rhs = cot[:, :, :, pl.ds(j * 512, 512)].reshape(512, 512)
            gd[i, :, :, :, pl.ds(j * 512, 512)] = (
                matmul_tn(lhs, rhs).astype(BF).reshape(2, 2, PAD, 512)
            )
        return carry

    lax.fori_loop(0, 2, down_grad, 0)
    r_d = ScatterDown(gd, "down", WIDTH, rd1, rd2, rd3)
    r_d.first()
    g_d.done()

    def hidden_grad(i, carry):
        w = wd[i].reshape(384, WIDTH)
        at = pl.multiple_of(i * 384, 384)
        for s in range(2):
            dh = matmul_nt(cot[s].reshape(256, WIDTH), w)
            d_up[s, :, pl.ds(at, 384)] = (dh * up_a[s, :, pl.ds(at, 384)]).astype(BF)
            d_up[s, :, pl.ds(pl.multiple_of(HID + at, 384), 384)] = (
                dh * up_b[s, :, pl.ds(at, 384)]
            ).astype(BF)
        return carry

    lax.fori_loop(0, 2, hidden_grad, 0)

    def normed_two_grad(i, carry):
        w = wi[i].reshape(256, 2 * HID)
        at = pl.multiple_of(i * 256, 256)
        for s in range(2):
            ps[1, s, :, :, pl.ds(at, 256)] = (
                matmul_nt(d_up[s], w).astype(BF).reshape(2, TOK, 256)
            )
        return carry

    lax.fori_loop(0, 4, normed_two_grad, 0)
    red = Reduce(1)
    r_d.second()

    def in_grad(i, carry):
        lhs = n2[:, :, :, pl.ds(pl.multiple_of(i * 256, 256), 256)].reshape(512, 256)
        for j in range(3):
            rhs = d_up[:, :, pl.ds(j * 512, 512)].reshape(512, 512)
            gi[i, :, :, :, :, pl.ds(j * 512, 512)] = (
                matmul_tn(lhs, rhs).astype(BF).reshape(2, 2, 2, 32, 512)
            )
        return carry

    lax.fori_loop(0, 4, in_grad, 0)
    red.cross()
    r_i = ScatterRows(gi, "rows", 2 * HID, ri1, ri2, ri3)
    r_i.first()

    e = red.total()
    n = unit2[...]
    d_middle = cot_in[...].astype(F32) + inv2[:, 0:1] * (
        e
        - jnp.mean(e, axis=-1, keepdims=True)
        - n * jnp.mean(e * n, axis=-1, keepdims=True)
    )
    dmid[...] = d_middle
    db[zp, c] = d_middle.astype(BF)
    share_db = Share(db)
    r_d.third()

    def down(i, carry):
        w = wd[...].reshape(HID, WIDTH)
        ps[2, i] = dot_nn(hidden[i], w).astype(BF).reshape(2, TOK, WIDTH)
        return carry

    lax.fori_loop(0, 2, down, 0)
    red_out = Reduce(2)
    share_db.forward()
    red_out.cross()
    r_i.second()
    r_d.fourth(gd_ref)
    share_db.done()

    def attended_grad(s, carry):
        rows = db[s].reshape(256, WIDTH)
        da = matmul_nt(rows, wo[...].reshape(256, WIDTH)).astype(BF)
        datt[s, 0] = da[:, 0:128]
        datt[s, 1] = da[:, 128:256]
        return carry

    lax.fori_loop(0, 2, attended_grad, 0)

    def attend_back(i, carry):
        s, j = i // 2, lax.rem(i, 2)
        q, k, v, da = q_buf[s, j], k_buf[s, j], v_buf[s, j], datt[s, j]
        dq, dk, dv = [], [], []
        for h in range(2):
            p = probs[i, h]
            dprob = matmul_nt(only(h, da), v)
            delta = jnp.sum(p * dprob, axis=-1, keepdims=True)
            ds = (p * (dprob - delta)).astype(BF)
            dq.append(dot_nn(ds, k))
            dk.append(matmul_tn(ds, q))
            dv.append(matmul_tn(p.astype(BF), da))
        for part, pieces in enumerate((dq, dk, dv)):
            u = jnp.where(first_head, pieces[0], pieces[1])
            if part < 2:
                u = u * 0.125
                u = u * cos_ref[...] - turned(u, low_half) * sin_ref[...]
            dqkv[part, j, s] = u.astype(BF)
        return carry

    lax.fori_loop(0, 4, attend_back, 0)
    r_i.third()

    def first_grads(i, carry):
        w = wq[i].reshape(256, QKV)
        at = pl.multiple_of(i * 256, 256)
        for s in range(2):
            rows = jnp.concatenate([dqkv[p, j, s] for p in range(3) for j in range(2)], axis=1)
            ps[3, s, :, :, pl.ds(at, 256)] = (
                matmul_nt(rows, w).astype(BF).reshape(2, TOK, 256)
            )
        return carry

    lax.fori_loop(0, 4, first_grads, 0)
    red_in = Reduce(3)

    def qkv_grad(i, carry):
        lhs = n1[:, :, :, pl.ds(pl.multiple_of(i * 256, 256), 256)].reshape(512, 256)
        for p in range(3):
            for j in range(2):
                rhs = dqkv[p, j].reshape(512, 128)
                gq[i, :, :, :, :, pl.ds(p * 256 + j * 128, 128)] = (
                    matmul_tn(lhs, rhs).astype(BF).reshape(2, 2, 2, 32, 128)
                )
        return carry

    lax.fori_loop(0, 4, qkv_grad, 0)
    r_q = ScatterRows(gq, "rows", QKV, rq1, rq2, rq3)
    r_q.first()

    lhs = att
    for j in range(2):
        for half in range(2):
            rhs = db[:, :, :, pl.ds(half * 512, 512)].reshape(512, 512)
            go[j, :, :, :, pl.ds(half * 512, 512)] = (
                matmul_tn(lhs[:, j].reshape(512, 128), rhs).astype(BF).reshape(2, 2, 32, 512)
            )
    r_o = ScatterOut(go, "out", WIDTH, ro1, ro2, ro3)
    r_o.first()
    red_in.cross()
    r_i.fourth(gi_ref)
    out_ref[...] = (middle[...] + red_out.total()).astype(BF)
    r_q.second()
    r_o.second()
    e = red_in.total()
    n = unit1[...]
    ig_ref[...] = dmid[...] + inv1[:, 0:1] * (
        e
        - jnp.mean(e, axis=-1, keepdims=True)
        - n * jnp.mean(e * n, axis=-1, keepdims=True)
    )
    r_q.third()
    r_o.third()
    r_q.fourth(gq_ref)
    r_o.fourth(go_ref)
    r_i.done()
    r_q.done()
    for cp in sent:
        cp.wait_send()


def block_device(inputs, segments, cotangent, ln1_gain, w_qkv, w_attn_out, ln2_gain, w_in, w_mlp_out):
    gain_one = ln1_gain.astype(F32)[:, None]
    gain_two = ln2_gain.astype(F32)[:, None]
    qkv_own = w_qkv.reshape(32, 3 * WIDTH).astype(F32)
    in_own = w_in.reshape(32, 2 * FF).astype(F32)
    wq_in = (
        (qkv_own * gain_one)
        .astype(BF)
        .reshape(32, 3, 2, 2, 256)
        .transpose(3, 2, 0, 1, 4)
        .reshape(4, 32, QKV)
    )
    wi_in = (in_own * gain_two).astype(BF).reshape(32, 2, 2, 2, 2, 2, 2, PART)
    wi_in = jnp.pad(wi_in, ((0, 0),) * 7 + ((0, PAD - PART),))
    wi_in = wi_in.transpose(3, 6, 0, 1, 2, 4, 5, 7).reshape(4, 32, 2 * HID)
    wd_in = jnp.pad(w_mlp_out.reshape(PART, WIDTH), ((0, PAD - PART), (0, 0)))
    wo_in = w_attn_out.reshape(32, WIDTH)
    seg = jnp.broadcast_to(segments.astype(F32), (8, TOK))
    cosines, sines = rope_tables(jnp.arange(2 * TOK, dtype=jnp.int32).astype(F32))
    signs = jnp.where(jnp.arange(HD) < HD // 2, -1.0, 1.0).astype(F32)
    cosines = jnp.tile(cosines, (1, 2))
    sines = jnp.tile(sines * signs, (1, 2))

    vm = pltpu.VMEM
    group = (2, 2, TOK, WIDTH)
    rows = (4, 2, 2, 2, 32)
    outs = pl.pallas_call(
        functools.partial(layer_kernel, [0]),
        out_shape=(
            jax.ShapeDtypeStruct((TOK, WIDTH), BF),
            jax.ShapeDtypeStruct((TOK, WIDTH), F32),
            jax.ShapeDtypeStruct((4, 32, QKV), BF),
            jax.ShapeDtypeStruct((32, WIDTH), BF),
            jax.ShapeDtypeStruct((4, 32, 2 * HID), BF),
            jax.ShapeDtypeStruct((PAD, WIDTH), F32),
        ),
        in_specs=[pl.BlockSpec(memory_space=vm)] * 9,
        out_specs=(pl.BlockSpec(memory_space=vm),) * 6,
        scratch_shapes=[
            vm((2, 2, 8, TOK), F32),
            vm(group, BF),
            vm(group, BF),
            vm(group, BF),
            vm(group, BF),
            vm(rows + (QKV,), BF),
            vm((2, 2, 2, 32, WIDTH), BF),
            vm(rows + (2 * HID,), BF),
            vm((2, 2, 2, PAD, WIDTH), BF),
            vm((TOK, WIDTH), F32),
            vm((TOK, 128), F32),
            vm((TOK, WIDTH), F32),
            vm((TOK, 128), F32),
            vm((TOK, WIDTH), F32),
            vm((TOK, WIDTH), F32),
            vm((2, 2, 256, 128), BF),
            vm((2, 2, 256, 128), BF),
            vm((2, 2, 256, 128), BF),
            vm((4, 2, 256, 256), F32),
            vm((2, 2, 256, 128), BF),
            vm((2, 2, 256, 128), BF),
            vm((2, 256, HID), F32),
            vm((2, 256, HID), F32),
            vm((2, 256, HID), BF),
            vm((2, 256, 2 * HID), BF),
            vm((3, 2, 2, 256, 128), BF),
            vm((4,) + group, BF),
            vm((4, 2, TOK, WIDTH), BF),
            vm((4, TOK, WIDTH), BF),
            vm((4, TOK, WIDTH), BF),
            vm(rows + (QKV,), BF),
            vm((2, 2, 2, 32, WIDTH), BF),
            vm(rows + (2 * HID,), BF),
            vm((2, 2, 2, PAD, WIDTH), BF),
            vm((2, 4, 2, 2, 32, QKV // 2), BF),
            vm((2, 4, 2, 32, QKV // 2), BF),
            vm((2, 2, 32, QKV), BF),
            vm((2, 2, 2, 32, WIDTH // 2), BF),
            vm((2, 2, 32, WIDTH // 2), BF),
            vm((2, 32, WIDTH), BF),
            vm((2, 4, 2, 2, 32, HID), BF),
            vm((2, 4, 2, 32, HID), BF),
            vm((2, 2, 32, 2 * HID), BF),
            vm((2, 2, 2, PAD, WIDTH // 2), BF),
            vm((2, 2, PAD, WIDTH // 2), BF),
            vm((PAD, WIDTH), BF),
            pltpu.SemaphoreType.DMA((N_COPIES,)),
            pltpu.SemaphoreType.DMA((N_COPIES,)),
        ],
        compiler_params=pltpu.CompilerParams(
            collective_id=0, has_side_effects=True, vmem_limit_bytes=60 * 2**20
        ),
    )(inputs[0], cotangent[0], seg, cosines, sines, wq_in, wo_in, wi_in, wd_in)
    output, input_grad, gq, go, gi, gd = outs

    raw_q = gq.astype(F32).reshape(2, 2, 32, 3, 256).transpose(2, 3, 1, 0, 4).reshape(32, 3 * WIDTH)
    raw_i = gi.astype(F32).reshape(2, 2, 32, 2, 2, 2, 2, PAD)[..., :PART]
    raw_i = raw_i.transpose(2, 3, 4, 0, 5, 6, 1, 7).reshape(32, 2 * FF)
    return (
        output[None],
        input_grad[None],
        jnp.sum(raw_q * qkv_own, axis=1),
        (raw_q * gain_one).reshape(-1),
        go.astype(F32).reshape(-1),
        jnp.sum(raw_i * in_own, axis=1),
        (raw_i * gain_two).reshape(-1),
        gd[:PART].reshape(-1),
    )


N_COPIES = 160


def solution(mesh):
    block = dict(mesh.shape) == {"dp": 16, "seq": 2}
    placed = (
        P("dp", "seq", None),
        P("dp", "seq"),
        P("dp", "seq", None),
        P(("dp", "seq")),
        P(("dp", "seq")),
        P(("dp", "seq")),
        P(("dp", "seq")),
        P(("dp", "seq")),
        P(("dp", "seq")),
    )
    return jax.shard_map(
        block_device if block else general_device,
        mesh=mesh,
        in_specs=placed,
        out_specs=(
            P("dp", "seq", None),
            P("dp", "seq", None),
            P(("dp", "seq")),
            P(("dp", "seq")),
            P(("dp", "seq")),
            P(("dp", "seq")),
            P(("dp", "seq")),
            P(("dp", "seq")),
        ),
        check_vma=False,
    )
```

```python
import functools
import math

import jax
import jax.numpy as jnp
import numpy as np
from jax import lax
from jax.experimental import pallas as pl
from jax.experimental.pallas import tpu as pltpu
from jax.sharding import PartitionSpec as P

HEADS = 16
HD = 64
FF = 2624


EPSILON = 1e-05
ROPE_BASE = 160000.0


def rope_tables(places):
    freqs = 1.0 / ROPE_BASE ** (jnp.arange(0, HD, 2, dtype=jnp.float32) / HD)
    angles = places[:, None] * freqs[None, :]
    angles = jnp.concatenate([angles, angles], axis=1)
    return (jnp.cos(angles), jnp.sin(angles))


def rotate(values_in, cosines, sines):
    halfway = values_in.shape[-1] // 2
    turned = jnp.concatenate([-values_in[..., halfway:], values_in[..., :halfway]], axis=-1)
    return values_in * cosines[:, None, :] + turned * sines[:, None, :]


def rotate_back(grads_in, cosines, sines):
    halfway = grads_in.shape[-1] // 2
    scaled = grads_in * sines[:, None, :]
    turned = jnp.concatenate([scaled[..., halfway:], -scaled[..., :halfway]], axis=-1)
    return grads_in * cosines[:, None, :] + turned


def norm_forward(values_in, gain):
    centred = values_in - jnp.mean(values_in, axis=-1, keepdims=True)
    inv_spread = lax.rsqrt(jnp.mean(centred * centred, axis=-1, keepdims=True) + EPSILON)
    unit_rows = centred * inv_spread
    return (unit_rows * gain, unit_rows, inv_spread)


def norm_back(grad_rows, unit_rows, inv_spread, gain):
    gain_grad = jnp.sum(grad_rows * unit_rows, axis=0)
    scaled = grad_rows * gain
    inner_mean = jnp.mean(scaled, axis=-1, keepdims=True)
    cross_mean = jnp.mean(scaled * unit_rows, axis=-1, keepdims=True)
    return (gain_grad, inv_spread * (scaled - inner_mean - unit_rows * cross_mean))


def matmul_tn(left, right):
    return lax.dot_general(
        left, right, (((0,), (0,)), ((), ())), preferred_element_type=jnp.float32
    )


def matmul_nt(left, right):
    return lax.dot_general(
        left, right, (((1,), (1,)), ((), ())), preferred_element_type=jnp.float32
    )


def masked_scores(query, key_block, seg_query, seg_block):
    scores = (
        jnp.einsum("qhd,khd->hqk", query, key_block, preferred_element_type=jnp.float32) * 0.125
    )
    same_doc = seg_query[:, None] == seg_block[None, :]
    return jnp.where(same_doc[None], scores, -1e30)


def gated(inner, gate):
    return jax.nn.gelu(inner, approximate=False) * gate


def general_device(inputs, segments, cotangent, ln1_gain, w_qkv, w_attn_out, ln2_gain, w_in, w_mlp_out):
    tok_rows = inputs.shape[1]
    model_width = inputs.shape[2]
    seq_devices = lax.axis_size("seq")
    dp_devices = lax.axis_size("dp")
    tokens_in = inputs[0].astype(jnp.float32)
    seg_send = segments.astype(jnp.bfloat16)
    seg_query = seg_send[0]
    gathered_attn = (
        lax.all_gather(ln1_gain, ("dp", "seq"), axis=0, tiled=True),
        lax.all_gather(w_qkv, ("dp", "seq"), axis=0, tiled=True),
        lax.all_gather(w_attn_out, ("dp", "seq"), axis=0, tiled=True),
    )
    gain_one = gathered_attn[0].astype(jnp.float32)
    qkv_mat = gathered_attn[1].reshape(model_width, 3 * model_width)
    proj_mat = gathered_attn[2].reshape(model_width, model_width)
    places = (lax.axis_index("seq") * tok_rows + jnp.arange(tok_rows, dtype=jnp.int32)).astype(
        jnp.float32
    )
    cosines, sines = rope_tables(places)
    normed_one, unit_one, spread_one = norm_forward(tokens_in, gain_one)
    normed_one_low = normed_one.astype(jnp.bfloat16)
    qkv_rows = jnp.dot(normed_one_low, qkv_mat, preferred_element_type=jnp.float32)
    query = rotate(qkv_rows[:, :model_width].reshape(tok_rows, HEADS, HD), cosines, sines).astype(
        jnp.bfloat16
    )
    key_rot = rotate(
        qkv_rows[:, model_width : 2 * model_width].reshape(tok_rows, HEADS, HD), cosines, sines
    ).astype(jnp.bfloat16)
    value_rows = qkv_rows[:, 2 * model_width :].astype(jnp.bfloat16)
    key_send = key_rot.reshape(1, tok_rows, model_width)
    value_send = value_rows.reshape(1, tok_rows, model_width)
    fwd_init = (
        jnp.full((HEADS, tok_rows), -1e30, jnp.float32),
        jnp.zeros((HEADS, tok_rows), jnp.float32),
        jnp.zeros((tok_rows, HEADS, HD), jnp.float32),
    )
    key_piece = lax.all_gather(key_send, "seq", axis=1, tiled=True)
    value_piece = lax.all_gather(value_send, "seq", axis=1, tiled=True)
    seg_piece = lax.all_gather(seg_send, "seq", axis=1, tiled=True)
    span = key_piece.shape[1]
    step_rows = math.gcd(span, 512)

    def one_block(block_id, inner_state):
        top_score, total, accum = inner_state
        begin = block_id * step_rows
        key_block = lax.dynamic_slice_in_dim(key_piece[0], begin, step_rows, 0).reshape(
            step_rows, HEADS, HD
        )
        value_block = lax.dynamic_slice_in_dim(value_piece[0], begin, step_rows, 0).reshape(
            step_rows, HEADS, HD
        )
        seg_block = lax.dynamic_slice_in_dim(seg_piece[0], begin, step_rows, 0)
        scores = masked_scores(query, key_block, seg_query, seg_block)
        new_top = jnp.maximum(top_score, jnp.max(scores, axis=-1))
        fading = jnp.exp(top_score - new_top)
        weights = jnp.exp(scores - new_top[..., None])
        total = total * fading + jnp.sum(weights, axis=-1)
        accum = accum * fading.T[:, :, None] + jnp.einsum(
            "hqk,khd->qhd",
            weights.astype(jnp.bfloat16),
            value_block,
            preferred_element_type=jnp.float32,
        )
        return (new_top, total, accum)

    fwd_state = lax.fori_loop(0, span // step_rows, one_block, fwd_init)
    run_top, run_total, run_accum = fwd_state
    log_total = run_top + jnp.log(run_total)
    attended = (run_accum / run_total.T[:, :, None]).astype(jnp.bfloat16)
    attended_rows = attended.reshape(tok_rows, model_width)
    middle = tokens_in + jnp.dot(attended_rows, proj_mat, preferred_element_type=jnp.float32)
    gathered_mlp = (
        lax.all_gather(ln2_gain, ("dp", "seq"), axis=0, tiled=True),
        lax.all_gather(w_in, ("dp", "seq"), axis=0, tiled=True),
        lax.all_gather(w_mlp_out, ("dp", "seq"), axis=0, tiled=True),
    )
    gain_two = gathered_mlp[0].astype(jnp.float32)
    in_mat = gathered_mlp[1].reshape(model_width, 2 * FF)
    down_mat = gathered_mlp[2].reshape(FF, model_width)
    normed_two, unit_two, spread_two = norm_forward(middle, gain_two)
    normed_two_low = normed_two.astype(jnp.bfloat16)
    upper = jnp.dot(normed_two_low, in_mat, preferred_element_type=jnp.float32)
    inner = upper[:, :FF]
    gate = upper[:, FF:]
    hidden_low = gated(inner, gate).astype(jnp.bfloat16)
    output = (middle + jnp.dot(hidden_low, down_mat, preferred_element_type=jnp.float32)).astype(
        jnp.bfloat16
    )
    gathered_mlp = (
        lax.all_gather(ln2_gain, ("dp", "seq"), axis=0, tiled=True),
        lax.all_gather(w_in, ("dp", "seq"), axis=0, tiled=True),
        lax.all_gather(w_mlp_out, ("dp", "seq"), axis=0, tiled=True),
    )
    gain_two = gathered_mlp[0].astype(jnp.float32)
    in_mat = gathered_mlp[1].reshape(model_width, 2 * FF)
    down_mat = gathered_mlp[2].reshape(FF, model_width)
    grad_low = cotangent[0]
    grad_rows = grad_low.astype(jnp.float32)
    d_hidden = matmul_nt(grad_low, down_mat)
    grad_down = matmul_tn(hidden_low, grad_low)
    gated_value, pull = jax.vjp(gated, inner, gate)
    d_inner, d_gate = pull(d_hidden)
    d_upper_low = jnp.concatenate([d_inner, d_gate], axis=1).astype(jnp.bfloat16)
    grad_in = matmul_tn(normed_two_low, d_upper_low)
    d_normed_two = matmul_nt(d_upper_low, in_mat)
    grad_gain_two, d_middle_part = norm_back(d_normed_two, unit_two, spread_two, gain_two)
    d_middle = grad_rows + d_middle_part
    mlp_parts = tuple(
        (g.reshape(dp_devices, seq_devices, -1) for g in (grad_gain_two, grad_in, grad_down))
    )
    mlp_mid = (
        lax.psum_scatter(
            mlp_parts[0].astype(jnp.bfloat16), "seq", scatter_dimension=1, tiled=True
        ).astype(jnp.float32),
        lax.psum_scatter(
            mlp_parts[1].astype(jnp.bfloat16), "seq", scatter_dimension=1, tiled=True
        ).astype(jnp.float32),
        lax.psum_scatter(
            mlp_parts[2].astype(jnp.bfloat16), "seq", scatter_dimension=1, tiled=True
        ).astype(jnp.float32),
    )
    mlp_shards = (
        lax.psum_scatter(
            mlp_mid[0].astype(jnp.bfloat16), "dp", scatter_dimension=0, tiled=True
        ).astype(jnp.float32),
        lax.psum_scatter(
            mlp_mid[1].astype(jnp.bfloat16), "dp", scatter_dimension=0, tiled=True
        ).astype(jnp.float32),
        lax.psum_scatter(
            mlp_mid[2].astype(jnp.bfloat16), "dp", scatter_dimension=0, tiled=True
        ).astype(jnp.float32),
    )
    gathered_attn = (
        lax.all_gather(ln1_gain, ("dp", "seq"), axis=0, tiled=True),
        lax.all_gather(w_qkv, ("dp", "seq"), axis=0, tiled=True),
        lax.all_gather(w_attn_out, ("dp", "seq"), axis=0, tiled=True),
    )
    gain_one = gathered_attn[0].astype(jnp.float32)
    qkv_mat = gathered_attn[1].reshape(model_width, 3 * model_width)
    proj_mat = gathered_attn[2].reshape(model_width, model_width)
    d_branch_low = d_middle.astype(jnp.bfloat16)
    grad_proj = matmul_tn(attended_rows, d_branch_low)
    d_attended = matmul_nt(d_branch_low, proj_mat).astype(jnp.bfloat16).reshape(tok_rows, HEADS, HD)
    delta_rows = jnp.einsum(
        "qhd,qhd->hq", d_attended.astype(jnp.float32), attended.astype(jnp.float32)
    )
    back_init = (
        jnp.zeros((tok_rows, HEADS, HD), jnp.float32),
        jnp.zeros((tok_rows * seq_devices, 2 * model_width), jnp.float32),
    )
    attend_key_piece = lax.all_gather(key_send, "seq", axis=1, tiled=True)
    attend_value_piece = lax.all_gather(value_send, "seq", axis=1, tiled=True)
    attend_seg_piece = lax.all_gather(seg_send, "seq", axis=1, tiled=True)
    span = attend_key_piece.shape[1]
    attend_step_rows = math.gcd(span, 512)

    def one_block(block_id, inner_state):
        grad_query, grad_kv = inner_state
        begin = block_id * attend_step_rows
        key_block = lax.dynamic_slice_in_dim(
            attend_key_piece[0], begin, attend_step_rows, 0
        ).reshape(attend_step_rows, HEADS, HD)
        value_block = lax.dynamic_slice_in_dim(
            attend_value_piece[0], begin, attend_step_rows, 0
        ).reshape(attend_step_rows, HEADS, HD)
        seg_block = lax.dynamic_slice_in_dim(attend_seg_piece[0], begin, attend_step_rows, 0)
        scores = masked_scores(query, key_block, seg_query, seg_block)
        probs = jnp.exp(scores - log_total[..., None])
        probs_low = probs.astype(jnp.bfloat16)
        value_grad = jnp.einsum(
            "hqk,qhd->khd", probs_low, d_attended, preferred_element_type=jnp.float32
        )
        d_probs = jnp.einsum(
            "qhd,khd->hqk", d_attended, value_block, preferred_element_type=jnp.float32
        )
        d_scores = (probs * (d_probs - delta_rows[..., None])).astype(jnp.bfloat16)
        grad_query = (
            grad_query
            + jnp.einsum("hqk,khd->qhd", d_scores, key_block, preferred_element_type=jnp.float32)
            * 0.125
        )
        key_grad = (
            jnp.einsum("hqk,qhd->khd", d_scores, query, preferred_element_type=jnp.float32) * 0.125
        )
        block_grads = jnp.concatenate(
            [
                key_grad.reshape(attend_step_rows, model_width),
                value_grad.reshape(attend_step_rows, model_width),
            ],
            axis=1,
        )
        grad_kv = lax.dynamic_update_slice_in_dim(grad_kv, block_grads, begin, 0)
        return (grad_query, grad_kv)

    back_state = lax.fori_loop(0, span // attend_step_rows, one_block, back_init)
    kv_grads = lax.psum_scatter(
        back_state[1].astype(jnp.bfloat16), "seq", scatter_dimension=0, tiled=True
    ).astype(jnp.float32)
    d_query = rotate_back(back_state[0], cosines, sines).reshape(tok_rows, model_width)
    d_key = rotate_back(
        kv_grads[:, :model_width].reshape(tok_rows, HEADS, HD), cosines, sines
    ).reshape(tok_rows, model_width)
    d_qkv_low = jnp.concatenate([d_query, d_key, kv_grads[:, model_width:]], axis=1).astype(
        jnp.bfloat16
    )
    grad_qkv = matmul_tn(normed_one_low, d_qkv_low)
    d_normed_one = matmul_nt(d_qkv_low, qkv_mat)
    grad_gain_one, d_input_part = norm_back(d_normed_one, unit_one, spread_one, gain_one)
    input_grad = d_middle + d_input_part
    attn_parts = tuple(
        (g.reshape(dp_devices, seq_devices, -1) for g in (grad_gain_one, grad_qkv, grad_proj))
    )
    attn_mid = (
        lax.psum_scatter(
            attn_parts[0].astype(jnp.bfloat16), "seq", scatter_dimension=1, tiled=True
        ).astype(jnp.float32),
        lax.psum_scatter(
            attn_parts[1].astype(jnp.bfloat16), "seq", scatter_dimension=1, tiled=True
        ).astype(jnp.float32),
        lax.psum_scatter(
            attn_parts[2].astype(jnp.bfloat16), "seq", scatter_dimension=1, tiled=True
        ).astype(jnp.float32),
    )
    attn_shards = (
        lax.psum_scatter(
            attn_mid[0].astype(jnp.bfloat16), "dp", scatter_dimension=0, tiled=True
        ).astype(jnp.float32),
        lax.psum_scatter(
            attn_mid[1].astype(jnp.bfloat16), "dp", scatter_dimension=0, tiled=True
        ).astype(jnp.float32),
        lax.psum_scatter(
            attn_mid[2].astype(jnp.bfloat16), "dp", scatter_dimension=0, tiled=True
        ).astype(jnp.float32),
    )
    return (
        output.reshape(1, tok_rows, model_width),
        input_grad.reshape(1, tok_rows, model_width),
        attn_shards[0].reshape(-1),
        attn_shards[1].reshape(-1),
        attn_shards[2].reshape(-1),
        mlp_shards[0].reshape(-1),
        mlp_shards[1].reshape(-1),
        mlp_shards[2].reshape(-1),
    )


MESH_IDS = pl.DeviceIdType.MESH
TOK = 128
WIDTH = 1024
PART = FF // 32
PAD = 96
HID = 8 * PAD
QKV = 3 * 256
BF = jnp.bfloat16
F32 = jnp.float32


def dot_nn(a, b):
    return lax.dot_general(a, b, (((1,), (0,)), ((), ())), preferred_element_type=F32)


def turned(u, low_half):
    return jnp.where(low_half, pltpu.roll(u, 96, axis=1), pltpu.roll(u, 32, axis=1))


def column(gain_ref):
    square = jnp.broadcast_to(gain_ref[...].astype(F32), (32, 32))
    rows = lax.broadcasted_iota(jnp.int32, (32, 32), 0)
    cols = lax.broadcasted_iota(jnp.int32, (32, 32), 1)
    return jnp.sum(jnp.where(rows == cols, square, 0.0), axis=1, keepdims=True)


def owner(r, k):
    return k // 4 * 16 + r // 2 * 8 + k // 2 % 2 * 4 + k % 2 * 2 + r % 2


def runs(places):
    found = []
    for lane, place in enumerate(places):
        if place is None:
            continue
        tile, shift = place[0], (place[1] - lane) % 128
        if found and found[-1][:2] == (tile, shift) and found[-1][3] == lane:
            found[-1] = found[-1][:3] + (lane + 1,)
        else:
            found.append((tile, shift, lane, lane + 1))
    return found


def in_moves(r, u):
    places = []
    for at in range(u * 128, u * 128 + 128):
        gate, rest = divmod(at, HID)
        k, i = divmod(rest, PAD)
        col = gate * FF + PART * owner(r, k) + i
        places.append(divmod(col, 128) if i < PART else None)
    return runs(places)


def out_moves(t):
    spots = {owner(r, k): (r, k) for r in range(4) for k in range(8)}
    places = []
    for col in range(t * 128, t * 128 + 128):
        gate, rest = divmod(col, FF)
        device, i = divmod(rest, PART)
        r, k = spots[device]
        u, lane = divmod(gate * HID + k * PAD + i, 128)
        places.append(((r, u), lane))
    return runs(places)


def moved(moves, load):
    lanes = lax.broadcasted_iota(jnp.int32, (1, 128), 1)
    out = jnp.zeros((32, 128), F32)
    for tile, shift, low, high in moves:
        piece = load(tile)
        if shift:
            piece = pltpu.roll(piece, 128 - shift, axis=1)
        out = jnp.where((lanes >= low) & (lanes < high), piece, out)
    return out


def finish_kernel(
    gq_in,
    go_in,
    gi_in,
    gd_in,
    out_in,
    ig_in,
    gain1_in,
    gain2_in,
    wq_flat,
    wi_flat,
    out_ref,
    ig_ref,
    gain1_ref,
    gq_ref,
    go_ref,
    gain2_ref,
    gi_ref,
    gd_ref,
    lines,
    gq_raw,
    go_raw,
    gi_raw,
    gd_raw,
    wq_raw,
    wi_raw,
    gq_own,
    go_own,
    gi_own,
    gd_own,
    ig_raw,
    out_raw,
    sems,
):
    count = [0]

    def start(src, dst):
        cp = pltpu.make_async_copy(src, dst, sems.at[count[0]])
        count[0] += 1
        cp.start()
        return cp

    gi_here = start(gi_in, gi_raw)
    wi_here = start(wi_flat, wi_raw)
    gq_here = start(gq_in, gq_raw)
    wq_here = start(wq_flat, wq_raw)
    gd_here = start(gd_in, gd_raw)
    go_here = start(go_in, go_raw)
    ig_here = start(ig_in, ig_raw)
    out_here = start(out_in, out_raw)
    written = []
    rows = lax.broadcasted_iota(jnp.int32, (32, 32), 0)
    cols = lax.broadcasted_iota(jnp.int32, (32, 32), 1)

    def line(total):
        total = jnp.sum(total, axis=1, keepdims=True)
        return jnp.sum(jnp.where(rows == cols, total, 0.0), axis=0, keepdims=True)

    in_rows = 2 * FF // TOK
    gain = column(gain2_in)
    total = jnp.zeros((32, 128), F32)
    wi_here.wait()
    lines[...] = wi_raw[...].astype(F32)
    gi_here.wait()
    for j in range(in_rows):
        g = moved(out_moves(j), lambda t: gi_raw[t[0], :, pl.ds(t[1] * 128, 128)].astype(F32))
        total = total + g * lines[pl.ds(j, 32, stride=in_rows), :]
        gi_own[pl.ds(j, 32, stride=in_rows), :] = g * gain
    written.append(start(gi_own, gi_ref))
    ig_here.wait()
    written.append(start(ig_raw, ig_ref))
    out_here.wait()
    written.append(start(out_raw, out_ref))
    gain2_ref[...] = line(total)
    qkv_rows = 3 * WIDTH // TOK
    gain = column(gain1_in)
    total = jnp.zeros((32, 128), F32)
    wq_here.wait()
    lines[0 : 32 * qkv_rows] = wq_raw[...].astype(F32)
    gq_here.wait()
    for j in range(qkv_rows):
        part, cut = divmod(j, 8)
        r = (cut // 2 % 2) * 2 + cut // 4
        g = gq_raw[r, :, pl.ds(part * 256 + cut % 2 * 128, 128)].astype(F32)
        total = total + g * lines[pl.ds(j, 32, stride=qkv_rows), :]
        gq_own[pl.ds(j, 32, stride=qkv_rows), :] = g * gain
    written.append(start(gq_own, gq_ref))
    gain1_ref[...] = line(total)
    gd_here.wait()
    for j in range(8):
        gd_own[pl.ds(j, PART, stride=8), :] = gd_raw[0:PART, pl.ds(j * 128, 128)]
    written.append(start(gd_own, gd_ref))
    go_here.wait()
    for j in range(8):
        go_own[pl.ds(j, 32, stride=8), :] = go_raw[:, pl.ds(j * 128, 128)].astype(F32)
    written.append(start(go_own, go_ref))
    for cp in written:
        cp.wait()


def layer_kernel(
    n_sems,
    x_ref,
    cot_in,
    seg_in,
    cos_ref,
    sin_ref,
    gain1_in,
    gain2_in,
    wq_flat,
    wo_flat,
    wi_flat,
    wd_flat,
    out_ref,
    ig_ref,
    gq_ref,
    go_ref,
    gi_ref,
    gd_ref,
    seg_buf,
    n1,
    n2,
    cot,
    db,
    wq,
    wo,
    wi,
    wd,
    unit1,
    inv1,
    unit2,
    inv2,
    middle,
    dmid,
    q_buf,
    k_buf,
    v_buf,
    probs,
    att,
    datt,
    up_a,
    up_b,
    hidden,
    d_up,
    dqkv,
    ps,
    ps_in,
    ps_far,
    ps_back,
    gq,
    go,
    gi,
    gd,
    rq1,
    rq2,
    rq3,
    ro1,
    ro2,
    ro3,
    ri1,
    ri2,
    ri3,
    rd1,
    rd2,
    rd3,
    wq_in,
    wo_in,
    wi_in,
    lines,
    wide,
    out_vm,
    ig_vm,
    gq_vm,
    go_vm,
    gi_vm,
    gd_vm,
    send_sems,
    recv_sems,
    local_sems,
):
    dp, c = lax.axis_index("dp"), lax.axis_index("seq")
    x, y, z = lax.rem(dp, 2), lax.rem(dp // 2, 2), dp // 4
    zh, zp = z // 2, lax.rem(z, 2)
    role = zp * 2 + c

    def device(X, Y, Z, C):
        return (Z * 4 + Y * 2 + X, C)

    core_dev = device(x, y, z, 1 - c)
    pair_dev = device(x, y, zh * 2 + 1 - zp, c)
    diag_dev = device(x, y, zh * 2 + 1 - zp, 1 - c)
    half_dev = device(x, y, (1 - zh) * 2 + zp, c)
    x_dev = device(1 - x, y, z, c)
    y_dev = device(x, 1 - y, z, c)

    barrier = pltpu.get_barrier_semaphore()
    for dev in (core_dev, pair_dev, diag_dev, half_dev, x_dev, y_dev):
        pl.semaphore_signal(barrier, inc=1, device_id=dev, device_id_type=MESH_IDS)

    sent = []

    def copy_to(src, dst, dev, keep=True):
        i = n_sems[0]
        n_sems[0] += 1
        cp = pltpu.make_async_remote_copy(
            src_ref=src,
            dst_ref=dst,
            send_sem=send_sems.at[i],
            recv_sem=recv_sems.at[i],
            device_id=dev,
            device_id_type=MESH_IDS,
        )
        if keep:
            sent.append(cp)
        return cp

    local = []

    def emit(i, src, dst):
        cp = pltpu.make_async_copy(src, dst, local_sems.at[i])
        cp.start()
        local.append(cp)

    def settle():
        for cp in sent:
            cp.wait_send()
        del sent[:]

    def go_copy(src, dst, dev):
        cp = copy_to(src, dst, dev)
        cp.start()
        return cp


    others = (
        (core_dev, zp * 2 + 1 - c),
        (pair_dev, (1 - zp) * 2 + c),
        (diag_dev, (1 - zp) * 2 + 1 - c),
    )

    def spread(own, buf):
        cps = [go_copy(own.at[r], buf.at[z, y, x, c], dev) for dev, r in others]
        return cps

    class Gather:
        def __init__(self, buf, cols):
            self.buf = buf
            self.halves = (pl.ds(0, cols // 2), pl.ds(cols // 2, cols // 2))
            self.per_half = buf.shape[0] // 2

        def of(self, which):
            return pl.ds(self.per_half * which, self.per_half)

        def spot(self, which, cut):
            return self.buf.at[(self.of(which), y, x) + (slice(None),) * (len(self.buf.shape) - 4) + (cut,)]

        def line(self, which, cut, i):
            rest = (slice(None),) * (len(self.buf.shape) - 4) + (cut,)
            at = (y, slice(None)) if i == 0 else (slice(None), x)
            return self.buf.at[(self.of(which),) + at + rest]

        def same(self, ref, dev):
            return go_copy(ref, ref, dev)

        def across(self):
            self.over = [self.same(self.spot(zh, cut), half_dev) for cut in self.halves]

        def own_first(self):
            self.a = [
                self.same(self.spot(zh, cut), dev) for cut, dev in zip(self.halves, (x_dev, y_dev))
            ]

        def own_second(self):
            self.b = []
            for i, dev in enumerate((y_dev, x_dev)):
                self.a[i].wait_recv()
                self.b.append(self.same(self.line(zh, self.halves[i], i), dev))

        def far_first(self):
            self.a2 = []
            for i, dev in enumerate((x_dev, y_dev)):
                self.over[i].wait_recv()
                self.a2.append(self.same(self.spot(1 - zh, self.halves[i]), dev))

        def far_second(self):
            self.b2 = []
            for i, dev in enumerate((y_dev, x_dev)):
                self.a2[i].wait_recv()
                self.b2.append(self.same(self.line(1 - zh, self.halves[i], i), dev))

        def done(self):
            for cp in self.b + self.b2:
                cp.wait_recv()

    class GatherOut:
        def __init__(self, buf, cols):
            self.buf = buf
            self.halves = (pl.ds(0, cols // 2), pl.ds(cols // 2, cols // 2))

        def start(self):
            self.s0 = copy_to(wo_in, self.buf.at[y, x, c], core_dev, keep=False)

            @pl.when(c != zh)
            def _():
                self.s0.start()

        def across(self):
            self.s1 = copy_to(self.buf.at[y, x], self.buf.at[y, x], half_dev, keep=False)

            @pl.when(c == zh)
            def _():
                self.buf[y, x, c] = wo_in[...]
                self.s0.wait_recv()
                self.s1.start()

        def first(self):
            @pl.when(c != zh)
            def _():
                self.s1.wait_recv()

            self.a = []
            for cut, dev in zip(self.halves, (x_dev, y_dev)):
                ref = self.buf.at[y, x, :, :, cut]
                self.a.append(go_copy(ref, ref, dev))

        def second(self):
            self.b = []
            for i, dev in enumerate((y_dev, x_dev)):
                self.a[i].wait_recv()
                cut = self.halves[i]
                ref = self.buf.at[y, :, :, :, cut] if i == 0 else self.buf.at[:, x, :, :, cut]
                self.b.append(go_copy(ref, ref, dev))

        def done(self):
            for cp in self.b:
                cp.wait_recv()

        def end(self):
            @pl.when(c != zh)
            def _():
                self.s0.wait_send()

            @pl.when(c == zh)
            def _():
                self.s1.wait_send()


    pieces = [pl.ds(i * (TOK // PIECES), TOK // PIECES) for i in range(PIECES)]

    class Share:
        def __init__(self, buf):
            self.buf = buf
            self.to_pair = [
                go_copy(buf.at[zp, c, cut], buf.at[zp, c, cut], pair_dev) for cut in pieces
            ]
            self.to_core = go_copy(buf.at[zp, c], buf.at[zp, c], core_dev)

        def forward(self):
            self.fwd = []
            for cp, cut in zip(self.to_pair, pieces):
                cp.wait_recv()
                ref = self.buf.at[1 - zp, c, cut]
                self.fwd.append(go_copy(ref, ref, core_dev))

        def done(self):
            self.to_core.wait_recv()
            for cp in self.fwd:
                cp.wait_recv()

    class Reduce:
        def __init__(self, i):
            self.i = i
            self.mine = go_copy(ps.at[i, :, 1 - c], ps_in.at[i], core_dev)

        def cross(self):
            i = self.i
            self.mine.wait_recv()
            self.far = []
            for cut in pieces:
                ps_far[i, cut] = (
                    ps[i, 1 - zp, c, cut].astype(F32) + ps_in[i, 1 - zp, cut].astype(F32)
                ).astype(BF)
                self.far.append(go_copy(ps_far.at[i, cut], ps_back.at[i, cut], pair_dev))

        def total(self):
            i = self.i
            near = ps[i, zp, c].astype(F32) + ps_in[i, zp].astype(F32)
            for cp in self.far:
                cp.wait_recv()
            return near + ps_back[i].astype(F32)


    def add_into(target, extra):
        target[...] = (target[...].astype(F32) + extra[...].astype(F32)).astype(BF)

    def add_all(mine, got):
        n = got.shape[0]
        if n == 1:
            add_into(mine.at[0], got.at[0])
            return

        def body(j, carry):
            add_into(mine.at[j], got.at[j])
            return carry

        lax.fori_loop(0, n, body, 0)

    class Scatter:
        def __init__(self, buf, cols, r1, r2, r3):
            self.buf, self.r1, self.r2, self.r3 = buf, r1, r2, r3
            self.halves = (pl.ds(0, cols // 2), pl.ds(cols // 2, cols // 2))
            self.per_half = buf.shape[0] // 2
            self.rest = (slice(None),) * (len(buf.shape) - 4)
            self.c1, self.c2 = {}, {}

        def of(self, which):
            return pl.ds(self.per_half * which, self.per_half)

        def line(self, i, which, other):
            if i == 0:
                at = (1 - y if other else y, slice(None))
            else:
                at = (slice(None), 1 - x if other else x)
            return self.buf.at[(self.of(which),) + at + self.rest + (self.halves[i],)]

        def spot(self, i, which, other):
            Y, X = (y, x) if not other else ((y, 1 - x) if i == 0 else (1 - y, x))
            return self.buf.at[(self.of(which), Y, X) + self.rest + (self.halves[i],)]

        def first(self, far):
            which = 1 - zh if far else zh
            self.c1[far] = [
                go_copy(self.line(i, which, True), self.r1.at[i, far], dev)
                for i, dev in enumerate((y_dev, x_dev))
            ]

        def second(self, far):
            which = 1 - zh if far else zh
            self.c2[far] = []
            for i, dev in enumerate((x_dev, y_dev)):
                self.c1[far][i].wait_recv()
                add_all(self.line(i, which, False), self.r1.at[i, far])
                self.c2[far].append(go_copy(self.spot(i, which, True), self.r2.at[i, far], dev))

        def third(self, far):
            which = 1 - zh if far else zh
            for i in range(2):
                self.c2[far][i].wait_recv()
                add_all(self.spot(i, which, False), self.r2.at[i, far])
            if far:
                self.c3 = go_copy(self.buf.at[self.of(which), y, x], self.r3, half_dev)

    class ScatterRows(Scatter):
        def fourth(self, out):
            self.c3.wait_recv()
            add_all(self.buf.at[self.of(zh), y, x], self.r3)
            self.c4 = []
            for dev, r in others:
                src = self.buf.at[2 * zh + r // 2, y, x, lax.rem(r, 2)]
                self.c4.append(go_copy(src, out.at[role], dev))
            out[role] = self.buf[z, y, x, c]

        def done(self):
            for cp in self.c4:
                cp.wait_recv()

    class ScatterDown(Scatter):
        def fourth(self, out):
            self.c3.wait_recv()
            out[...] = self.buf[zh, y, x].astype(F32) + self.r3[0].astype(F32)

    class ScatterOut:
        def __init__(self, buf, cols, r1, r2, r3):
            self.buf, self.r1, self.r2, self.r3 = buf, r1, r2, r3
            self.halves = (pl.ds(0, cols // 2), pl.ds(cols // 2, cols // 2))

        def line(self, i, other):
            cut = self.halves[i]
            if i == 0:
                return self.buf.at[1 - y if other else y, :, :, :, cut]
            return self.buf.at[:, 1 - x if other else x, :, :, cut]

        def spot(self, i, other):
            Y, X = (y, x) if not other else ((y, 1 - x) if i == 0 else (1 - y, x))
            return self.buf.at[Y, X, :, :, self.halves[i]]

        def first(self):
            self.c1 = [
                go_copy(self.line(i, True), self.r1.at[i], dev)
                for i, dev in enumerate((y_dev, x_dev))
            ]

        def second(self):
            self.c2 = []
            for i, dev in enumerate((x_dev, y_dev)):
                self.c1[i].wait_recv()
                add_all(self.line(i, False), self.r1.at[i])
                self.c2.append(go_copy(self.spot(i, True), self.r2.at[i], dev))

        def third(self):
            for i in range(2):
                self.c2[i].wait_recv()
                add_all(self.spot(i, False), self.r2.at[i])
            self.c3 = copy_to(self.buf.at[y, x], self.r3, half_dev, keep=False)

            @pl.when(c != zh)
            def _():
                self.c3.start()

        def fourth(self, out):
            self.c4 = copy_to(self.r3.at[1 - c], out, core_dev, keep=False)

            @pl.when(c == zh)
            def _():
                self.c3.wait_recv()
                add_all(self.r3, self.buf.at[y, x])
                self.c4.start()
                out[...] = self.r3[c]

        def done(self):
            @pl.when(c != zh)
            def _():
                self.c4.wait_recv()
                self.c3.wait_send()

            @pl.when(c == zh)
            def _():
                self.c4.wait_send()

    tokens = x_ref[...].astype(F32)
    centred = tokens - jnp.mean(tokens, axis=-1, keepdims=True)
    inv = lax.rsqrt(jnp.mean(centred * centred, axis=-1, keepdims=True) + EPSILON)
    unit = centred * inv
    unit1[...] = unit
    inv1[...] = jnp.broadcast_to(inv, (TOK, 128))
    n1[zp, c] = unit.astype(BF)
    qkv_rows = 3 * WIDTH // TOK
    lines[0 : 32 * qkv_rows] = wq_flat[...].astype(F32)
    gain = column(gain1_in)
    for j in range(qkv_rows):
        part, cut = divmod(j, 8)
        r = (cut // 2 % 2) * 2 + cut // 4
        w = lines[pl.ds(j, 32, stride=qkv_rows), :] * gain
        wq_in[r, :, pl.ds(part * 256 + cut % 2 * 128, 128)] = w.astype(BF)
    seg_buf[zp, c] = jnp.broadcast_to(seg_in[...].astype(F32), (8, TOK))
    wq[z, y, x, c] = wq_in[role]
    cot[zp, c] = cot_in[...]
    lines2 = wide
    lines2[0 : 8 * PART] = wd_flat[...].astype(F32)
    lines2[8 * PART : 8 * PAD] = jnp.zeros((8 * (PAD - PART), TOK), F32)
    for j in range(8):
        wd[zh, y, x, :, pl.ds(j * 128, 128)] = lines2[pl.ds(j, PAD, stride=8), :].astype(BF)

    g_q, g_i, g_d = Gather(wq, QKV), Gather(wi, 2 * HID), Gather(wd, WIDTH)
    g_o = GatherOut(wo, WIDTH)

    pl.semaphore_wait(barrier, 6)
    s_q = spread(wq_in, wq)
    g_d.own_first()
    wide[0:256] = wo_flat[...].astype(F32)
    for j in range(8):
        wo_in[:, pl.ds(j * 128, 128)] = wide[pl.ds(j, 32, stride=8), :].astype(BF)
    g_o.start()
    s_seg = [go_copy(seg_buf.at[zp, c], seg_buf.at[zp, c], dev) for dev, _ in others]
    in_rows = 2 * FF // TOK
    lines[...] = wi_flat[...].astype(F32)
    gain = column(gain2_in)
    for j in range(in_rows):
        wide[pl.ds(j * 32, 32), :] = lines[pl.ds(j, 32, stride=in_rows), :] * gain
    for r in range(4):
        for u in range(2 * HID // TOK):
            tile = moved(in_moves(r, u), lambda t: wide[pl.ds(t * 32, 32), :])
            wi_in[r, :, pl.ds(u * 128, 128)] = tile.astype(BF)
    wi[z, y, x, c] = wi_in[role]
    for cp in s_q:
        cp.wait_recv()
    g_o.across()
    g_q.across()
    g_q.own_first()
    g_d.own_second()
    s_i = spread(wi_in, wi)
    share_n1 = Share(n1)
    g_q.own_second()
    g_d.across()
    g_q.far_first()
    for cp in s_i:
        cp.wait_recv()
    g_i.across()
    g_i.own_first()
    g_q.far_second()
    g_o.first()
    share_n1.forward()
    share_n1.done()
    g_o.second()
    for cp in s_seg:
        cp.wait_recv()
    g_q.done()
    g_i.own_second()

    lanes = lax.broadcasted_iota(jnp.int32, (1, 128), 1)
    low_half = lax.rem(lanes, 64) < 32
    first_head = lanes < 64

    def qkv_step(s, carry):
        rows = n1[s].reshape(256, WIDTH)
        for part, dst in enumerate((q_buf, k_buf, v_buf)):
            for j in range(2):
                at = part * 256 + j * 128
                w = wq[:, :, :, :, :, pl.ds(at, 128)].reshape(WIDTH, 128)
                u = dot_nn(rows, w)
                if part < 2:
                    u = u * cos_ref[...] + turned(u, low_half) * sin_ref[...]
                dst[s, j] = u.astype(BF)
        return carry

    lax.fori_loop(0, 2, qkv_step, 0)

    def only(head, u):
        return jnp.where(first_head if head == 0 else ~first_head, u, jnp.zeros_like(u))

    def attend(i, carry):
        s, j = i // 2, lax.rem(i, 2)
        q, k, v = q_buf[s, j], k_buf[s, j], v_buf[s, j]
        seg_row = jnp.concatenate([seg_buf[s, 0, 0:1], seg_buf[s, 1, 0:1]], axis=1)
        seg_col = jnp.broadcast_to(seg_row, (128, 256)).T[:, 0:1]
        same = seg_col == seg_row
        heads = []
        for h in range(2):
            scores = matmul_nt(only(h, q), k) * 0.125
            scores = jnp.where(same, scores, -1e30)
            weights = jnp.exp(scores - jnp.max(scores, axis=-1, keepdims=True))
            p = weights * (1.0 / jnp.sum(weights, axis=-1, keepdims=True))
            probs[i, h] = p
            heads.append(dot_nn(p.astype(BF), v))
        att[s, j] = jnp.where(first_head, heads[0], heads[1]).astype(BF)
        return carry

    lax.fori_loop(0, 4, attend, 0)
    g_o.done()

    def att_rows(s):
        return jnp.concatenate([att[s, 0], att[s, 1]], axis=1)

    def branch(s, carry):
        w = wo[...].reshape(256, WIDTH)
        ps[0, s] = dot_nn(att_rows(s), w).astype(BF).reshape(2, TOK, WIDTH)
        return carry

    lax.fori_loop(0, 2, branch, 0)
    red = Reduce(0)
    red.cross()
    g_d.far_first()
    g_i.far_first()
    mid = x_ref[...].astype(F32) + red.total()
    middle[...] = mid
    centred = mid - jnp.mean(mid, axis=-1, keepdims=True)
    inv = lax.rsqrt(jnp.mean(centred * centred, axis=-1, keepdims=True) + EPSILON)
    unit = centred * inv
    unit2[...] = unit
    inv2[...] = jnp.broadcast_to(inv, (TOK, 128))
    n2[zp, c] = unit.astype(BF)
    share_n2 = Share(n2)
    g_i.far_second()
    share_n2.forward()
    share_cot = Share(cot)
    share_n2.done()
    g_d.far_second()
    g_i.done()

    def upper(j, carry):
        at = pl.multiple_of(j * 256, 256)
        for s in range(2):
            rows = n2[s].reshape(256, WIDTH)
            inner = dot_nn(rows, wi[:, :, :, :, :, pl.ds(at, 256)].reshape(WIDTH, 256))
            gate = dot_nn(
                rows,
                wi[:, :, :, :, :, pl.ds(pl.multiple_of(HID + at, 256), 256)].reshape(WIDTH, 256),
            )
            cdf = 0.5 * (1.0 + lax.erf(inner * math.sqrt(0.5)))
            slope = cdf + inner * jnp.exp(-0.5 * inner * inner) * (1.0 / math.sqrt(2 * math.pi))
            bent = inner * cdf
            up_a[s, :, pl.ds(at, 256)] = gate * slope
            up_b[s, :, pl.ds(at, 256)] = bent
            hidden[s, :, pl.ds(at, 256)] = (bent * gate).astype(BF)
        return carry

    lax.fori_loop(0, HID // 256, upper, 0)
    share_cot.forward()
    share_cot.done()

    def down_grad(i, carry):
        lhs = hidden[:, :, pl.ds(pl.multiple_of(i * 384, 384), 384)].reshape(512, 384)
        for j in range(2):
            rhs = cot[:, :, :, pl.ds(j * 512, 512)].reshape(512, 512)
            gd[i, :, :, :, pl.ds(j * 512, 512)] = (
                matmul_tn(lhs, rhs).astype(BF).reshape(2, 2, PAD, 512)
            )
        return carry

    lax.fori_loop(0, 2, down_grad, 0)
    r_d = ScatterDown(gd, WIDTH, rd1, rd2, rd3)
    r_d.first(1)
    g_d.done()

    def hidden_grad(i, carry):
        w = wd[i].reshape(384, WIDTH)
        at = pl.multiple_of(i * 384, 384)
        for s in range(2):
            dh = matmul_nt(cot[s].reshape(256, WIDTH), w)
            d_up[s, :, pl.ds(at, 384)] = (dh * up_a[s, :, pl.ds(at, 384)]).astype(BF)
            d_up[s, :, pl.ds(pl.multiple_of(HID + at, 384), 384)] = (
                dh * up_b[s, :, pl.ds(at, 384)]
            ).astype(BF)
        return carry

    lax.fori_loop(0, 2, hidden_grad, 0)

    def normed_two_grad(i, carry):
        w = wi[i].reshape(256, 2 * HID)
        at = pl.multiple_of(i * 256, 256)
        for s in range(2):
            ps[1, s, :, :, pl.ds(at, 256)] = (
                matmul_nt(d_up[s], w).astype(BF).reshape(2, TOK, 256)
            )
        return carry

    lax.fori_loop(0, 4, normed_two_grad, 0)
    red = Reduce(1)

    def in_grad(k, carry):
        i = k
        lhs = n2[:, :, :, pl.ds(pl.multiple_of(i * 256, 256), 256)].reshape(512, 256)
        for j in range(3):
            rhs = d_up[:, :, pl.ds(j * 512, 512)].reshape(512, 512)
            gi[i, :, :, :, :, pl.ds(j * 512, 512)] = (
                matmul_tn(lhs, rhs).astype(BF).reshape(2, 2, 2, 32, 512)
            )
        return carry

    lax.fori_loop(2 * (1 - zh), 2 * (1 - zh) + 2, in_grad, 0)
    r_i = ScatterRows(gi, 2 * HID, ri1, ri2, ri3)
    r_i.first(1)
    red.cross()
    lax.fori_loop(2 * zh, 2 * zh + 2, in_grad, 0)
    r_d.second(1)
    r_d.first(0)

    e = red.total()
    n = unit2[...]
    d_middle = cot_in[...].astype(F32) + inv2[:, 0:1] * (
        e
        - jnp.mean(e, axis=-1, keepdims=True)
        - n * jnp.mean(e * n, axis=-1, keepdims=True)
    )
    dmid[...] = d_middle
    db[zp, c] = d_middle.astype(BF)
    share_db = Share(db)

    def down(i, carry):
        w = wd[...].reshape(HID, WIDTH)
        ps[2, i] = dot_nn(hidden[i], w).astype(BF).reshape(2, TOK, WIDTH)
        return carry

    lax.fori_loop(0, 2, down, 0)
    share_db.forward()
    r_d.third(1)
    r_i.second(1)
    red_out = Reduce(2)
    share_db.done()

    def attended_grad(s, carry):
        rows = db[s].reshape(256, WIDTH)
        da = matmul_nt(rows, wo[...].reshape(256, WIDTH)).astype(BF)
        datt[s, 0] = da[:, 0:128]
        datt[s, 1] = da[:, 128:256]
        return carry

    lax.fori_loop(0, 2, attended_grad, 0)

    lhs = att
    for j in range(2):
        for half in range(2):
            rhs = db[:, :, :, pl.ds(half * 512, 512)].reshape(512, 512)
            go[j, :, :, :, pl.ds(half * 512, 512)] = (
                matmul_tn(lhs[:, j].reshape(512, 128), rhs).astype(BF).reshape(2, 2, 32, 512)
            )
    r_o = ScatterOut(go, WIDTH, ro1, ro2, ro3)
    r_o.first()

    def attend_back(i, carry):
        s, j = i // 2, lax.rem(i, 2)
        q, k, v, da = q_buf[s, j], k_buf[s, j], v_buf[s, j], datt[s, j]
        dq, dk, dv = [], [], []
        for h in range(2):
            p = probs[i, h]
            dprob = matmul_nt(only(h, da), v)
            delta = jnp.sum(p * dprob, axis=-1, keepdims=True)
            ds = (p * (dprob - delta)).astype(BF)
            dq.append(dot_nn(ds, k))
            dk.append(matmul_tn(ds, q))
            dv.append(matmul_tn(p.astype(BF), da))
        for part, pieces in enumerate((dq, dk, dv)):
            u = jnp.where(first_head, pieces[0], pieces[1])
            if part < 2:
                u = u * 0.125
                u = u * cos_ref[...] - turned(u, low_half) * sin_ref[...]
            dqkv[part, j, s] = u.astype(BF)
        return carry

    r_d.second(0)
    red_out.cross()
    lax.fori_loop(0, 4, attend_back, 0)
    r_i.third(1)

    def qkv_grad(i, carry):
        lhs = n1[:, :, :, pl.ds(pl.multiple_of(i * 256, 256), 256)].reshape(512, 256)
        for p in range(3):
            for j in range(2):
                rhs = dqkv[p, j].reshape(512, 128)
                gq[i, :, :, :, :, pl.ds(p * 256 + j * 128, 128)] = (
                    matmul_tn(lhs, rhs).astype(BF).reshape(2, 2, 2, 32, 128)
                )
        return carry

    lax.fori_loop(2 * (1 - zh), 2 * (1 - zh) + 2, qkv_grad, 0)
    r_q = ScatterRows(gq, QKV, rq1, rq2, rq3)
    r_q.first(1)
    lax.fori_loop(2 * zh, 2 * zh + 2, qkv_grad, 0)

    def first_grads(i, carry):
        w = wq[i].reshape(256, QKV)
        at = pl.multiple_of(i * 256, 256)
        for s in range(2):
            rows = jnp.concatenate([dqkv[p, j, s] for p in range(3) for j in range(2)], axis=1)
            ps[3, s, :, :, pl.ds(at, 256)] = (
                matmul_nt(rows, w).astype(BF).reshape(2, TOK, 256)
            )
        return carry

    lax.fori_loop(0, 4, first_grads, 0)
    red_in = Reduce(3)

    r_q.second(1)
    r_i.first(0)
    red_in.cross()
    r_o.second()
    r_q.third(1)
    r_q.first(0)
    r_d.third(0)
    r_d.fourth(gd_vm)
    emit(2, gd_vm, gd_ref)
    e = red_in.total()
    n = unit1[...]
    ig_vm[...] = dmid[...] + inv1[:, 0:1] * (
        e
        - jnp.mean(e, axis=-1, keepdims=True)
        - n * jnp.mean(e * n, axis=-1, keepdims=True)
    )
    emit(1, ig_vm, ig_ref)
    out_vm[...] = (middle[...] + red_out.total()).astype(BF)
    emit(0, out_vm, out_ref)
    r_i.second(0)
    r_q.second(0)
    r_o.third()
    settle()
    r_i.third(0)
    r_i.fourth(gi_vm)
    r_o.fourth(go_vm)
    r_q.third(0)
    r_q.fourth(gq_vm)
    r_i.done()
    emit(3, gi_vm, gi_ref)
    r_o.done()
    emit(4, go_vm, go_ref)
    r_q.done()
    emit(5, gq_vm, gq_ref)
    g_o.end()
    settle()
    for cp in local:
        cp.wait()


def block_device(inputs, segments, cotangent, ln1_gain, w_qkv, w_attn_out, ln2_gain, w_in, w_mlp_out):
    places = np.arange(2 * TOK, dtype=np.float32)
    freqs = (1.0 / ROPE_BASE ** (np.arange(0, HD, 2, dtype=np.float64) / HD)).astype(np.float32)
    angles = np.tile(places[:, None] * freqs[None, :], (1, 4))
    signs = np.where(np.arange(2 * HD) % HD < HD // 2, -1.0, 1.0).astype(np.float32)
    cosines = jnp.asarray(np.cos(angles))
    sines = jnp.asarray(np.sin(angles) * signs)
    gain_one, gain_two = ln1_gain[None], ln2_gain[None]
    wq_flat, wo_flat = w_qkv.reshape(-1, TOK), w_attn_out.reshape(-1, TOK)
    wi_flat, wd_flat = w_in.reshape(-1, TOK), w_mlp_out.reshape(-1, TOK)

    vm = pltpu.VMEM
    group = (2, 2, TOK, WIDTH)
    rows = (4, 2, 2, 2, 32)
    outs = pl.pallas_call(
        functools.partial(layer_kernel, [0]),
        out_shape=(
            jax.ShapeDtypeStruct((TOK, WIDTH), BF),
            jax.ShapeDtypeStruct((TOK, WIDTH), F32),
            jax.ShapeDtypeStruct((4, 32, QKV), BF),
            jax.ShapeDtypeStruct((32, WIDTH), BF),
            jax.ShapeDtypeStruct((4, 32, 2 * HID), BF),
            jax.ShapeDtypeStruct((PAD, WIDTH), F32),
        ),
        in_specs=[pl.BlockSpec(memory_space=vm)] * 11,
        out_specs=(pl.BlockSpec(memory_space=pl.ANY),) * 6,
        scratch_shapes=[
            vm((2, 2, 8, TOK), F32),
            vm(group, BF),
            vm(group, BF),
            vm(group, BF),
            vm(group, BF),
            vm(rows + (QKV,), BF),
            vm((2, 2, 2, 32, WIDTH), BF),
            vm(rows + (2 * HID,), BF),
            vm((2, 2, 2, PAD, WIDTH), BF),
            vm((TOK, WIDTH), F32),
            vm((TOK, 128), F32),
            vm((TOK, WIDTH), F32),
            vm((TOK, 128), F32),
            vm((TOK, WIDTH), F32),
            vm((TOK, WIDTH), F32),
            vm((2, 2, 256, 128), BF),
            vm((2, 2, 256, 128), BF),
            vm((2, 2, 256, 128), BF),
            vm((4, 2, 256, 256), F32),
            vm((2, 2, 256, 128), BF),
            vm((2, 2, 256, 128), BF),
            vm((2, 256, HID), F32),
            vm((2, 256, HID), F32),
            vm((2, 256, HID), BF),
            vm((2, 256, 2 * HID), BF),
            vm((3, 2, 2, 256, 128), BF),
            vm((4,) + group, BF),
            vm((4, 2, TOK, WIDTH), BF),
            vm((4, TOK, WIDTH), BF),
            vm((4, TOK, WIDTH), BF),
            vm(rows + (QKV,), BF),
            vm((2, 2, 2, 32, WIDTH), BF),
            vm(rows + (2 * HID,), BF),
            vm((2, 2, 2, PAD, WIDTH), BF),
            vm((2, 2, 2, 2, 2, 32, QKV // 2), BF),
            vm((2, 2, 2, 2, 32, QKV // 2), BF),
            vm((2, 2, 32, QKV), BF),
            vm((2, 2, 2, 32, WIDTH // 2), BF),
            vm((2, 2, 32, WIDTH // 2), BF),
            vm((2, 32, WIDTH), BF),
            vm((2, 2, 2, 2, 2, 32, HID), BF),
            vm((2, 2, 2, 2, 32, HID), BF),
            vm((2, 2, 32, 2 * HID), BF),
            vm((2, 2, 1, 2, PAD, WIDTH // 2), BF),
            vm((2, 2, 1, PAD, WIDTH // 2), BF),
            vm((1, PAD, WIDTH), BF),
            vm((4, 32, QKV), BF),
            vm((32, WIDTH), BF),
            vm((4, 32, 2 * HID), BF),
            vm((64 * FF // TOK, TOK), F32),
            vm((64 * FF // TOK, TOK), F32),
            vm((TOK, WIDTH), BF),
            vm((TOK, WIDTH), F32),
            vm((4, 32, QKV), BF),
            vm((32, WIDTH), BF),
            vm((4, 32, 2 * HID), BF),
            vm((PAD, WIDTH), F32),
            pltpu.SemaphoreType.DMA((N_COPIES,)),
            pltpu.SemaphoreType.DMA((N_COPIES,)),
            pltpu.SemaphoreType.DMA((6,)),
        ],
        compiler_params=pltpu.CompilerParams(
            collective_id=0, has_side_effects=True, vmem_limit_bytes=60 * 2**20
        ),
    )(
        inputs[0],
        cotangent[0],
        segments,
        cosines,
        sines,
        gain_one,
        gain_two,
        wq_flat,
        wo_flat,
        wi_flat,
        wd_flat,
    )
    output, input_grad, gq, go, gi, gd = outs
    final = pl.pallas_call(
        finish_kernel,
        out_shape=(
            jax.ShapeDtypeStruct((TOK, WIDTH), BF),
            jax.ShapeDtypeStruct((TOK, WIDTH), F32),
            jax.ShapeDtypeStruct((1, 32), F32),
            jax.ShapeDtypeStruct(wq_flat.shape, F32),
            jax.ShapeDtypeStruct(wo_flat.shape, F32),
            jax.ShapeDtypeStruct((1, 32), F32),
            jax.ShapeDtypeStruct(wi_flat.shape, F32),
            jax.ShapeDtypeStruct(wd_flat.shape, F32),
        ),
        in_specs=[pl.BlockSpec(memory_space=pl.ANY)] * 6
        + [pl.BlockSpec(memory_space=vm)] * 2
        + [pl.BlockSpec(memory_space=pl.ANY)] * 2,
        out_specs=tuple(
            pl.BlockSpec(memory_space=vm if i in (2, 5) else pl.ANY) for i in range(8)
        ),
        scratch_shapes=[
            vm(wi_flat.shape, F32),
            vm((4, 32, QKV), BF),
            vm((32, WIDTH), BF),
            vm((4, 32, 2 * HID), BF),
            vm((PAD, WIDTH), F32),
            vm(wq_flat.shape, BF),
            vm(wi_flat.shape, BF),
            vm(wq_flat.shape, F32),
            vm(wo_flat.shape, F32),
            vm(wi_flat.shape, F32),
            vm(wd_flat.shape, F32),
            vm((TOK, WIDTH), F32),
            vm((TOK, WIDTH), BF),
            pltpu.SemaphoreType.DMA((14,)),
        ],
        compiler_params=pltpu.CompilerParams(vmem_limit_bytes=60 * 2**20),
    )(gq, go, gi, gd, output, input_grad, gain_one, gain_two, wq_flat, wi_flat)
    return (final[0][None], final[1][None]) + tuple(f.reshape(-1) for f in final[2:])


N_COPIES = 116
PIECES = 2


def solution(mesh):
    block = dict(mesh.shape) == {"dp": 16, "seq": 2}
    placed = (
        P("dp", "seq", None),
        P("dp", "seq"),
        P("dp", "seq", None),
        P(("dp", "seq")),
        P(("dp", "seq")),
        P(("dp", "seq")),
        P(("dp", "seq")),
        P(("dp", "seq")),
        P(("dp", "seq")),
    )
    return jax.shard_map(
        block_device if block else general_device,
        mesh=mesh,
        in_specs=placed,
        out_specs=(
            P("dp", "seq", None),
            P("dp", "seq", None),
            P(("dp", "seq")),
            P(("dp", "seq")),
            P(("dp", "seq")),
            P(("dp", "seq")),
            P(("dp", "seq")),
            P(("dp", "seq")),
        ),
        check_vma=False,
    )
```

```python
import functools
import math

import jax
import jax.numpy as jnp
import numpy as np
from jax import lax
from jax.experimental import pallas as pl
from jax.experimental.pallas import tpu as pltpu
from jax.sharding import PartitionSpec as P

HEADS = 16
HD = 64
FF = 2624


EPSILON = 1e-05
ROPE_BASE = 160000.0


def rope_tables(places):
    freqs = 1.0 / ROPE_BASE ** (jnp.arange(0, HD, 2, dtype=jnp.float32) / HD)
    angles = places[:, None] * freqs[None, :]
    angles = jnp.concatenate([angles, angles], axis=1)
    return (jnp.cos(angles), jnp.sin(angles))


def rotate(values_in, cosines, sines):
    halfway = values_in.shape[-1] // 2
    turned = jnp.concatenate([-values_in[..., halfway:], values_in[..., :halfway]], axis=-1)
    return values_in * cosines[:, None, :] + turned * sines[:, None, :]


def rotate_back(grads_in, cosines, sines):
    halfway = grads_in.shape[-1] // 2
    scaled = grads_in * sines[:, None, :]
    turned = jnp.concatenate([scaled[..., halfway:], -scaled[..., :halfway]], axis=-1)
    return grads_in * cosines[:, None, :] + turned


def norm_forward(values_in, gain):
    centred = values_in - jnp.mean(values_in, axis=-1, keepdims=True)
    inv_spread = lax.rsqrt(jnp.mean(centred * centred, axis=-1, keepdims=True) + EPSILON)
    unit_rows = centred * inv_spread
    return (unit_rows * gain, unit_rows, inv_spread)


def norm_back(grad_rows, unit_rows, inv_spread, gain):
    gain_grad = jnp.sum(grad_rows * unit_rows, axis=0)
    scaled = grad_rows * gain
    inner_mean = jnp.mean(scaled, axis=-1, keepdims=True)
    cross_mean = jnp.mean(scaled * unit_rows, axis=-1, keepdims=True)
    return (gain_grad, inv_spread * (scaled - inner_mean - unit_rows * cross_mean))


def matmul_tn(left, right):
    return lax.dot_general(
        left, right, (((0,), (0,)), ((), ())), preferred_element_type=jnp.float32
    )


def matmul_nt(left, right):
    return lax.dot_general(
        left, right, (((1,), (1,)), ((), ())), preferred_element_type=jnp.float32
    )


def masked_scores(query, key_block, seg_query, seg_block):
    scores = (
        jnp.einsum("qhd,khd->hqk", query, key_block, preferred_element_type=jnp.float32) * 0.125
    )
    same_doc = seg_query[:, None] == seg_block[None, :]
    return jnp.where(same_doc[None], scores, -1e30)


def gated(inner, gate):
    return jax.nn.gelu(inner, approximate=False) * gate


def general_device(inputs, segments, cotangent, ln1_gain, w_qkv, w_attn_out, ln2_gain, w_in, w_mlp_out):
    tok_rows = inputs.shape[1]
    model_width = inputs.shape[2]
    seq_devices = lax.axis_size("seq")
    dp_devices = lax.axis_size("dp")
    tokens_in = inputs[0].astype(jnp.float32)
    seg_send = segments.astype(jnp.bfloat16)
    seg_query = seg_send[0]
    gathered_attn = (
        lax.all_gather(ln1_gain, ("dp", "seq"), axis=0, tiled=True),
        lax.all_gather(w_qkv, ("dp", "seq"), axis=0, tiled=True),
        lax.all_gather(w_attn_out, ("dp", "seq"), axis=0, tiled=True),
    )
    gain_one = gathered_attn[0].astype(jnp.float32)
    qkv_mat = gathered_attn[1].reshape(model_width, 3 * model_width)
    proj_mat = gathered_attn[2].reshape(model_width, model_width)
    places = (lax.axis_index("seq") * tok_rows + jnp.arange(tok_rows, dtype=jnp.int32)).astype(
        jnp.float32
    )
    cosines, sines = rope_tables(places)
    normed_one, unit_one, spread_one = norm_forward(tokens_in, gain_one)
    normed_one_low = normed_one.astype(jnp.bfloat16)
    qkv_rows = jnp.dot(normed_one_low, qkv_mat, preferred_element_type=jnp.float32)
    query = rotate(qkv_rows[:, :model_width].reshape(tok_rows, HEADS, HD), cosines, sines).astype(
        jnp.bfloat16
    )
    key_rot = rotate(
        qkv_rows[:, model_width : 2 * model_width].reshape(tok_rows, HEADS, HD), cosines, sines
    ).astype(jnp.bfloat16)
    value_rows = qkv_rows[:, 2 * model_width :].astype(jnp.bfloat16)
    key_send = key_rot.reshape(1, tok_rows, model_width)
    value_send = value_rows.reshape(1, tok_rows, model_width)
    fwd_init = (
        jnp.full((HEADS, tok_rows), -1e30, jnp.float32),
        jnp.zeros((HEADS, tok_rows), jnp.float32),
        jnp.zeros((tok_rows, HEADS, HD), jnp.float32),
    )
    key_piece = lax.all_gather(key_send, "seq", axis=1, tiled=True)
    value_piece = lax.all_gather(value_send, "seq", axis=1, tiled=True)
    seg_piece = lax.all_gather(seg_send, "seq", axis=1, tiled=True)
    span = key_piece.shape[1]
    step_rows = math.gcd(span, 512)

    def one_block(block_id, inner_state):
        top_score, total, accum = inner_state
        begin = block_id * step_rows
        key_block = lax.dynamic_slice_in_dim(key_piece[0], begin, step_rows, 0).reshape(
            step_rows, HEADS, HD
        )
        value_block = lax.dynamic_slice_in_dim(value_piece[0], begin, step_rows, 0).reshape(
            step_rows, HEADS, HD
        )
        seg_block = lax.dynamic_slice_in_dim(seg_piece[0], begin, step_rows, 0)
        scores = masked_scores(query, key_block, seg_query, seg_block)
        new_top = jnp.maximum(top_score, jnp.max(scores, axis=-1))
        fading = jnp.exp(top_score - new_top)
        weights = jnp.exp(scores - new_top[..., None])
        total = total * fading + jnp.sum(weights, axis=-1)
        accum = accum * fading.T[:, :, None] + jnp.einsum(
            "hqk,khd->qhd",
            weights.astype(jnp.bfloat16),
            value_block,
            preferred_element_type=jnp.float32,
        )
        return (new_top, total, accum)

    fwd_state = lax.fori_loop(0, span // step_rows, one_block, fwd_init)
    run_top, run_total, run_accum = fwd_state
    log_total = run_top + jnp.log(run_total)
    attended = (run_accum / run_total.T[:, :, None]).astype(jnp.bfloat16)
    attended_rows = attended.reshape(tok_rows, model_width)
    middle = tokens_in + jnp.dot(attended_rows, proj_mat, preferred_element_type=jnp.float32)
    gathered_mlp = (
        lax.all_gather(ln2_gain, ("dp", "seq"), axis=0, tiled=True),
        lax.all_gather(w_in, ("dp", "seq"), axis=0, tiled=True),
        lax.all_gather(w_mlp_out, ("dp", "seq"), axis=0, tiled=True),
    )
    gain_two = gathered_mlp[0].astype(jnp.float32)
    in_mat = gathered_mlp[1].reshape(model_width, 2 * FF)
    down_mat = gathered_mlp[2].reshape(FF, model_width)
    normed_two, unit_two, spread_two = norm_forward(middle, gain_two)
    normed_two_low = normed_two.astype(jnp.bfloat16)
    upper = jnp.dot(normed_two_low, in_mat, preferred_element_type=jnp.float32)
    inner = upper[:, :FF]
    gate = upper[:, FF:]
    hidden_low = gated(inner, gate).astype(jnp.bfloat16)
    output = (middle + jnp.dot(hidden_low, down_mat, preferred_element_type=jnp.float32)).astype(
        jnp.bfloat16
    )
    gathered_mlp = (
        lax.all_gather(ln2_gain, ("dp", "seq"), axis=0, tiled=True),
        lax.all_gather(w_in, ("dp", "seq"), axis=0, tiled=True),
        lax.all_gather(w_mlp_out, ("dp", "seq"), axis=0, tiled=True),
    )
    gain_two = gathered_mlp[0].astype(jnp.float32)
    in_mat = gathered_mlp[1].reshape(model_width, 2 * FF)
    down_mat = gathered_mlp[2].reshape(FF, model_width)
    grad_low = cotangent[0]
    grad_rows = grad_low.astype(jnp.float32)
    d_hidden = matmul_nt(grad_low, down_mat)
    grad_down = matmul_tn(hidden_low, grad_low)
    gated_value, pull = jax.vjp(gated, inner, gate)
    d_inner, d_gate = pull(d_hidden)
    d_upper_low = jnp.concatenate([d_inner, d_gate], axis=1).astype(jnp.bfloat16)
    grad_in = matmul_tn(normed_two_low, d_upper_low)
    d_normed_two = matmul_nt(d_upper_low, in_mat)
    grad_gain_two, d_middle_part = norm_back(d_normed_two, unit_two, spread_two, gain_two)
    d_middle = grad_rows + d_middle_part
    mlp_parts = tuple(
        (g.reshape(dp_devices, seq_devices, -1) for g in (grad_gain_two, grad_in, grad_down))
    )
    mlp_mid = (
        lax.psum_scatter(
            mlp_parts[0].astype(jnp.bfloat16), "seq", scatter_dimension=1, tiled=True
        ).astype(jnp.float32),
        lax.psum_scatter(
            mlp_parts[1].astype(jnp.bfloat16), "seq", scatter_dimension=1, tiled=True
        ).astype(jnp.float32),
        lax.psum_scatter(
            mlp_parts[2].astype(jnp.bfloat16), "seq", scatter_dimension=1, tiled=True
        ).astype(jnp.float32),
    )
    mlp_shards = (
        lax.psum_scatter(
            mlp_mid[0].astype(jnp.bfloat16), "dp", scatter_dimension=0, tiled=True
        ).astype(jnp.float32),
        lax.psum_scatter(
            mlp_mid[1].astype(jnp.bfloat16), "dp", scatter_dimension=0, tiled=True
        ).astype(jnp.float32),
        lax.psum_scatter(
            mlp_mid[2].astype(jnp.bfloat16), "dp", scatter_dimension=0, tiled=True
        ).astype(jnp.float32),
    )
    gathered_attn = (
        lax.all_gather(ln1_gain, ("dp", "seq"), axis=0, tiled=True),
        lax.all_gather(w_qkv, ("dp", "seq"), axis=0, tiled=True),
        lax.all_gather(w_attn_out, ("dp", "seq"), axis=0, tiled=True),
    )
    gain_one = gathered_attn[0].astype(jnp.float32)
    qkv_mat = gathered_attn[1].reshape(model_width, 3 * model_width)
    proj_mat = gathered_attn[2].reshape(model_width, model_width)
    d_branch_low = d_middle.astype(jnp.bfloat16)
    grad_proj = matmul_tn(attended_rows, d_branch_low)
    d_attended = matmul_nt(d_branch_low, proj_mat).astype(jnp.bfloat16).reshape(tok_rows, HEADS, HD)
    delta_rows = jnp.einsum(
        "qhd,qhd->hq", d_attended.astype(jnp.float32), attended.astype(jnp.float32)
    )
    back_init = (
        jnp.zeros((tok_rows, HEADS, HD), jnp.float32),
        jnp.zeros((tok_rows * seq_devices, 2 * model_width), jnp.float32),
    )
    attend_key_piece = lax.all_gather(key_send, "seq", axis=1, tiled=True)
    attend_value_piece = lax.all_gather(value_send, "seq", axis=1, tiled=True)
    attend_seg_piece = lax.all_gather(seg_send, "seq", axis=1, tiled=True)
    span = attend_key_piece.shape[1]
    attend_step_rows = math.gcd(span, 512)

    def one_block(block_id, inner_state):
        grad_query, grad_kv = inner_state
        begin = block_id * attend_step_rows
        key_block = lax.dynamic_slice_in_dim(
            attend_key_piece[0], begin, attend_step_rows, 0
        ).reshape(attend_step_rows, HEADS, HD)
        value_block = lax.dynamic_slice_in_dim(
            attend_value_piece[0], begin, attend_step_rows, 0
        ).reshape(attend_step_rows, HEADS, HD)
        seg_block = lax.dynamic_slice_in_dim(attend_seg_piece[0], begin, attend_step_rows, 0)
        scores = masked_scores(query, key_block, seg_query, seg_block)
        probs = jnp.exp(scores - log_total[..., None])
        probs_low = probs.astype(jnp.bfloat16)
        value_grad = jnp.einsum(
            "hqk,qhd->khd", probs_low, d_attended, preferred_element_type=jnp.float32
        )
        d_probs = jnp.einsum(
            "qhd,khd->hqk", d_attended, value_block, preferred_element_type=jnp.float32
        )
        d_scores = (probs * (d_probs - delta_rows[..., None])).astype(jnp.bfloat16)
        grad_query = (
            grad_query
            + jnp.einsum("hqk,khd->qhd", d_scores, key_block, preferred_element_type=jnp.float32)
            * 0.125
        )
        key_grad = (
            jnp.einsum("hqk,qhd->khd", d_scores, query, preferred_element_type=jnp.float32) * 0.125
        )
        block_grads = jnp.concatenate(
            [
                key_grad.reshape(attend_step_rows, model_width),
                value_grad.reshape(attend_step_rows, model_width),
            ],
            axis=1,
        )
        grad_kv = lax.dynamic_update_slice_in_dim(grad_kv, block_grads, begin, 0)
        return (grad_query, grad_kv)

    back_state = lax.fori_loop(0, span // attend_step_rows, one_block, back_init)
    kv_grads = lax.psum_scatter(
        back_state[1].astype(jnp.bfloat16), "seq", scatter_dimension=0, tiled=True
    ).astype(jnp.float32)
    d_query = rotate_back(back_state[0], cosines, sines).reshape(tok_rows, model_width)
    d_key = rotate_back(
        kv_grads[:, :model_width].reshape(tok_rows, HEADS, HD), cosines, sines
    ).reshape(tok_rows, model_width)
    d_qkv_low = jnp.concatenate([d_query, d_key, kv_grads[:, model_width:]], axis=1).astype(
        jnp.bfloat16
    )
    grad_qkv = matmul_tn(normed_one_low, d_qkv_low)
    d_normed_one = matmul_nt(d_qkv_low, qkv_mat)
    grad_gain_one, d_input_part = norm_back(d_normed_one, unit_one, spread_one, gain_one)
    input_grad = d_middle + d_input_part
    attn_parts = tuple(
        (g.reshape(dp_devices, seq_devices, -1) for g in (grad_gain_one, grad_qkv, grad_proj))
    )
    attn_mid = (
        lax.psum_scatter(
            attn_parts[0].astype(jnp.bfloat16), "seq", scatter_dimension=1, tiled=True
        ).astype(jnp.float32),
        lax.psum_scatter(
            attn_parts[1].astype(jnp.bfloat16), "seq", scatter_dimension=1, tiled=True
        ).astype(jnp.float32),
        lax.psum_scatter(
            attn_parts[2].astype(jnp.bfloat16), "seq", scatter_dimension=1, tiled=True
        ).astype(jnp.float32),
    )
    attn_shards = (
        lax.psum_scatter(
            attn_mid[0].astype(jnp.bfloat16), "dp", scatter_dimension=0, tiled=True
        ).astype(jnp.float32),
        lax.psum_scatter(
            attn_mid[1].astype(jnp.bfloat16), "dp", scatter_dimension=0, tiled=True
        ).astype(jnp.float32),
        lax.psum_scatter(
            attn_mid[2].astype(jnp.bfloat16), "dp", scatter_dimension=0, tiled=True
        ).astype(jnp.float32),
    )
    return (
        output.reshape(1, tok_rows, model_width),
        input_grad.reshape(1, tok_rows, model_width),
        attn_shards[0].reshape(-1),
        attn_shards[1].reshape(-1),
        attn_shards[2].reshape(-1),
        mlp_shards[0].reshape(-1),
        mlp_shards[1].reshape(-1),
        mlp_shards[2].reshape(-1),
    )


MESH_IDS = pl.DeviceIdType.MESH
TOK = 128
WIDTH = 1024
PART = FF // 32
PAD = 96
HID = 8 * PAD
QKV = 3 * 256
BF = jnp.bfloat16
F32 = jnp.float32


def dot_nn(a, b):
    return lax.dot_general(a, b, (((1,), (0,)), ((), ())), preferred_element_type=F32)


def turned(u, low_half):
    return jnp.where(low_half, pltpu.roll(u, 96, axis=1), pltpu.roll(u, 32, axis=1))


def column(gain_ref):
    square = jnp.broadcast_to(gain_ref[...].astype(F32), (32, 32))
    rows = lax.broadcasted_iota(jnp.int32, (32, 32), 0)
    cols = lax.broadcasted_iota(jnp.int32, (32, 32), 1)
    return jnp.sum(jnp.where(rows == cols, square, 0.0), axis=1, keepdims=True)


def owner(r, k):
    return k // 4 * 16 + r // 2 * 8 + k // 2 % 2 * 4 + k % 2 * 2 + r % 2


def runs(places):
    found = []
    for lane, place in enumerate(places):
        if place is None:
            continue
        tile, shift = place[0], (place[1] - lane) % 128
        if found and found[-1][:2] == (tile, shift) and found[-1][3] == lane:
            found[-1] = found[-1][:3] + (lane + 1,)
        else:
            found.append((tile, shift, lane, lane + 1))
    return found


def in_moves(r, u):
    places = []
    for at in range(u * 128, u * 128 + 128):
        gate, rest = divmod(at, HID)
        k, i = divmod(rest, PAD)
        col = gate * FF + PART * owner(r, k) + i
        places.append(divmod(col, 128) if i < PART else None)
    return runs(places)


def out_moves(t):
    spots = {owner(r, k): (r, k) for r in range(4) for k in range(8)}
    places = []
    for col in range(t * 128, t * 128 + 128):
        gate, rest = divmod(col, FF)
        device, i = divmod(rest, PART)
        r, k = spots[device]
        u, lane = divmod(gate * HID + k * PAD + i, 128)
        places.append(((r, u), lane))
    return runs(places)


def moved(moves, load):
    lanes = lax.broadcasted_iota(jnp.int32, (1, 128), 1)
    out = jnp.zeros((32, 128), F32)
    for tile, shift, low, high in moves:
        piece = load(tile)
        if shift:
            piece = pltpu.roll(piece, 128 - shift, axis=1)
        out = jnp.where((lanes >= low) & (lanes < high), piece, out)
    return out


def finish_kernel(
    gq_in,
    go_in,
    gi_in,
    gd_in,
    out_in,
    ig_in,
    gain1_in,
    gain2_in,
    wq_flat,
    wi_flat,
    out_ref,
    ig_ref,
    gain1_ref,
    gq_ref,
    go_ref,
    gain2_ref,
    gi_ref,
    gd_ref,
    lines,
    gq_raw,
    go_raw,
    gi_raw,
    gd_raw,
    wq_raw,
    wi_raw,
    gq_own,
    go_own,
    gi_own,
    gd_own,
    ig_raw,
    out_raw,
    sems,
):
    count = [0]

    def start(src, dst):
        cp = pltpu.make_async_copy(src, dst, sems.at[count[0]])
        count[0] += 1
        cp.start()
        return cp

    gi_here = start(gi_in, gi_raw)
    wi_here = start(wi_flat, wi_raw)
    gq_here = start(gq_in, gq_raw)
    wq_here = start(wq_flat, wq_raw)
    gd_here = start(gd_in, gd_raw)
    go_here = start(go_in, go_raw)
    ig_here = start(ig_in, ig_raw)
    out_here = start(out_in, out_raw)
    written = []
    rows = lax.broadcasted_iota(jnp.int32, (32, 32), 0)
    cols = lax.broadcasted_iota(jnp.int32, (32, 32), 1)

    def line(total):
        total = jnp.sum(total, axis=1, keepdims=True)
        return jnp.sum(jnp.where(rows == cols, total, 0.0), axis=0, keepdims=True)

    qkv_rows = 3 * WIDTH // TOK
    in_rows = 2 * FF // TOK
    gain = column(gain2_in)
    total = jnp.zeros((32, 128), F32)
    wi_here.wait()
    lines[...] = wi_raw[...].astype(F32)
    ig_here.wait()
    written.append(start(ig_raw, ig_ref))
    out_here.wait()
    written.append(start(out_raw, out_ref))
    gd_here.wait()
    for j in range(8):
        gd_own[pl.ds(j, PART, stride=8), :] = gd_raw[0:PART, pl.ds(j * 128, 128)]
    written.append(start(gd_own, gd_ref))
    gi_here.wait()
    for j in range(in_rows):
        g = moved(out_moves(j), lambda t: gi_raw[t[0], :, pl.ds(t[1] * 128, 128)].astype(F32))
        total = total + g * lines[pl.ds(j, 32, stride=in_rows), :]
        gi_own[pl.ds(j, 32, stride=in_rows), :] = g * gain
    written.append(start(gi_own, gi_ref))
    gain2_ref[...] = line(total)
    gain = column(gain1_in)
    total = jnp.zeros((32, 128), F32)
    wq_here.wait()
    lines[0 : 32 * qkv_rows] = wq_raw[...].astype(F32)
    gq_here.wait()
    for j in range(qkv_rows):
        part, cut = divmod(j, 8)
        r = (cut // 2 % 2) * 2 + cut // 4
        g = gq_raw[r, :, pl.ds(part * 256 + cut % 2 * 128, 128)].astype(F32)
        total = total + g * lines[pl.ds(j, 32, stride=qkv_rows), :]
        gq_own[pl.ds(j, 32, stride=qkv_rows), :] = g * gain
    written.append(start(gq_own, gq_ref))
    gain1_ref[...] = line(total)
    go_here.wait()
    for j in range(8):
        go_own[pl.ds(j, 32, stride=8), :] = go_raw[:, pl.ds(j * 128, 128)].astype(F32)
    written.append(start(go_own, go_ref))
    for cp in written:
        cp.wait()


def layer_kernel(
    x_ref,
    cot_in,
    seg_in,
    cos_ref,
    sin_ref,
    gain1_in,
    gain2_in,
    wq_flat,
    wo_flat,
    wi_flat,
    wd_flat,
    out_ref,
    ig_ref,
    gq_ref,
    go_ref,
    gi_ref,
    gd_ref,
    seg_buf,
    n1,
    n2,
    cot,
    db,
    wq,
    wo,
    wi,
    wd,
    unit1,
    inv1,
    unit2,
    inv2,
    middle,
    dmid,
    q_buf,
    k_buf,
    v_buf,
    probs,
    att,
    datt,
    up_a,
    up_b,
    hidden,
    d_up,
    dqkv,
    ps,
    ps_in,
    ps_far,
    ps_back,
    gq,
    go,
    gi,
    gd,
    rq1,
    rq2,
    rq3,
    ro1,
    ro2,
    ro3,
    ri1,
    ri2,
    ri3,
    rd1,
    rd2,
    rd3,
    wq_in,
    wo_in,
    wi_in,
    lines,
    wide,
    out_vm,
    ig_vm,
    gq_vm,
    go_vm,
    gi_vm,
    gd_vm,
    send_sems,
    recv_sems,
    local_sems,
):
    dp, c = lax.axis_index("dp"), lax.axis_index("seq")
    x, y, z = lax.rem(dp, 2), lax.rem(dp // 2, 2), dp // 4
    zh, zp = z // 2, lax.rem(z, 2)
    role = zp * 2 + c

    def device(X, Y, Z, C):
        return (Z * 4 + Y * 2 + X, C)

    core_dev = device(x, y, z, 1 - c)
    pair_dev = device(x, y, zh * 2 + 1 - zp, c)
    diag_dev = device(x, y, zh * 2 + 1 - zp, 1 - c)
    half_dev = device(x, y, (1 - zh) * 2 + zp, c)
    x_dev = device(1 - x, y, z, c)
    y_dev = device(x, 1 - y, z, c)

    barrier = pltpu.get_barrier_semaphore()
    for dev in (core_dev, pair_dev, diag_dev, half_dev, x_dev, y_dev):
        pl.semaphore_signal(barrier, inc=1, device_id=dev, device_id_type=MESH_IDS)

    sent = []
    n_sems = [0]
    free = list(range(N_SENDS))

    def copy_to(src, dst, dev, keep=True):
        i, k = n_sems[0], free.pop(0)
        n_sems[0] += 1
        cp = pltpu.make_async_remote_copy(
            src_ref=src,
            dst_ref=dst,
            send_sem=send_sems.at[k],
            recv_sem=recv_sems.at[i],
            device_id=dev,
            device_id_type=MESH_IDS,
        )
        if keep:
            sent.append((cp, k))
        return cp

    local = []

    def emit(i, src, dst):
        cp = pltpu.make_async_copy(src, dst, local_sems.at[i])
        cp.start()
        local.append(cp)

    def settle(first):
        for cp, k in sent[:first]:
            cp.wait_send()
            free.append(k)
        del sent[:first]

    def go_copy(src, dst, dev):
        cp = copy_to(src, dst, dev)
        cp.start()
        return cp


    others = (
        (core_dev, zp * 2 + 1 - c),
        (pair_dev, (1 - zp) * 2 + c),
        (diag_dev, (1 - zp) * 2 + 1 - c),
    )

    def spread(own, buf):
        cps = [go_copy(own.at[r], buf.at[z, y, x, c], dev) for dev, r in others]
        return cps

    class Gather:
        def __init__(self, buf, cols, base=0):
            self.buf = buf
            self.halves = (pl.ds(base, cols // 2), pl.ds(base + cols // 2, cols // 2))
            self.per_half = buf.shape[0] // 2

        def of(self, which):
            return pl.ds(self.per_half * which, self.per_half)

        def spot(self, which, cut):
            return self.buf.at[(self.of(which), y, x) + (slice(None),) * (len(self.buf.shape) - 4) + (cut,)]

        def line(self, which, cut, i):
            rest = (slice(None),) * (len(self.buf.shape) - 4) + (cut,)
            at = (y, slice(None)) if i == 0 else (slice(None), x)
            return self.buf.at[(self.of(which),) + at + rest]

        def same(self, ref, dev):
            return go_copy(ref, ref, dev)

        def across(self):
            self.over = [self.same(self.spot(zh, cut), half_dev) for cut in self.halves]

        def own_first(self):
            self.a = [
                self.same(self.spot(zh, cut), dev) for cut, dev in zip(self.halves, (x_dev, y_dev))
            ]

        def own_second(self):
            self.b = []
            for i, dev in enumerate((y_dev, x_dev)):
                self.a[i].wait_recv()
                self.b.append(self.same(self.line(zh, self.halves[i], i), dev))

        def far_first(self):
            self.a2 = []
            for i, dev in enumerate((x_dev, y_dev)):
                self.over[i].wait_recv()
                self.a2.append(self.same(self.spot(1 - zh, self.halves[i]), dev))

        def far_second(self):
            self.b2 = []
            for i, dev in enumerate((y_dev, x_dev)):
                self.a2[i].wait_recv()
                self.b2.append(self.same(self.line(1 - zh, self.halves[i], i), dev))

        def done(self):
            for cp in self.b + self.b2:
                cp.wait_recv()

    class GatherOut:
        def __init__(self, buf, cols):
            self.buf = buf
            self.halves = (pl.ds(0, cols // 2), pl.ds(cols // 2, cols // 2))

        def start(self):
            self.s0 = copy_to(wo_in, self.buf.at[y, x, c], core_dev, keep=False)

            @pl.when(c != zh)
            def _():
                self.s0.start()

        def across(self):
            self.s1 = copy_to(self.buf.at[y, x], self.buf.at[y, x], half_dev, keep=False)

            @pl.when(c == zh)
            def _():
                self.buf[y, x, c] = wo_in[...]
                self.s0.wait_recv()
                self.s1.start()

        def first(self):
            @pl.when(c != zh)
            def _():
                self.s1.wait_recv()

            self.a = []
            for cut, dev in zip(self.halves, (x_dev, y_dev)):
                ref = self.buf.at[y, x, :, :, cut]
                self.a.append(go_copy(ref, ref, dev))

        def second(self):
            self.b = []
            for i, dev in enumerate((y_dev, x_dev)):
                self.a[i].wait_recv()
                cut = self.halves[i]
                ref = self.buf.at[y, :, :, :, cut] if i == 0 else self.buf.at[:, x, :, :, cut]
                self.b.append(go_copy(ref, ref, dev))

        def done(self):
            for cp in self.b:
                cp.wait_recv()

        def end(self):
            @pl.when(c != zh)
            def _():
                self.s0.wait_send()

            @pl.when(c == zh)
            def _():
                self.s1.wait_send()


    pieces = [pl.ds(i * (TOK // PIECES), TOK // PIECES) for i in range(PIECES)]

    class Share:
        def __init__(self, buf):
            self.buf = buf
            self.to_pair = [
                go_copy(buf.at[zp, c, cut], buf.at[zp, c, cut], pair_dev) for cut in pieces
            ]
            self.to_core = go_copy(buf.at[zp, c], buf.at[zp, c], core_dev)

        def forward(self):
            self.fwd = []
            for cp, cut in zip(self.to_pair, pieces):
                cp.wait_recv()
                ref = self.buf.at[1 - zp, c, cut]
                self.fwd.append(go_copy(ref, ref, core_dev))

        def core(self):
            self.to_core.wait_recv()

        def done(self):
            for cp in self.fwd:
                cp.wait_recv()

    class Reduce:
        def __init__(self, i):
            self.i = i

        def far_terms(self):
            i = self.i
            self.mine_far = go_copy(ps.at[i, 1 - zp, 1 - c], ps_in.at[i, 1 - zp], core_dev)

        def near_terms(self):
            i = self.i
            self.mine_near = go_copy(ps.at[i, zp, 1 - c], ps_in.at[i, zp], core_dev)

        def cross(self):
            i = self.i
            self.mine_far.wait_recv()
            self.far = []
            for cut in pieces:
                ps_far[i, cut] = (
                    ps[i, 1 - zp, c, cut].astype(F32) + ps_in[i, 1 - zp, cut].astype(F32)
                ).astype(BF)
                self.far.append(go_copy(ps_far.at[i, cut], ps_back.at[i, cut], pair_dev))

        def total(self):
            i = self.i
            self.mine_near.wait_recv()
            near = ps[i, zp, c].astype(F32) + ps_in[i, zp].astype(F32)
            for cp in self.far:
                cp.wait_recv()
            return near + ps_back[i].astype(F32)


    def add_into(target, extra):
        target[...] = (target[...].astype(F32) + extra[...].astype(F32)).astype(BF)

    def add_all(mine, got):
        n = got.shape[0]
        if n == 1:
            add_into(mine.at[0], got.at[0])
            return

        def body(j, carry):
            add_into(mine.at[j], got.at[j])
            return carry

        lax.fori_loop(0, n, body, 0)

    class Scatter:
        def __init__(self, buf, cols, r1, r2, r3, base=0):
            self.buf, self.r1, self.r2, self.r3 = buf, r1, r2, r3
            self.halves = (pl.ds(base, cols // 2), pl.ds(base + cols // 2, cols // 2))
            self.cols = pl.ds(base, cols)
            self.per_half = buf.shape[0] // 2
            self.rest = (slice(None),) * (len(buf.shape) - 4)
            self.c1, self.c2 = {}, {}

        def of(self, which):
            return pl.ds(self.per_half * which, self.per_half)

        def line(self, i, which, other):
            if i == 0:
                at = (1 - y if other else y, slice(None))
            else:
                at = (slice(None), 1 - x if other else x)
            return self.buf.at[(self.of(which),) + at + self.rest + (self.halves[i],)]

        def spot(self, i, which, other):
            Y, X = (y, x) if not other else ((y, 1 - x) if i == 0 else (1 - y, x))
            return self.buf.at[(self.of(which), Y, X) + self.rest + (self.halves[i],)]

        def first(self, far):
            which = 1 - zh if far else zh
            self.c1[far] = [
                go_copy(self.line(i, which, True), self.r1.at[i, far], dev)
                for i, dev in enumerate((y_dev, x_dev))
            ]

        def second(self, far):
            which = 1 - zh if far else zh
            self.c2[far] = []
            for i, dev in enumerate((x_dev, y_dev)):
                self.c1[far][i].wait_recv()
                add_all(self.line(i, which, False), self.r1.at[i, far])
                self.c2[far].append(go_copy(self.spot(i, which, True), self.r2.at[i, far], dev))

        def third(self, far):
            which = 1 - zh if far else zh
            for i in range(2):
                self.c2[far][i].wait_recv()
                add_all(self.spot(i, which, False), self.r2.at[i, far])
            if far:
                src = self.buf.at[(self.of(which), y, x) + self.rest + (self.cols,)]
                self.c3 = go_copy(src, self.r3, half_dev)

    class ScatterRows(Scatter):
        def fourth(self, out):
            self.c3.wait_recv()
            cols = self.cols
            add_all(self.buf.at[self.of(zh), y, x, :, :, cols], self.r3)
            self.c4 = []
            for dev, r in others:
                src = self.buf.at[2 * zh + r // 2, y, x, lax.rem(r, 2), :, cols]
                self.c4.append(go_copy(src, out.at[role, :, cols], dev))
            out[role, :, cols] = self.buf[z, y, x, c, :, cols]

        def done(self):
            for cp in self.c4:
                cp.wait_recv()

    class ScatterDown(Scatter):
        def fourth(self, out):
            self.c3.wait_recv()
            out[...] = self.buf[zh, y, x].astype(F32) + self.r3[0].astype(F32)

    class ScatterOut:
        def __init__(self, buf, cols, r1, r2, r3):
            self.buf, self.r1, self.r2, self.r3 = buf, r1, r2, r3
            self.halves = (pl.ds(0, cols // 2), pl.ds(cols // 2, cols // 2))

        def line(self, i, other):
            cut = self.halves[i]
            if i == 0:
                return self.buf.at[1 - y if other else y, :, :, :, cut]
            return self.buf.at[:, 1 - x if other else x, :, :, cut]

        def spot(self, i, other):
            Y, X = (y, x) if not other else ((y, 1 - x) if i == 0 else (1 - y, x))
            return self.buf.at[Y, X, :, :, self.halves[i]]

        def first(self):
            self.c1 = [
                go_copy(self.line(i, True), self.r1.at[i], dev)
                for i, dev in enumerate((y_dev, x_dev))
            ]

        def second(self):
            self.c2 = []
            for i, dev in enumerate((x_dev, y_dev)):
                self.c1[i].wait_recv()
                add_all(self.line(i, False), self.r1.at[i])
                self.c2.append(go_copy(self.spot(i, True), self.r2.at[i], dev))

        def third(self):
            for i in range(2):
                self.c2[i].wait_recv()
                add_all(self.spot(i, False), self.r2.at[i])
            self.c3 = copy_to(self.buf.at[y, x], self.r3, half_dev, keep=False)

            @pl.when(c != zh)
            def _():
                self.c3.start()

        def fourth(self, out):
            self.c4 = copy_to(self.r3.at[1 - c], out, core_dev, keep=False)

            @pl.when(c == zh)
            def _():
                self.c3.wait_recv()
                add_all(self.r3, self.buf.at[y, x])
                self.c4.start()
                out[...] = self.r3[c]

        def done(self):
            @pl.when(c != zh)
            def _():
                self.c4.wait_recv()
                self.c3.wait_send()

            @pl.when(c == zh)
            def _():
                self.c4.wait_send()

    tokens = x_ref[...].astype(F32)
    centred = tokens - jnp.mean(tokens, axis=-1, keepdims=True)
    inv = lax.rsqrt(jnp.mean(centred * centred, axis=-1, keepdims=True) + EPSILON)
    unit = centred * inv
    unit1[...] = unit
    inv1[...] = jnp.broadcast_to(inv, (TOK, 128))
    n1[zp, c] = unit.astype(BF)
    qkv_rows = 3 * WIDTH // TOK
    lines[0 : 32 * qkv_rows] = wq_flat[...].astype(F32)
    gain = column(gain1_in)
    for j in range(qkv_rows):
        part, cut = divmod(j, 8)
        r = (cut // 2 % 2) * 2 + cut // 4
        w = lines[pl.ds(j, 32, stride=qkv_rows), :] * gain
        wq_in[r, :, pl.ds(part * 256 + cut % 2 * 128, 128)] = w.astype(BF)
    seg_buf[zp, c] = jnp.broadcast_to(seg_in[...].astype(F32), (8, TOK))
    wq[z, y, x, c] = wq_in[role]
    cot[zp, c] = cot_in[...]
    lines2 = wide
    lines2[0 : 8 * PART] = wd_flat[...].astype(F32)
    lines2[8 * PART : 8 * PAD] = jnp.zeros((8 * (PAD - PART), TOK), F32)
    for j in range(8):
        wd[zh, y, x, :, pl.ds(j * 128, 128)] = lines2[pl.ds(j, PAD, stride=8), :].astype(BF)

    g_q, g_d = Gather(wq, QKV), Gather(wd, WIDTH)
    g_i, g_j = Gather(wi, HID), Gather(wi, HID, HID)
    g_o = GatherOut(wo, WIDTH)


    r_d = ScatterDown(gd, WIDTH, rd1, rd2, rd3)
    r_i = ScatterRows(gi, HID, ri1.at[0], ri2.at[0], ri3.at[0])
    r_j = ScatterRows(gi, HID, ri1.at[1], ri2.at[1], ri3.at[1], HID)
    r_q = ScatterRows(gq, QKV, rq1, rq2, rq3)
    r_o = ScatterOut(go, WIDTH, ro1, ro2, ro3)
    on = {}
    red = [Reduce(i) for i in range(4)]
    lanes = lax.broadcasted_iota(jnp.int32, (1, 128), 1)
    low_half = lax.rem(lanes, 64) < 32
    first_head = lanes < 64

    def qkv_step(s, carry):
        rows = n1[s].reshape(256, WIDTH)
        for part, dst in enumerate((q_buf, k_buf, v_buf)):
            for j in range(2):
                at = part * 256 + j * 128
                w = wq[:, :, :, :, :, pl.ds(at, 128)].reshape(WIDTH, 128)
                u = dot_nn(rows, w)
                if part < 2:
                    u = u * cos_ref[...] + turned(u, low_half) * sin_ref[...]
                dst[s, j] = u.astype(BF)
        return carry

    def only(head, u):
        return jnp.where(first_head if head == 0 else ~first_head, u, jnp.zeros_like(u))

    def attend(i, carry):
        s, j = i // 2, lax.rem(i, 2)
        q, k, v = q_buf[s, j], k_buf[s, j], v_buf[s, j]
        seg_row = jnp.concatenate([seg_buf[s, 0, 0:1], seg_buf[s, 1, 0:1]], axis=1)
        seg_col = jnp.broadcast_to(seg_row, (128, 256)).T[:, 0:1]
        same = seg_col == seg_row
        heads = []
        for h in range(2):
            scores = matmul_nt(only(h, q), k) * 0.125
            scores = jnp.where(same, scores, -1e30)
            weights = jnp.exp(scores - jnp.max(scores, axis=-1, keepdims=True))
            p = weights * (1.0 / jnp.sum(weights, axis=-1, keepdims=True))
            probs[i, h] = p
            heads.append(dot_nn(p.astype(BF), v))
        att[s, j] = jnp.where(first_head, heads[0], heads[1]).astype(BF)
        return carry

    def att_rows(s):
        return jnp.concatenate([att[s, 0], att[s, 1]], axis=1)

    def branch(s, carry):
        w = wo[...].reshape(256, WIDTH)
        ps[0, s] = dot_nn(att_rows(s), w).astype(BF).reshape(2, TOK, WIDTH)
        return carry

    def upper_for(s):
        def upper(j, carry):
            at = pl.multiple_of(j * 256, 256)
            rows = n2[s].reshape(256, WIDTH)
            inner = dot_nn(rows, wi[:, :, :, :, :, pl.ds(at, 256)].reshape(WIDTH, 256))
            gate = dot_nn(
                rows,
                wi[:, :, :, :, :, pl.ds(pl.multiple_of(HID + at, 256), 256)].reshape(WIDTH, 256),
            )
            cdf = 0.5 * (1.0 + lax.erf(inner * math.sqrt(0.5)))
            slope = cdf + inner * jnp.exp(-0.5 * inner * inner) * (1.0 / math.sqrt(2 * math.pi))
            bent = inner * cdf
            up_a[s, :, pl.ds(at, 256)] = gate * slope
            up_b[s, :, pl.ds(at, 256)] = bent
            hidden[s, :, pl.ds(at, 256)] = (bent * gate).astype(BF)
            return carry

        lax.fori_loop(0, HID // 256, upper, 0)

    def down_grad(i, carry):
        lhs = hidden[:, :, pl.ds(pl.multiple_of(i * 384, 384), 384)].reshape(512, 384)
        for j in range(2):
            rhs = cot[:, :, :, pl.ds(j * 512, 512)].reshape(512, 512)
            gd[i, :, :, :, pl.ds(j * 512, 512)] = (
                matmul_tn(lhs, rhs).astype(BF).reshape(2, 2, PAD, 512)
            )
        return carry

    def hidden_grad(i, carry):
        w = wd[i].reshape(384, WIDTH)
        at = pl.multiple_of(i * 384, 384)
        for s in range(2):
            dh = matmul_nt(cot[s].reshape(256, WIDTH), w)
            d_up[s, :, pl.ds(at, 384)] = (dh * up_a[s, :, pl.ds(at, 384)]).astype(BF)
            d_up[s, :, pl.ds(pl.multiple_of(HID + at, 384), 384)] = (
                dh * up_b[s, :, pl.ds(at, 384)]
            ).astype(BF)
        return carry

    def normed_two_grad_for(s):
        def normed_two_grad(i, carry):
            w = wi[i].reshape(256, 2 * HID)
            at = pl.multiple_of(i * 256, 256)
            ps[1, s, :, :, pl.ds(at, 256)] = matmul_nt(d_up[s], w).astype(BF).reshape(2, TOK, 256)
            return carry

        lax.fori_loop(0, 4, normed_two_grad, 0)

    def in_grad_for(base, first):
        def in_grad(i, carry):
            lhs = n2[:, :, :, pl.ds(pl.multiple_of(i * 256, 256), 256)].reshape(512, 256)
            for j in range(HID // 256):
                at = base + j * 256
                rhs = d_up[:, :, pl.ds(at, 256)].reshape(512, 256)
                gi[i, :, :, :, :, pl.ds(at, 256)] = (
                    matmul_tn(lhs, rhs).astype(BF).reshape(2, 2, 2, 32, 256)
                )
            return carry

        lax.fori_loop(first, first + 2, in_grad, 0)

    def down(i, carry):
        w = wd[...].reshape(HID, WIDTH)
        ps[2, i] = dot_nn(hidden[i], w).astype(BF).reshape(2, TOK, WIDTH)
        return carry

    def attended_grad(s, carry):
        rows = db[s].reshape(256, WIDTH)
        da = matmul_nt(rows, wo[...].reshape(256, WIDTH)).astype(BF)
        datt[s, 0] = da[:, 0:128]
        datt[s, 1] = da[:, 128:256]
        return carry

    def attend_back(i, carry):
        s, j = i // 2, lax.rem(i, 2)
        q, k, v, da = q_buf[s, j], k_buf[s, j], v_buf[s, j], datt[s, j]
        dq, dk, dv = [], [], []
        for h in range(2):
            p = probs[i, h]
            dprob = matmul_nt(only(h, da), v)
            delta = jnp.sum(p * dprob, axis=-1, keepdims=True)
            ds = (p * (dprob - delta)).astype(BF)
            dq.append(dot_nn(ds, k))
            dk.append(matmul_tn(ds, q))
            dv.append(matmul_tn(p.astype(BF), da))
        for part, pieces in enumerate((dq, dk, dv)):
            u = jnp.where(first_head, pieces[0], pieces[1])
            if part < 2:
                u = u * 0.125
                u = u * cos_ref[...] - turned(u, low_half) * sin_ref[...]
            dqkv[part, j, s] = u.astype(BF)
        return carry

    def first_grads_for(s):
        rows = jnp.concatenate([dqkv[p, j, s] for p in range(3) for j in range(2)], axis=1)

        def first_grads(i, carry):
            w = wq[i].reshape(256, QKV)
            at = pl.multiple_of(i * 256, 256)
            ps[3, s, :, :, pl.ds(at, 256)] = matmul_nt(rows, w).astype(BF).reshape(2, TOK, 256)
            return carry

        lax.fori_loop(0, 4, first_grads, 0)

    def qkv_grad(i, carry):
        lhs = n1[:, :, :, pl.ds(pl.multiple_of(i * 256, 256), 256)].reshape(512, 256)
        for p in range(3):
            for j in range(2):
                rhs = dqkv[p, j].reshape(512, 128)
                gq[i, :, :, :, :, pl.ds(p * 256 + j * 128, 128)] = (
                    matmul_tn(lhs, rhs).astype(BF).reshape(2, 2, 2, 32, 128)
                )
        return carry

    pl.semaphore_wait(barrier, 6)
    on["s_q"] = spread(wq_in, wq)
    wide[0:256] = wo_flat[...].astype(F32)
    for j in range(8):
        wo_in[:, pl.ds(j * 128, 128)] = wide[pl.ds(j, 32, stride=8), :].astype(BF)
    on["seg"] = [go_copy(seg_buf.at[zp, c], seg_buf.at[zp, c], dev) for dev, _ in others]
    g_o.start()
    g_o.across()
    in_rows = 2 * FF // TOK
    lines[...] = wi_flat[...].astype(F32)
    gain = column(gain2_in)
    for j in range(in_rows):
        wide[pl.ds(j * 32, 32), :] = lines[pl.ds(j, 32, stride=in_rows), :] * gain
    for r in range(4):
        for u in range(2 * HID // TOK):
            tile = moved(in_moves(r, u), lambda t: wide[pl.ds(t * 32, 32), :])
            wi_in[r, :, pl.ds(u * 128, 128)] = tile.astype(BF)
    wi[z, y, x, c] = wi_in[role]
    on["s_i"] = spread(wi_in, wi)
    g_d.own_first()
    g_d.own_second()
    for cp in on["s_q"]:
        cp.wait_recv()
    g_q.across()
    g_q.own_first()
    on["n1"] = Share(n1)
    g_d.across()
    for cp in on["seg"]:
        cp.wait_recv()
    g_o.first()
    g_q.own_second()
    g_o.second()
    g_q.far_first()
    for cp in on["s_i"]:
        cp.wait_recv()
    g_i.own_first()
    g_i.across()
    g_q.far_second()
    on["cot"] = Share(cot)
    g_o.done()
    g_i.own_second()
    on["n1"].forward()
    g_j.own_first()
    on["n1"].done()
    on["n1"].core()
    g_q.done()
    lax.fori_loop(1 - zp, 2 - zp, qkv_step, 0)
    lax.fori_loop(zp, zp + 1, qkv_step, 0)
    g_d.far_first()
    g_j.across()
    lax.fori_loop(2 * zp, 2 * zp + 2, attend, 0)
    on["cot"].core()
    g_i.far_first()
    lax.fori_loop(2 * (1 - zp), 2 * (1 - zp) + 2, attend, 0)
    lax.fori_loop(1 - zp, 2 - zp, branch, 0)
    red[0].far_terms()
    red[0].cross()
    g_j.own_second()
    on["cot"].forward()
    g_i.far_second()
    lax.fori_loop(zp, zp + 1, branch, 0)
    red[0].near_terms()
    g_j.far_first()
    mid = x_ref[...].astype(F32) + red[0].total()
    middle[...] = mid
    centred = mid - jnp.mean(mid, axis=-1, keepdims=True)
    inv = lax.rsqrt(jnp.mean(centred * centred, axis=-1, keepdims=True) + EPSILON)
    unit = centred * inv
    unit2[...] = unit
    inv2[...] = jnp.broadcast_to(inv, (TOK, 128))
    n2[zp, c] = unit.astype(BF)
    on["n2"] = Share(n2)
    g_j.far_second()
    g_d.far_second()
    g_i.done()
    on["n2"].forward()
    g_j.done()
    on["n2"].core()
    on["mark"] = len(sent)
    upper_for(zp)
    on["cot"].done()
    on["n2"].done()
    upper_for(1 - zp)
    lax.fori_loop(0, 2, down_grad, 0)
    g_d.done()
    r_d.first(1)
    lax.fori_loop(0, 2, hidden_grad, 0)
    normed_two_grad_for(1 - zp)
    red[1].far_terms()
    in_grad_for(HID, 2 * (1 - zh))
    r_j.first(1)
    red[1].cross()
    in_grad_for(0, 2 * (1 - zh))
    r_i.first(1)
    normed_two_grad_for(zp)
    red[1].near_terms()
    in_grad_for(HID, 2 * zh)
    r_j.second(1)
    r_d.first(0)
    settle(on["mark"])
    e = red[1].total()
    n = unit2[...]
    d_middle = cot_in[...].astype(F32) + inv2[:, 0:1] * (
        e
        - jnp.mean(e, axis=-1, keepdims=True)
        - n * jnp.mean(e * n, axis=-1, keepdims=True)
    )
    dmid[...] = d_middle
    db[zp, c] = d_middle.astype(BF)
    on["db"] = Share(db)
    r_d.second(1)
    lax.fori_loop(1 - zp, 2 - zp, down, 0)
    red[2].far_terms()
    r_j.third(1)
    in_grad_for(0, 2 * zh)
    r_j.first(0)
    on["db"].forward()
    on["db"].core()
    r_i.second(1)
    lax.fori_loop(zp, zp + 1, attended_grad, 0)
    r_d.second(0)
    red[2].cross()
    lax.fori_loop(2 * zp, 2 * zp + 2, attend_back, 0)
    r_i.first(0)
    on["db"].done()
    r_d.third(1)
    lax.fori_loop(1 - zp, 2 - zp, attended_grad, 0)
    lhs = att
    for j in range(2):
        for half in range(2):
            rhs = db[:, :, :, pl.ds(half * 512, 512)].reshape(512, 512)
            go[j, :, :, :, pl.ds(half * 512, 512)] = (
                matmul_tn(lhs[:, j].reshape(512, 128), rhs).astype(BF).reshape(2, 2, 32, 512)
            )
    lax.fori_loop(zp, zp + 1, down, 0)
    red[2].near_terms()
    r_o.first()
    lax.fori_loop(2 * (1 - zp), 2 * (1 - zp) + 2, attend_back, 0)
    lax.fori_loop(2 * zh, 2 * zh + 2, qkv_grad, 0)
    lax.fori_loop(2 * (1 - zh), 2 * (1 - zh) + 2, qkv_grad, 0)
    r_q.first(1)
    first_grads_for(1 - zp)
    red[3].far_terms()
    out_vm[...] = (middle[...] + red[2].total()).astype(BF)
    emit(0, out_vm, out_ref)
    r_i.third(1)
    r_i.second(0)
    red[3].cross()
    first_grads_for(zp)
    red[3].near_terms()
    r_o.second()
    r_q.second(1)
    r_d.third(0)
    r_i.third(0)
    r_o.third()
    r_q.first(0)
    r_i.fourth(gi_vm)
    r_j.second(0)
    r_q.third(1)
    r_d.fourth(gd_vm)
    emit(2, gd_vm, gd_ref)
    r_o.fourth(go_vm)
    r_q.second(0)
    e = red[3].total()
    n = unit1[...]
    ig_vm[...] = dmid[...] + inv1[:, 0:1] * (
        e
        - jnp.mean(e, axis=-1, keepdims=True)
        - n * jnp.mean(e * n, axis=-1, keepdims=True)
    )
    emit(1, ig_vm, ig_ref)
    r_j.third(0)
    r_i.done()
    emit(3, gi_vm.at[:, :, pl.ds(0, HID)], gi_ref.at[:, :, pl.ds(0, HID)])
    r_j.fourth(gi_vm)
    r_q.third(0)
    r_q.fourth(gq_vm)
    r_j.done()
    emit(6, gi_vm.at[:, :, pl.ds(HID, HID)], gi_ref.at[:, :, pl.ds(HID, HID)])
    r_o.done()
    emit(4, go_vm, go_ref)
    r_q.done()
    emit(5, gq_vm, gq_ref)
    g_o.end()
    assert n_sems[0] == N_COPIES
    settle(len(sent))
    for cp in local:
        cp.wait()


def block_device(inputs, segments, cotangent, ln1_gain, w_qkv, w_attn_out, ln2_gain, w_in, w_mlp_out):
    places = np.arange(2 * TOK, dtype=np.float32)
    freqs = (1.0 / ROPE_BASE ** (np.arange(0, HD, 2, dtype=np.float64) / HD)).astype(np.float32)
    angles = np.tile(places[:, None] * freqs[None, :], (1, 4))
    signs = np.where(np.arange(2 * HD) % HD < HD // 2, -1.0, 1.0).astype(np.float32)
    cosines = jnp.asarray(np.cos(angles))
    sines = jnp.asarray(np.sin(angles) * signs)
    gain_one, gain_two = ln1_gain[None], ln2_gain[None]
    wq_flat, wo_flat = w_qkv.reshape(-1, TOK), w_attn_out.reshape(-1, TOK)
    wi_flat, wd_flat = w_in.reshape(-1, TOK), w_mlp_out.reshape(-1, TOK)

    vm = pltpu.VMEM
    group = (2, 2, TOK, WIDTH)
    rows = (4, 2, 2, 2, 32)
    outs = pl.pallas_call(
        layer_kernel,
        out_shape=(
            jax.ShapeDtypeStruct((TOK, WIDTH), BF),
            jax.ShapeDtypeStruct((TOK, WIDTH), F32),
            jax.ShapeDtypeStruct((4, 32, QKV), BF),
            jax.ShapeDtypeStruct((32, WIDTH), BF),
            jax.ShapeDtypeStruct((4, 32, 2 * HID), BF),
            jax.ShapeDtypeStruct((PAD, WIDTH), F32),
        ),
        in_specs=[pl.BlockSpec(memory_space=vm)] * 11,
        out_specs=(pl.BlockSpec(memory_space=pl.ANY),) * 6,
        scratch_shapes=[
            vm((2, 2, 8, TOK), F32),
            vm(group, BF),
            vm(group, BF),
            vm(group, BF),
            vm(group, BF),
            vm(rows + (QKV,), BF),
            vm((2, 2, 2, 32, WIDTH), BF),
            vm(rows + (2 * HID,), BF),
            vm((2, 2, 2, PAD, WIDTH), BF),
            vm((TOK, WIDTH), F32),
            vm((TOK, 128), F32),
            vm((TOK, WIDTH), F32),
            vm((TOK, 128), F32),
            vm((TOK, WIDTH), F32),
            vm((TOK, WIDTH), F32),
            vm((2, 2, 256, 128), BF),
            vm((2, 2, 256, 128), BF),
            vm((2, 2, 256, 128), BF),
            vm((4, 2, 256, 256), F32),
            vm((2, 2, 256, 128), BF),
            vm((2, 2, 256, 128), BF),
            vm((2, 256, HID), F32),
            vm((2, 256, HID), F32),
            vm((2, 256, HID), BF),
            vm((2, 256, 2 * HID), BF),
            vm((3, 2, 2, 256, 128), BF),
            vm((4,) + group, BF),
            vm((4, 2, TOK, WIDTH), BF),
            vm((4, TOK, WIDTH), BF),
            vm((4, TOK, WIDTH), BF),
            vm(rows + (QKV,), BF),
            vm((2, 2, 2, 32, WIDTH), BF),
            vm(rows + (2 * HID,), BF),
            vm((2, 2, 2, PAD, WIDTH), BF),
            vm((2, 2, 2, 2, 2, 32, QKV // 2), BF),
            vm((2, 2, 2, 2, 32, QKV // 2), BF),
            vm((2, 2, 32, QKV), BF),
            vm((2, 2, 2, 32, WIDTH // 2), BF),
            vm((2, 2, 32, WIDTH // 2), BF),
            vm((2, 32, WIDTH), BF),
            vm((2, 2, 2, 2, 2, 2, 32, HID // 2), BF),
            vm((2, 2, 2, 2, 2, 32, HID // 2), BF),
            vm((2, 2, 2, 32, HID), BF),
            vm((2, 2, 1, 2, PAD, WIDTH // 2), BF),
            vm((2, 2, 1, PAD, WIDTH // 2), BF),
            vm((1, PAD, WIDTH), BF),
            vm((4, 32, QKV), BF),
            vm((32, WIDTH), BF),
            vm((4, 32, 2 * HID), BF),
            vm((64 * FF // TOK, TOK), F32),
            vm((64 * FF // TOK, TOK), F32),
            vm((TOK, WIDTH), BF),
            vm((TOK, WIDTH), F32),
            vm((4, 32, QKV), BF),
            vm((32, WIDTH), BF),
            vm((4, 32, 2 * HID), BF),
            vm((PAD, WIDTH), F32),
            pltpu.SemaphoreType.DMA((N_SENDS,)),
            pltpu.SemaphoreType.DMA((N_COPIES,)),
            pltpu.SemaphoreType.DMA((7,)),
        ],
        compiler_params=pltpu.CompilerParams(
            collective_id=0, has_side_effects=True, vmem_limit_bytes=60 * 2**20
        ),
    )(
        inputs[0],
        cotangent[0],
        segments,
        cosines,
        sines,
        gain_one,
        gain_two,
        wq_flat,
        wo_flat,
        wi_flat,
        wd_flat,
    )
    output, input_grad, gq, go, gi, gd = outs
    final = pl.pallas_call(
        finish_kernel,
        out_shape=(
            jax.ShapeDtypeStruct((TOK, WIDTH), BF),
            jax.ShapeDtypeStruct((TOK, WIDTH), F32),
            jax.ShapeDtypeStruct((1, 32), F32),
            jax.ShapeDtypeStruct(wq_flat.shape, F32),
            jax.ShapeDtypeStruct(wo_flat.shape, F32),
            jax.ShapeDtypeStruct((1, 32), F32),
            jax.ShapeDtypeStruct(wi_flat.shape, F32),
            jax.ShapeDtypeStruct(wd_flat.shape, F32),
        ),
        in_specs=[pl.BlockSpec(memory_space=pl.ANY)] * 6
        + [pl.BlockSpec(memory_space=vm)] * 2
        + [pl.BlockSpec(memory_space=pl.ANY)] * 2,
        out_specs=tuple(
            pl.BlockSpec(memory_space=vm if i in (2, 5) else pl.ANY) for i in range(8)
        ),
        scratch_shapes=[
            vm(wi_flat.shape, F32),
            vm((4, 32, QKV), BF),
            vm((32, WIDTH), BF),
            vm((4, 32, 2 * HID), BF),
            vm((PAD, WIDTH), F32),
            vm(wq_flat.shape, BF),
            vm(wi_flat.shape, BF),
            vm(wq_flat.shape, F32),
            vm(wo_flat.shape, F32),
            vm(wi_flat.shape, F32),
            vm(wd_flat.shape, F32),
            vm((TOK, WIDTH), F32),
            vm((TOK, WIDTH), BF),
            pltpu.SemaphoreType.DMA((14,)),
        ],
        compiler_params=pltpu.CompilerParams(vmem_limit_bytes=60 * 2**20),
    )(gq, go, gi, gd, output, input_grad, gain_one, gain_two, wq_flat, wi_flat)
    return (final[0][None], final[1][None]) + tuple(f.reshape(-1) for f in final[2:])


N_COPIES = 142
N_SENDS = 100
PIECES = 2


def solution(mesh):
    block = dict(mesh.shape) == {"dp": 16, "seq": 2}
    placed = (
        P("dp", "seq", None),
        P("dp", "seq"),
        P("dp", "seq", None),
        P(("dp", "seq")),
        P(("dp", "seq")),
        P(("dp", "seq")),
        P(("dp", "seq")),
        P(("dp", "seq")),
        P(("dp", "seq")),
    )
    return jax.shard_map(
        block_device if block else general_device,
        mesh=mesh,
        in_specs=placed,
        out_specs=(
            P("dp", "seq", None),
            P("dp", "seq", None),
            P(("dp", "seq")),
            P(("dp", "seq")),
            P(("dp", "seq")),
            P(("dp", "seq")),
            P(("dp", "seq")),
            P(("dp", "seq")),
        ),
        check_vma=False,
    )
```

```python
import functools
import math

import jax
import jax.numpy as jnp
import numpy as np
from jax import lax
from jax.experimental import pallas as pl
from jax.experimental.pallas import tpu as pltpu
from jax.sharding import PartitionSpec as P

HEADS = 16
HD = 64
FF = 2624


EPSILON = 1e-05
ROPE_BASE = 160000.0


def rope_tables(places):
    freqs = 1.0 / ROPE_BASE ** (jnp.arange(0, HD, 2, dtype=jnp.float32) / HD)
    angles = places[:, None] * freqs[None, :]
    angles = jnp.concatenate([angles, angles], axis=1)
    return (jnp.cos(angles), jnp.sin(angles))


def rotate(values_in, cosines, sines):
    halfway = values_in.shape[-1] // 2
    turned = jnp.concatenate([-values_in[..., halfway:], values_in[..., :halfway]], axis=-1)
    return values_in * cosines[:, None, :] + turned * sines[:, None, :]


def rotate_back(grads_in, cosines, sines):
    halfway = grads_in.shape[-1] // 2
    scaled = grads_in * sines[:, None, :]
    turned = jnp.concatenate([scaled[..., halfway:], -scaled[..., :halfway]], axis=-1)
    return grads_in * cosines[:, None, :] + turned


def norm_forward(values_in, gain):
    centred = values_in - jnp.mean(values_in, axis=-1, keepdims=True)
    inv_spread = lax.rsqrt(jnp.mean(centred * centred, axis=-1, keepdims=True) + EPSILON)
    unit_rows = centred * inv_spread
    return (unit_rows * gain, unit_rows, inv_spread)


def norm_back(grad_rows, unit_rows, inv_spread, gain):
    gain_grad = jnp.sum(grad_rows * unit_rows, axis=0)
    scaled = grad_rows * gain
    inner_mean = jnp.mean(scaled, axis=-1, keepdims=True)
    cross_mean = jnp.mean(scaled * unit_rows, axis=-1, keepdims=True)
    return (gain_grad, inv_spread * (scaled - inner_mean - unit_rows * cross_mean))


def matmul_tn(left, right):
    return lax.dot_general(
        left, right, (((0,), (0,)), ((), ())), preferred_element_type=jnp.float32
    )


def matmul_nt(left, right):
    return lax.dot_general(
        left, right, (((1,), (1,)), ((), ())), preferred_element_type=jnp.float32
    )


def masked_scores(query, key_block, seg_query, seg_block):
    scores = (
        jnp.einsum("qhd,khd->hqk", query, key_block, preferred_element_type=jnp.float32) * 0.125
    )
    same_doc = seg_query[:, None] == seg_block[None, :]
    return jnp.where(same_doc[None], scores, -1e30)


def gated(inner, gate):
    return jax.nn.gelu(inner, approximate=False) * gate


def general_device(inputs, segments, cotangent, ln1_gain, w_qkv, w_attn_out, ln2_gain, w_in, w_mlp_out):
    tok_rows = inputs.shape[1]
    model_width = inputs.shape[2]
    seq_devices = lax.axis_size("seq")
    dp_devices = lax.axis_size("dp")
    tokens_in = inputs[0].astype(jnp.float32)
    seg_send = segments.astype(jnp.bfloat16)
    seg_query = seg_send[0]
    gathered_attn = (
        lax.all_gather(ln1_gain, ("dp", "seq"), axis=0, tiled=True),
        lax.all_gather(w_qkv, ("dp", "seq"), axis=0, tiled=True),
        lax.all_gather(w_attn_out, ("dp", "seq"), axis=0, tiled=True),
    )
    gain_one = gathered_attn[0].astype(jnp.float32)
    qkv_mat = gathered_attn[1].reshape(model_width, 3 * model_width)
    proj_mat = gathered_attn[2].reshape(model_width, model_width)
    places = (lax.axis_index("seq") * tok_rows + jnp.arange(tok_rows, dtype=jnp.int32)).astype(
        jnp.float32
    )
    cosines, sines = rope_tables(places)
    normed_one, unit_one, spread_one = norm_forward(tokens_in, gain_one)
    normed_one_low = normed_one.astype(jnp.bfloat16)
    qkv_rows = jnp.dot(normed_one_low, qkv_mat, preferred_element_type=jnp.float32)
    query = rotate(qkv_rows[:, :model_width].reshape(tok_rows, HEADS, HD), cosines, sines).astype(
        jnp.bfloat16
    )
    key_rot = rotate(
        qkv_rows[:, model_width : 2 * model_width].reshape(tok_rows, HEADS, HD), cosines, sines
    ).astype(jnp.bfloat16)
    value_rows = qkv_rows[:, 2 * model_width :].astype(jnp.bfloat16)
    key_send = key_rot.reshape(1, tok_rows, model_width)
    value_send = value_rows.reshape(1, tok_rows, model_width)
    fwd_init = (
        jnp.full((HEADS, tok_rows), -1e30, jnp.float32),
        jnp.zeros((HEADS, tok_rows), jnp.float32),
        jnp.zeros((tok_rows, HEADS, HD), jnp.float32),
    )
    key_piece = lax.all_gather(key_send, "seq", axis=1, tiled=True)
    value_piece = lax.all_gather(value_send, "seq", axis=1, tiled=True)
    seg_piece = lax.all_gather(seg_send, "seq", axis=1, tiled=True)
    span = key_piece.shape[1]
    step_rows = math.gcd(span, 512)

    def one_block(block_id, inner_state):
        top_score, total, accum = inner_state
        begin = block_id * step_rows
        key_block = lax.dynamic_slice_in_dim(key_piece[0], begin, step_rows, 0).reshape(
            step_rows, HEADS, HD
        )
        value_block = lax.dynamic_slice_in_dim(value_piece[0], begin, step_rows, 0).reshape(
            step_rows, HEADS, HD
        )
        seg_block = lax.dynamic_slice_in_dim(seg_piece[0], begin, step_rows, 0)
        scores = masked_scores(query, key_block, seg_query, seg_block)
        new_top = jnp.maximum(top_score, jnp.max(scores, axis=-1))
        fading = jnp.exp(top_score - new_top)
        weights = jnp.exp(scores - new_top[..., None])
        total = total * fading + jnp.sum(weights, axis=-1)
        accum = accum * fading.T[:, :, None] + jnp.einsum(
            "hqk,khd->qhd",
            weights.astype(jnp.bfloat16),
            value_block,
            preferred_element_type=jnp.float32,
        )
        return (new_top, total, accum)

    fwd_state = lax.fori_loop(0, span // step_rows, one_block, fwd_init)
    run_top, run_total, run_accum = fwd_state
    log_total = run_top + jnp.log(run_total)
    attended = (run_accum / run_total.T[:, :, None]).astype(jnp.bfloat16)
    attended_rows = attended.reshape(tok_rows, model_width)
    middle = tokens_in + jnp.dot(attended_rows, proj_mat, preferred_element_type=jnp.float32)
    gathered_mlp = (
        lax.all_gather(ln2_gain, ("dp", "seq"), axis=0, tiled=True),
        lax.all_gather(w_in, ("dp", "seq"), axis=0, tiled=True),
        lax.all_gather(w_mlp_out, ("dp", "seq"), axis=0, tiled=True),
    )
    gain_two = gathered_mlp[0].astype(jnp.float32)
    in_mat = gathered_mlp[1].reshape(model_width, 2 * FF)
    down_mat = gathered_mlp[2].reshape(FF, model_width)
    normed_two, unit_two, spread_two = norm_forward(middle, gain_two)
    normed_two_low = normed_two.astype(jnp.bfloat16)
    upper = jnp.dot(normed_two_low, in_mat, preferred_element_type=jnp.float32)
    inner = upper[:, :FF]
    gate = upper[:, FF:]
    hidden_low = gated(inner, gate).astype(jnp.bfloat16)
    output = (middle + jnp.dot(hidden_low, down_mat, preferred_element_type=jnp.float32)).astype(
        jnp.bfloat16
    )
    gathered_mlp = (
        lax.all_gather(ln2_gain, ("dp", "seq"), axis=0, tiled=True),
        lax.all_gather(w_in, ("dp", "seq"), axis=0, tiled=True),
        lax.all_gather(w_mlp_out, ("dp", "seq"), axis=0, tiled=True),
    )
    gain_two = gathered_mlp[0].astype(jnp.float32)
    in_mat = gathered_mlp[1].reshape(model_width, 2 * FF)
    down_mat = gathered_mlp[2].reshape(FF, model_width)
    grad_low = cotangent[0]
    grad_rows = grad_low.astype(jnp.float32)
    d_hidden = matmul_nt(grad_low, down_mat)
    grad_down = matmul_tn(hidden_low, grad_low)
    gated_value, pull = jax.vjp(gated, inner, gate)
    d_inner, d_gate = pull(d_hidden)
    d_upper_low = jnp.concatenate([d_inner, d_gate], axis=1).astype(jnp.bfloat16)
    grad_in = matmul_tn(normed_two_low, d_upper_low)
    d_normed_two = matmul_nt(d_upper_low, in_mat)
    grad_gain_two, d_middle_part = norm_back(d_normed_two, unit_two, spread_two, gain_two)
    d_middle = grad_rows + d_middle_part
    mlp_parts = tuple(
        (g.reshape(dp_devices, seq_devices, -1) for g in (grad_gain_two, grad_in, grad_down))
    )
    mlp_mid = (
        lax.psum_scatter(
            mlp_parts[0].astype(jnp.bfloat16), "seq", scatter_dimension=1, tiled=True
        ).astype(jnp.float32),
        lax.psum_scatter(
            mlp_parts[1].astype(jnp.bfloat16), "seq", scatter_dimension=1, tiled=True
        ).astype(jnp.float32),
        lax.psum_scatter(
            mlp_parts[2].astype(jnp.bfloat16), "seq", scatter_dimension=1, tiled=True
        ).astype(jnp.float32),
    )
    mlp_shards = (
        lax.psum_scatter(
            mlp_mid[0].astype(jnp.bfloat16), "dp", scatter_dimension=0, tiled=True
        ).astype(jnp.float32),
        lax.psum_scatter(
            mlp_mid[1].astype(jnp.bfloat16), "dp", scatter_dimension=0, tiled=True
        ).astype(jnp.float32),
        lax.psum_scatter(
            mlp_mid[2].astype(jnp.bfloat16), "dp", scatter_dimension=0, tiled=True
        ).astype(jnp.float32),
    )
    gathered_attn = (
        lax.all_gather(ln1_gain, ("dp", "seq"), axis=0, tiled=True),
        lax.all_gather(w_qkv, ("dp", "seq"), axis=0, tiled=True),
        lax.all_gather(w_attn_out, ("dp", "seq"), axis=0, tiled=True),
    )
    gain_one = gathered_attn[0].astype(jnp.float32)
    qkv_mat = gathered_attn[1].reshape(model_width, 3 * model_width)
    proj_mat = gathered_attn[2].reshape(model_width, model_width)
    d_branch_low = d_middle.astype(jnp.bfloat16)
    grad_proj = matmul_tn(attended_rows, d_branch_low)
    d_attended = matmul_nt(d_branch_low, proj_mat).astype(jnp.bfloat16).reshape(tok_rows, HEADS, HD)
    delta_rows = jnp.einsum(
        "qhd,qhd->hq", d_attended.astype(jnp.float32), attended.astype(jnp.float32)
    )
    back_init = (
        jnp.zeros((tok_rows, HEADS, HD), jnp.float32),
        jnp.zeros((tok_rows * seq_devices, 2 * model_width), jnp.float32),
    )
    attend_key_piece = lax.all_gather(key_send, "seq", axis=1, tiled=True)
    attend_value_piece = lax.all_gather(value_send, "seq", axis=1, tiled=True)
    attend_seg_piece = lax.all_gather(seg_send, "seq", axis=1, tiled=True)
    span = attend_key_piece.shape[1]
    attend_step_rows = math.gcd(span, 512)

    def one_block(block_id, inner_state):
        grad_query, grad_kv = inner_state
        begin = block_id * attend_step_rows
        key_block = lax.dynamic_slice_in_dim(
            attend_key_piece[0], begin, attend_step_rows, 0
        ).reshape(attend_step_rows, HEADS, HD)
        value_block = lax.dynamic_slice_in_dim(
            attend_value_piece[0], begin, attend_step_rows, 0
        ).reshape(attend_step_rows, HEADS, HD)
        seg_block = lax.dynamic_slice_in_dim(attend_seg_piece[0], begin, attend_step_rows, 0)
        scores = masked_scores(query, key_block, seg_query, seg_block)
        probs = jnp.exp(scores - log_total[..., None])
        probs_low = probs.astype(jnp.bfloat16)
        value_grad = jnp.einsum(
            "hqk,qhd->khd", probs_low, d_attended, preferred_element_type=jnp.float32
        )
        d_probs = jnp.einsum(
            "qhd,khd->hqk", d_attended, value_block, preferred_element_type=jnp.float32
        )
        d_scores = (probs * (d_probs - delta_rows[..., None])).astype(jnp.bfloat16)
        grad_query = (
            grad_query
            + jnp.einsum("hqk,khd->qhd", d_scores, key_block, preferred_element_type=jnp.float32)
            * 0.125
        )
        key_grad = (
            jnp.einsum("hqk,qhd->khd", d_scores, query, preferred_element_type=jnp.float32) * 0.125
        )
        block_grads = jnp.concatenate(
            [
                key_grad.reshape(attend_step_rows, model_width),
                value_grad.reshape(attend_step_rows, model_width),
            ],
            axis=1,
        )
        grad_kv = lax.dynamic_update_slice_in_dim(grad_kv, block_grads, begin, 0)
        return (grad_query, grad_kv)

    back_state = lax.fori_loop(0, span // attend_step_rows, one_block, back_init)
    kv_grads = lax.psum_scatter(
        back_state[1].astype(jnp.bfloat16), "seq", scatter_dimension=0, tiled=True
    ).astype(jnp.float32)
    d_query = rotate_back(back_state[0], cosines, sines).reshape(tok_rows, model_width)
    d_key = rotate_back(
        kv_grads[:, :model_width].reshape(tok_rows, HEADS, HD), cosines, sines
    ).reshape(tok_rows, model_width)
    d_qkv_low = jnp.concatenate([d_query, d_key, kv_grads[:, model_width:]], axis=1).astype(
        jnp.bfloat16
    )
    grad_qkv = matmul_tn(normed_one_low, d_qkv_low)
    d_normed_one = matmul_nt(d_qkv_low, qkv_mat)
    grad_gain_one, d_input_part = norm_back(d_normed_one, unit_one, spread_one, gain_one)
    input_grad = d_middle + d_input_part
    attn_parts = tuple(
        (g.reshape(dp_devices, seq_devices, -1) for g in (grad_gain_one, grad_qkv, grad_proj))
    )
    attn_mid = (
        lax.psum_scatter(
            attn_parts[0].astype(jnp.bfloat16), "seq", scatter_dimension=1, tiled=True
        ).astype(jnp.float32),
        lax.psum_scatter(
            attn_parts[1].astype(jnp.bfloat16), "seq", scatter_dimension=1, tiled=True
        ).astype(jnp.float32),
        lax.psum_scatter(
            attn_parts[2].astype(jnp.bfloat16), "seq", scatter_dimension=1, tiled=True
        ).astype(jnp.float32),
    )
    attn_shards = (
        lax.psum_scatter(
            attn_mid[0].astype(jnp.bfloat16), "dp", scatter_dimension=0, tiled=True
        ).astype(jnp.float32),
        lax.psum_scatter(
            attn_mid[1].astype(jnp.bfloat16), "dp", scatter_dimension=0, tiled=True
        ).astype(jnp.float32),
        lax.psum_scatter(
            attn_mid[2].astype(jnp.bfloat16), "dp", scatter_dimension=0, tiled=True
        ).astype(jnp.float32),
    )
    return (
        output.reshape(1, tok_rows, model_width),
        input_grad.reshape(1, tok_rows, model_width),
        attn_shards[0].reshape(-1),
        attn_shards[1].reshape(-1),
        attn_shards[2].reshape(-1),
        mlp_shards[0].reshape(-1),
        mlp_shards[1].reshape(-1),
        mlp_shards[2].reshape(-1),
    )


MESH_IDS = pl.DeviceIdType.MESH
TOK = 128
WIDTH = 1024
PART = FF // 32
PAD = 96
HID = 8 * PAD
QKV = 3 * 256
BF = jnp.bfloat16
F32 = jnp.float32


def dot_nn(a, b):
    return lax.dot_general(a, b, (((1,), (0,)), ((), ())), preferred_element_type=F32)


def turned(u, low_half):
    return jnp.where(low_half, pltpu.roll(u, 96, axis=1), pltpu.roll(u, 32, axis=1))


def column(gain_ref):
    square = jnp.broadcast_to(gain_ref[...].astype(F32), (32, 32))
    rows = lax.broadcasted_iota(jnp.int32, (32, 32), 0)
    cols = lax.broadcasted_iota(jnp.int32, (32, 32), 1)
    return jnp.sum(jnp.where(rows == cols, square, 0.0), axis=1, keepdims=True)


def owner(r, k):
    return k // 4 * 16 + (r // 2 + k // 4) % 2 * 8 + k // 2 % 2 * 4 + k % 2 * 2 + r % 2


def runs(places):
    found = []
    for lane, place in enumerate(places):
        if place is None:
            continue
        tile, shift = place[0], (place[1] - lane) % 128
        if found and found[-1][:2] == (tile, shift) and found[-1][3] == lane:
            found[-1] = found[-1][:3] + (lane + 1,)
        else:
            found.append((tile, shift, lane, lane + 1))
    return found


def in_moves(r, u):
    places = []
    for at in range(u * 128, u * 128 + 128):
        gate, rest = divmod(at, HID)
        k, i = divmod(rest, PAD)
        col = gate * FF + PART * owner(r, k) + i
        places.append(divmod(col, 128) if i < PART else None)
    return runs(places)


def out_moves(t):
    spots = {owner(r, k): (r, k) for r in range(4) for k in range(8)}
    places = []
    for col in range(t * 128, t * 128 + 128):
        gate, rest = divmod(col, FF)
        device, i = divmod(rest, PART)
        r, k = spots[device]
        u, lane = divmod(gate * HID + k * PAD + i, 128)
        places.append(((r, u), lane))
    return runs(places)


def moved(moves, load):
    lanes = lax.broadcasted_iota(jnp.int32, (1, 128), 1)
    out = jnp.zeros((32, 128), F32)
    for tile, shift, low, high in moves:
        piece = load(tile)
        if shift:
            piece = pltpu.roll(piece, 128 - shift, axis=1)
        out = jnp.where((lanes >= low) & (lanes < high), piece, out)
    return out


def finish_kernel(
    gq_in,
    go_in,
    gi_in,
    gd_in,
    out_in,
    ig_in,
    gain1_in,
    sums_in,
    wq_flat,
    out_ref,
    ig_ref,
    gain1_ref,
    gq_ref,
    go_ref,
    gain2_ref,
    gi_ref,
    gd_ref,
    lines,
    gq_raw,
    go_raw,
    gi_raw,
    gd_raw,
    wq_raw,
    gq_own,
    go_own,
    gd_own,
    ig_raw,
    out_raw,
    sems,
):
    count = [0]

    def start(src, dst):
        cp = pltpu.make_async_copy(src, dst, sems.at[count[0]])
        count[0] += 1
        cp.start()
        return cp

    gq_here = start(gq_in, gq_raw)
    wq_here = start(wq_flat, wq_raw)
    gi_here = start(gi_in, gi_raw)
    gd_here = start(gd_in, gd_raw)
    go_here = start(go_in, go_raw)
    ig_here = start(ig_in, ig_raw)
    out_here = start(out_in, out_raw)
    written = []
    rows = lax.broadcasted_iota(jnp.int32, (32, 32), 0)
    cols = lax.broadcasted_iota(jnp.int32, (32, 32), 1)

    def line(total):
        total = jnp.sum(total, axis=1, keepdims=True)
        return jnp.sum(jnp.where(rows == cols, total, 0.0), axis=0, keepdims=True)

    qkv_rows = 3 * WIDTH // TOK
    ig_here.wait()
    written.append(start(ig_raw, ig_ref))
    out_here.wait()
    written.append(start(out_raw, out_ref))
    gi_here.wait()
    written.append(start(gi_raw, gi_ref))
    gain2_ref[...] = line(sums_in[...])
    gd_here.wait()
    for j in range(8):
        gd_own[pl.ds(j, PART, stride=8), :] = gd_raw[0:PART, pl.ds(j * 128, 128)]
    written.append(start(gd_own, gd_ref))
    gain = column(gain1_in)
    total = jnp.zeros((32, 128), F32)
    wq_here.wait()
    lines[0 : 32 * qkv_rows] = wq_raw[...].astype(F32)
    gq_here.wait()
    for j in range(qkv_rows):
        part, cut = divmod(j, 8)
        r = (cut // 2 + cut // 4) % 2 * 2 + cut // 4
        g = gq_raw[r, :, pl.ds(part * 256 + cut % 2 * 128, 128)].astype(F32)
        total = total + g * lines[pl.ds(j, 32, stride=qkv_rows), :]
        gq_own[pl.ds(j, 32, stride=qkv_rows), :] = g * gain
    written.append(start(gq_own, gq_ref))
    gain1_ref[...] = line(total)
    go_here.wait()
    for j in range(8):
        go_own[pl.ds(j, 32, stride=8), :] = go_raw[:, pl.ds(j * 128, 128)].astype(F32)
    written.append(start(go_own, go_ref))
    for cp in written:
        cp.wait()


def layer_kernel(
    x_ref,
    cot_in,
    seg_in,
    cos_ref,
    sin_ref,
    gain1_in,
    gain2_in,
    wq_flat,
    wo_flat,
    wi_flat,
    wd_flat,
    out_ref,
    ig_ref,
    gq_ref,
    go_ref,
    gi_ref,
    gd_ref,
    sums_ref,
    seg_buf,
    n1,
    n2,
    cot,
    db,
    wq,
    wo,
    wi,
    wd,
    unit1,
    inv1,
    unit2,
    inv2,
    middle,
    dmid,
    q_buf,
    k_buf,
    v_buf,
    probs,
    att,
    datt,
    up_a,
    up_b,
    hidden,
    d_up,
    dqkv,
    ps,
    ps_in,
    ps_far,
    ps_back,
    gq,
    go,
    gi,
    gd,
    rq1,
    rq2,
    rq3,
    ro1,
    ro2,
    ro3,
    ri1,
    ri2,
    ri3,
    rd1,
    rd2,
    rd3,
    wq_in,
    wo_in,
    wi_in,
    lines,
    wide,
    out_vm,
    ig_vm,
    gq_vm,
    go_vm,
    gi_vm,
    gd_vm,
    gi_own,
    sums,
    send_sems,
    recv_sems,
    local_sems,
):
    dp, c = lax.axis_index("dp"), lax.axis_index("seq")
    x, y, z = lax.rem(dp, 2), lax.rem(dp // 2, 2), dp // 4
    zh, zp = z // 2, lax.rem(z, 2)
    kind = lax.rem(zp + zh, 2)
    role = kind * 2 + c

    def device(X, Y, Z, C):
        return (Z * 4 + Y * 2 + X, C)

    core_dev = device(x, y, z, 1 - c)
    pair_dev = device(x, y, zh * 2 + 1 - zp, c)
    diag_dev = device(x, y, zh * 2 + 1 - zp, 1 - c)
    half_dev = device(x, y, 3 - z, c)
    x_dev = device(1 - x, y, z, c)
    y_dev = device(x, 1 - y, z, c)

    barrier = pltpu.get_barrier_semaphore()
    for dev in (core_dev, pair_dev, diag_dev, half_dev, x_dev, y_dev):
        pl.semaphore_signal(barrier, inc=1, device_id=dev, device_id_type=MESH_IDS)

    sent = []
    n_sems = [0]
    free = list(range(N_SENDS))

    def copy_to(src, dst, dev, keep=True):
        i, k = n_sems[0], free.pop(0)
        n_sems[0] += 1
        cp = pltpu.make_async_remote_copy(
            src_ref=src,
            dst_ref=dst,
            send_sem=send_sems.at[k],
            recv_sem=recv_sems.at[i],
            device_id=dev,
            device_id_type=MESH_IDS,
        )
        if keep:
            sent.append((cp, k))
        return cp

    local = []

    def emit(i, src, dst):
        cp = pltpu.make_async_copy(src, dst, local_sems.at[i])
        cp.start()
        local.append(cp)

    def settle(first):
        for cp, k in sent[:first]:
            cp.wait_send()
            free.append(k)
        del sent[:first]

    def go_copy(src, dst, dev):
        cp = copy_to(src, dst, dev)
        cp.start()
        return cp


    others = (
        (core_dev, kind * 2 + 1 - c, (z, 1 - c)),
        (pair_dev, (1 - kind) * 2 + c, (zh * 2 + 1 - zp, c)),
        (diag_dev, (1 - kind) * 2 + 1 - c, (zh * 2 + 1 - zp, 1 - c)),
    )

    def spread(own, buf):
        cps = [go_copy(own.at[r], buf.at[z, y, x, c], dev) for dev, r, _ in others]
        return cps

    class Gather:
        def __init__(self, buf, cols, base=0):
            self.buf = buf
            self.halves = (pl.ds(base, cols // 2), pl.ds(base + cols // 2, cols // 2))
            self.per_half = buf.shape[0] // 2

        def of(self, which):
            return pl.ds(self.per_half * which, self.per_half)

        def spot(self, which, cut):
            return self.buf.at[(self.of(which), y, x) + (slice(None),) * (len(self.buf.shape) - 4) + (cut,)]

        def line(self, which, cut, i):
            rest = (slice(None),) * (len(self.buf.shape) - 4) + (cut,)
            at = (y, slice(None)) if i == 0 else (slice(None), x)
            return self.buf.at[(self.of(which),) + at + rest]

        def same(self, ref, dev):
            return go_copy(ref, ref, dev)

        def across(self):
            self.over = [self.same(self.spot(zh, cut), half_dev) for cut in self.halves]

        def own_first(self):
            self.a = [
                self.same(self.spot(zh, cut), dev) for cut, dev in zip(self.halves, (x_dev, y_dev))
            ]

        def own_second(self):
            self.b = []
            for i, dev in enumerate((y_dev, x_dev)):
                self.a[i].wait_recv()
                self.b.append(self.same(self.line(zh, self.halves[i], i), dev))

        def far_first(self):
            self.a2 = []
            for i, dev in enumerate((x_dev, y_dev)):
                self.over[i].wait_recv()
                self.a2.append(self.same(self.spot(1 - zh, self.halves[i]), dev))

        def far_second(self):
            self.b2 = []
            for i, dev in enumerate((y_dev, x_dev)):
                self.a2[i].wait_recv()
                self.b2.append(self.same(self.line(1 - zh, self.halves[i], i), dev))

        def done(self):
            for cp in self.b + self.b2:
                cp.wait_recv()

    class GatherOut:
        def __init__(self, buf, cols):
            self.buf = buf
            self.halves = (pl.ds(0, cols // 2), pl.ds(cols // 2, cols // 2))

        def start(self):
            self.s0 = copy_to(wo_in, self.buf.at[y, x, c], core_dev, keep=False)

            @pl.when(c != zh)
            def _():
                self.s0.start()

        def across(self):
            self.s1 = copy_to(self.buf.at[y, x], self.buf.at[y, x], half_dev, keep=False)

            @pl.when(c == zh)
            def _():
                self.buf[y, x, c] = wo_in[...]
                self.s0.wait_recv()
                self.s1.start()

        def first(self):
            @pl.when(c != zh)
            def _():
                self.s1.wait_recv()

            self.a = []
            for cut, dev in zip(self.halves, (x_dev, y_dev)):
                ref = self.buf.at[y, x, :, :, cut]
                self.a.append(go_copy(ref, ref, dev))

        def second(self):
            self.b = []
            for i, dev in enumerate((y_dev, x_dev)):
                self.a[i].wait_recv()
                cut = self.halves[i]
                ref = self.buf.at[y, :, :, :, cut] if i == 0 else self.buf.at[:, x, :, :, cut]
                self.b.append(go_copy(ref, ref, dev))

        def done(self):
            for cp in self.b:
                cp.wait_recv()

        def end(self):
            @pl.when(c != zh)
            def _():
                self.s0.wait_send()

            @pl.when(c == zh)
            def _():
                self.s1.wait_send()


    pieces = [pl.ds(i * (TOK // PIECES), TOK // PIECES) for i in range(PIECES)]

    class Share:
        def __init__(self, buf):
            self.buf = buf
            self.to_pair = [
                go_copy(buf.at[zp, c, cut], buf.at[zp, c, cut], pair_dev) for cut in pieces
            ]
            self.to_core = go_copy(buf.at[zp, c], buf.at[zp, c], core_dev)

        def forward(self):
            self.fwd = []
            for cp, cut in zip(self.to_pair, pieces):
                cp.wait_recv()
                ref = self.buf.at[1 - zp, c, cut]
                self.fwd.append(go_copy(ref, ref, core_dev))

        def core(self):
            self.to_core.wait_recv()

        def done(self):
            for cp in self.fwd:
                cp.wait_recv()

    class Reduce:
        def __init__(self, i):
            self.i = i

        def far_terms(self):
            i = self.i
            self.mine_far = go_copy(ps.at[i, 1 - zp, 1 - c], ps_in.at[i, 1 - zp], core_dev)

        def near_terms(self):
            i = self.i
            self.mine_near = go_copy(ps.at[i, zp, 1 - c], ps_in.at[i, zp], core_dev)

        def cross(self):
            i = self.i
            self.mine_far.wait_recv()
            self.far = []
            for cut in pieces:
                ps_far[i, cut] = (
                    ps[i, 1 - zp, c, cut].astype(F32) + ps_in[i, 1 - zp, cut].astype(F32)
                ).astype(BF)
                self.far.append(go_copy(ps_far.at[i, cut], ps_back.at[i, cut], pair_dev))

        def total(self):
            i = self.i
            self.mine_near.wait_recv()
            near = ps[i, zp, c].astype(F32) + ps_in[i, zp].astype(F32)
            for cp in self.far:
                cp.wait_recv()
            return near + ps_back[i].astype(F32)


    def add_into(target, extra):
        target[...] = (target[...].astype(F32) + extra[...].astype(F32)).astype(BF)

    def add_all(mine, got):
        n = got.shape[0]
        if n == 1:
            add_into(mine.at[0], got.at[0])
            return

        def body(j, carry):
            add_into(mine.at[j], got.at[j])
            return carry

        lax.fori_loop(0, n, body, 0)

    class Scatter:
        def __init__(self, buf, cols, r1, r2, r3, base=0):
            self.buf, self.r1, self.r2, self.r3 = buf, r1, r2, r3
            self.halves = (pl.ds(base, cols // 2), pl.ds(base + cols // 2, cols // 2))
            self.cols = pl.ds(base, cols)
            self.per_half = buf.shape[0] // 2
            self.rest = (slice(None),) * (len(buf.shape) - 4)
            self.c1, self.c2 = {}, {}

        def of(self, which):
            return pl.ds(self.per_half * which, self.per_half)

        def line(self, i, which, other):
            if i == 0:
                at = (1 - y if other else y, slice(None))
            else:
                at = (slice(None), 1 - x if other else x)
            return self.buf.at[(self.of(which),) + at + self.rest + (self.halves[i],)]

        def spot(self, i, which, other):
            Y, X = (y, x) if not other else ((y, 1 - x) if i == 0 else (1 - y, x))
            return self.buf.at[(self.of(which), Y, X) + self.rest + (self.halves[i],)]

        def first(self, far):
            which = 1 - zh if far else zh
            self.c1[far] = [
                go_copy(self.line(i, which, True), self.r1.at[i, far], dev)
                for i, dev in enumerate((y_dev, x_dev))
            ]

        def second(self, far):
            which = 1 - zh if far else zh
            self.c2[far] = []
            for i, dev in enumerate((x_dev, y_dev)):
                self.c1[far][i].wait_recv()
                add_all(self.line(i, which, False), self.r1.at[i, far])
                self.c2[far].append(go_copy(self.spot(i, which, True), self.r2.at[i, far], dev))

        def third(self, far):
            which = 1 - zh if far else zh
            for i in range(2):
                self.c2[far][i].wait_recv()
                add_all(self.spot(i, which, False), self.r2.at[i, far])
            if far:
                src = self.buf.at[(self.of(which), y, x) + self.rest + (self.cols,)]
                self.c3 = go_copy(src, self.r3, half_dev)

    class ScatterRows(Scatter):
        def fourth(self, out):
            self.c3.wait_recv()
            cols = self.cols
            add_all(self.buf.at[self.of(zh), y, x, :, :, cols], self.r3)
            self.c4 = []
            for dev, _, (there, core) in others:
                src = self.buf.at[there, y, x, core, :, cols]
                self.c4.append(go_copy(src, out.at[role, :, cols], dev))
            out[role, :, cols] = self.buf[z, y, x, c, :, cols]

        def done(self):
            for cp in self.c4:
                cp.wait_recv()

    class ScatterDown(Scatter):
        def fourth(self, out):
            self.c3.wait_recv()
            out[...] = self.buf[zh, y, x].astype(F32) + self.r3[0].astype(F32)

    class ScatterOut:
        def __init__(self, buf, cols, r1, r2, r3):
            self.buf, self.r1, self.r2, self.r3 = buf, r1, r2, r3
            self.halves = (pl.ds(0, cols // 2), pl.ds(cols // 2, cols // 2))

        def line(self, i, other):
            cut = self.halves[i]
            if i == 0:
                return self.buf.at[1 - y if other else y, :, :, :, cut]
            return self.buf.at[:, 1 - x if other else x, :, :, cut]

        def spot(self, i, other):
            Y, X = (y, x) if not other else ((y, 1 - x) if i == 0 else (1 - y, x))
            return self.buf.at[Y, X, :, :, self.halves[i]]

        def first(self):
            self.c1 = [
                go_copy(self.line(i, True), self.r1.at[i], dev)
                for i, dev in enumerate((y_dev, x_dev))
            ]

        def second(self):
            self.c2 = []
            for i, dev in enumerate((x_dev, y_dev)):
                self.c1[i].wait_recv()
                add_all(self.line(i, False), self.r1.at[i])
                self.c2.append(go_copy(self.spot(i, True), self.r2.at[i], dev))

        def third(self):
            for i in range(2):
                self.c2[i].wait_recv()
                add_all(self.spot(i, False), self.r2.at[i])
            self.c3 = copy_to(self.buf.at[y, x], self.r3, half_dev, keep=False)

            @pl.when(c != zh)
            def _():
                self.c3.start()

        def fourth(self, out):
            self.c4 = copy_to(self.r3.at[1 - c], out, core_dev, keep=False)

            @pl.when(c == zh)
            def _():
                self.c3.wait_recv()
                add_all(self.r3, self.buf.at[y, x])
                self.c4.start()
                out[...] = self.r3[c]

        def done(self):
            @pl.when(c != zh)
            def _():
                self.c4.wait_recv()
                self.c3.wait_send()

            @pl.when(c == zh)
            def _():
                self.c4.wait_send()

    qkv_rows = 3 * WIDTH // TOK
    lines[0 : 32 * qkv_rows] = wq_flat[...].astype(F32)
    gain = column(gain1_in)
    for j in range(qkv_rows):
        part, cut = divmod(j, 8)
        r = (cut // 2 + cut // 4) % 2 * 2 + cut // 4
        w = lines[pl.ds(j, 32, stride=qkv_rows), :] * gain
        wq_in[r, :, pl.ds(part * 256 + cut % 2 * 128, 128)] = w.astype(BF)
    wq[z, y, x, c] = wq_in[role]
    g_q, g_d = Gather(wq, QKV), Gather(wd, WIDTH)
    g_i, g_j = Gather(wi, HID), Gather(wi, HID, HID)
    g_o = GatherOut(wo, WIDTH)


    r_d = ScatterDown(gd, WIDTH, rd1, rd2, rd3)
    r_i = ScatterRows(gi, HID, ri1.at[0], ri2.at[0], ri3.at[0])
    r_j = ScatterRows(gi, HID, ri1.at[1], ri2.at[1], ri3.at[1], HID)
    r_q = ScatterRows(gq, QKV, rq1, rq2, rq3)
    r_o = ScatterOut(go, WIDTH, ro1, ro2, ro3)
    on = {}
    red = [Reduce(i) for i in range(4)]
    lanes = lax.broadcasted_iota(jnp.int32, (1, 128), 1)
    low_half = lax.rem(lanes, 64) < 32
    first_head = lanes < 64

    def qkv_step(s, carry):
        rows = n1[s].reshape(256, WIDTH)
        for part, dst in enumerate((q_buf, k_buf, v_buf)):
            for j in range(2):
                at = part * 256 + j * 128
                w = wq[:, :, :, :, :, pl.ds(at, 128)].reshape(WIDTH, 128)
                u = dot_nn(rows, w)
                if part < 2:
                    u = u * cos_ref[...] + turned(u, low_half) * sin_ref[...]
                dst[s, j] = u.astype(BF)
        return carry

    def only(head, u):
        return jnp.where(first_head if head == 0 else ~first_head, u, jnp.zeros_like(u))

    def attend(i, carry):
        s, j = i // 2, lax.rem(i, 2)
        q, k, v = q_buf[s, j], k_buf[s, j], v_buf[s, j]
        seg_row = jnp.concatenate([seg_buf[s, 0, 0:1], seg_buf[s, 1, 0:1]], axis=1)
        seg_col = jnp.broadcast_to(seg_row, (128, 256)).T[:, 0:1]
        same = seg_col == seg_row
        heads = []
        for h in range(2):
            scores = matmul_nt(only(h, q), k) * 0.125
            scores = jnp.where(same, scores, -1e30)
            weights = jnp.exp(scores - jnp.max(scores, axis=-1, keepdims=True))
            p = weights * (1.0 / jnp.sum(weights, axis=-1, keepdims=True))
            probs[i, h] = p
            heads.append(dot_nn(p.astype(BF), v))
        att[s, j] = jnp.where(first_head, heads[0], heads[1]).astype(BF)
        return carry

    def att_rows(s):
        return jnp.concatenate([att[s, 0], att[s, 1]], axis=1)

    def branch(s, carry):
        w = wo[...].reshape(256, WIDTH)
        ps[0, s] = dot_nn(att_rows(s), w).astype(BF).reshape(2, TOK, WIDTH)
        return carry

    def upper_for(s):
        def upper(j, carry):
            at = pl.multiple_of(j * 256, 256)
            rows = n2[s].reshape(256, WIDTH)
            inner = dot_nn(rows, wi[:, :, :, :, :, pl.ds(at, 256)].reshape(WIDTH, 256))
            gate = dot_nn(
                rows,
                wi[:, :, :, :, :, pl.ds(pl.multiple_of(HID + at, 256), 256)].reshape(WIDTH, 256),
            )
            cdf = 0.5 * (1.0 + lax.erf(inner * math.sqrt(0.5)))
            slope = cdf + inner * jnp.exp(-0.5 * inner * inner) * (1.0 / math.sqrt(2 * math.pi))
            bent = inner * cdf
            up_a[s, :, pl.ds(at, 256)] = gate * slope
            up_b[s, :, pl.ds(at, 256)] = bent
            hidden[s, :, pl.ds(at, 256)] = (bent * gate).astype(BF)
            return carry

        lax.fori_loop(0, HID // 256, upper, 0)

    def down_grad(i, carry):
        lhs = hidden[:, :, pl.ds(pl.multiple_of(i * 384, 384), 384)].reshape(512, 384)
        for j in range(2):
            rhs = cot[:, :, :, pl.ds(j * 512, 512)].reshape(512, 512)
            gd[i, :, :, :, pl.ds(j * 512, 512)] = (
                matmul_tn(lhs, rhs).astype(BF).reshape(2, 2, PAD, 512)
            )
        return carry

    def hidden_grad(i, carry):
        w = wd[i].reshape(384, WIDTH)
        at = pl.multiple_of(i * 384, 384)
        for s in range(2):
            dh = matmul_nt(cot[s].reshape(256, WIDTH), w)
            d_up[s, :, pl.ds(at, 384)] = (dh * up_a[s, :, pl.ds(at, 384)]).astype(BF)
            d_up[s, :, pl.ds(pl.multiple_of(HID + at, 384), 384)] = (
                dh * up_b[s, :, pl.ds(at, 384)]
            ).astype(BF)
        return carry

    def normed_two_grad_for(s):
        def normed_two_grad(i, carry):
            w = wi[i].reshape(256, 2 * HID)
            at = pl.multiple_of(i * 256, 256)
            ps[1, s, :, :, pl.ds(at, 256)] = matmul_nt(d_up[s], w).astype(BF).reshape(2, TOK, 256)
            return carry

        lax.fori_loop(0, 4, normed_two_grad, 0)

    def in_grad_for(base, first):
        def in_grad(i, carry):
            lhs = n2[:, :, :, pl.ds(pl.multiple_of(i * 256, 256), 256)].reshape(512, 256)
            for j in range(HID // 256):
                at = base + j * 256
                rhs = d_up[:, :, pl.ds(at, 256)].reshape(512, 256)
                gi[i, :, :, :, :, pl.ds(at, 256)] = (
                    matmul_tn(lhs, rhs).astype(BF).reshape(2, 2, 2, 32, 256)
                )
            return carry

        lax.fori_loop(first, first + 2, in_grad, 0)

    def down(i, carry):
        w = wd[...].reshape(HID, WIDTH)
        ps[2, i] = dot_nn(hidden[i], w).astype(BF).reshape(2, TOK, WIDTH)
        return carry

    def attended_grad(s, carry):
        rows = db[s].reshape(256, WIDTH)
        da = matmul_nt(rows, wo[...].reshape(256, WIDTH)).astype(BF)
        datt[s, 0] = da[:, 0:128]
        datt[s, 1] = da[:, 128:256]
        return carry

    def attend_back(i, carry):
        s, j = i // 2, lax.rem(i, 2)
        q, k, v, da = q_buf[s, j], k_buf[s, j], v_buf[s, j], datt[s, j]
        dq, dk, dv = [], [], []
        for h in range(2):
            p = probs[i, h]
            dprob = matmul_nt(only(h, da), v)
            delta = jnp.sum(p * dprob, axis=-1, keepdims=True)
            ds = (p * (dprob - delta)).astype(BF)
            dq.append(dot_nn(ds, k))
            dk.append(matmul_tn(ds, q))
            dv.append(matmul_tn(p.astype(BF), da))
        for part, pieces in enumerate((dq, dk, dv)):
            u = jnp.where(first_head, pieces[0], pieces[1])
            if part < 2:
                u = u * 0.125
                u = u * cos_ref[...] - turned(u, low_half) * sin_ref[...]
            dqkv[part, j, s] = u.astype(BF)
        return carry

    def first_grads_for(s):
        rows = jnp.concatenate([dqkv[p, j, s] for p in range(3) for j in range(2)], axis=1)

        def first_grads(i, carry):
            w = wq[i].reshape(256, QKV)
            at = pl.multiple_of(i * 256, 256)
            ps[3, s, :, :, pl.ds(at, 256)] = matmul_nt(rows, w).astype(BF).reshape(2, TOK, 256)
            return carry

        lax.fori_loop(0, 4, first_grads, 0)

    def qkv_grad(i, carry):
        lhs = n1[:, :, :, pl.ds(pl.multiple_of(i * 256, 256), 256)].reshape(512, 256)
        for p in range(3):
            for j in range(2):
                rhs = dqkv[p, j].reshape(512, 128)
                gq[i, :, :, :, :, pl.ds(p * 256 + j * 128, 128)] = (
                    matmul_tn(lhs, rhs).astype(BF).reshape(2, 2, 2, 32, 128)
                )
        return carry

    pl.semaphore_wait(barrier, 6)
    on["s_q"] = spread(wq_in, wq)
    wide[0 : 8 * PART] = wd_flat[...].astype(F32)
    wide[8 * PART : 8 * PAD] = jnp.zeros((8 * (PAD - PART), TOK), F32)
    for j in range(8):
        wd[zh, y, x, :, pl.ds(j * 128, 128)] = wide[pl.ds(j, PAD, stride=8), :].astype(BF)
    g_d.own_first()
    tokens = x_ref[...].astype(F32)
    centred = tokens - jnp.mean(tokens, axis=-1, keepdims=True)
    inv = lax.rsqrt(jnp.mean(centred * centred, axis=-1, keepdims=True) + EPSILON)
    unit = centred * inv
    unit1[...] = unit
    inv1[...] = jnp.broadcast_to(inv, (TOK, 128))
    n1[zp, c] = unit.astype(BF)
    seg_buf[zp, c] = jnp.broadcast_to(seg_in[...].astype(F32), (8, TOK))
    cot[zp, c] = cot_in[...]
    wide[0:256] = wo_flat[...].astype(F32)
    for j in range(8):
        wo_in[:, pl.ds(j * 128, 128)] = wide[pl.ds(j, 32, stride=8), :].astype(BF)
    on["seg"] = [go_copy(seg_buf.at[zp, c], seg_buf.at[zp, c], dev) for dev, _, _ in others]
    g_o.start()
    g_o.across()
    in_rows = 2 * FF // TOK
    lines[...] = wi_flat[...].astype(F32)
    gain = column(gain2_in)
    for j in range(in_rows):
        wide[pl.ds(j * 32, 32), :] = lines[pl.ds(j, 32, stride=in_rows), :] * gain
    for r in range(4):
        for u in range(2 * HID // TOK):
            tile = moved(in_moves(r, u), lambda t: wide[pl.ds(t * 32, 32), :])
            wi_in[r, :, pl.ds(u * 128, 128)] = tile.astype(BF)
    wi[z, y, x, c] = wi_in[role]
    on["s_i"] = spread(wi_in, wi)
    g_d.own_second()
    for cp in on["s_q"]:
        cp.wait_recv()
    g_q.own_first()
    g_q.across()
    on["n1"] = Share(n1)
    for cp in on["seg"]:
        cp.wait_recv()
    g_d.across()
    g_o.first()
    g_q.own_second()
    g_o.second()
    for cp in on["s_i"]:
        cp.wait_recv()
    g_q.far_first()
    g_i.across()
    g_o.done()
    on["cot"] = Share(cot)
    g_i.own_first()
    g_q.far_second()
    g_j.own_first()
    on["n1"].forward()
    g_i.own_second()
    on["n1"].done()
    on["n1"].core()
    g_q.done()
    lax.fori_loop(1 - zp, 2 - zp, qkv_step, 0)
    lax.fori_loop(zp, zp + 1, qkv_step, 0)
    g_j.own_second()
    g_j.across()
    g_i.far_first()
    g_d.far_first()
    lax.fori_loop(2 * (1 - zp), 2 * (1 - zp) + 2, attend, 0)
    on["cot"].core()
    lax.fori_loop(2 * zp, 2 * zp + 2, attend, 0)
    lax.fori_loop(1 - zp, 2 - zp, branch, 0)
    red[0].far_terms()
    red[0].cross()
    g_j.far_first()
    g_i.far_second()
    lax.fori_loop(zp, zp + 1, branch, 0)
    red[0].near_terms()
    mid = x_ref[...].astype(F32) + red[0].total()
    middle[...] = mid
    centred = mid - jnp.mean(mid, axis=-1, keepdims=True)
    inv = lax.rsqrt(jnp.mean(centred * centred, axis=-1, keepdims=True) + EPSILON)
    unit = centred * inv
    unit2[...] = unit
    inv2[...] = jnp.broadcast_to(inv, (TOK, 128))
    n2[zp, c] = unit.astype(BF)
    on["n2"] = Share(n2)
    on["cot"].forward()
    g_j.far_second()
    on["cot"].done()
    on["n2"].core()
    g_i.done()
    g_d.far_second()
    on["n2"].forward()
    g_j.done()
    on["mark"] = len(sent)
    upper_for(zp)
    on["n2"].done()
    upper_for(1 - zp)
    lax.fori_loop(0, 2, down_grad, 0)
    g_d.done()
    r_d.first(1)
    lax.fori_loop(0, 2, hidden_grad, 0)
    normed_two_grad_for(1 - zp)
    red[1].far_terms()
    in_grad_for(HID, 2 * (1 - zh))
    r_j.first(1)
    red[1].cross()
    in_grad_for(0, 2 * (1 - zh))
    r_i.first(1)
    normed_two_grad_for(zp)
    red[1].near_terms()
    lax.fori_loop(1 - zp, 2 - zp, down, 0)
    red[2].far_terms()
    r_j.second(1)
    r_d.first(0)
    r_d.second(1)
    settle(on["mark"])
    e = red[1].total()
    n = unit2[...]
    d_middle = cot_in[...].astype(F32) + inv2[:, 0:1] * (
        e
        - jnp.mean(e, axis=-1, keepdims=True)
        - n * jnp.mean(e * n, axis=-1, keepdims=True)
    )
    dmid[...] = d_middle
    db[zp, c] = d_middle.astype(BF)
    on["db"] = Share(db)
    r_j.third(1)
    in_grad_for(HID, 2 * zh)
    r_d.second(0)
    r_i.second(1)
    red[2].cross()
    on["db"].forward()
    r_j.first(0)
    in_grad_for(0, 2 * zh)
    on["db"].done()
    r_d.third(1)
    r_i.first(0)
    on["db"].core()
    lax.fori_loop(zp, zp + 1, attended_grad, 0)
    lax.fori_loop(1 - zp, 2 - zp, attended_grad, 0)
    lax.fori_loop(2 * (1 - zp), 2 * (1 - zp) + 2, attend_back, 0)
    first_grads_for(1 - zp)
    red[3].far_terms()
    lhs = att
    for j in range(2):
        for half in range(2):
            rhs = db[:, :, :, pl.ds(half * 512, 512)].reshape(512, 512)
            go[j, :, :, :, pl.ds(half * 512, 512)] = (
                matmul_tn(lhs[:, j].reshape(512, 128), rhs).astype(BF).reshape(2, 2, 32, 512)
            )
    r_i.third(1)
    lax.fori_loop(2 * zp, 2 * zp + 2, attend_back, 0)
    lax.fori_loop(2 * zh, 2 * zh + 2, qkv_grad, 0)
    r_o.first()
    r_d.third(0)
    red[3].cross()
    lax.fori_loop(2 * (1 - zh), 2 * (1 - zh) + 2, qkv_grad, 0)
    r_q.first(1)
    lax.fori_loop(zp, zp + 1, down, 0)
    red[2].near_terms()
    r_o.second()
    r_i.second(0)
    r_q.second(1)
    r_d.fourth(gd_vm)
    emit(2, gd_vm, gd_ref)
    r_o.third()
    first_grads_for(zp)
    red[3].near_terms()
    r_i.third(0)
    r_q.first(0)
    r_j.second(0)
    r_i.fourth(gi_vm)
    r_q.third(1)
    r_q.second(0)
    r_j.third(0)
    e = red[3].total()
    n = unit1[...]
    ig_vm[...] = dmid[...] + inv1[:, 0:1] * (
        e
        - jnp.mean(e, axis=-1, keepdims=True)
        - n * jnp.mean(e * n, axis=-1, keepdims=True)
    )
    emit(1, ig_vm, ig_ref)
    out_vm[...] = (middle[...] + red[2].total()).astype(BF)
    emit(0, out_vm, out_ref)
    r_o.fourth(go_vm)
    r_j.fourth(gi_vm)
    r_i.done()
    r_q.third(0)
    r_o.done()
    emit(4, go_vm, go_ref)
    r_q.fourth(gq_vm)
    r_q.done()
    emit(5, gq_vm, gq_ref)
    r_j.done()
    in_rows = 2 * FF // TOK
    lines[...] = wi_flat[...].astype(F32)
    gain = column(gain2_in)
    total = jnp.zeros((32, 128), F32)
    for j in range(in_rows):
        g = moved(out_moves(j), lambda t: gi_vm[t[0], :, pl.ds(t[1] * 128, 128)].astype(F32))
        total = total + g * lines[pl.ds(j, 32, stride=in_rows), :]
        gi_own[pl.ds(j, 32, stride=in_rows), :] = g * gain
    sums[...] = total
    emit(3, gi_own, gi_ref)
    emit(6, sums, sums_ref)
    g_o.end()
    assert n_sems[0] == N_COPIES
    settle(len(sent))
    for cp in local:
        cp.wait()


def block_device(inputs, segments, cotangent, ln1_gain, w_qkv, w_attn_out, ln2_gain, w_in, w_mlp_out):
    places = np.arange(2 * TOK, dtype=np.float32)
    freqs = (1.0 / ROPE_BASE ** (np.arange(0, HD, 2, dtype=np.float64) / HD)).astype(np.float32)
    angles = np.tile(places[:, None] * freqs[None, :], (1, 4))
    signs = np.where(np.arange(2 * HD) % HD < HD // 2, -1.0, 1.0).astype(np.float32)
    cosines = jnp.asarray(np.cos(angles))
    sines = jnp.asarray(np.sin(angles) * signs)
    gain_one, gain_two = ln1_gain[None], ln2_gain[None]
    wq_flat, wo_flat = w_qkv.reshape(-1, TOK), w_attn_out.reshape(-1, TOK)
    wi_flat, wd_flat = w_in.reshape(-1, TOK), w_mlp_out.reshape(-1, TOK)

    vm = pltpu.VMEM
    group = (2, 2, TOK, WIDTH)
    rows = (4, 2, 2, 2, 32)
    outs = pl.pallas_call(
        layer_kernel,
        out_shape=(
            jax.ShapeDtypeStruct((TOK, WIDTH), BF),
            jax.ShapeDtypeStruct((TOK, WIDTH), F32),
            jax.ShapeDtypeStruct((4, 32, QKV), BF),
            jax.ShapeDtypeStruct((32, WIDTH), BF),
            jax.ShapeDtypeStruct(wi_flat.shape, F32),
            jax.ShapeDtypeStruct((PAD, WIDTH), F32),
            jax.ShapeDtypeStruct((32, TOK), F32),
        ),
        in_specs=[pl.BlockSpec(memory_space=vm)] * 11,
        out_specs=(pl.BlockSpec(memory_space=pl.ANY),) * 7,
        scratch_shapes=[
            vm((2, 2, 8, TOK), F32),
            vm(group, BF),
            vm(group, BF),
            vm(group, BF),
            vm(group, BF),
            vm(rows + (QKV,), BF),
            vm((2, 2, 2, 32, WIDTH), BF),
            vm(rows + (2 * HID,), BF),
            vm((2, 2, 2, PAD, WIDTH), BF),
            vm((TOK, WIDTH), F32),
            vm((TOK, 128), F32),
            vm((TOK, WIDTH), F32),
            vm((TOK, 128), F32),
            vm((TOK, WIDTH), F32),
            vm((TOK, WIDTH), F32),
            vm((2, 2, 256, 128), BF),
            vm((2, 2, 256, 128), BF),
            vm((2, 2, 256, 128), BF),
            vm((4, 2, 256, 256), F32),
            vm((2, 2, 256, 128), BF),
            vm((2, 2, 256, 128), BF),
            vm((2, 256, HID), F32),
            vm((2, 256, HID), F32),
            vm((2, 256, HID), BF),
            vm((2, 256, 2 * HID), BF),
            vm((3, 2, 2, 256, 128), BF),
            vm((4,) + group, BF),
            vm((4, 2, TOK, WIDTH), BF),
            vm((4, TOK, WIDTH), BF),
            vm((4, TOK, WIDTH), BF),
            vm(rows + (QKV,), BF),
            vm((2, 2, 2, 32, WIDTH), BF),
            vm(rows + (2 * HID,), BF),
            vm((2, 2, 2, PAD, WIDTH), BF),
            vm((2, 2, 2, 2, 2, 32, QKV // 2), BF),
            vm((2, 2, 2, 2, 32, QKV // 2), BF),
            vm((2, 2, 32, QKV), BF),
            vm((2, 2, 2, 32, WIDTH // 2), BF),
            vm((2, 2, 32, WIDTH // 2), BF),
            vm((2, 32, WIDTH), BF),
            vm((2, 2, 2, 2, 2, 2, 32, HID // 2), BF),
            vm((2, 2, 2, 2, 2, 32, HID // 2), BF),
            vm((2, 2, 2, 32, HID), BF),
            vm((2, 2, 1, 2, PAD, WIDTH // 2), BF),
            vm((2, 2, 1, PAD, WIDTH // 2), BF),
            vm((1, PAD, WIDTH), BF),
            vm((4, 32, QKV), BF),
            vm((32, WIDTH), BF),
            vm((4, 32, 2 * HID), BF),
            vm((64 * FF // TOK, TOK), F32),
            vm((64 * FF // TOK, TOK), F32),
            vm((TOK, WIDTH), BF),
            vm((TOK, WIDTH), F32),
            vm((4, 32, QKV), BF),
            vm((32, WIDTH), BF),
            vm((4, 32, 2 * HID), BF),
            vm((PAD, WIDTH), F32),
            vm(wi_flat.shape, F32),
            vm((32, TOK), F32),
            pltpu.SemaphoreType.DMA((N_SENDS,)),
            pltpu.SemaphoreType.DMA((N_COPIES,)),
            pltpu.SemaphoreType.DMA((7,)),
        ],
        compiler_params=pltpu.CompilerParams(
            collective_id=0, has_side_effects=True, vmem_limit_bytes=60 * 2**20
        ),
    )(
        inputs[0],
        cotangent[0],
        segments,
        cosines,
        sines,
        gain_one,
        gain_two,
        wq_flat,
        wo_flat,
        wi_flat,
        wd_flat,
    )
    output, input_grad, gq, go, gi, gd, sums = outs
    final = pl.pallas_call(
        finish_kernel,
        out_shape=(
            jax.ShapeDtypeStruct((TOK, WIDTH), BF),
            jax.ShapeDtypeStruct((TOK, WIDTH), F32),
            jax.ShapeDtypeStruct((1, 32), F32),
            jax.ShapeDtypeStruct(wq_flat.shape, F32),
            jax.ShapeDtypeStruct(wo_flat.shape, F32),
            jax.ShapeDtypeStruct((1, 32), F32),
            jax.ShapeDtypeStruct(wi_flat.shape, F32),
            jax.ShapeDtypeStruct(wd_flat.shape, F32),
        ),
        in_specs=[pl.BlockSpec(memory_space=pl.ANY)] * 6
        + [pl.BlockSpec(memory_space=vm)] * 2
        + [pl.BlockSpec(memory_space=pl.ANY)],
        out_specs=tuple(
            pl.BlockSpec(memory_space=vm if i in (2, 5) else pl.ANY) for i in range(8)
        ),
        scratch_shapes=[
            vm(wq_flat.shape, F32),
            vm((4, 32, QKV), BF),
            vm((32, WIDTH), BF),
            vm(wi_flat.shape, F32),
            vm((PAD, WIDTH), F32),
            vm(wq_flat.shape, BF),
            vm(wq_flat.shape, F32),
            vm(wo_flat.shape, F32),
            vm(wd_flat.shape, F32),
            vm((TOK, WIDTH), F32),
            vm((TOK, WIDTH), BF),
            pltpu.SemaphoreType.DMA((14,)),
        ],
        compiler_params=pltpu.CompilerParams(vmem_limit_bytes=60 * 2**20),
    )(gq, go, gi, gd, output, input_grad, gain_one, sums, wq_flat)
    return (final[0][None], final[1][None]) + tuple(f.reshape(-1) for f in final[2:])


N_COPIES = 142
N_SENDS = 100
PIECES = 2


def solution(mesh):
    block = dict(mesh.shape) == {"dp": 16, "seq": 2}
    placed = (
        P("dp", "seq", None),
        P("dp", "seq"),
        P("dp", "seq", None),
        P(("dp", "seq")),
        P(("dp", "seq")),
        P(("dp", "seq")),
        P(("dp", "seq")),
        P(("dp", "seq")),
        P(("dp", "seq")),
    )
    return jax.shard_map(
        block_device if block else general_device,
        mesh=mesh,
        in_specs=placed,
        out_specs=(
            P("dp", "seq", None),
            P("dp", "seq", None),
            P(("dp", "seq")),
            P(("dp", "seq")),
            P(("dp", "seq")),
            P(("dp", "seq")),
            P(("dp", "seq")),
            P(("dp", "seq")),
        ),
        check_vma=False,
    )
```

```python
import functools
import math

import jax
import jax.numpy as jnp
import numpy as np
from jax import lax
from jax.experimental import pallas as pl
from jax.experimental.pallas import tpu as pltpu
from jax.sharding import PartitionSpec as P

HEADS = 16
HD = 64
FF = 2624


EPSILON = 1e-05
ROPE_BASE = 160000.0


def rope_tables(places):
    freqs = 1.0 / ROPE_BASE ** (jnp.arange(0, HD, 2, dtype=jnp.float32) / HD)
    angles = places[:, None] * freqs[None, :]
    angles = jnp.concatenate([angles, angles], axis=1)
    return (jnp.cos(angles), jnp.sin(angles))


def rotate(values_in, cosines, sines):
    halfway = values_in.shape[-1] // 2
    turned = jnp.concatenate([-values_in[..., halfway:], values_in[..., :halfway]], axis=-1)
    return values_in * cosines[:, None, :] + turned * sines[:, None, :]


def rotate_back(grads_in, cosines, sines):
    halfway = grads_in.shape[-1] // 2
    scaled = grads_in * sines[:, None, :]
    turned = jnp.concatenate([scaled[..., halfway:], -scaled[..., :halfway]], axis=-1)
    return grads_in * cosines[:, None, :] + turned


def norm_forward(values_in, gain):
    centred = values_in - jnp.mean(values_in, axis=-1, keepdims=True)
    inv_spread = lax.rsqrt(jnp.mean(centred * centred, axis=-1, keepdims=True) + EPSILON)
    unit_rows = centred * inv_spread
    return (unit_rows * gain, unit_rows, inv_spread)


def norm_back(grad_rows, unit_rows, inv_spread, gain):
    gain_grad = jnp.sum(grad_rows * unit_rows, axis=0)
    scaled = grad_rows * gain
    inner_mean = jnp.mean(scaled, axis=-1, keepdims=True)
    cross_mean = jnp.mean(scaled * unit_rows, axis=-1, keepdims=True)
    return (gain_grad, inv_spread * (scaled - inner_mean - unit_rows * cross_mean))


def matmul_tn(left, right):
    return lax.dot_general(
        left, right, (((0,), (0,)), ((), ())), preferred_element_type=jnp.float32
    )


def matmul_nt(left, right):
    return lax.dot_general(
        left, right, (((1,), (1,)), ((), ())), preferred_element_type=jnp.float32
    )


def masked_scores(query, key_block, seg_query, seg_block):
    scores = (
        jnp.einsum("qhd,khd->hqk", query, key_block, preferred_element_type=jnp.float32) * 0.125
    )
    same_doc = seg_query[:, None] == seg_block[None, :]
    return jnp.where(same_doc[None], scores, -1e30)


def gated(inner, gate):
    return jax.nn.gelu(inner, approximate=False) * gate


def general_device(inputs, segments, cotangent, ln1_gain, w_qkv, w_attn_out, ln2_gain, w_in, w_mlp_out):
    tok_rows = inputs.shape[1]
    model_width = inputs.shape[2]
    seq_devices = lax.axis_size("seq")
    dp_devices = lax.axis_size("dp")
    tokens_in = inputs[0].astype(jnp.float32)
    seg_send = segments.astype(jnp.bfloat16)
    seg_query = seg_send[0]
    gathered_attn = (
        lax.all_gather(ln1_gain, ("dp", "seq"), axis=0, tiled=True),
        lax.all_gather(w_qkv, ("dp", "seq"), axis=0, tiled=True),
        lax.all_gather(w_attn_out, ("dp", "seq"), axis=0, tiled=True),
    )
    gain_one = gathered_attn[0].astype(jnp.float32)
    qkv_mat = gathered_attn[1].reshape(model_width, 3 * model_width)
    proj_mat = gathered_attn[2].reshape(model_width, model_width)
    places = (lax.axis_index("seq") * tok_rows + jnp.arange(tok_rows, dtype=jnp.int32)).astype(
        jnp.float32
    )
    cosines, sines = rope_tables(places)
    normed_one, unit_one, spread_one = norm_forward(tokens_in, gain_one)
    normed_one_low = normed_one.astype(jnp.bfloat16)
    qkv_rows = jnp.dot(normed_one_low, qkv_mat, preferred_element_type=jnp.float32)
    query = rotate(qkv_rows[:, :model_width].reshape(tok_rows, HEADS, HD), cosines, sines).astype(
        jnp.bfloat16
    )
    key_rot = rotate(
        qkv_rows[:, model_width : 2 * model_width].reshape(tok_rows, HEADS, HD), cosines, sines
    ).astype(jnp.bfloat16)
    value_rows = qkv_rows[:, 2 * model_width :].astype(jnp.bfloat16)
    key_send = key_rot.reshape(1, tok_rows, model_width)
    value_send = value_rows.reshape(1, tok_rows, model_width)
    fwd_init = (
        jnp.full((HEADS, tok_rows), -1e30, jnp.float32),
        jnp.zeros((HEADS, tok_rows), jnp.float32),
        jnp.zeros((tok_rows, HEADS, HD), jnp.float32),
    )
    key_piece = lax.all_gather(key_send, "seq", axis=1, tiled=True)
    value_piece = lax.all_gather(value_send, "seq", axis=1, tiled=True)
    seg_piece = lax.all_gather(seg_send, "seq", axis=1, tiled=True)
    span = key_piece.shape[1]
    step_rows = math.gcd(span, 512)

    def one_block(block_id, inner_state):
        top_score, total, accum = inner_state
        begin = block_id * step_rows
        key_block = lax.dynamic_slice_in_dim(key_piece[0], begin, step_rows, 0).reshape(
            step_rows, HEADS, HD
        )
        value_block = lax.dynamic_slice_in_dim(value_piece[0], begin, step_rows, 0).reshape(
            step_rows, HEADS, HD
        )
        seg_block = lax.dynamic_slice_in_dim(seg_piece[0], begin, step_rows, 0)
        scores = masked_scores(query, key_block, seg_query, seg_block)
        new_top = jnp.maximum(top_score, jnp.max(scores, axis=-1))
        fading = jnp.exp(top_score - new_top)
        weights = jnp.exp(scores - new_top[..., None])
        total = total * fading + jnp.sum(weights, axis=-1)
        accum = accum * fading.T[:, :, None] + jnp.einsum(
            "hqk,khd->qhd",
            weights.astype(jnp.bfloat16),
            value_block,
            preferred_element_type=jnp.float32,
        )
        return (new_top, total, accum)

    fwd_state = lax.fori_loop(0, span // step_rows, one_block, fwd_init)
    run_top, run_total, run_accum = fwd_state
    log_total = run_top + jnp.log(run_total)
    attended = (run_accum / run_total.T[:, :, None]).astype(jnp.bfloat16)
    attended_rows = attended.reshape(tok_rows, model_width)
    middle = tokens_in + jnp.dot(attended_rows, proj_mat, preferred_element_type=jnp.float32)
    gathered_mlp = (
        lax.all_gather(ln2_gain, ("dp", "seq"), axis=0, tiled=True),
        lax.all_gather(w_in, ("dp", "seq"), axis=0, tiled=True),
        lax.all_gather(w_mlp_out, ("dp", "seq"), axis=0, tiled=True),
    )
    gain_two = gathered_mlp[0].astype(jnp.float32)
    in_mat = gathered_mlp[1].reshape(model_width, 2 * FF)
    down_mat = gathered_mlp[2].reshape(FF, model_width)
    normed_two, unit_two, spread_two = norm_forward(middle, gain_two)
    normed_two_low = normed_two.astype(jnp.bfloat16)
    upper = jnp.dot(normed_two_low, in_mat, preferred_element_type=jnp.float32)
    inner = upper[:, :FF]
    gate = upper[:, FF:]
    hidden_low = gated(inner, gate).astype(jnp.bfloat16)
    output = (middle + jnp.dot(hidden_low, down_mat, preferred_element_type=jnp.float32)).astype(
        jnp.bfloat16
    )
    gathered_mlp = (
        lax.all_gather(ln2_gain, ("dp", "seq"), axis=0, tiled=True),
        lax.all_gather(w_in, ("dp", "seq"), axis=0, tiled=True),
        lax.all_gather(w_mlp_out, ("dp", "seq"), axis=0, tiled=True),
    )
    gain_two = gathered_mlp[0].astype(jnp.float32)
    in_mat = gathered_mlp[1].reshape(model_width, 2 * FF)
    down_mat = gathered_mlp[2].reshape(FF, model_width)
    grad_low = cotangent[0]
    grad_rows = grad_low.astype(jnp.float32)
    d_hidden = matmul_nt(grad_low, down_mat)
    grad_down = matmul_tn(hidden_low, grad_low)
    gated_value, pull = jax.vjp(gated, inner, gate)
    d_inner, d_gate = pull(d_hidden)
    d_upper_low = jnp.concatenate([d_inner, d_gate], axis=1).astype(jnp.bfloat16)
    grad_in = matmul_tn(normed_two_low, d_upper_low)
    d_normed_two = matmul_nt(d_upper_low, in_mat)
    grad_gain_two, d_middle_part = norm_back(d_normed_two, unit_two, spread_two, gain_two)
    d_middle = grad_rows + d_middle_part
    mlp_parts = tuple(
        (g.reshape(dp_devices, seq_devices, -1) for g in (grad_gain_two, grad_in, grad_down))
    )
    mlp_mid = (
        lax.psum_scatter(
            mlp_parts[0].astype(jnp.bfloat16), "seq", scatter_dimension=1, tiled=True
        ).astype(jnp.float32),
        lax.psum_scatter(
            mlp_parts[1].astype(jnp.bfloat16), "seq", scatter_dimension=1, tiled=True
        ).astype(jnp.float32),
        lax.psum_scatter(
            mlp_parts[2].astype(jnp.bfloat16), "seq", scatter_dimension=1, tiled=True
        ).astype(jnp.float32),
    )
    mlp_shards = (
        lax.psum_scatter(
            mlp_mid[0].astype(jnp.bfloat16), "dp", scatter_dimension=0, tiled=True
        ).astype(jnp.float32),
        lax.psum_scatter(
            mlp_mid[1].astype(jnp.bfloat16), "dp", scatter_dimension=0, tiled=True
        ).astype(jnp.float32),
        lax.psum_scatter(
            mlp_mid[2].astype(jnp.bfloat16), "dp", scatter_dimension=0, tiled=True
        ).astype(jnp.float32),
    )
    gathered_attn = (
        lax.all_gather(ln1_gain, ("dp", "seq"), axis=0, tiled=True),
        lax.all_gather(w_qkv, ("dp", "seq"), axis=0, tiled=True),
        lax.all_gather(w_attn_out, ("dp", "seq"), axis=0, tiled=True),
    )
    gain_one = gathered_attn[0].astype(jnp.float32)
    qkv_mat = gathered_attn[1].reshape(model_width, 3 * model_width)
    proj_mat = gathered_attn[2].reshape(model_width, model_width)
    d_branch_low = d_middle.astype(jnp.bfloat16)
    grad_proj = matmul_tn(attended_rows, d_branch_low)
    d_attended = matmul_nt(d_branch_low, proj_mat).astype(jnp.bfloat16).reshape(tok_rows, HEADS, HD)
    delta_rows = jnp.einsum(
        "qhd,qhd->hq", d_attended.astype(jnp.float32), attended.astype(jnp.float32)
    )
    back_init = (
        jnp.zeros((tok_rows, HEADS, HD), jnp.float32),
        jnp.zeros((tok_rows * seq_devices, 2 * model_width), jnp.float32),
    )
    attend_key_piece = lax.all_gather(key_send, "seq", axis=1, tiled=True)
    attend_value_piece = lax.all_gather(value_send, "seq", axis=1, tiled=True)
    attend_seg_piece = lax.all_gather(seg_send, "seq", axis=1, tiled=True)
    span = attend_key_piece.shape[1]
    attend_step_rows = math.gcd(span, 512)

    def one_block(block_id, inner_state):
        grad_query, grad_kv = inner_state
        begin = block_id * attend_step_rows
        key_block = lax.dynamic_slice_in_dim(
            attend_key_piece[0], begin, attend_step_rows, 0
        ).reshape(attend_step_rows, HEADS, HD)
        value_block = lax.dynamic_slice_in_dim(
            attend_value_piece[0], begin, attend_step_rows, 0
        ).reshape(attend_step_rows, HEADS, HD)
        seg_block = lax.dynamic_slice_in_dim(attend_seg_piece[0], begin, attend_step_rows, 0)
        scores = masked_scores(query, key_block, seg_query, seg_block)
        probs = jnp.exp(scores - log_total[..., None])
        probs_low = probs.astype(jnp.bfloat16)
        value_grad = jnp.einsum(
            "hqk,qhd->khd", probs_low, d_attended, preferred_element_type=jnp.float32
        )
        d_probs = jnp.einsum(
            "qhd,khd->hqk", d_attended, value_block, preferred_element_type=jnp.float32
        )
        d_scores = (probs * (d_probs - delta_rows[..., None])).astype(jnp.bfloat16)
        grad_query = (
            grad_query
            + jnp.einsum("hqk,khd->qhd", d_scores, key_block, preferred_element_type=jnp.float32)
            * 0.125
        )
        key_grad = (
            jnp.einsum("hqk,qhd->khd", d_scores, query, preferred_element_type=jnp.float32) * 0.125
        )
        block_grads = jnp.concatenate(
            [
                key_grad.reshape(attend_step_rows, model_width),
                value_grad.reshape(attend_step_rows, model_width),
            ],
            axis=1,
        )
        grad_kv = lax.dynamic_update_slice_in_dim(grad_kv, block_grads, begin, 0)
        return (grad_query, grad_kv)

    back_state = lax.fori_loop(0, span // attend_step_rows, one_block, back_init)
    kv_grads = lax.psum_scatter(
        back_state[1].astype(jnp.bfloat16), "seq", scatter_dimension=0, tiled=True
    ).astype(jnp.float32)
    d_query = rotate_back(back_state[0], cosines, sines).reshape(tok_rows, model_width)
    d_key = rotate_back(
        kv_grads[:, :model_width].reshape(tok_rows, HEADS, HD), cosines, sines
    ).reshape(tok_rows, model_width)
    d_qkv_low = jnp.concatenate([d_query, d_key, kv_grads[:, model_width:]], axis=1).astype(
        jnp.bfloat16
    )
    grad_qkv = matmul_tn(normed_one_low, d_qkv_low)
    d_normed_one = matmul_nt(d_qkv_low, qkv_mat)
    grad_gain_one, d_input_part = norm_back(d_normed_one, unit_one, spread_one, gain_one)
    input_grad = d_middle + d_input_part
    attn_parts = tuple(
        (g.reshape(dp_devices, seq_devices, -1) for g in (grad_gain_one, grad_qkv, grad_proj))
    )
    attn_mid = (
        lax.psum_scatter(
            attn_parts[0].astype(jnp.bfloat16), "seq", scatter_dimension=1, tiled=True
        ).astype(jnp.float32),
        lax.psum_scatter(
            attn_parts[1].astype(jnp.bfloat16), "seq", scatter_dimension=1, tiled=True
        ).astype(jnp.float32),
        lax.psum_scatter(
            attn_parts[2].astype(jnp.bfloat16), "seq", scatter_dimension=1, tiled=True
        ).astype(jnp.float32),
    )
    attn_shards = (
        lax.psum_scatter(
            attn_mid[0].astype(jnp.bfloat16), "dp", scatter_dimension=0, tiled=True
        ).astype(jnp.float32),
        lax.psum_scatter(
            attn_mid[1].astype(jnp.bfloat16), "dp", scatter_dimension=0, tiled=True
        ).astype(jnp.float32),
        lax.psum_scatter(
            attn_mid[2].astype(jnp.bfloat16), "dp", scatter_dimension=0, tiled=True
        ).astype(jnp.float32),
    )
    return (
        output.reshape(1, tok_rows, model_width),
        input_grad.reshape(1, tok_rows, model_width),
        attn_shards[0].reshape(-1),
        attn_shards[1].reshape(-1),
        attn_shards[2].reshape(-1),
        mlp_shards[0].reshape(-1),
        mlp_shards[1].reshape(-1),
        mlp_shards[2].reshape(-1),
    )


MESH_IDS = pl.DeviceIdType.MESH
TOK = 128
WIDTH = 1024
PART = FF // 32
PAD = 96
HID = 8 * PAD
QKV = 3 * 256
BF = jnp.bfloat16
F32 = jnp.float32


def dot_nn(a, b):
    return lax.dot_general(a, b, (((1,), (0,)), ((), ())), preferred_element_type=F32)


def turned(u, low_half):
    return jnp.where(low_half, pltpu.roll(u, 96, axis=1), pltpu.roll(u, 32, axis=1))


def column(gain_ref):
    square = jnp.broadcast_to(gain_ref[...].astype(F32), (32, 32))
    rows = lax.broadcasted_iota(jnp.int32, (32, 32), 0)
    cols = lax.broadcasted_iota(jnp.int32, (32, 32), 1)
    return jnp.sum(jnp.where(rows == cols, square, 0.0), axis=1, keepdims=True)


def owner(r, k):
    return k // 4 * 16 + (r // 2 + k // 4) % 2 * 8 + k // 2 % 2 * 4 + k % 2 * 2 + r % 2


def runs(places):
    found = []
    for lane, place in enumerate(places):
        if place is None:
            continue
        tile, shift = place[0], (place[1] - lane) % 128
        if found and found[-1][:2] == (tile, shift) and found[-1][3] == lane:
            found[-1] = found[-1][:3] + (lane + 1,)
        else:
            found.append((tile, shift, lane, lane + 1))
    return found


def in_moves(r, u):
    places = []
    for at in range(u * 128, u * 128 + 128):
        gate, rest = divmod(at, HID)
        k, i = divmod(rest, PAD)
        col = gate * FF + PART * owner(r, k) + i
        places.append(divmod(col, 128) if i < PART else None)
    return runs(places)


def out_moves(t):
    spots = {owner(r, k): (r, k) for r in range(4) for k in range(8)}
    places = []
    for col in range(t * 128, t * 128 + 128):
        gate, rest = divmod(col, FF)
        device, i = divmod(rest, PART)
        r, k = spots[device]
        u, lane = divmod(gate * HID + k * PAD + i, 128)
        places.append(((r, u), lane))
    return runs(places)


def moved(moves, load):
    lanes = lax.broadcasted_iota(jnp.int32, (1, 128), 1)
    out = jnp.zeros((32, 128), F32)
    for tile, shift, low, high in moves:
        piece = load(tile)
        if shift:
            piece = pltpu.roll(piece, 128 - shift, axis=1)
        out = jnp.where((lanes >= low) & (lanes < high), piece, out)
    return out


def finish_kernel(
    gq_in,
    go_in,
    gi_in,
    gd_in,
    out_in,
    ig_in,
    gain1_in,
    sums_in,
    wq_flat,
    out_ref,
    ig_ref,
    gain1_ref,
    gq_ref,
    go_ref,
    gain2_ref,
    gi_ref,
    gd_ref,
    lines,
    gq_raw,
    go_raw,
    gi_raw,
    gd_raw,
    wq_raw,
    gq_own,
    go_own,
    gd_own,
    ig_raw,
    out_raw,
    sems,
):
    count = [0]

    def start(src, dst):
        cp = pltpu.make_async_copy(src, dst, sems.at[count[0]])
        count[0] += 1
        cp.start()
        return cp

    gi_here = start(gi_in, gi_raw)
    ig_here = start(ig_in, ig_raw)
    out_here = start(out_in, out_raw)
    gd_here = start(gd_in, gd_raw)
    gq_here = start(gq_in, gq_raw)
    wq_here = start(wq_flat, wq_raw)
    go_here = start(go_in, go_raw)
    written = []
    rows = lax.broadcasted_iota(jnp.int32, (32, 32), 0)
    cols = lax.broadcasted_iota(jnp.int32, (32, 32), 1)

    def line(total):
        total = jnp.sum(total, axis=1, keepdims=True)
        return jnp.sum(jnp.where(rows == cols, total, 0.0), axis=0, keepdims=True)

    qkv_rows = 3 * WIDTH // TOK
    gi_here.wait()
    written.append(start(gi_raw, gi_ref))
    ig_here.wait()
    written.append(start(ig_raw, ig_ref))
    out_here.wait()
    written.append(start(out_raw, out_ref))
    gain2_ref[...] = line(sums_in[...])
    gd_here.wait()
    for j in range(8):
        gd_own[pl.ds(j, PART, stride=8), :] = gd_raw[0:PART, pl.ds(j * 128, 128)]
    written.append(start(gd_own, gd_ref))
    gain = column(gain1_in)
    total = jnp.zeros((32, 128), F32)
    wq_here.wait()
    lines[0 : 32 * qkv_rows] = wq_raw[...].astype(F32)
    gq_here.wait()
    for j in range(qkv_rows):
        part, cut = divmod(j, 8)
        r = (cut // 2 + cut // 4) % 2 * 2 + cut // 4
        g = gq_raw[r, :, pl.ds(part * 256 + cut % 2 * 128, 128)].astype(F32)
        total = total + g * lines[pl.ds(j, 32, stride=qkv_rows), :]
        gq_own[pl.ds(j, 32, stride=qkv_rows), :] = g * gain
    written.append(start(gq_own, gq_ref))
    gain1_ref[...] = line(total)
    go_here.wait()
    for j in range(8):
        go_own[pl.ds(j, 32, stride=8), :] = go_raw[:, pl.ds(j * 128, 128)].astype(F32)
    written.append(start(go_own, go_ref))
    for cp in written:
        cp.wait()


def layer_kernel(
    x_ref,
    cot_in,
    seg_in,
    cos_ref,
    sin_ref,
    gain1_in,
    gain2_in,
    wq_flat,
    wo_flat,
    wi_flat,
    wd_flat,
    out_ref,
    ig_ref,
    gq_ref,
    go_ref,
    gi_ref,
    gd_ref,
    sums_ref,
    seg_buf,
    n1,
    n2,
    cot,
    db,
    wq,
    wo,
    wi,
    wd,
    unit1,
    inv1,
    unit2,
    inv2,
    middle,
    dmid,
    q_buf,
    k_buf,
    v_buf,
    probs,
    att,
    datt,
    up_a,
    up_b,
    hidden,
    d_up,
    dqkv,
    ps,
    ps_in,
    ps_far,
    ps_back,
    gq,
    go,
    gi,
    gd,
    rq1,
    rq2,
    rq3,
    ro1,
    ro2,
    ro3,
    ri1,
    ri2,
    ri3,
    rd1,
    rd2,
    rd3,
    wq_in,
    wo_in,
    wi_in,
    lines,
    wide,
    out_vm,
    ig_vm,
    gq_vm,
    go_vm,
    gi_vm,
    gd_vm,
    gi_own,
    sums,
    send_sems,
    recv_sems,
    local_sems,
):
    dp, c = lax.axis_index("dp"), lax.axis_index("seq")
    x, y, z = lax.rem(dp, 2), lax.rem(dp // 2, 2), dp // 4
    zh, zp = z // 2, lax.rem(z, 2)
    kind = lax.rem(zp + zh, 2)
    role = kind * 2 + c

    def device(X, Y, Z, C):
        return (Z * 4 + Y * 2 + X, C)

    core_dev = device(x, y, z, 1 - c)
    pair_dev = device(x, y, zh * 2 + 1 - zp, c)
    diag_dev = device(x, y, zh * 2 + 1 - zp, 1 - c)
    half_dev = device(x, y, 3 - z, c)
    x_dev = device(1 - x, y, z, c)
    y_dev = device(x, 1 - y, z, c)

    barrier = pltpu.get_barrier_semaphore()
    for dev in (core_dev, pair_dev, diag_dev, half_dev, x_dev, y_dev):
        pl.semaphore_signal(barrier, inc=1, device_id=dev, device_id_type=MESH_IDS)

    sent = []
    n_sems = [0]
    free = list(range(N_SENDS))

    def copy_to(src, dst, dev, keep=True):
        i, k = n_sems[0], free.pop(0)
        n_sems[0] += 1
        cp = pltpu.make_async_remote_copy(
            src_ref=src,
            dst_ref=dst,
            send_sem=send_sems.at[k],
            recv_sem=recv_sems.at[i],
            device_id=dev,
            device_id_type=MESH_IDS,
        )
        if keep:
            sent.append((cp, k))
        return cp

    local = []

    def emit(i, src, dst):
        cp = pltpu.make_async_copy(src, dst, local_sems.at[i])
        cp.start()
        local.append(cp)

    def settle(first):
        for cp, k in sent[:first]:
            cp.wait_send()
            free.append(k)
        del sent[:first]

    def go_copy(src, dst, dev):
        cp = copy_to(src, dst, dev)
        cp.start()
        return cp


    others = (
        (core_dev, kind * 2 + 1 - c, (z, 1 - c)),
        (pair_dev, (1 - kind) * 2 + c, (zh * 2 + 1 - zp, c)),
        (diag_dev, (1 - kind) * 2 + 1 - c, (zh * 2 + 1 - zp, 1 - c)),
    )

    def spread(own, buf):
        cps = [go_copy(own.at[r], buf.at[z, y, x, c], dev) for dev, r, _ in others]
        return cps

    class Gather:
        def __init__(self, buf, cols, base=0):
            self.buf = buf
            self.halves = (pl.ds(base, cols // 2), pl.ds(base + cols // 2, cols // 2))
            self.per_half = buf.shape[0] // 2

        def of(self, which):
            return pl.ds(self.per_half * which, self.per_half)

        def spot(self, which, cut):
            return self.buf.at[(self.of(which), y, x) + (slice(None),) * (len(self.buf.shape) - 4) + (cut,)]

        def line(self, which, cut, i):
            rest = (slice(None),) * (len(self.buf.shape) - 4) + (cut,)
            at = (y, slice(None)) if i == 0 else (slice(None), x)
            return self.buf.at[(self.of(which),) + at + rest]

        def same(self, ref, dev):
            return go_copy(ref, ref, dev)

        def across(self):
            self.over = [self.same(self.spot(zh, cut), half_dev) for cut in self.halves]

        def own_first(self):
            self.a = [
                self.same(self.spot(zh, cut), dev) for cut, dev in zip(self.halves, (x_dev, y_dev))
            ]

        def own_second(self):
            self.b = []
            for i, dev in enumerate((y_dev, x_dev)):
                self.a[i].wait_recv()
                self.b.append(self.same(self.line(zh, self.halves[i], i), dev))

        def far_first(self):
            self.a2 = []
            for i, dev in enumerate((x_dev, y_dev)):
                self.over[i].wait_recv()
                self.a2.append(self.same(self.spot(1 - zh, self.halves[i]), dev))

        def far_second(self):
            self.b2 = []
            for i, dev in enumerate((y_dev, x_dev)):
                self.a2[i].wait_recv()
                self.b2.append(self.same(self.line(1 - zh, self.halves[i], i), dev))

        def done(self):
            for cp in self.b + self.b2:
                cp.wait_recv()

    class GatherOut:
        def __init__(self, buf, cols):
            self.buf = buf
            self.halves = (pl.ds(0, cols // 2), pl.ds(cols // 2, cols // 2))

        def start(self):
            self.s0 = copy_to(wo_in, self.buf.at[y, x, c], core_dev, keep=False)

            @pl.when(c != zh)
            def _():
                self.s0.start()

        def across(self):
            self.s1 = copy_to(self.buf.at[y, x], self.buf.at[y, x], half_dev, keep=False)

            @pl.when(c == zh)
            def _():
                self.buf[y, x, c] = wo_in[...]
                self.s0.wait_recv()
                self.s1.start()

        def first(self):
            @pl.when(c != zh)
            def _():
                self.s1.wait_recv()

            self.a = []
            for cut, dev in zip(self.halves, (x_dev, y_dev)):
                ref = self.buf.at[y, x, :, :, cut]
                self.a.append(go_copy(ref, ref, dev))

        def second(self):
            self.b = []
            for i, dev in enumerate((y_dev, x_dev)):
                self.a[i].wait_recv()
                cut = self.halves[i]
                ref = self.buf.at[y, :, :, :, cut] if i == 0 else self.buf.at[:, x, :, :, cut]
                self.b.append(go_copy(ref, ref, dev))

        def done(self):
            for cp in self.b:
                cp.wait_recv()

        def end(self):
            @pl.when(c != zh)
            def _():
                self.s0.wait_send()

            @pl.when(c == zh)
            def _():
                self.s1.wait_send()


    pieces = [pl.ds(i * (TOK // PIECES), TOK // PIECES) for i in range(PIECES)]

    class Share:
        def __init__(self, buf):
            self.buf = buf
            self.to_pair = [
                go_copy(buf.at[zp, c, cut], buf.at[zp, c, cut], pair_dev) for cut in pieces
            ]
            self.to_core = go_copy(buf.at[zp, c], buf.at[zp, c], core_dev)

        def forward(self):
            self.fwd = []
            for cp, cut in zip(self.to_pair, pieces):
                cp.wait_recv()
                ref = self.buf.at[1 - zp, c, cut]
                self.fwd.append(go_copy(ref, ref, core_dev))

        def core(self):
            self.to_core.wait_recv()

        def done(self):
            for cp in self.fwd:
                cp.wait_recv()

    class Reduce:
        def __init__(self, i):
            self.i = i

        def far_terms(self):
            i = self.i
            self.mine_far = go_copy(ps.at[i, 1 - zp, 1 - c], ps_in.at[i, 1 - zp], core_dev)

        def near_terms(self):
            i = self.i
            self.mine_near = go_copy(ps.at[i, zp, 1 - c], ps_in.at[i, zp], core_dev)

        def cross(self):
            i = self.i
            self.mine_far.wait_recv()
            self.far = []
            for cut in pieces:
                ps_far[i, cut] = (
                    ps[i, 1 - zp, c, cut].astype(F32) + ps_in[i, 1 - zp, cut].astype(F32)
                ).astype(BF)
                self.far.append(go_copy(ps_far.at[i, cut], ps_back.at[i, cut], pair_dev))

        def total(self):
            i = self.i
            self.mine_near.wait_recv()
            near = ps[i, zp, c].astype(F32) + ps_in[i, zp].astype(F32)
            for cp in self.far:
                cp.wait_recv()
            return near + ps_back[i].astype(F32)


    def add_into(target, extra):
        target[...] = (target[...].astype(F32) + extra[...].astype(F32)).astype(BF)

    def add_all(mine, got):
        n = got.shape[0]
        if n == 1:
            add_into(mine.at[0], got.at[0])
            return

        def body(j, carry):
            add_into(mine.at[j], got.at[j])
            return carry

        lax.fori_loop(0, n, body, 0)

    class Scatter:
        def __init__(self, buf, cols, r1, r2, r3, base=0):
            self.buf, self.r1, self.r2, self.r3 = buf, r1, r2, r3
            self.halves = (pl.ds(base, cols // 2), pl.ds(base + cols // 2, cols // 2))
            self.cols = pl.ds(base, cols)
            self.per_half = buf.shape[0] // 2
            self.rest = (slice(None),) * (len(buf.shape) - 4)
            self.c1, self.c2 = {}, {}

        def of(self, which):
            return pl.ds(self.per_half * which, self.per_half)

        def line(self, i, which, other):
            if i == 0:
                at = (1 - y if other else y, slice(None))
            else:
                at = (slice(None), 1 - x if other else x)
            return self.buf.at[(self.of(which),) + at + self.rest + (self.halves[i],)]

        def spot(self, i, which, other):
            Y, X = (y, x) if not other else ((y, 1 - x) if i == 0 else (1 - y, x))
            return self.buf.at[(self.of(which), Y, X) + self.rest + (self.halves[i],)]

        def first(self, far):
            which = 1 - zh if far else zh
            self.c1[far] = [
                go_copy(self.line(i, which, True), self.r1.at[i, far], dev)
                for i, dev in enumerate((y_dev, x_dev))
            ]

        def second(self, far):
            which = 1 - zh if far else zh
            self.c2[far] = []
            for i, dev in enumerate((x_dev, y_dev)):
                self.c1[far][i].wait_recv()
                add_all(self.line(i, which, False), self.r1.at[i, far])
                self.c2[far].append(go_copy(self.spot(i, which, True), self.r2.at[i, far], dev))

        def third(self, far):
            which = 1 - zh if far else zh
            for i in range(2):
                self.c2[far][i].wait_recv()
                add_all(self.spot(i, which, False), self.r2.at[i, far])
            if far:
                src = self.buf.at[(self.of(which), y, x) + self.rest + (self.cols,)]
                self.c3 = go_copy(src, self.r3, half_dev)

    class ScatterRows(Scatter):
        def fourth(self, out):
            self.c3.wait_recv()
            cols = self.cols
            add_all(self.buf.at[self.of(zh), y, x, :, :, cols], self.r3)
            self.c4 = []
            for dev, _, (there, core) in others:
                src = self.buf.at[there, y, x, core, :, cols]
                self.c4.append(go_copy(src, out.at[role, :, cols], dev))
            out[role, :, cols] = self.buf[z, y, x, c, :, cols]

        def done(self):
            for cp in self.c4:
                cp.wait_recv()

    class ScatterDown(Scatter):
        def fourth(self, out):
            self.c3.wait_recv()
            out[...] = self.buf[zh, y, x].astype(F32) + self.r3[0].astype(F32)

    class ScatterOut:
        def __init__(self, buf, cols, r1, r2, r3):
            self.buf, self.r1, self.r2, self.r3 = buf, r1, r2, r3
            self.halves = (pl.ds(0, cols // 2), pl.ds(cols // 2, cols // 2))

        def line(self, i, other):
            cut = self.halves[i]
            if i == 0:
                return self.buf.at[1 - y if other else y, :, :, :, cut]
            return self.buf.at[:, 1 - x if other else x, :, :, cut]

        def spot(self, i, other):
            Y, X = (y, x) if not other else ((y, 1 - x) if i == 0 else (1 - y, x))
            return self.buf.at[Y, X, :, :, self.halves[i]]

        def first(self):
            self.c1 = [
                go_copy(self.line(i, True), self.r1.at[i], dev)
                for i, dev in enumerate((y_dev, x_dev))
            ]

        def second(self):
            self.c2 = []
            for i, dev in enumerate((x_dev, y_dev)):
                self.c1[i].wait_recv()
                add_all(self.line(i, False), self.r1.at[i])
                self.c2.append(go_copy(self.spot(i, True), self.r2.at[i], dev))

        def third(self):
            for i in range(2):
                self.c2[i].wait_recv()
                add_all(self.spot(i, False), self.r2.at[i])
            self.c3 = copy_to(self.buf.at[y, x], self.r3, half_dev, keep=False)

            @pl.when(c != zh)
            def _():
                self.c3.start()

        def fourth(self, out):
            self.c4 = copy_to(self.r3.at[1 - c], out, core_dev, keep=False)

            @pl.when(c == zh)
            def _():
                self.c3.wait_recv()
                add_all(self.r3, self.buf.at[y, x])
                self.c4.start()
                out[...] = self.r3[c]

        def done(self):
            @pl.when(c != zh)
            def _():
                self.c4.wait_recv()
                self.c3.wait_send()

            @pl.when(c == zh)
            def _():
                self.c4.wait_send()

    qkv_rows = 3 * WIDTH // TOK
    lines[0 : 32 * qkv_rows] = wq_flat[...].astype(F32)
    gain = column(gain1_in)
    for j in range(qkv_rows):
        part, cut = divmod(j, 8)
        r = (cut // 2 + cut // 4) % 2 * 2 + cut // 4
        w = lines[pl.ds(j, 32, stride=qkv_rows), :] * gain
        wq_in[r, :, pl.ds(part * 256 + cut % 2 * 128, 128)] = w.astype(BF)
    wq[z, y, x, c] = wq_in[role]
    g_q, g_d = Gather(wq, QKV), Gather(wd, WIDTH)
    g_i, g_j = Gather(wi, HID), Gather(wi, HID, HID)
    g_o = GatherOut(wo, WIDTH)


    r_d = ScatterDown(gd, WIDTH, rd1, rd2, rd3)
    r_i = ScatterRows(gi, HID, ri1.at[0], ri2.at[0], ri3.at[0])
    r_j = ScatterRows(gi, HID, ri1.at[1], ri2.at[1], ri3.at[1], HID)
    r_q = ScatterRows(gq, QKV, rq1, rq2, rq3)
    r_o = ScatterOut(go, WIDTH, ro1, ro2, ro3)
    on = {}
    red = [Reduce(i) for i in range(4)]
    lanes = lax.broadcasted_iota(jnp.int32, (1, 128), 1)
    low_half = lax.rem(lanes, 64) < 32
    first_head = lanes < 64

    def qkv_step(s, carry):
        rows = n1[s].reshape(256, WIDTH)
        for part, dst in enumerate((q_buf, k_buf, v_buf)):
            for j in range(2):
                at = part * 256 + j * 128
                w = wq[:, :, :, :, :, pl.ds(at, 128)].reshape(WIDTH, 128)
                u = dot_nn(rows, w)
                if part < 2:
                    u = u * cos_ref[...] + turned(u, low_half) * sin_ref[...]
                dst[s, j] = u.astype(BF)
        return carry

    def only(head, u):
        return jnp.where(first_head if head == 0 else ~first_head, u, jnp.zeros_like(u))

    def attend(i, carry):
        s, j = i // 2, lax.rem(i, 2)
        q, k, v = q_buf[s, j], k_buf[s, j], v_buf[s, j]
        seg_row = jnp.concatenate([seg_buf[s, 0, 0:1], seg_buf[s, 1, 0:1]], axis=1)
        seg_col = jnp.broadcast_to(seg_row, (128, 256)).T[:, 0:1]
        same = seg_col == seg_row
        heads = []
        for h in range(2):
            scores = matmul_nt(only(h, q), k) * 0.125
            scores = jnp.where(same, scores, -1e30)
            weights = jnp.exp(scores - jnp.max(scores, axis=-1, keepdims=True))
            p = weights * (1.0 / jnp.sum(weights, axis=-1, keepdims=True))
            probs[i, h] = p
            heads.append(dot_nn(p.astype(BF), v))
        att[s, j] = jnp.where(first_head, heads[0], heads[1]).astype(BF)
        return carry

    def att_rows(s):
        return jnp.concatenate([att[s, 0], att[s, 1]], axis=1)

    def branch(s, carry):
        w = wo[...].reshape(256, WIDTH)
        ps[0, s] = dot_nn(att_rows(s), w).astype(BF).reshape(2, TOK, WIDTH)
        return carry

    def upper_for(s):
        def upper(j, carry):
            at = pl.multiple_of(j * 256, 256)
            rows = n2[s].reshape(256, WIDTH)
            inner = dot_nn(rows, wi[:, :, :, :, :, pl.ds(at, 256)].reshape(WIDTH, 256))
            gate = dot_nn(
                rows,
                wi[:, :, :, :, :, pl.ds(pl.multiple_of(HID + at, 256), 256)].reshape(WIDTH, 256),
            )
            cdf = 0.5 * (1.0 + lax.erf(inner * math.sqrt(0.5)))
            slope = cdf + inner * jnp.exp(-0.5 * inner * inner) * (1.0 / math.sqrt(2 * math.pi))
            bent = inner * cdf
            up_a[s, :, pl.ds(at, 256)] = gate * slope
            up_b[s, :, pl.ds(at, 256)] = bent
            hidden[s, :, pl.ds(at, 256)] = (bent * gate).astype(BF)
            return carry

        lax.fori_loop(0, HID // 256, upper, 0)

    def down_grad(i, carry):
        lhs = hidden[:, :, pl.ds(pl.multiple_of(i * 384, 384), 384)].reshape(512, 384)
        for j in range(2):
            rhs = cot[:, :, :, pl.ds(j * 512, 512)].reshape(512, 512)
            gd[i, :, :, :, pl.ds(j * 512, 512)] = (
                matmul_tn(lhs, rhs).astype(BF).reshape(2, 2, PAD, 512)
            )
        return carry

    def hidden_grad_for(s):
        def hidden_grad(i, carry):
            w = wd[i].reshape(384, WIDTH)
            at = pl.multiple_of(i * 384, 384)
            dh = matmul_nt(cot[s].reshape(256, WIDTH), w)
            d_up[s, :, pl.ds(at, 384)] = (dh * up_a[s, :, pl.ds(at, 384)]).astype(BF)
            d_up[s, :, pl.ds(pl.multiple_of(HID + at, 384), 384)] = (
                dh * up_b[s, :, pl.ds(at, 384)]
            ).astype(BF)
            return carry

        lax.fori_loop(0, 2, hidden_grad, 0)

    def normed_two_grad_for(s):
        def normed_two_grad(i, carry):
            w = wi[i].reshape(256, 2 * HID)
            at = pl.multiple_of(i * 256, 256)
            ps[1, s, :, :, pl.ds(at, 256)] = matmul_nt(d_up[s], w).astype(BF).reshape(2, TOK, 256)
            return carry

        lax.fori_loop(0, 4, normed_two_grad, 0)

    def in_grad_for(base, first):
        def in_grad(i, carry):
            lhs = n2[:, :, :, pl.ds(pl.multiple_of(i * 256, 256), 256)].reshape(512, 256)
            for j in range(HID // 256):
                at = base + j * 256
                rhs = d_up[:, :, pl.ds(at, 256)].reshape(512, 256)
                gi[i, :, :, :, :, pl.ds(at, 256)] = (
                    matmul_tn(lhs, rhs).astype(BF).reshape(2, 2, 2, 32, 256)
                )
            return carry

        lax.fori_loop(first, first + 2, in_grad, 0)

    def down(i, carry):
        w = wd[...].reshape(HID, WIDTH)
        ps[2, i] = dot_nn(hidden[i], w).astype(BF).reshape(2, TOK, WIDTH)
        return carry

    def attended_grad(s, carry):
        rows = db[s].reshape(256, WIDTH)
        da = matmul_nt(rows, wo[...].reshape(256, WIDTH)).astype(BF)
        datt[s, 0] = da[:, 0:128]
        datt[s, 1] = da[:, 128:256]
        return carry

    def attend_back(i, carry):
        s, j = i // 2, lax.rem(i, 2)
        q, k, v, da = q_buf[s, j], k_buf[s, j], v_buf[s, j], datt[s, j]
        dq, dk, dv = [], [], []
        for h in range(2):
            p = probs[i, h]
            dprob = matmul_nt(only(h, da), v)
            delta = jnp.sum(p * dprob, axis=-1, keepdims=True)
            ds = (p * (dprob - delta)).astype(BF)
            dq.append(dot_nn(ds, k))
            dk.append(matmul_tn(ds, q))
            dv.append(matmul_tn(p.astype(BF), da))
        for part, pieces in enumerate((dq, dk, dv)):
            u = jnp.where(first_head, pieces[0], pieces[1])
            if part < 2:
                u = u * 0.125
                u = u * cos_ref[...] - turned(u, low_half) * sin_ref[...]
            dqkv[part, j, s] = u.astype(BF)
        return carry

    def first_grads_for(s):
        rows = jnp.concatenate([dqkv[p, j, s] for p in range(3) for j in range(2)], axis=1)

        def first_grads(i, carry):
            w = wq[i].reshape(256, QKV)
            at = pl.multiple_of(i * 256, 256)
            ps[3, s, :, :, pl.ds(at, 256)] = matmul_nt(rows, w).astype(BF).reshape(2, TOK, 256)
            return carry

        lax.fori_loop(0, 4, first_grads, 0)

    def qkv_grad(i, carry):
        lhs = n1[:, :, :, pl.ds(pl.multiple_of(i * 256, 256), 256)].reshape(512, 256)
        for p in range(3):
            for j in range(2):
                rhs = dqkv[p, j].reshape(512, 128)
                gq[i, :, :, :, :, pl.ds(p * 256 + j * 128, 128)] = (
                    matmul_tn(lhs, rhs).astype(BF).reshape(2, 2, 2, 32, 128)
                )
        return carry

    pl.semaphore_wait(barrier, 6)
    on["s_q"] = spread(wq_in, wq)
    wide[0 : 8 * PART] = wd_flat[...].astype(F32)
    wide[8 * PART : 8 * PAD] = jnp.zeros((8 * (PAD - PART), TOK), F32)
    for j in range(8):
        wd[zh, y, x, :, pl.ds(j * 128, 128)] = wide[pl.ds(j, PAD, stride=8), :].astype(BF)
    wide[0:256] = wo_flat[...].astype(F32)
    for j in range(8):
        wo_in[:, pl.ds(j * 128, 128)] = wide[pl.ds(j, 32, stride=8), :].astype(BF)
    g_o.start()
    g_d.own_first()
    in_rows = 2 * FF // TOK
    lines[...] = wi_flat[...].astype(F32)
    gain = column(gain2_in)
    for j in range(in_rows):
        wide[pl.ds(j * 32, 32), :] = lines[pl.ds(j, 32, stride=in_rows), :] * gain
    for r in range(4):
        for u in range(2 * HID // TOK):
            tile = moved(in_moves(r, u), lambda t: wide[pl.ds(t * 32, 32), :])
            wi_in[r, :, pl.ds(u * 128, 128)] = tile.astype(BF)
    wi[z, y, x, c] = wi_in[role]
    g_o.across()
    on["s_i"] = spread(wi_in, wi)
    tokens = x_ref[...].astype(F32)
    centred = tokens - jnp.mean(tokens, axis=-1, keepdims=True)
    inv = lax.rsqrt(jnp.mean(centred * centred, axis=-1, keepdims=True) + EPSILON)
    unit = centred * inv
    unit1[...] = unit
    inv1[...] = jnp.broadcast_to(inv, (TOK, 128))
    n1[zp, c] = unit.astype(BF)
    seg_buf[zp, c] = jnp.broadcast_to(seg_in[...].astype(F32), (8, TOK))
    cot[zp, c] = cot_in[...]
    for cp in on["s_q"]:
        cp.wait_recv()
    g_q.across()
    g_q.own_first()
    on["n1"] = Share(n1)
    g_d.own_second()
    g_o.first()
    for cp in on["s_i"]:
        cp.wait_recv()
    on["seg"] = [go_copy(seg_buf.at[zp, c], seg_buf.at[zp, c], dev) for dev, _, _ in others]
    g_q.own_second()
    g_q.far_first()
    g_o.second()
    g_i.across()
    on["cot"] = Share(cot)
    g_q.far_second()
    g_i.own_first()
    g_j.own_first()
    g_j.across()
    on["n1"].forward()
    g_q.done()
    g_i.far_first()
    on["n1"].core()
    on["cot"].core()
    for cp in on["seg"]:
        cp.wait_recv()
    g_o.done()
    on["n1"].done()
    lax.fori_loop(1 - zp, 2 - zp, qkv_step, 0)
    lax.fori_loop(2 * (1 - zp), 2 * (1 - zp) + 2, attend, 0)
    lax.fori_loop(1 - zp, 2 - zp, branch, 0)
    red[0].far_terms()
    g_i.own_second()
    lax.fori_loop(zp, zp + 1, qkv_step, 0)
    g_i.far_second()
    red[0].cross()
    g_d.across()
    lax.fori_loop(2 * zp, 2 * zp + 2, attend, 0)
    on["cot"].forward()
    g_j.far_first()
    g_j.own_second()
    lax.fori_loop(zp, zp + 1, branch, 0)
    red[0].near_terms()
    on["cot"].done()
    g_d.far_first()
    g_j.far_second()
    mid = x_ref[...].astype(F32) + red[0].total()
    middle[...] = mid
    centred = mid - jnp.mean(mid, axis=-1, keepdims=True)
    inv = lax.rsqrt(jnp.mean(centred * centred, axis=-1, keepdims=True) + EPSILON)
    unit = centred * inv
    unit2[...] = unit
    inv2[...] = jnp.broadcast_to(inv, (TOK, 128))
    n2[zp, c] = unit.astype(BF)
    on["n2"] = Share(n2)
    g_i.done()
    on["n2"].forward()
    g_d.far_second()
    g_j.done()
    on["n2"].core()
    on["n2"].done()
    on["mark"] = len(sent)
    upper_for(zp)
    upper_for(1 - zp)
    lax.fori_loop(0, 2, down_grad, 0)
    r_d.first(1)
    g_d.done()
    hidden_grad_for(1 - zp)
    hidden_grad_for(zp)
    in_grad_for(HID, 2 * (1 - zh))
    r_j.first(1)
    normed_two_grad_for(1 - zp)
    red[1].far_terms()
    red[1].cross()
    r_d.second(1)
    in_grad_for(0, 2 * (1 - zh))
    r_i.first(1)
    normed_two_grad_for(zp)
    red[1].near_terms()
    lax.fori_loop(zp, zp + 1, down, 0)
    red[2].near_terms()
    r_j.second(1)
    lax.fori_loop(1 - zp, 2 - zp, down, 0)
    red[2].far_terms()
    settle(on["mark"])
    e = red[1].total()
    n = unit2[...]
    d_middle = cot_in[...].astype(F32) + inv2[:, 0:1] * (
        e
        - jnp.mean(e, axis=-1, keepdims=True)
        - n * jnp.mean(e * n, axis=-1, keepdims=True)
    )
    dmid[...] = d_middle
    db[zp, c] = d_middle.astype(BF)
    on["db"] = Share(db)
    r_d.first(0)
    red[2].cross()
    in_grad_for(0, 2 * zh)
    r_d.third(1)
    r_i.first(0)
    r_i.second(1)
    on["db"].core()
    in_grad_for(HID, 2 * zh)
    r_j.third(1)
    r_j.first(0)
    on["db"].forward()
    on["db"].done()
    lax.fori_loop(1 - zp, 2 - zp, attended_grad, 0)
    lax.fori_loop(2 * (1 - zp), 2 * (1 - zp) + 2, attend_back, 0)
    lax.fori_loop(zp, zp + 1, attended_grad, 0)
    lax.fori_loop(2 * zp, 2 * zp + 2, attend_back, 0)
    first_grads_for(1 - zp)
    red[3].far_terms()
    lax.fori_loop(2 * (1 - zh), 2 * (1 - zh) + 2, qkv_grad, 0)
    r_q.first(1)
    r_i.second(0)
    out_vm[...] = (middle[...] + red[2].total()).astype(BF)
    emit(0, out_vm, out_ref)
    r_i.third(1)
    lhs = att
    for j in range(2):
        for half in range(2):
            rhs = db[:, :, :, pl.ds(half * 512, 512)].reshape(512, 512)
            go[j, :, :, :, pl.ds(half * 512, 512)] = (
                matmul_tn(lhs[:, j].reshape(512, 128), rhs).astype(BF).reshape(2, 2, 32, 512)
            )
    red[3].cross()
    lax.fori_loop(2 * zh, 2 * zh + 2, qkv_grad, 0)
    r_q.second(1)
    r_j.second(0)
    r_i.third(0)
    first_grads_for(zp)
    red[3].near_terms()
    r_o.first()
    r_q.third(1)
    r_j.third(0)
    r_q.first(0)
    r_j.fourth(gi_vm)
    r_o.second()
    r_i.fourth(gi_vm)
    r_q.second(0)
    r_d.second(0)
    r_o.third()
    e = red[3].total()
    n = unit1[...]
    ig_vm[...] = dmid[...] + inv1[:, 0:1] * (
        e
        - jnp.mean(e, axis=-1, keepdims=True)
        - n * jnp.mean(e * n, axis=-1, keepdims=True)
    )
    emit(1, ig_vm, ig_ref)
    r_q.third(0)
    r_q.fourth(gq_vm)
    r_i.done()
    r_d.third(0)
    r_o.fourth(go_vm)
    r_j.done()
    r_d.fourth(gd_vm)
    emit(2, gd_vm, gd_ref)
    in_rows = 2 * FF // TOK
    lines[...] = wi_flat[...].astype(F32)
    gain = column(gain2_in)
    total = jnp.zeros((32, 128), F32)
    for j in range(in_rows):
        g = moved(out_moves(j), lambda t: gi_vm[t[0], :, pl.ds(t[1] * 128, 128)].astype(F32))
        total = total + g * lines[pl.ds(j, 32, stride=in_rows), :]
        gi_own[pl.ds(j, 32, stride=in_rows), :] = g * gain
    sums[...] = total
    emit(3, gi_own, gi_ref)
    emit(6, sums, sums_ref)
    r_o.done()
    emit(4, go_vm, go_ref)
    r_q.done()
    emit(5, gq_vm, gq_ref)
    g_o.end()
    assert n_sems[0] == N_COPIES
    settle(len(sent))
    for cp in local:
        cp.wait()


def block_device(inputs, segments, cotangent, ln1_gain, w_qkv, w_attn_out, ln2_gain, w_in, w_mlp_out):
    places = np.arange(2 * TOK, dtype=np.float32)
    freqs = (1.0 / ROPE_BASE ** (np.arange(0, HD, 2, dtype=np.float64) / HD)).astype(np.float32)
    angles = np.tile(places[:, None] * freqs[None, :], (1, 4))
    signs = np.where(np.arange(2 * HD) % HD < HD // 2, -1.0, 1.0).astype(np.float32)
    cosines = jnp.asarray(np.cos(angles))
    sines = jnp.asarray(np.sin(angles) * signs)
    gain_one, gain_two = ln1_gain[None], ln2_gain[None]
    wq_flat, wo_flat = w_qkv.reshape(-1, TOK), w_attn_out.reshape(-1, TOK)
    wi_flat, wd_flat = w_in.reshape(-1, TOK), w_mlp_out.reshape(-1, TOK)

    vm = pltpu.VMEM
    group = (2, 2, TOK, WIDTH)
    rows = (4, 2, 2, 2, 32)
    outs = pl.pallas_call(
        layer_kernel,
        out_shape=(
            jax.ShapeDtypeStruct((TOK, WIDTH), BF),
            jax.ShapeDtypeStruct((TOK, WIDTH), F32),
            jax.ShapeDtypeStruct((4, 32, QKV), BF),
            jax.ShapeDtypeStruct((32, WIDTH), BF),
            jax.ShapeDtypeStruct(wi_flat.shape, F32),
            jax.ShapeDtypeStruct((PAD, WIDTH), F32),
            jax.ShapeDtypeStruct((32, TOK), F32),
        ),
        in_specs=[pl.BlockSpec(memory_space=vm)] * 11,
        out_specs=(pl.BlockSpec(memory_space=pl.ANY),) * 7,
        scratch_shapes=[
            vm((2, 2, 8, TOK), F32),
            vm(group, BF),
            vm(group, BF),
            vm(group, BF),
            vm(group, BF),
            vm(rows + (QKV,), BF),
            vm((2, 2, 2, 32, WIDTH), BF),
            vm(rows + (2 * HID,), BF),
            vm((2, 2, 2, PAD, WIDTH), BF),
            vm((TOK, WIDTH), F32),
            vm((TOK, 128), F32),
            vm((TOK, WIDTH), F32),
            vm((TOK, 128), F32),
            vm((TOK, WIDTH), F32),
            vm((TOK, WIDTH), F32),
            vm((2, 2, 256, 128), BF),
            vm((2, 2, 256, 128), BF),
            vm((2, 2, 256, 128), BF),
            vm((4, 2, 256, 256), F32),
            vm((2, 2, 256, 128), BF),
            vm((2, 2, 256, 128), BF),
            vm((2, 256, HID), F32),
            vm((2, 256, HID), F32),
            vm((2, 256, HID), BF),
            vm((2, 256, 2 * HID), BF),
            vm((3, 2, 2, 256, 128), BF),
            vm((4,) + group, BF),
            vm((4, 2, TOK, WIDTH), BF),
            vm((4, TOK, WIDTH), BF),
            vm((4, TOK, WIDTH), BF),
            vm(rows + (QKV,), BF),
            vm((2, 2, 2, 32, WIDTH), BF),
            vm(rows + (2 * HID,), BF),
            vm((2, 2, 2, PAD, WIDTH), BF),
            vm((2, 2, 2, 2, 2, 32, QKV // 2), BF),
            vm((2, 2, 2, 2, 32, QKV // 2), BF),
            vm((2, 2, 32, QKV), BF),
            vm((2, 2, 2, 32, WIDTH // 2), BF),
            vm((2, 2, 32, WIDTH // 2), BF),
            vm((2, 32, WIDTH), BF),
            vm((2, 2, 2, 2, 2, 2, 32, HID // 2), BF),
            vm((2, 2, 2, 2, 2, 32, HID // 2), BF),
            vm((2, 2, 2, 32, HID), BF),
            vm((2, 2, 1, 2, PAD, WIDTH // 2), BF),
            vm((2, 2, 1, PAD, WIDTH // 2), BF),
            vm((1, PAD, WIDTH), BF),
            vm((4, 32, QKV), BF),
            vm((32, WIDTH), BF),
            vm((4, 32, 2 * HID), BF),
            vm((64 * FF // TOK, TOK), F32),
            vm((64 * FF // TOK, TOK), F32),
            vm((TOK, WIDTH), BF),
            vm((TOK, WIDTH), F32),
            vm((4, 32, QKV), BF),
            vm((32, WIDTH), BF),
            vm((4, 32, 2 * HID), BF),
            vm((PAD, WIDTH), F32),
            vm(wi_flat.shape, F32),
            vm((32, TOK), F32),
            pltpu.SemaphoreType.DMA((N_SENDS,)),
            pltpu.SemaphoreType.DMA((N_COPIES,)),
            pltpu.SemaphoreType.DMA((7,)),
        ],
        compiler_params=pltpu.CompilerParams(
            collective_id=0, has_side_effects=True, vmem_limit_bytes=60 * 2**20
        ),
    )(
        inputs[0],
        cotangent[0],
        segments,
        cosines,
        sines,
        gain_one,
        gain_two,
        wq_flat,
        wo_flat,
        wi_flat,
        wd_flat,
    )
    output, input_grad, gq, go, gi, gd, sums = outs
    final = pl.pallas_call(
        finish_kernel,
        out_shape=(
            jax.ShapeDtypeStruct((TOK, WIDTH), BF),
            jax.ShapeDtypeStruct((TOK, WIDTH), F32),
            jax.ShapeDtypeStruct((1, 32), F32),
            jax.ShapeDtypeStruct(wq_flat.shape, F32),
            jax.ShapeDtypeStruct(wo_flat.shape, F32),
            jax.ShapeDtypeStruct((1, 32), F32),
            jax.ShapeDtypeStruct(wi_flat.shape, F32),
            jax.ShapeDtypeStruct(wd_flat.shape, F32),
        ),
        in_specs=[pl.BlockSpec(memory_space=pl.ANY)] * 6
        + [pl.BlockSpec(memory_space=vm)] * 2
        + [pl.BlockSpec(memory_space=pl.ANY)],
        out_specs=tuple(
            pl.BlockSpec(memory_space=vm if i in (2, 5) else pl.ANY) for i in range(8)
        ),
        scratch_shapes=[
            vm(wq_flat.shape, F32),
            vm((4, 32, QKV), BF),
            vm((32, WIDTH), BF),
            vm(wi_flat.shape, F32),
            vm((PAD, WIDTH), F32),
            vm(wq_flat.shape, BF),
            vm(wq_flat.shape, F32),
            vm(wo_flat.shape, F32),
            vm(wd_flat.shape, F32),
            vm((TOK, WIDTH), F32),
            vm((TOK, WIDTH), BF),
            pltpu.SemaphoreType.DMA((14,)),
        ],
        compiler_params=pltpu.CompilerParams(vmem_limit_bytes=60 * 2**20),
    )(gq, go, gi, gd, output, input_grad, gain_one, sums, wq_flat)
    return (final[0][None], final[1][None]) + tuple(f.reshape(-1) for f in final[2:])


N_COPIES = 142
N_SENDS = 100
PIECES = 2


def solution(mesh):
    block = dict(mesh.shape) == {"dp": 16, "seq": 2}
    placed = (
        P("dp", "seq", None),
        P("dp", "seq"),
        P("dp", "seq", None),
        P(("dp", "seq")),
        P(("dp", "seq")),
        P(("dp", "seq")),
        P(("dp", "seq")),
        P(("dp", "seq")),
        P(("dp", "seq")),
    )
    return jax.shard_map(
        block_device if block else general_device,
        mesh=mesh,
        in_specs=placed,
        out_specs=(
            P("dp", "seq", None),
            P("dp", "seq", None),
            P(("dp", "seq")),
            P(("dp", "seq")),
            P(("dp", "seq")),
            P(("dp", "seq")),
            P(("dp", "seq")),
            P(("dp", "seq")),
        ),
        check_vma=False,
    )
```

```python
import functools
import math

import jax
import jax.numpy as jnp
import numpy as np
from jax import lax
from jax.experimental import pallas as pl
from jax.experimental.pallas import tpu as pltpu
from jax.sharding import PartitionSpec as P

HEADS = 16
HD = 64
FF = 2624


EPSILON = 1e-05
ROPE_BASE = 160000.0


def rope_tables(places):
    freqs = 1.0 / ROPE_BASE ** (jnp.arange(0, HD, 2, dtype=jnp.float32) / HD)
    angles = places[:, None] * freqs[None, :]
    angles = jnp.concatenate([angles, angles], axis=1)
    return (jnp.cos(angles), jnp.sin(angles))


def rotate(values_in, cosines, sines):
    halfway = values_in.shape[-1] // 2
    turned = jnp.concatenate([-values_in[..., halfway:], values_in[..., :halfway]], axis=-1)
    return values_in * cosines[:, None, :] + turned * sines[:, None, :]


def rotate_back(grads_in, cosines, sines):
    halfway = grads_in.shape[-1] // 2
    scaled = grads_in * sines[:, None, :]
    turned = jnp.concatenate([scaled[..., halfway:], -scaled[..., :halfway]], axis=-1)
    return grads_in * cosines[:, None, :] + turned


def norm_forward(values_in, gain):
    centred = values_in - jnp.mean(values_in, axis=-1, keepdims=True)
    inv_spread = lax.rsqrt(jnp.mean(centred * centred, axis=-1, keepdims=True) + EPSILON)
    unit_rows = centred * inv_spread
    return (unit_rows * gain, unit_rows, inv_spread)


def norm_back(grad_rows, unit_rows, inv_spread, gain):
    gain_grad = jnp.sum(grad_rows * unit_rows, axis=0)
    scaled = grad_rows * gain
    inner_mean = jnp.mean(scaled, axis=-1, keepdims=True)
    cross_mean = jnp.mean(scaled * unit_rows, axis=-1, keepdims=True)
    return (gain_grad, inv_spread * (scaled - inner_mean - unit_rows * cross_mean))


def matmul_tn(left, right):
    return lax.dot_general(
        left, right, (((0,), (0,)), ((), ())), preferred_element_type=jnp.float32
    )


def matmul_nt(left, right):
    return lax.dot_general(
        left, right, (((1,), (1,)), ((), ())), preferred_element_type=jnp.float32
    )


def masked_scores(query, key_block, seg_query, seg_block):
    scores = (
        jnp.einsum("qhd,khd->hqk", query, key_block, preferred_element_type=jnp.float32) * 0.125
    )
    same_doc = seg_query[:, None] == seg_block[None, :]
    return jnp.where(same_doc[None], scores, -1e30)


def gated(inner, gate):
    return jax.nn.gelu(inner, approximate=False) * gate


def general_device(inputs, segments, cotangent, ln1_gain, w_qkv, w_attn_out, ln2_gain, w_in, w_mlp_out):
    tok_rows = inputs.shape[1]
    model_width = inputs.shape[2]
    seq_devices = lax.axis_size("seq")
    dp_devices = lax.axis_size("dp")
    tokens_in = inputs[0].astype(jnp.float32)
    seg_send = segments.astype(jnp.bfloat16)
    seg_query = seg_send[0]
    gathered_attn = (
        lax.all_gather(ln1_gain, ("dp", "seq"), axis=0, tiled=True),
        lax.all_gather(w_qkv, ("dp", "seq"), axis=0, tiled=True),
        lax.all_gather(w_attn_out, ("dp", "seq"), axis=0, tiled=True),
    )
    gain_one = gathered_attn[0].astype(jnp.float32)
    qkv_mat = gathered_attn[1].reshape(model_width, 3 * model_width)
    proj_mat = gathered_attn[2].reshape(model_width, model_width)
    places = (lax.axis_index("seq") * tok_rows + jnp.arange(tok_rows, dtype=jnp.int32)).astype(
        jnp.float32
    )
    cosines, sines = rope_tables(places)
    normed_one, unit_one, spread_one = norm_forward(tokens_in, gain_one)
    normed_one_low = normed_one.astype(jnp.bfloat16)
    qkv_rows = jnp.dot(normed_one_low, qkv_mat, preferred_element_type=jnp.float32)
    query = rotate(qkv_rows[:, :model_width].reshape(tok_rows, HEADS, HD), cosines, sines).astype(
        jnp.bfloat16
    )
    key_rot = rotate(
        qkv_rows[:, model_width : 2 * model_width].reshape(tok_rows, HEADS, HD), cosines, sines
    ).astype(jnp.bfloat16)
    value_rows = qkv_rows[:, 2 * model_width :].astype(jnp.bfloat16)
    key_send = key_rot.reshape(1, tok_rows, model_width)
    value_send = value_rows.reshape(1, tok_rows, model_width)
    fwd_init = (
        jnp.full((HEADS, tok_rows), -1e30, jnp.float32),
        jnp.zeros((HEADS, tok_rows), jnp.float32),
        jnp.zeros((tok_rows, HEADS, HD), jnp.float32),
    )
    key_piece = lax.all_gather(key_send, "seq", axis=1, tiled=True)
    value_piece = lax.all_gather(value_send, "seq", axis=1, tiled=True)
    seg_piece = lax.all_gather(seg_send, "seq", axis=1, tiled=True)
    span = key_piece.shape[1]
    step_rows = math.gcd(span, 512)

    def one_block(block_id, inner_state):
        top_score, total, accum = inner_state
        begin = block_id * step_rows
        key_block = lax.dynamic_slice_in_dim(key_piece[0], begin, step_rows, 0).reshape(
            step_rows, HEADS, HD
        )
        value_block = lax.dynamic_slice_in_dim(value_piece[0], begin, step_rows, 0).reshape(
            step_rows, HEADS, HD
        )
        seg_block = lax.dynamic_slice_in_dim(seg_piece[0], begin, step_rows, 0)
        scores = masked_scores(query, key_block, seg_query, seg_block)
        new_top = jnp.maximum(top_score, jnp.max(scores, axis=-1))
        fading = jnp.exp(top_score - new_top)
        weights = jnp.exp(scores - new_top[..., None])
        total = total * fading + jnp.sum(weights, axis=-1)
        accum = accum * fading.T[:, :, None] + jnp.einsum(
            "hqk,khd->qhd",
            weights.astype(jnp.bfloat16),
            value_block,
            preferred_element_type=jnp.float32,
        )
        return (new_top, total, accum)

    fwd_state = lax.fori_loop(0, span // step_rows, one_block, fwd_init)
    run_top, run_total, run_accum = fwd_state
    log_total = run_top + jnp.log(run_total)
    attended = (run_accum / run_total.T[:, :, None]).astype(jnp.bfloat16)
    attended_rows = attended.reshape(tok_rows, model_width)
    middle = tokens_in + jnp.dot(attended_rows, proj_mat, preferred_element_type=jnp.float32)
    gathered_mlp = (
        lax.all_gather(ln2_gain, ("dp", "seq"), axis=0, tiled=True),
        lax.all_gather(w_in, ("dp", "seq"), axis=0, tiled=True),
        lax.all_gather(w_mlp_out, ("dp", "seq"), axis=0, tiled=True),
    )
    gain_two = gathered_mlp[0].astype(jnp.float32)
    in_mat = gathered_mlp[1].reshape(model_width, 2 * FF)
    down_mat = gathered_mlp[2].reshape(FF, model_width)
    normed_two, unit_two, spread_two = norm_forward(middle, gain_two)
    normed_two_low = normed_two.astype(jnp.bfloat16)
    upper = jnp.dot(normed_two_low, in_mat, preferred_element_type=jnp.float32)
    inner = upper[:, :FF]
    gate = upper[:, FF:]
    hidden_low = gated(inner, gate).astype(jnp.bfloat16)
    output = (middle + jnp.dot(hidden_low, down_mat, preferred_element_type=jnp.float32)).astype(
        jnp.bfloat16
    )
    gathered_mlp = (
        lax.all_gather(ln2_gain, ("dp", "seq"), axis=0, tiled=True),
        lax.all_gather(w_in, ("dp", "seq"), axis=0, tiled=True),
        lax.all_gather(w_mlp_out, ("dp", "seq"), axis=0, tiled=True),
    )
    gain_two = gathered_mlp[0].astype(jnp.float32)
    in_mat = gathered_mlp[1].reshape(model_width, 2 * FF)
    down_mat = gathered_mlp[2].reshape(FF, model_width)
    grad_low = cotangent[0]
    grad_rows = grad_low.astype(jnp.float32)
    d_hidden = matmul_nt(grad_low, down_mat)
    grad_down = matmul_tn(hidden_low, grad_low)
    gated_value, pull = jax.vjp(gated, inner, gate)
    d_inner, d_gate = pull(d_hidden)
    d_upper_low = jnp.concatenate([d_inner, d_gate], axis=1).astype(jnp.bfloat16)
    grad_in = matmul_tn(normed_two_low, d_upper_low)
    d_normed_two = matmul_nt(d_upper_low, in_mat)
    grad_gain_two, d_middle_part = norm_back(d_normed_two, unit_two, spread_two, gain_two)
    d_middle = grad_rows + d_middle_part
    mlp_parts = tuple(
        (g.reshape(dp_devices, seq_devices, -1) for g in (grad_gain_two, grad_in, grad_down))
    )
    mlp_mid = (
        lax.psum_scatter(
            mlp_parts[0].astype(jnp.bfloat16), "seq", scatter_dimension=1, tiled=True
        ).astype(jnp.float32),
        lax.psum_scatter(
            mlp_parts[1].astype(jnp.bfloat16), "seq", scatter_dimension=1, tiled=True
        ).astype(jnp.float32),
        lax.psum_scatter(
            mlp_parts[2].astype(jnp.bfloat16), "seq", scatter_dimension=1, tiled=True
        ).astype(jnp.float32),
    )
    mlp_shards = (
        lax.psum_scatter(
            mlp_mid[0].astype(jnp.bfloat16), "dp", scatter_dimension=0, tiled=True
        ).astype(jnp.float32),
        lax.psum_scatter(
            mlp_mid[1].astype(jnp.bfloat16), "dp", scatter_dimension=0, tiled=True
        ).astype(jnp.float32),
        lax.psum_scatter(
            mlp_mid[2].astype(jnp.bfloat16), "dp", scatter_dimension=0, tiled=True
        ).astype(jnp.float32),
    )
    gathered_attn = (
        lax.all_gather(ln1_gain, ("dp", "seq"), axis=0, tiled=True),
        lax.all_gather(w_qkv, ("dp", "seq"), axis=0, tiled=True),
        lax.all_gather(w_attn_out, ("dp", "seq"), axis=0, tiled=True),
    )
    gain_one = gathered_attn[0].astype(jnp.float32)
    qkv_mat = gathered_attn[1].reshape(model_width, 3 * model_width)
    proj_mat = gathered_attn[2].reshape(model_width, model_width)
    d_branch_low = d_middle.astype(jnp.bfloat16)
    grad_proj = matmul_tn(attended_rows, d_branch_low)
    d_attended = matmul_nt(d_branch_low, proj_mat).astype(jnp.bfloat16).reshape(tok_rows, HEADS, HD)
    delta_rows = jnp.einsum(
        "qhd,qhd->hq", d_attended.astype(jnp.float32), attended.astype(jnp.float32)
    )
    back_init = (
        jnp.zeros((tok_rows, HEADS, HD), jnp.float32),
        jnp.zeros((tok_rows * seq_devices, 2 * model_width), jnp.float32),
    )
    attend_key_piece = lax.all_gather(key_send, "seq", axis=1, tiled=True)
    attend_value_piece = lax.all_gather(value_send, "seq", axis=1, tiled=True)
    attend_seg_piece = lax.all_gather(seg_send, "seq", axis=1, tiled=True)
    span = attend_key_piece.shape[1]
    attend_step_rows = math.gcd(span, 512)

    def one_block(block_id, inner_state):
        grad_query, grad_kv = inner_state
        begin = block_id * attend_step_rows
        key_block = lax.dynamic_slice_in_dim(
            attend_key_piece[0], begin, attend_step_rows, 0
        ).reshape(attend_step_rows, HEADS, HD)
        value_block = lax.dynamic_slice_in_dim(
            attend_value_piece[0], begin, attend_step_rows, 0
        ).reshape(attend_step_rows, HEADS, HD)
        seg_block = lax.dynamic_slice_in_dim(attend_seg_piece[0], begin, attend_step_rows, 0)
        scores = masked_scores(query, key_block, seg_query, seg_block)
        probs = jnp.exp(scores - log_total[..., None])
        probs_low = probs.astype(jnp.bfloat16)
        value_grad = jnp.einsum(
            "hqk,qhd->khd", probs_low, d_attended, preferred_element_type=jnp.float32
        )
        d_probs = jnp.einsum(
            "qhd,khd->hqk", d_attended, value_block, preferred_element_type=jnp.float32
        )
        d_scores = (probs * (d_probs - delta_rows[..., None])).astype(jnp.bfloat16)
        grad_query = (
            grad_query
            + jnp.einsum("hqk,khd->qhd", d_scores, key_block, preferred_element_type=jnp.float32)
            * 0.125
        )
        key_grad = (
            jnp.einsum("hqk,qhd->khd", d_scores, query, preferred_element_type=jnp.float32) * 0.125
        )
        block_grads = jnp.concatenate(
            [
                key_grad.reshape(attend_step_rows, model_width),
                value_grad.reshape(attend_step_rows, model_width),
            ],
            axis=1,
        )
        grad_kv = lax.dynamic_update_slice_in_dim(grad_kv, block_grads, begin, 0)
        return (grad_query, grad_kv)

    back_state = lax.fori_loop(0, span // attend_step_rows, one_block, back_init)
    kv_grads = lax.psum_scatter(
        back_state[1].astype(jnp.bfloat16), "seq", scatter_dimension=0, tiled=True
    ).astype(jnp.float32)
    d_query = rotate_back(back_state[0], cosines, sines).reshape(tok_rows, model_width)
    d_key = rotate_back(
        kv_grads[:, :model_width].reshape(tok_rows, HEADS, HD), cosines, sines
    ).reshape(tok_rows, model_width)
    d_qkv_low = jnp.concatenate([d_query, d_key, kv_grads[:, model_width:]], axis=1).astype(
        jnp.bfloat16
    )
    grad_qkv = matmul_tn(normed_one_low, d_qkv_low)
    d_normed_one = matmul_nt(d_qkv_low, qkv_mat)
    grad_gain_one, d_input_part = norm_back(d_normed_one, unit_one, spread_one, gain_one)
    input_grad = d_middle + d_input_part
    attn_parts = tuple(
        (g.reshape(dp_devices, seq_devices, -1) for g in (grad_gain_one, grad_qkv, grad_proj))
    )
    attn_mid = (
        lax.psum_scatter(
            attn_parts[0].astype(jnp.bfloat16), "seq", scatter_dimension=1, tiled=True
        ).astype(jnp.float32),
        lax.psum_scatter(
            attn_parts[1].astype(jnp.bfloat16), "seq", scatter_dimension=1, tiled=True
        ).astype(jnp.float32),
        lax.psum_scatter(
            attn_parts[2].astype(jnp.bfloat16), "seq", scatter_dimension=1, tiled=True
        ).astype(jnp.float32),
    )
    attn_shards = (
        lax.psum_scatter(
            attn_mid[0].astype(jnp.bfloat16), "dp", scatter_dimension=0, tiled=True
        ).astype(jnp.float32),
        lax.psum_scatter(
            attn_mid[1].astype(jnp.bfloat16), "dp", scatter_dimension=0, tiled=True
        ).astype(jnp.float32),
        lax.psum_scatter(
            attn_mid[2].astype(jnp.bfloat16), "dp", scatter_dimension=0, tiled=True
        ).astype(jnp.float32),
    )
    return (
        output.reshape(1, tok_rows, model_width),
        input_grad.reshape(1, tok_rows, model_width),
        attn_shards[0].reshape(-1),
        attn_shards[1].reshape(-1),
        attn_shards[2].reshape(-1),
        mlp_shards[0].reshape(-1),
        mlp_shards[1].reshape(-1),
        mlp_shards[2].reshape(-1),
    )


MESH_IDS = pl.DeviceIdType.MESH
TOK = 128
WIDTH = 1024
PART = FF // 32
PAD = 96
HID = 8 * PAD
QKV = 3 * 256
BF = jnp.bfloat16
F32 = jnp.float32


def dot_nn(a, b):
    return lax.dot_general(a, b, (((1,), (0,)), ((), ())), preferred_element_type=F32)


def turned(u, low_half):
    return jnp.where(low_half, pltpu.roll(u, 96, axis=1), pltpu.roll(u, 32, axis=1))


def column(gain_ref):
    square = jnp.broadcast_to(gain_ref[...].astype(F32), (32, 32))
    rows = lax.broadcasted_iota(jnp.int32, (32, 32), 0)
    cols = lax.broadcasted_iota(jnp.int32, (32, 32), 1)
    return jnp.sum(jnp.where(rows == cols, square, 0.0), axis=1, keepdims=True)


def owner(r, k):
    return k // 4 * 16 + (r // 2 + k // 4) % 2 * 8 + k // 2 % 2 * 4 + k % 2 * 2 + r % 2


def runs(places):
    found = []
    for lane, place in enumerate(places):
        if place is None:
            continue
        tile, shift = place[0], (place[1] - lane) % 128
        if found and found[-1][:2] == (tile, shift) and found[-1][3] == lane:
            found[-1] = found[-1][:3] + (lane + 1,)
        else:
            found.append((tile, shift, lane, lane + 1))
    return found


def in_moves(r, u):
    places = []
    for at in range(u * 128, u * 128 + 128):
        gate, rest = divmod(at, HID)
        k, i = divmod(rest, PAD)
        col = gate * FF + PART * owner(r, k) + i
        places.append(divmod(col, 128) if i < PART else None)
    return runs(places)


def out_moves(t):
    spots = {owner(r, k): (r, k) for r in range(4) for k in range(8)}
    places = []
    for col in range(t * 128, t * 128 + 128):
        gate, rest = divmod(col, FF)
        device, i = divmod(rest, PART)
        r, k = spots[device]
        u, lane = divmod(gate * HID + k * PAD + i, 128)
        places.append(((r, u), lane))
    return runs(places)


def moved(moves, load):
    lanes = lax.broadcasted_iota(jnp.int32, (1, 128), 1)
    out = jnp.zeros((32, 128), F32)
    for tile, shift, low, high in moves:
        piece = load(tile)
        if shift:
            piece = pltpu.roll(piece, 128 - shift, axis=1)
        out = jnp.where((lanes >= low) & (lanes < high), piece, out)
    return out


def finish_kernel(
    gq_in,
    go_in,
    gi_in,
    gd_in,
    out_in,
    ig_in,
    gain1_in,
    sums_in,
    wq_flat,
    out_ref,
    ig_ref,
    gain1_ref,
    gq_ref,
    go_ref,
    gain2_ref,
    gi_ref,
    gd_ref,
    lines,
    gq_raw,
    go_raw,
    gi_raw,
    gd_raw,
    wq_raw,
    gq_own,
    go_own,
    gd_own,
    ig_raw,
    out_raw,
    sems,
):
    count = [0]

    def start(src, dst):
        cp = pltpu.make_async_copy(src, dst, sems.at[count[0]])
        count[0] += 1
        cp.start()
        return cp

    gi_here = start(gi_in, gi_raw)
    ig_here = start(ig_in, ig_raw)
    out_here = start(out_in, out_raw)
    gd_here = start(gd_in, gd_raw)
    gq_here = start(gq_in, gq_raw)
    wq_here = start(wq_flat, wq_raw)
    go_here = start(go_in, go_raw)
    written = []
    rows = lax.broadcasted_iota(jnp.int32, (32, 32), 0)
    cols = lax.broadcasted_iota(jnp.int32, (32, 32), 1)

    def line(total):
        total = jnp.sum(total, axis=1, keepdims=True)
        return jnp.sum(jnp.where(rows == cols, total, 0.0), axis=0, keepdims=True)

    qkv_rows = 3 * WIDTH // TOK
    gi_here.wait()
    written.append(start(gi_raw, gi_ref))
    ig_here.wait()
    written.append(start(ig_raw, ig_ref))
    out_here.wait()
    written.append(start(out_raw, out_ref))
    gain2_ref[...] = line(sums_in[...])
    gd_here.wait()
    for j in range(8):
        gd_own[pl.ds(j, PART, stride=8), :] = gd_raw[0:PART, pl.ds(j * 128, 128)]
    written.append(start(gd_own, gd_ref))
    gain = column(gain1_in)
    total = jnp.zeros((32, 128), F32)
    wq_here.wait()
    lines[0 : 32 * qkv_rows] = wq_raw[...].astype(F32)
    gq_here.wait()
    for j in range(qkv_rows):
        part, cut = divmod(j, 8)
        r = (cut // 2 + cut // 4) % 2 * 2 + cut // 4
        g = gq_raw[r, :, pl.ds(part * 256 + cut % 2 * 128, 128)].astype(F32)
        total = total + g * lines[pl.ds(j, 32, stride=qkv_rows), :]
        gq_own[pl.ds(j, 32, stride=qkv_rows), :] = g * gain
    written.append(start(gq_own, gq_ref))
    gain1_ref[...] = line(total)
    go_here.wait()
    for j in range(8):
        go_own[pl.ds(j, 32, stride=8), :] = go_raw[:, pl.ds(j * 128, 128)].astype(F32)
    written.append(start(go_own, go_ref))
    for cp in written:
        cp.wait()


def layer_kernel(
    x_ref,
    cot_in,
    seg_in,
    cos_ref,
    sin_ref,
    gain1_in,
    gain2_in,
    wq_flat,
    wo_flat,
    wi_flat,
    wd_flat,
    out_ref,
    ig_ref,
    gq_ref,
    go_ref,
    gi_ref,
    gd_ref,
    sums_ref,
    seg_buf,
    n1,
    n2,
    cot,
    db,
    wq,
    wo,
    wi,
    wd,
    unit1,
    inv1,
    unit2,
    inv2,
    middle,
    dmid,
    q_buf,
    k_buf,
    v_buf,
    probs,
    att,
    datt,
    up_a,
    up_b,
    hidden,
    d_up,
    dqkv,
    ps,
    ps_in,
    ps_far,
    ps_back,
    gq,
    go,
    gi,
    gd,
    rq1,
    rq2,
    rq3,
    ro1,
    ro2,
    ro3,
    ri1,
    ri2,
    ri3,
    rd1,
    rd2,
    rd3,
    wq_in,
    wo_in,
    wi_in,
    lines,
    wide,
    out_vm,
    ig_vm,
    gq_vm,
    go_vm,
    gi_vm,
    gd_vm,
    gi_own,
    sums,
    send_sems,
    recv_sems,
    local_sems,
):
    dp, c = lax.axis_index("dp"), lax.axis_index("seq")
    x, y, z = lax.rem(dp, 2), lax.rem(dp // 2, 2), dp // 4
    zh, zp = z // 2, lax.rem(z, 2)
    kind = lax.rem(zp + zh, 2)
    role = kind * 2 + c

    def device(X, Y, Z, C):
        return (Z * 4 + Y * 2 + X, C)

    core_dev = device(x, y, z, 1 - c)
    pair_dev = device(x, y, zh * 2 + 1 - zp, c)
    diag_dev = device(x, y, zh * 2 + 1 - zp, 1 - c)
    half_dev = device(x, y, 3 - z, c)
    x_dev = device(1 - x, y, z, c)
    y_dev = device(x, 1 - y, z, c)

    barrier = pltpu.get_barrier_semaphore()
    for dev in (core_dev, pair_dev, diag_dev, half_dev, x_dev, y_dev):
        pl.semaphore_signal(barrier, inc=1, device_id=dev, device_id_type=MESH_IDS)

    sent = []
    n_sems = [0]
    free = list(range(N_SENDS))

    def copy_to(src, dst, dev, keep=True):
        i, k = n_sems[0], free.pop(0)
        n_sems[0] += 1
        cp = pltpu.make_async_remote_copy(
            src_ref=src,
            dst_ref=dst,
            send_sem=send_sems.at[k],
            recv_sem=recv_sems.at[i],
            device_id=dev,
            device_id_type=MESH_IDS,
        )
        if keep:
            sent.append((cp, k))
        return cp

    local = []

    def emit(i, src, dst):
        cp = pltpu.make_async_copy(src, dst, local_sems.at[i])
        cp.start()
        local.append(cp)

    def settle(first):
        for cp, k in sent[:first]:
            cp.wait_send()
            free.append(k)
        del sent[:first]

    def go_copy(src, dst, dev):
        cp = copy_to(src, dst, dev)
        cp.start()
        return cp


    others = (
        (core_dev, kind * 2 + 1 - c, (z, 1 - c)),
        (pair_dev, (1 - kind) * 2 + c, (zh * 2 + 1 - zp, c)),
        (diag_dev, (1 - kind) * 2 + 1 - c, (zh * 2 + 1 - zp, 1 - c)),
    )

    def spread(own, buf):
        cps = [go_copy(own.at[r], buf.at[z, y, x, c], dev) for dev, r, _ in others]
        return cps

    class Gather:
        def __init__(self, buf, cols, base=0):
            self.buf = buf
            self.halves = (pl.ds(base, cols // 2), pl.ds(base + cols // 2, cols // 2))
            self.per_half = buf.shape[0] // 2

        def of(self, which):
            return pl.ds(self.per_half * which, self.per_half)

        def spot(self, which, cut):
            return self.buf.at[(self.of(which), y, x) + (slice(None),) * (len(self.buf.shape) - 4) + (cut,)]

        def line(self, which, cut, i):
            rest = (slice(None),) * (len(self.buf.shape) - 4) + (cut,)
            at = (y, slice(None)) if i == 0 else (slice(None), x)
            return self.buf.at[(self.of(which),) + at + rest]

        def same(self, ref, dev):
            return go_copy(ref, ref, dev)

        def across(self):
            self.over = [self.same(self.spot(zh, cut), half_dev) for cut in self.halves]

        def own_first(self):
            self.a = [
                self.same(self.spot(zh, cut), dev) for cut, dev in zip(self.halves, (x_dev, y_dev))
            ]

        def own_second(self):
            self.b = []
            for i, dev in enumerate((y_dev, x_dev)):
                self.a[i].wait_recv()
                self.b.append(self.same(self.line(zh, self.halves[i], i), dev))

        def far_first(self):
            self.a2 = []
            for i, dev in enumerate((x_dev, y_dev)):
                self.over[i].wait_recv()
                self.a2.append(self.same(self.spot(1 - zh, self.halves[i]), dev))

        def far_second(self):
            self.b2 = []
            for i, dev in enumerate((y_dev, x_dev)):
                self.a2[i].wait_recv()
                self.b2.append(self.same(self.line(1 - zh, self.halves[i], i), dev))

        def done(self):
            for cp in self.b + self.b2:
                cp.wait_recv()

    class GatherOut:
        def __init__(self, buf, cols):
            self.buf = buf
            self.halves = (pl.ds(0, cols // 2), pl.ds(cols // 2, cols // 2))

        def start(self):
            self.s0 = copy_to(wo_in, self.buf.at[y, x, c], core_dev, keep=False)

            @pl.when(c != zh)
            def _():
                self.s0.start()

        def across(self):
            self.s1 = copy_to(self.buf.at[y, x], self.buf.at[y, x], half_dev, keep=False)

            @pl.when(c == zh)
            def _():
                self.buf[y, x, c] = wo_in[...]
                self.s0.wait_recv()
                self.s1.start()

        def first(self):
            @pl.when(c != zh)
            def _():
                self.s1.wait_recv()

            self.a = []
            for cut, dev in zip(self.halves, (x_dev, y_dev)):
                ref = self.buf.at[y, x, :, :, cut]
                self.a.append(go_copy(ref, ref, dev))

        def second(self):
            self.b = []
            for i, dev in enumerate((y_dev, x_dev)):
                self.a[i].wait_recv()
                cut = self.halves[i]
                ref = self.buf.at[y, :, :, :, cut] if i == 0 else self.buf.at[:, x, :, :, cut]
                self.b.append(go_copy(ref, ref, dev))

        def done(self):
            for cp in self.b:
                cp.wait_recv()

        def end(self):
            @pl.when(c != zh)
            def _():
                self.s0.wait_send()

            @pl.when(c == zh)
            def _():
                self.s1.wait_send()


    pieces = [pl.ds(i * (TOK // PIECES), TOK // PIECES) for i in range(PIECES)]

    class Share:
        def __init__(self, buf):
            self.buf = buf
            self.to_pair = [
                go_copy(buf.at[zp, c, cut], buf.at[zp, c, cut], pair_dev) for cut in pieces
            ]
            self.to_core = go_copy(buf.at[zp, c], buf.at[zp, c], core_dev)

        def forward(self):
            self.fwd = []
            for cp, cut in zip(self.to_pair, pieces):
                cp.wait_recv()
                ref = self.buf.at[1 - zp, c, cut]
                self.fwd.append(go_copy(ref, ref, core_dev))

        def core(self):
            self.to_core.wait_recv()

        def done(self):
            for cp in self.fwd:
                cp.wait_recv()

    class Reduce:
        def __init__(self, i):
            self.i = i

        def far_terms(self):
            i = self.i
            self.mine_far = go_copy(ps.at[i, 1 - zp, 1 - c], ps_in.at[i, 1 - zp], core_dev)

        def near_terms(self):
            i = self.i
            self.mine_near = go_copy(ps.at[i, zp, 1 - c], ps_in.at[i, zp], core_dev)

        def cross(self):
            i = self.i
            self.mine_far.wait_recv()
            self.far = []
            for cut in pieces:
                ps_far[i, cut] = (
                    ps[i, 1 - zp, c, cut].astype(F32) + ps_in[i, 1 - zp, cut].astype(F32)
                ).astype(BF)
                self.far.append(go_copy(ps_far.at[i, cut], ps_back.at[i, cut], pair_dev))

        def total(self):
            i = self.i
            self.mine_near.wait_recv()
            near = ps[i, zp, c].astype(F32) + ps_in[i, zp].astype(F32)
            for cp in self.far:
                cp.wait_recv()
            return near + ps_back[i].astype(F32)


    def add_into(target, extra):
        target[...] = (target[...].astype(F32) + extra[...].astype(F32)).astype(BF)

    def add_all(mine, got):
        n = got.shape[0]
        if n == 1:
            add_into(mine.at[0], got.at[0])
            return

        def body(j, carry):
            add_into(mine.at[j], got.at[j])
            return carry

        lax.fori_loop(0, n, body, 0)

    class Scatter:
        def __init__(self, buf, cols, r1, r2, r3, base=0):
            self.buf, self.r1, self.r2, self.r3 = buf, r1, r2, r3
            self.halves = (pl.ds(base, cols // 2), pl.ds(base + cols // 2, cols // 2))
            self.cols = pl.ds(base, cols)
            self.per_half = buf.shape[0] // 2
            self.rest = (slice(None),) * (len(buf.shape) - 4)
            self.c1, self.c2 = {}, {}

        def of(self, which):
            return pl.ds(self.per_half * which, self.per_half)

        def line(self, i, which, other):
            if i == 0:
                at = (1 - y if other else y, slice(None))
            else:
                at = (slice(None), 1 - x if other else x)
            return self.buf.at[(self.of(which),) + at + self.rest + (self.halves[i],)]

        def spot(self, i, which, other):
            Y, X = (y, x) if not other else ((y, 1 - x) if i == 0 else (1 - y, x))
            return self.buf.at[(self.of(which), Y, X) + self.rest + (self.halves[i],)]

        def first(self, far):
            which = 1 - zh if far else zh
            self.c1[far] = [
                go_copy(self.line(i, which, True), self.r1.at[i, far], dev)
                for i, dev in enumerate((y_dev, x_dev))
            ]

        def second(self, far):
            which = 1 - zh if far else zh
            self.c2[far] = []
            for i, dev in enumerate((x_dev, y_dev)):
                self.c1[far][i].wait_recv()
                add_all(self.line(i, which, False), self.r1.at[i, far])
                self.c2[far].append(go_copy(self.spot(i, which, True), self.r2.at[i, far], dev))

        def third(self, far):
            which = 1 - zh if far else zh
            for i in range(2):
                self.c2[far][i].wait_recv()
                add_all(self.spot(i, which, False), self.r2.at[i, far])
            if far:
                src = self.buf.at[(self.of(which), y, x) + self.rest + (self.cols,)]
                self.c3 = go_copy(src, self.r3, half_dev)

    class ScatterRows(Scatter):
        def fourth(self, out):
            self.c3.wait_recv()
            cols = self.cols
            add_all(self.buf.at[self.of(zh), y, x, :, :, cols], self.r3)
            self.c4 = []
            for dev, _, (there, core) in others:
                src = self.buf.at[there, y, x, core, :, cols]
                self.c4.append(go_copy(src, out.at[role, :, cols], dev))
            out[role, :, cols] = self.buf[z, y, x, c, :, cols]

        def done(self):
            for cp in self.c4:
                cp.wait_recv()

    class ScatterDown(Scatter):
        def fourth(self, out):
            self.c3.wait_recv()
            out[...] = self.buf[zh, y, x].astype(F32) + self.r3[0].astype(F32)

    class ScatterOut:
        def __init__(self, buf, cols, r1, r2, r3):
            self.buf, self.r1, self.r2, self.r3 = buf, r1, r2, r3
            self.halves = (pl.ds(0, cols // 2), pl.ds(cols // 2, cols // 2))

        def line(self, i, other):
            cut = self.halves[i]
            if i == 0:
                return self.buf.at[1 - y if other else y, :, :, :, cut]
            return self.buf.at[:, 1 - x if other else x, :, :, cut]

        def spot(self, i, other):
            Y, X = (y, x) if not other else ((y, 1 - x) if i == 0 else (1 - y, x))
            return self.buf.at[Y, X, :, :, self.halves[i]]

        def first(self):
            self.c1 = [
                go_copy(self.line(i, True), self.r1.at[i], dev)
                for i, dev in enumerate((y_dev, x_dev))
            ]

        def second(self):
            self.c2 = []
            for i, dev in enumerate((x_dev, y_dev)):
                self.c1[i].wait_recv()
                add_all(self.line(i, False), self.r1.at[i])
                self.c2.append(go_copy(self.spot(i, True), self.r2.at[i], dev))

        def third(self):
            for i in range(2):
                self.c2[i].wait_recv()
                add_all(self.spot(i, False), self.r2.at[i])
            self.c3 = copy_to(self.buf.at[y, x], self.r3, half_dev, keep=False)

            @pl.when(c != zh)
            def _():
                self.c3.start()

        def fourth(self, out):
            self.c4 = copy_to(self.r3.at[1 - c], out, core_dev, keep=False)

            @pl.when(c == zh)
            def _():
                self.c3.wait_recv()
                add_all(self.r3, self.buf.at[y, x])
                self.c4.start()
                out[...] = self.r3[c]

        def done(self):
            @pl.when(c != zh)
            def _():
                self.c4.wait_recv()
                self.c3.wait_send()

            @pl.when(c == zh)
            def _():
                self.c4.wait_send()

    qkv_rows = 3 * WIDTH // TOK
    lines[0 : 32 * qkv_rows] = wq_flat[...].astype(F32)
    gain = column(gain1_in)
    for j in range(qkv_rows):
        part, cut = divmod(j, 8)
        r = (cut // 2 + cut // 4) % 2 * 2 + cut // 4
        w = lines[pl.ds(j, 32, stride=qkv_rows), :] * gain
        wq_in[r, :, pl.ds(part * 256 + cut % 2 * 128, 128)] = w.astype(BF)
    wq[z, y, x, c] = wq_in[role]
    g_q, g_d = Gather(wq, QKV), Gather(wd, WIDTH)
    g_i, g_j = Gather(wi, HID), Gather(wi, HID, HID)
    g_o = GatherOut(wo, WIDTH)


    r_d = ScatterDown(gd, WIDTH, rd1, rd2, rd3)
    r_i = ScatterRows(gi, HID, ri1.at[0], ri2.at[0], ri3.at[0])
    r_j = ScatterRows(gi, HID, ri1.at[1], ri2.at[1], ri3.at[1], HID)
    r_q = ScatterRows(gq, QKV, rq1, rq2, rq3)
    r_o = ScatterOut(go, WIDTH, ro1, ro2, ro3)
    on = {}
    red = [Reduce(i) for i in range(4)]
    lanes = lax.broadcasted_iota(jnp.int32, (1, 128), 1)
    low_half = lax.rem(lanes, 64) < 32
    first_head = lanes < 64

    def qkv_step(s, carry):
        rows = n1[s].reshape(256, WIDTH)
        for part, dst in enumerate((q_buf, k_buf, v_buf)):
            for j in range(2):
                at = part * 256 + j * 128
                w = wq[:, :, :, :, :, pl.ds(at, 128)].reshape(WIDTH, 128)
                u = dot_nn(rows, w)
                if part < 2:
                    u = u * cos_ref[...] + turned(u, low_half) * sin_ref[...]
                dst[s, j] = u.astype(BF)
        return carry

    def only(head, u):
        return jnp.where(first_head if head == 0 else ~first_head, u, jnp.zeros_like(u))

    def attend(i, carry):
        s, j = i // 2, lax.rem(i, 2)
        q, k, v = q_buf[s, j], k_buf[s, j], v_buf[s, j]
        seg_row = jnp.concatenate([seg_buf[s, 0, 0:1], seg_buf[s, 1, 0:1]], axis=1)
        seg_col = jnp.broadcast_to(seg_row, (128, 256)).T[:, 0:1]
        same = seg_col == seg_row
        heads = []
        for h in range(2):
            scores = matmul_nt(only(h, q), k) * 0.125
            scores = jnp.where(same, scores, -1e30)
            weights = jnp.exp(scores - jnp.max(scores, axis=-1, keepdims=True))
            p = weights * (1.0 / jnp.sum(weights, axis=-1, keepdims=True))
            probs[i, h] = p
            heads.append(dot_nn(p.astype(BF), v))
        att[s, j] = jnp.where(first_head, heads[0], heads[1]).astype(BF)
        return carry

    def att_rows(s):
        return jnp.concatenate([att[s, 0], att[s, 1]], axis=1)

    def branch(s, carry):
        w = wo[...].reshape(256, WIDTH)
        ps[0, s] = dot_nn(att_rows(s), w).astype(BF).reshape(2, TOK, WIDTH)
        return carry

    def upper_for(s):
        def upper(j, carry):
            at = pl.multiple_of(j * 256, 256)
            rows = n2[s].reshape(256, WIDTH)
            inner = dot_nn(rows, wi[:, :, :, :, :, pl.ds(at, 256)].reshape(WIDTH, 256))
            gate = dot_nn(
                rows,
                wi[:, :, :, :, :, pl.ds(pl.multiple_of(HID + at, 256), 256)].reshape(WIDTH, 256),
            )
            cdf = 0.5 * (1.0 + lax.erf(inner * math.sqrt(0.5)))
            slope = cdf + inner * jnp.exp(-0.5 * inner * inner) * (1.0 / math.sqrt(2 * math.pi))
            bent = inner * cdf
            up_a[s, :, pl.ds(at, 256)] = gate * slope
            up_b[s, :, pl.ds(at, 256)] = bent
            hidden[s, :, pl.ds(at, 256)] = (bent * gate).astype(BF)
            return carry

        lax.fori_loop(0, HID // 256, upper, 0)

    def down_grad(i, carry):
        lhs = hidden[:, :, pl.ds(pl.multiple_of(i * 384, 384), 384)].reshape(512, 384)
        for j in range(2):
            rhs = cot[:, :, :, pl.ds(j * 512, 512)].reshape(512, 512)
            gd[i, :, :, :, pl.ds(j * 512, 512)] = (
                matmul_tn(lhs, rhs).astype(BF).reshape(2, 2, PAD, 512)
            )
        return carry

    def hidden_grad_for(s):
        def hidden_grad(i, carry):
            w = wd[i].reshape(384, WIDTH)
            at = pl.multiple_of(i * 384, 384)
            dh = matmul_nt(cot[s].reshape(256, WIDTH), w)
            d_up[s, :, pl.ds(at, 384)] = (dh * up_a[s, :, pl.ds(at, 384)]).astype(BF)
            d_up[s, :, pl.ds(pl.multiple_of(HID + at, 384), 384)] = (
                dh * up_b[s, :, pl.ds(at, 384)]
            ).astype(BF)
            return carry

        lax.fori_loop(0, 2, hidden_grad, 0)

    def normed_two_grad_for(s):
        def normed_two_grad(i, carry):
            w = wi[i].reshape(256, 2 * HID)
            at = pl.multiple_of(i * 256, 256)
            ps[1, s, :, :, pl.ds(at, 256)] = matmul_nt(d_up[s], w).astype(BF).reshape(2, TOK, 256)
            return carry

        lax.fori_loop(0, 4, normed_two_grad, 0)

    def in_grad_for(base, first):
        def in_grad(i, carry):
            lhs = n2[:, :, :, pl.ds(pl.multiple_of(i * 256, 256), 256)].reshape(512, 256)
            for j in range(HID // 256):
                at = base + j * 256
                rhs = d_up[:, :, pl.ds(at, 256)].reshape(512, 256)
                gi[i, :, :, :, :, pl.ds(at, 256)] = (
                    matmul_tn(lhs, rhs).astype(BF).reshape(2, 2, 2, 32, 256)
                )
            return carry

        lax.fori_loop(first, first + 2, in_grad, 0)

    def down(i, carry):
        w = wd[...].reshape(HID, WIDTH)
        ps[2, i] = dot_nn(hidden[i], w).astype(BF).reshape(2, TOK, WIDTH)
        return carry

    def attended_grad(s, carry):
        rows = db[s].reshape(256, WIDTH)
        da = matmul_nt(rows, wo[...].reshape(256, WIDTH)).astype(BF)
        datt[s, 0] = da[:, 0:128]
        datt[s, 1] = da[:, 128:256]
        return carry

    def attend_back(i, carry):
        s, j = i // 2, lax.rem(i, 2)
        q, k, v, da = q_buf[s, j], k_buf[s, j], v_buf[s, j], datt[s, j]
        dq, dk, dv = [], [], []
        for h in range(2):
            p = probs[i, h]
            dprob = matmul_nt(only(h, da), v)
            delta = jnp.sum(p * dprob, axis=-1, keepdims=True)
            ds = (p * (dprob - delta)).astype(BF)
            dq.append(dot_nn(ds, k))
            dk.append(matmul_tn(ds, q))
            dv.append(matmul_tn(p.astype(BF), da))
        for part, pieces in enumerate((dq, dk, dv)):
            u = jnp.where(first_head, pieces[0], pieces[1])
            if part < 2:
                u = u * 0.125
                u = u * cos_ref[...] - turned(u, low_half) * sin_ref[...]
            dqkv[part, j, s] = u.astype(BF)
        return carry

    def first_grads_for(s):
        rows = jnp.concatenate([dqkv[p, j, s] for p in range(3) for j in range(2)], axis=1)

        def first_grads(i, carry):
            w = wq[i].reshape(256, QKV)
            at = pl.multiple_of(i * 256, 256)
            ps[3, s, :, :, pl.ds(at, 256)] = matmul_nt(rows, w).astype(BF).reshape(2, TOK, 256)
            return carry

        lax.fori_loop(0, 4, first_grads, 0)

    def qkv_grad(i, carry):
        lhs = n1[:, :, :, pl.ds(pl.multiple_of(i * 256, 256), 256)].reshape(512, 256)
        for p in range(3):
            for j in range(2):
                rhs = dqkv[p, j].reshape(512, 128)
                gq[i, :, :, :, :, pl.ds(p * 256 + j * 128, 128)] = (
                    matmul_tn(lhs, rhs).astype(BF).reshape(2, 2, 2, 32, 128)
                )
        return carry

    pl.semaphore_wait(barrier, 6)
    on["s_q"] = spread(wq_in, wq)
    wide[0:256] = wo_flat[...].astype(F32)
    for j in range(8):
        wo_in[:, pl.ds(j * 128, 128)] = wide[pl.ds(j, 32, stride=8), :].astype(BF)
    g_o.start()
    wide[0 : 8 * PART] = wd_flat[...].astype(F32)
    wide[8 * PART : 8 * PAD] = jnp.zeros((8 * (PAD - PART), TOK), F32)
    for j in range(8):
        wd[zh, y, x, :, pl.ds(j * 128, 128)] = wide[pl.ds(j, PAD, stride=8), :].astype(BF)
    g_d.own_first()
    in_rows = 2 * FF // TOK
    lines[...] = wi_flat[...].astype(F32)
    gain = column(gain2_in)
    for j in range(in_rows):
        wide[pl.ds(j * 32, 32), :] = lines[pl.ds(j, 32, stride=in_rows), :] * gain
    for r in range(4):
        for u in range(2 * HID // TOK):
            tile = moved(in_moves(r, u), lambda t: wide[pl.ds(t * 32, 32), :])
            wi_in[r, :, pl.ds(u * 128, 128)] = tile.astype(BF)
    wi[z, y, x, c] = wi_in[role]
    tokens = x_ref[...].astype(F32)
    centred = tokens - jnp.mean(tokens, axis=-1, keepdims=True)
    inv = lax.rsqrt(jnp.mean(centred * centred, axis=-1, keepdims=True) + EPSILON)
    unit = centred * inv
    unit1[...] = unit
    inv1[...] = jnp.broadcast_to(inv, (TOK, 128))
    n1[zp, c] = unit.astype(BF)
    seg_buf[zp, c] = jnp.broadcast_to(seg_in[...].astype(F32), (8, TOK))
    cot[zp, c] = cot_in[...]
    for cp in on["s_q"]:
        cp.wait_recv()
    g_q.own_first()
    g_o.across()
    on["s_i"] = spread(wi_in, wi)
    g_o.first()
    g_q.across()
    on["n1"] = Share(n1)
    g_d.own_second()
    g_q.own_second()
    on["seg"] = [go_copy(seg_buf.at[zp, c], seg_buf.at[zp, c], dev) for dev, _, _ in others]
    g_q.far_first()
    g_o.second()
    for cp in on["s_i"]:
        cp.wait_recv()
    g_i.across()
    g_q.far_second()
    g_i.own_first()
    on["cot"] = Share(cot)
    g_j.across()
    on["n1"].forward()
    on["n1"].core()
    g_j.own_first()
    g_q.done()
    on["n1"].done()
    g_i.far_first()
    for cp in on["seg"]:
        cp.wait_recv()
    lax.fori_loop(1 - zp, 2 - zp, qkv_step, 0)
    lax.fori_loop(2 * (1 - zp), 2 * (1 - zp) + 2, attend, 0)
    g_o.done()
    lax.fori_loop(zp, zp + 1, qkv_step, 0)
    lax.fori_loop(1 - zp, 2 - zp, branch, 0)
    red[0].far_terms()
    g_i.own_second()
    red[0].cross()
    g_j.far_first()
    g_i.far_second()
    g_d.across()
    lax.fori_loop(2 * zp, 2 * zp + 2, attend, 0)
    g_j.own_second()
    lax.fori_loop(zp, zp + 1, branch, 0)
    red[0].near_terms()
    g_d.far_first()
    on["cot"].forward()
    g_i.done()
    mid = x_ref[...].astype(F32) + red[0].total()
    middle[...] = mid
    centred = mid - jnp.mean(mid, axis=-1, keepdims=True)
    inv = lax.rsqrt(jnp.mean(centred * centred, axis=-1, keepdims=True) + EPSILON)
    unit = centred * inv
    unit2[...] = unit
    inv2[...] = jnp.broadcast_to(inv, (TOK, 128))
    n2[zp, c] = unit.astype(BF)
    on["n2"] = Share(n2)
    g_j.far_second()
    g_d.far_second()
    on["n2"].core()
    on["cot"].core()
    on["n2"].forward()
    g_j.done()
    on["cot"].done()
    on["mark"] = len(sent)
    upper_for(zp)
    on["n2"].done()
    upper_for(1 - zp)
    lax.fori_loop(0, 2, down_grad, 0)
    r_d.first(1)
    g_d.done()
    hidden_grad_for(1 - zp)
    hidden_grad_for(zp)
    in_grad_for(HID, 2 * (1 - zh))
    r_j.first(1)
    normed_two_grad_for(1 - zp)
    red[1].far_terms()
    red[1].cross()
    r_d.second(1)
    in_grad_for(0, 2 * (1 - zh))
    r_i.first(1)
    lax.fori_loop(1 - zp, 2 - zp, down, 0)
    red[2].far_terms()
    normed_two_grad_for(zp)
    red[1].near_terms()
    r_j.second(1)
    in_grad_for(HID, 2 * zh)
    settle(on["mark"])
    e = red[1].total()
    n = unit2[...]
    d_middle = cot_in[...].astype(F32) + inv2[:, 0:1] * (
        e
        - jnp.mean(e, axis=-1, keepdims=True)
        - n * jnp.mean(e * n, axis=-1, keepdims=True)
    )
    dmid[...] = d_middle
    db[zp, c] = d_middle.astype(BF)
    on["db"] = Share(db)
    red[2].cross()
    lax.fori_loop(zp, zp + 1, down, 0)
    red[2].near_terms()
    r_d.third(1)
    in_grad_for(0, 2 * zh)
    on["db"].core()
    r_i.first(0)
    r_i.second(1)
    r_j.first(0)
    r_j.third(1)
    lax.fori_loop(zp, zp + 1, attended_grad, 0)
    r_d.first(0)
    lax.fori_loop(2 * zp, 2 * zp + 2, attend_back, 0)
    on["db"].forward()
    on["db"].done()
    lax.fori_loop(1 - zp, 2 - zp, attended_grad, 0)
    lax.fori_loop(2 * (1 - zp), 2 * (1 - zp) + 2, attend_back, 0)
    lax.fori_loop(2 * (1 - zh), 2 * (1 - zh) + 2, qkv_grad, 0)
    first_grads_for(zp)
    red[3].near_terms()
    first_grads_for(1 - zp)
    red[3].far_terms()
    r_j.second(0)
    lhs = att
    for j in range(2):
        for half in range(2):
            rhs = db[:, :, :, pl.ds(half * 512, 512)].reshape(512, 512)
            go[j, :, :, :, pl.ds(half * 512, 512)] = (
                matmul_tn(lhs[:, j].reshape(512, 128), rhs).astype(BF).reshape(2, 2, 32, 512)
            )
    red[3].cross()
    r_i.third(1)
    r_q.first(1)
    r_i.second(0)
    r_j.third(0)
    lax.fori_loop(2 * zh, 2 * zh + 2, qkv_grad, 0)
    r_q.second(1)
    r_o.first()
    r_q.first(0)
    r_q.third(1)
    r_i.third(0)
    r_o.second()
    e = red[3].total()
    n = unit1[...]
    ig_vm[...] = dmid[...] + inv1[:, 0:1] * (
        e
        - jnp.mean(e, axis=-1, keepdims=True)
        - n * jnp.mean(e * n, axis=-1, keepdims=True)
    )
    emit(1, ig_vm, ig_ref)
    r_i.fourth(gi_vm)
    r_j.fourth(gi_vm)
    r_q.second(0)
    out_vm[...] = (middle[...] + red[2].total()).astype(BF)
    emit(0, out_vm, out_ref)
    r_o.third()
    r_i.done()
    r_d.second(0)
    r_q.third(0)
    r_q.fourth(gq_vm)
    r_j.done()
    in_rows = 2 * FF // TOK
    lines[...] = wi_flat[...].astype(F32)
    gain = column(gain2_in)
    total = jnp.zeros((32, 128), F32)
    for j in range(in_rows):
        g = moved(out_moves(j), lambda t: gi_vm[t[0], :, pl.ds(t[1] * 128, 128)].astype(F32))
        total = total + g * lines[pl.ds(j, 32, stride=in_rows), :]
        gi_own[pl.ds(j, 32, stride=in_rows), :] = g * gain
    sums[...] = total
    emit(3, gi_own, gi_ref)
    emit(6, sums, sums_ref)
    r_o.fourth(go_vm)
    r_d.third(0)
    r_d.fourth(gd_vm)
    emit(2, gd_vm, gd_ref)
    r_q.done()
    emit(5, gq_vm, gq_ref)
    r_o.done()
    emit(4, go_vm, go_ref)
    g_o.end()
    assert n_sems[0] == N_COPIES
    settle(len(sent))
    for cp in local:
        cp.wait()


def block_device(inputs, segments, cotangent, ln1_gain, w_qkv, w_attn_out, ln2_gain, w_in, w_mlp_out):
    places = np.arange(2 * TOK, dtype=np.float32)
    freqs = (1.0 / ROPE_BASE ** (np.arange(0, HD, 2, dtype=np.float64) / HD)).astype(np.float32)
    angles = np.tile(places[:, None] * freqs[None, :], (1, 4))
    signs = np.where(np.arange(2 * HD) % HD < HD // 2, -1.0, 1.0).astype(np.float32)
    cosines = jnp.asarray(np.cos(angles))
    sines = jnp.asarray(np.sin(angles) * signs)
    gain_one, gain_two = ln1_gain[None], ln2_gain[None]
    wq_flat, wo_flat = w_qkv.reshape(-1, TOK), w_attn_out.reshape(-1, TOK)
    wi_flat, wd_flat = w_in.reshape(-1, TOK), w_mlp_out.reshape(-1, TOK)

    vm = pltpu.VMEM
    group = (2, 2, TOK, WIDTH)
    rows = (4, 2, 2, 2, 32)
    outs = pl.pallas_call(
        layer_kernel,
        out_shape=(
            jax.ShapeDtypeStruct((TOK, WIDTH), BF),
            jax.ShapeDtypeStruct((TOK, WIDTH), F32),
            jax.ShapeDtypeStruct((4, 32, QKV), BF),
            jax.ShapeDtypeStruct((32, WIDTH), BF),
            jax.ShapeDtypeStruct(wi_flat.shape, F32),
            jax.ShapeDtypeStruct((PAD, WIDTH), F32),
            jax.ShapeDtypeStruct((32, TOK), F32),
        ),
        in_specs=[pl.BlockSpec(memory_space=vm)] * 11,
        out_specs=(pl.BlockSpec(memory_space=pl.ANY),) * 7,
        scratch_shapes=[
            vm((2, 2, 8, TOK), F32),
            vm(group, BF),
            vm(group, BF),
            vm(group, BF),
            vm(group, BF),
            vm(rows + (QKV,), BF),
            vm((2, 2, 2, 32, WIDTH), BF),
            vm(rows + (2 * HID,), BF),
            vm((2, 2, 2, PAD, WIDTH), BF),
            vm((TOK, WIDTH), F32),
            vm((TOK, 128), F32),
            vm((TOK, WIDTH), F32),
            vm((TOK, 128), F32),
            vm((TOK, WIDTH), F32),
            vm((TOK, WIDTH), F32),
            vm((2, 2, 256, 128), BF),
            vm((2, 2, 256, 128), BF),
            vm((2, 2, 256, 128), BF),
            vm((4, 2, 256, 256), F32),
            vm((2, 2, 256, 128), BF),
            vm((2, 2, 256, 128), BF),
            vm((2, 256, HID), F32),
            vm((2, 256, HID), F32),
            vm((2, 256, HID), BF),
            vm((2, 256, 2 * HID), BF),
            vm((3, 2, 2, 256, 128), BF),
            vm((4,) + group, BF),
            vm((4, 2, TOK, WIDTH), BF),
            vm((4, TOK, WIDTH), BF),
            vm((4, TOK, WIDTH), BF),
            vm(rows + (QKV,), BF),
            vm((2, 2, 2, 32, WIDTH), BF),
            vm(rows + (2 * HID,), BF),
            vm((2, 2, 2, PAD, WIDTH), BF),
            vm((2, 2, 2, 2, 2, 32, QKV // 2), BF),
            vm((2, 2, 2, 2, 32, QKV // 2), BF),
            vm((2, 2, 32, QKV), BF),
            vm((2, 2, 2, 32, WIDTH // 2), BF),
            vm((2, 2, 32, WIDTH // 2), BF),
            vm((2, 32, WIDTH), BF),
            vm((2, 2, 2, 2, 2, 2, 32, HID // 2), BF),
            vm((2, 2, 2, 2, 2, 32, HID // 2), BF),
            vm((2, 2, 2, 32, HID), BF),
            vm((2, 2, 1, 2, PAD, WIDTH // 2), BF),
            vm((2, 2, 1, PAD, WIDTH // 2), BF),
            vm((1, PAD, WIDTH), BF),
            vm((4, 32, QKV), BF),
            vm((32, WIDTH), BF),
            vm((4, 32, 2 * HID), BF),
            vm((64 * FF // TOK, TOK), F32),
            vm((64 * FF // TOK, TOK), F32),
            vm((TOK, WIDTH), BF),
            vm((TOK, WIDTH), F32),
            vm((4, 32, QKV), BF),
            vm((32, WIDTH), BF),
            vm((4, 32, 2 * HID), BF),
            vm((PAD, WIDTH), F32),
            vm(wi_flat.shape, F32),
            vm((32, TOK), F32),
            pltpu.SemaphoreType.DMA((N_SENDS,)),
            pltpu.SemaphoreType.DMA((N_COPIES,)),
            pltpu.SemaphoreType.DMA((7,)),
        ],
        compiler_params=pltpu.CompilerParams(
            collective_id=0, has_side_effects=True, vmem_limit_bytes=60 * 2**20
        ),
    )(
        inputs[0],
        cotangent[0],
        segments,
        cosines,
        sines,
        gain_one,
        gain_two,
        wq_flat,
        wo_flat,
        wi_flat,
        wd_flat,
    )
    output, input_grad, gq, go, gi, gd, sums = outs
    final = pl.pallas_call(
        finish_kernel,
        out_shape=(
            jax.ShapeDtypeStruct((TOK, WIDTH), BF),
            jax.ShapeDtypeStruct((TOK, WIDTH), F32),
            jax.ShapeDtypeStruct((1, 32), F32),
            jax.ShapeDtypeStruct(wq_flat.shape, F32),
            jax.ShapeDtypeStruct(wo_flat.shape, F32),
            jax.ShapeDtypeStruct((1, 32), F32),
            jax.ShapeDtypeStruct(wi_flat.shape, F32),
            jax.ShapeDtypeStruct(wd_flat.shape, F32),
        ),
        in_specs=[pl.BlockSpec(memory_space=pl.ANY)] * 6
        + [pl.BlockSpec(memory_space=vm)] * 2
        + [pl.BlockSpec(memory_space=pl.ANY)],
        out_specs=tuple(
            pl.BlockSpec(memory_space=vm if i in (2, 5) else pl.ANY) for i in range(8)
        ),
        scratch_shapes=[
            vm(wq_flat.shape, F32),
            vm((4, 32, QKV), BF),
            vm((32, WIDTH), BF),
            vm(wi_flat.shape, F32),
            vm((PAD, WIDTH), F32),
            vm(wq_flat.shape, BF),
            vm(wq_flat.shape, F32),
            vm(wo_flat.shape, F32),
            vm(wd_flat.shape, F32),
            vm((TOK, WIDTH), F32),
            vm((TOK, WIDTH), BF),
            pltpu.SemaphoreType.DMA((14,)),
        ],
        compiler_params=pltpu.CompilerParams(vmem_limit_bytes=60 * 2**20),
    )(gq, go, gi, gd, output, input_grad, gain_one, sums, wq_flat)
    return (final[0][None], final[1][None]) + tuple(f.reshape(-1) for f in final[2:])


N_COPIES = 142
N_SENDS = 100
PIECES = 2


def solution(mesh):
    block = dict(mesh.shape) == {"dp": 16, "seq": 2}
    placed = (
        P("dp", "seq", None),
        P("dp", "seq"),
        P("dp", "seq", None),
        P(("dp", "seq")),
        P(("dp", "seq")),
        P(("dp", "seq")),
        P(("dp", "seq")),
        P(("dp", "seq")),
        P(("dp", "seq")),
    )
    return jax.shard_map(
        block_device if block else general_device,
        mesh=mesh,
        in_specs=placed,
        out_specs=(
            P("dp", "seq", None),
            P("dp", "seq", None),
            P(("dp", "seq")),
            P(("dp", "seq")),
            P(("dp", "seq")),
            P(("dp", "seq")),
            P(("dp", "seq")),
            P(("dp", "seq")),
        ),
        check_vma=False,
    )
```

```python
import functools
import math

import jax
import jax.numpy as jnp
import numpy as np
from jax import lax
from jax.experimental import pallas as pl
from jax.experimental.pallas import tpu as pltpu
from jax.sharding import PartitionSpec as P

HEADS = 16
HD = 64
FF = 2624


EPSILON = 1e-05
ROPE_BASE = 160000.0


def rope_tables(places):
    freqs = 1.0 / ROPE_BASE ** (jnp.arange(0, HD, 2, dtype=jnp.float32) / HD)
    angles = places[:, None] * freqs[None, :]
    angles = jnp.concatenate([angles, angles], axis=1)
    return (jnp.cos(angles), jnp.sin(angles))


def rotate(values_in, cosines, sines):
    halfway = values_in.shape[-1] // 2
    turned = jnp.concatenate([-values_in[..., halfway:], values_in[..., :halfway]], axis=-1)
    return values_in * cosines[:, None, :] + turned * sines[:, None, :]


def rotate_back(grads_in, cosines, sines):
    halfway = grads_in.shape[-1] // 2
    scaled = grads_in * sines[:, None, :]
    turned = jnp.concatenate([scaled[..., halfway:], -scaled[..., :halfway]], axis=-1)
    return grads_in * cosines[:, None, :] + turned


def norm_forward(values_in, gain):
    centred = values_in - jnp.mean(values_in, axis=-1, keepdims=True)
    inv_spread = lax.rsqrt(jnp.mean(centred * centred, axis=-1, keepdims=True) + EPSILON)
    unit_rows = centred * inv_spread
    return (unit_rows * gain, unit_rows, inv_spread)


def norm_back(grad_rows, unit_rows, inv_spread, gain):
    gain_grad = jnp.sum(grad_rows * unit_rows, axis=0)
    scaled = grad_rows * gain
    inner_mean = jnp.mean(scaled, axis=-1, keepdims=True)
    cross_mean = jnp.mean(scaled * unit_rows, axis=-1, keepdims=True)
    return (gain_grad, inv_spread * (scaled - inner_mean - unit_rows * cross_mean))


def matmul_tn(left, right):
    return lax.dot_general(
        left, right, (((0,), (0,)), ((), ())), preferred_element_type=jnp.float32
    )


def matmul_nt(left, right):
    return lax.dot_general(
        left, right, (((1,), (1,)), ((), ())), preferred_element_type=jnp.float32
    )


def masked_scores(query, key_block, seg_query, seg_block):
    scores = (
        jnp.einsum("qhd,khd->hqk", query, key_block, preferred_element_type=jnp.float32) * 0.125
    )
    same_doc = seg_query[:, None] == seg_block[None, :]
    return jnp.where(same_doc[None], scores, -1e30)


def gated(inner, gate):
    return jax.nn.gelu(inner, approximate=False) * gate


def general_device(inputs, segments, cotangent, ln1_gain, w_qkv, w_attn_out, ln2_gain, w_in, w_mlp_out):
    tok_rows = inputs.shape[1]
    model_width = inputs.shape[2]
    seq_devices = lax.axis_size("seq")
    dp_devices = lax.axis_size("dp")
    tokens_in = inputs[0].astype(jnp.float32)
    seg_send = segments.astype(jnp.bfloat16)
    seg_query = seg_send[0]
    gathered_attn = (
        lax.all_gather(ln1_gain, ("dp", "seq"), axis=0, tiled=True),
        lax.all_gather(w_qkv, ("dp", "seq"), axis=0, tiled=True),
        lax.all_gather(w_attn_out, ("dp", "seq"), axis=0, tiled=True),
    )
    gain_one = gathered_attn[0].astype(jnp.float32)
    qkv_mat = gathered_attn[1].reshape(model_width, 3 * model_width)
    proj_mat = gathered_attn[2].reshape(model_width, model_width)
    places = (lax.axis_index("seq") * tok_rows + jnp.arange(tok_rows, dtype=jnp.int32)).astype(
        jnp.float32
    )
    cosines, sines = rope_tables(places)
    normed_one, unit_one, spread_one = norm_forward(tokens_in, gain_one)
    normed_one_low = normed_one.astype(jnp.bfloat16)
    qkv_rows = jnp.dot(normed_one_low, qkv_mat, preferred_element_type=jnp.float32)
    query = rotate(qkv_rows[:, :model_width].reshape(tok_rows, HEADS, HD), cosines, sines).astype(
        jnp.bfloat16
    )
    key_rot = rotate(
        qkv_rows[:, model_width : 2 * model_width].reshape(tok_rows, HEADS, HD), cosines, sines
    ).astype(jnp.bfloat16)
    value_rows = qkv_rows[:, 2 * model_width :].astype(jnp.bfloat16)
    key_send = key_rot.reshape(1, tok_rows, model_width)
    value_send = value_rows.reshape(1, tok_rows, model_width)
    fwd_init = (
        jnp.full((HEADS, tok_rows), -1e30, jnp.float32),
        jnp.zeros((HEADS, tok_rows), jnp.float32),
        jnp.zeros((tok_rows, HEADS, HD), jnp.float32),
    )
    key_piece = lax.all_gather(key_send, "seq", axis=1, tiled=True)
    value_piece = lax.all_gather(value_send, "seq", axis=1, tiled=True)
    seg_piece = lax.all_gather(seg_send, "seq", axis=1, tiled=True)
    span = key_piece.shape[1]
    step_rows = math.gcd(span, 512)

    def one_block(block_id, inner_state):
        top_score, total, accum = inner_state
        begin = block_id * step_rows
        key_block = lax.dynamic_slice_in_dim(key_piece[0], begin, step_rows, 0).reshape(
            step_rows, HEADS, HD
        )
        value_block = lax.dynamic_slice_in_dim(value_piece[0], begin, step_rows, 0).reshape(
            step_rows, HEADS, HD
        )
        seg_block = lax.dynamic_slice_in_dim(seg_piece[0], begin, step_rows, 0)
        scores = masked_scores(query, key_block, seg_query, seg_block)
        new_top = jnp.maximum(top_score, jnp.max(scores, axis=-1))
        fading = jnp.exp(top_score - new_top)
        weights = jnp.exp(scores - new_top[..., None])
        total = total * fading + jnp.sum(weights, axis=-1)
        accum = accum * fading.T[:, :, None] + jnp.einsum(
            "hqk,khd->qhd",
            weights.astype(jnp.bfloat16),
            value_block,
            preferred_element_type=jnp.float32,
        )
        return (new_top, total, accum)

    fwd_state = lax.fori_loop(0, span // step_rows, one_block, fwd_init)
    run_top, run_total, run_accum = fwd_state
    log_total = run_top + jnp.log(run_total)
    attended = (run_accum / run_total.T[:, :, None]).astype(jnp.bfloat16)
    attended_rows = attended.reshape(tok_rows, model_width)
    middle = tokens_in + jnp.dot(attended_rows, proj_mat, preferred_element_type=jnp.float32)
    gathered_mlp = (
        lax.all_gather(ln2_gain, ("dp", "seq"), axis=0, tiled=True),
        lax.all_gather(w_in, ("dp", "seq"), axis=0, tiled=True),
        lax.all_gather(w_mlp_out, ("dp", "seq"), axis=0, tiled=True),
    )
    gain_two = gathered_mlp[0].astype(jnp.float32)
    in_mat = gathered_mlp[1].reshape(model_width, 2 * FF)
    down_mat = gathered_mlp[2].reshape(FF, model_width)
    normed_two, unit_two, spread_two = norm_forward(middle, gain_two)
    normed_two_low = normed_two.astype(jnp.bfloat16)
    upper = jnp.dot(normed_two_low, in_mat, preferred_element_type=jnp.float32)
    inner = upper[:, :FF]
    gate = upper[:, FF:]
    hidden_low = gated(inner, gate).astype(jnp.bfloat16)
    output = (middle + jnp.dot(hidden_low, down_mat, preferred_element_type=jnp.float32)).astype(
        jnp.bfloat16
    )
    gathered_mlp = (
        lax.all_gather(ln2_gain, ("dp", "seq"), axis=0, tiled=True),
        lax.all_gather(w_in, ("dp", "seq"), axis=0, tiled=True),
        lax.all_gather(w_mlp_out, ("dp", "seq"), axis=0, tiled=True),
    )
    gain_two = gathered_mlp[0].astype(jnp.float32)
    in_mat = gathered_mlp[1].reshape(model_width, 2 * FF)
    down_mat = gathered_mlp[2].reshape(FF, model_width)
    grad_low = cotangent[0]
    grad_rows = grad_low.astype(jnp.float32)
    d_hidden = matmul_nt(grad_low, down_mat)
    grad_down = matmul_tn(hidden_low, grad_low)
    gated_value, pull = jax.vjp(gated, inner, gate)
    d_inner, d_gate = pull(d_hidden)
    d_upper_low = jnp.concatenate([d_inner, d_gate], axis=1).astype(jnp.bfloat16)
    grad_in = matmul_tn(normed_two_low, d_upper_low)
    d_normed_two = matmul_nt(d_upper_low, in_mat)
    grad_gain_two, d_middle_part = norm_back(d_normed_two, unit_two, spread_two, gain_two)
    d_middle = grad_rows + d_middle_part
    mlp_parts = tuple(
        (g.reshape(dp_devices, seq_devices, -1) for g in (grad_gain_two, grad_in, grad_down))
    )
    mlp_mid = (
        lax.psum_scatter(
            mlp_parts[0].astype(jnp.bfloat16), "seq", scatter_dimension=1, tiled=True
        ).astype(jnp.float32),
        lax.psum_scatter(
            mlp_parts[1].astype(jnp.bfloat16), "seq", scatter_dimension=1, tiled=True
        ).astype(jnp.float32),
        lax.psum_scatter(
            mlp_parts[2].astype(jnp.bfloat16), "seq", scatter_dimension=1, tiled=True
        ).astype(jnp.float32),
    )
    mlp_shards = (
        lax.psum_scatter(
            mlp_mid[0].astype(jnp.bfloat16), "dp", scatter_dimension=0, tiled=True
        ).astype(jnp.float32),
        lax.psum_scatter(
            mlp_mid[1].astype(jnp.bfloat16), "dp", scatter_dimension=0, tiled=True
        ).astype(jnp.float32),
        lax.psum_scatter(
            mlp_mid[2].astype(jnp.bfloat16), "dp", scatter_dimension=0, tiled=True
        ).astype(jnp.float32),
    )
    gathered_attn = (
        lax.all_gather(ln1_gain, ("dp", "seq"), axis=0, tiled=True),
        lax.all_gather(w_qkv, ("dp", "seq"), axis=0, tiled=True),
        lax.all_gather(w_attn_out, ("dp", "seq"), axis=0, tiled=True),
    )
    gain_one = gathered_attn[0].astype(jnp.float32)
    qkv_mat = gathered_attn[1].reshape(model_width, 3 * model_width)
    proj_mat = gathered_attn[2].reshape(model_width, model_width)
    d_branch_low = d_middle.astype(jnp.bfloat16)
    grad_proj = matmul_tn(attended_rows, d_branch_low)
    d_attended = matmul_nt(d_branch_low, proj_mat).astype(jnp.bfloat16).reshape(tok_rows, HEADS, HD)
    delta_rows = jnp.einsum(
        "qhd,qhd->hq", d_attended.astype(jnp.float32), attended.astype(jnp.float32)
    )
    back_init = (
        jnp.zeros((tok_rows, HEADS, HD), jnp.float32),
        jnp.zeros((tok_rows * seq_devices, 2 * model_width), jnp.float32),
    )
    attend_key_piece = lax.all_gather(key_send, "seq", axis=1, tiled=True)
    attend_value_piece = lax.all_gather(value_send, "seq", axis=1, tiled=True)
    attend_seg_piece = lax.all_gather(seg_send, "seq", axis=1, tiled=True)
    span = attend_key_piece.shape[1]
    attend_step_rows = math.gcd(span, 512)

    def one_block(block_id, inner_state):
        grad_query, grad_kv = inner_state
        begin = block_id * attend_step_rows
        key_block = lax.dynamic_slice_in_dim(
            attend_key_piece[0], begin, attend_step_rows, 0
        ).reshape(attend_step_rows, HEADS, HD)
        value_block = lax.dynamic_slice_in_dim(
            attend_value_piece[0], begin, attend_step_rows, 0
        ).reshape(attend_step_rows, HEADS, HD)
        seg_block = lax.dynamic_slice_in_dim(attend_seg_piece[0], begin, attend_step_rows, 0)
        scores = masked_scores(query, key_block, seg_query, seg_block)
        probs = jnp.exp(scores - log_total[..., None])
        probs_low = probs.astype(jnp.bfloat16)
        value_grad = jnp.einsum(
            "hqk,qhd->khd", probs_low, d_attended, preferred_element_type=jnp.float32
        )
        d_probs = jnp.einsum(
            "qhd,khd->hqk", d_attended, value_block, preferred_element_type=jnp.float32
        )
        d_scores = (probs * (d_probs - delta_rows[..., None])).astype(jnp.bfloat16)
        grad_query = (
            grad_query
            + jnp.einsum("hqk,khd->qhd", d_scores, key_block, preferred_element_type=jnp.float32)
            * 0.125
        )
        key_grad = (
            jnp.einsum("hqk,qhd->khd", d_scores, query, preferred_element_type=jnp.float32) * 0.125
        )
        block_grads = jnp.concatenate(
            [
                key_grad.reshape(attend_step_rows, model_width),
                value_grad.reshape(attend_step_rows, model_width),
            ],
            axis=1,
        )
        grad_kv = lax.dynamic_update_slice_in_dim(grad_kv, block_grads, begin, 0)
        return (grad_query, grad_kv)

    back_state = lax.fori_loop(0, span // attend_step_rows, one_block, back_init)
    kv_grads = lax.psum_scatter(
        back_state[1].astype(jnp.bfloat16), "seq", scatter_dimension=0, tiled=True
    ).astype(jnp.float32)
    d_query = rotate_back(back_state[0], cosines, sines).reshape(tok_rows, model_width)
    d_key = rotate_back(
        kv_grads[:, :model_width].reshape(tok_rows, HEADS, HD), cosines, sines
    ).reshape(tok_rows, model_width)
    d_qkv_low = jnp.concatenate([d_query, d_key, kv_grads[:, model_width:]], axis=1).astype(
        jnp.bfloat16
    )
    grad_qkv = matmul_tn(normed_one_low, d_qkv_low)
    d_normed_one = matmul_nt(d_qkv_low, qkv_mat)
    grad_gain_one, d_input_part = norm_back(d_normed_one, unit_one, spread_one, gain_one)
    input_grad = d_middle + d_input_part
    attn_parts = tuple(
        (g.reshape(dp_devices, seq_devices, -1) for g in (grad_gain_one, grad_qkv, grad_proj))
    )
    attn_mid = (
        lax.psum_scatter(
            attn_parts[0].astype(jnp.bfloat16), "seq", scatter_dimension=1, tiled=True
        ).astype(jnp.float32),
        lax.psum_scatter(
            attn_parts[1].astype(jnp.bfloat16), "seq", scatter_dimension=1, tiled=True
        ).astype(jnp.float32),
        lax.psum_scatter(
            attn_parts[2].astype(jnp.bfloat16), "seq", scatter_dimension=1, tiled=True
        ).astype(jnp.float32),
    )
    attn_shards = (
        lax.psum_scatter(
            attn_mid[0].astype(jnp.bfloat16), "dp", scatter_dimension=0, tiled=True
        ).astype(jnp.float32),
        lax.psum_scatter(
            attn_mid[1].astype(jnp.bfloat16), "dp", scatter_dimension=0, tiled=True
        ).astype(jnp.float32),
        lax.psum_scatter(
            attn_mid[2].astype(jnp.bfloat16), "dp", scatter_dimension=0, tiled=True
        ).astype(jnp.float32),
    )
    return (
        output.reshape(1, tok_rows, model_width),
        input_grad.reshape(1, tok_rows, model_width),
        attn_shards[0].reshape(-1),
        attn_shards[1].reshape(-1),
        attn_shards[2].reshape(-1),
        mlp_shards[0].reshape(-1),
        mlp_shards[1].reshape(-1),
        mlp_shards[2].reshape(-1),
    )


MESH_IDS = pl.DeviceIdType.MESH
TOK = 128
WIDTH = 1024
PART = FF // 32
PAD = 96
HID = 8 * PAD
QKV = 3 * 256
BF = jnp.bfloat16
F32 = jnp.float32


def dot_nn(a, b):
    return lax.dot_general(a, b, (((1,), (0,)), ((), ())), preferred_element_type=F32)


def turned(u, low_half):
    return jnp.where(low_half, pltpu.roll(u, 96, axis=1), pltpu.roll(u, 32, axis=1))


def column(gain_ref):
    square = jnp.broadcast_to(gain_ref[...].astype(F32), (32, 32))
    rows = lax.broadcasted_iota(jnp.int32, (32, 32), 0)
    cols = lax.broadcasted_iota(jnp.int32, (32, 32), 1)
    return jnp.sum(jnp.where(rows == cols, square, 0.0), axis=1, keepdims=True)


def owner(r, k):
    return k // 4 * 16 + (r // 2 + k // 4) % 2 * 8 + k // 2 % 2 * 4 + k % 2 * 2 + r % 2


def runs(places):
    found = []
    for lane, place in enumerate(places):
        if place is None:
            continue
        tile, shift = place[0], (place[1] - lane) % 128
        if found and found[-1][:2] == (tile, shift) and found[-1][3] == lane:
            found[-1] = found[-1][:3] + (lane + 1,)
        else:
            found.append((tile, shift, lane, lane + 1))
    return found


def in_moves(r, u):
    places = []
    for at in range(u * 128, u * 128 + 128):
        gate, rest = divmod(at, HID)
        k, i = divmod(rest, PAD)
        col = gate * FF + PART * owner(r, k) + i
        places.append(divmod(col, 128) if i < PART else None)
    return runs(places)


def out_moves(t):
    spots = {owner(r, k): (r, k) for r in range(4) for k in range(8)}
    places = []
    for col in range(t * 128, t * 128 + 128):
        gate, rest = divmod(col, FF)
        device, i = divmod(rest, PART)
        r, k = spots[device]
        u, lane = divmod(gate * HID + k * PAD + i, 128)
        places.append(((r, u), lane))
    return runs(places)


def moved(moves, load):
    lanes = lax.broadcasted_iota(jnp.int32, (1, 128), 1)
    out = jnp.zeros((32, 128), F32)
    for tile, shift, low, high in moves:
        piece = load(tile)
        if shift:
            piece = pltpu.roll(piece, 128 - shift, axis=1)
        out = jnp.where((lanes >= low) & (lanes < high), piece, out)
    return out


def finish_kernel(
    gq_in,
    go_in,
    gi_in,
    gd_in,
    out_in,
    ig_in,
    gain1_in,
    sums_in,
    wq_flat,
    out_ref,
    ig_ref,
    gain1_ref,
    gq_ref,
    go_ref,
    gain2_ref,
    gi_ref,
    gd_ref,
    lines,
    gq_raw,
    go_raw,
    gi_raw,
    gd_raw,
    wq_raw,
    gq_own,
    go_own,
    gd_own,
    ig_raw,
    out_raw,
    sems,
):
    count = [0]

    def start(src, dst):
        cp = pltpu.make_async_copy(src, dst, sems.at[count[0]])
        count[0] += 1
        cp.start()
        return cp

    gi_here = start(gi_in, gi_raw)
    ig_here = start(ig_in, ig_raw)
    out_here = start(out_in, out_raw)
    gd_here = start(gd_in, gd_raw)
    gq_here = start(gq_in, gq_raw)
    wq_here = start(wq_flat, wq_raw)
    go_here = start(go_in, go_raw)
    written = []
    rows = lax.broadcasted_iota(jnp.int32, (32, 32), 0)
    cols = lax.broadcasted_iota(jnp.int32, (32, 32), 1)

    def line(total):
        total = jnp.sum(total, axis=1, keepdims=True)
        return jnp.sum(jnp.where(rows == cols, total, 0.0), axis=0, keepdims=True)

    qkv_rows = 3 * WIDTH // TOK
    gi_here.wait()
    written.append(start(gi_raw, gi_ref))
    ig_here.wait()
    written.append(start(ig_raw, ig_ref))
    out_here.wait()
    written.append(start(out_raw, out_ref))
    gain2_ref[...] = line(sums_in[...])
    gd_here.wait()
    for j in range(8):
        gd_own[pl.ds(j, PART, stride=8), :] = gd_raw[0:PART, pl.ds(j * 128, 128)]
    written.append(start(gd_own, gd_ref))
    gain = column(gain1_in)
    total = jnp.zeros((32, 128), F32)
    wq_here.wait()
    lines[0 : 32 * qkv_rows] = wq_raw[...].astype(F32)
    gq_here.wait()
    for j in range(qkv_rows):
        part, cut = divmod(j, 8)
        r = (cut // 2 + cut // 4) % 2 * 2 + cut // 4
        g = gq_raw[r, :, pl.ds(part * 256 + cut % 2 * 128, 128)].astype(F32)
        total = total + g * lines[pl.ds(j, 32, stride=qkv_rows), :]
        gq_own[pl.ds(j, 32, stride=qkv_rows), :] = g * gain
    written.append(start(gq_own, gq_ref))
    gain1_ref[...] = line(total)
    go_here.wait()
    for j in range(8):
        go_own[pl.ds(j, 32, stride=8), :] = go_raw[:, pl.ds(j * 128, 128)].astype(F32)
    written.append(start(go_own, go_ref))
    for cp in written:
        cp.wait()


def layer_kernel(
    x_ref,
    cot_in,
    seg_in,
    cos_ref,
    sin_ref,
    gain1_in,
    gain2_in,
    wq_flat,
    wo_flat,
    wi_flat,
    wd_flat,
    out_ref,
    ig_ref,
    gq_ref,
    go_ref,
    gi_ref,
    gd_ref,
    sums_ref,
    seg_buf,
    n1,
    n2,
    cot,
    db,
    wq,
    wo,
    wi,
    wd,
    unit1,
    inv1,
    unit2,
    inv2,
    middle,
    dmid,
    q_buf,
    k_buf,
    v_buf,
    probs,
    att,
    datt,
    up_a,
    up_b,
    hidden,
    d_up,
    dqkv,
    ps,
    ps_in,
    ps_far,
    ps_back,
    gq,
    go,
    gi,
    gd,
    rq1,
    rq2,
    rq3,
    ro1,
    ro2,
    ro3,
    ri1,
    ri2,
    ri3,
    rd1,
    rd2,
    rd3,
    wq_in,
    wo_in,
    wi_in,
    lines,
    wide,
    out_vm,
    ig_vm,
    gq_vm,
    go_vm,
    gi_vm,
    gd_vm,
    gi_own,
    sums,
    send_sems,
    recv_sems,
    local_sems,
):
    dp, c = lax.axis_index("dp"), lax.axis_index("seq")
    x, y, z = lax.rem(dp, 2), lax.rem(dp // 2, 2), dp // 4
    zh, zp = z // 2, lax.rem(z, 2)
    kind = lax.rem(zp + zh, 2)
    role = kind * 2 + c

    def device(X, Y, Z, C):
        return (Z * 4 + Y * 2 + X, C)

    core_dev = device(x, y, z, 1 - c)
    pair_dev = device(x, y, zh * 2 + 1 - zp, c)
    diag_dev = device(x, y, zh * 2 + 1 - zp, 1 - c)
    half_dev = device(x, y, 3 - z, c)
    x_dev = device(1 - x, y, z, c)
    y_dev = device(x, 1 - y, z, c)

    barrier = pltpu.get_barrier_semaphore()
    for dev in (core_dev, pair_dev, diag_dev, half_dev, x_dev, y_dev):
        pl.semaphore_signal(barrier, inc=1, device_id=dev, device_id_type=MESH_IDS)

    sent = []
    n_sems = [0]
    free = list(range(N_SENDS))

    def copy_to(src, dst, dev, keep=True):
        i, k = n_sems[0], free.pop(0)
        n_sems[0] += 1
        cp = pltpu.make_async_remote_copy(
            src_ref=src,
            dst_ref=dst,
            send_sem=send_sems.at[k],
            recv_sem=recv_sems.at[i],
            device_id=dev,
            device_id_type=MESH_IDS,
        )
        if keep:
            sent.append((cp, k))
        return cp

    local = []

    def emit(i, src, dst):
        cp = pltpu.make_async_copy(src, dst, local_sems.at[i])
        cp.start()
        local.append(cp)

    def settle(first):
        for cp, k in sent[:first]:
            cp.wait_send()
            free.append(k)
        del sent[:first]
        free.sort()

    def go_copy(src, dst, dev):
        cp = copy_to(src, dst, dev)
        cp.start()
        return cp


    others = (
        (core_dev, kind * 2 + 1 - c, (z, 1 - c)),
        (pair_dev, (1 - kind) * 2 + c, (zh * 2 + 1 - zp, c)),
        (diag_dev, (1 - kind) * 2 + 1 - c, (zh * 2 + 1 - zp, 1 - c)),
    )

    def spread(own, buf):
        cps = [go_copy(own.at[r], buf.at[z, y, x, c], dev) for dev, r, _ in others]
        return cps

    class Gather:
        def __init__(self, buf, cols, base=0):
            self.buf = buf
            self.halves = (pl.ds(base, cols // 2), pl.ds(base + cols // 2, cols // 2))
            self.per_half = buf.shape[0] // 2

        def of(self, which):
            return pl.ds(self.per_half * which, self.per_half)

        def spot(self, which, cut):
            return self.buf.at[(self.of(which), y, x) + (slice(None),) * (len(self.buf.shape) - 4) + (cut,)]

        def line(self, which, cut, i):
            rest = (slice(None),) * (len(self.buf.shape) - 4) + (cut,)
            at = (y, slice(None)) if i == 0 else (slice(None), x)
            return self.buf.at[(self.of(which),) + at + rest]

        def same(self, ref, dev):
            return go_copy(ref, ref, dev)

        def across(self):
            self.over = [self.same(self.spot(zh, cut), half_dev) for cut in self.halves]

        def own_first(self):
            self.a = [
                self.same(self.spot(zh, cut), dev) for cut, dev in zip(self.halves, (x_dev, y_dev))
            ]

        def own_second(self):
            self.b = []
            for i, dev in enumerate((y_dev, x_dev)):
                self.a[i].wait_recv()
                self.b.append(self.same(self.line(zh, self.halves[i], i), dev))

        def far_first(self):
            self.a2 = []
            for i, dev in enumerate((x_dev, y_dev)):
                self.over[i].wait_recv()
                self.a2.append(self.same(self.spot(1 - zh, self.halves[i]), dev))

        def far_second(self):
            self.b2 = []
            for i, dev in enumerate((y_dev, x_dev)):
                self.a2[i].wait_recv()
                self.b2.append(self.same(self.line(1 - zh, self.halves[i], i), dev))

        def done(self):
            for cp in self.b + self.b2:
                cp.wait_recv()

    class GatherOut:
        def __init__(self, buf, cols):
            self.buf = buf
            self.halves = (pl.ds(0, cols // 2), pl.ds(cols // 2, cols // 2))

        def start(self):
            self.s0 = copy_to(wo_in, self.buf.at[y, x, c], core_dev, keep=False)

            @pl.when(c != zh)
            def _():
                self.s0.start()

        def across(self):
            self.s1 = copy_to(self.buf.at[y, x], self.buf.at[y, x], half_dev, keep=False)

            @pl.when(c == zh)
            def _():
                self.buf[y, x, c] = wo_in[...]
                self.s0.wait_recv()
                self.s1.start()

        def first(self):
            @pl.when(c != zh)
            def _():
                self.s1.wait_recv()

            self.a = []
            for cut, dev in zip(self.halves, (x_dev, y_dev)):
                ref = self.buf.at[y, x, :, :, cut]
                self.a.append(go_copy(ref, ref, dev))

        def second(self):
            self.b = []
            for i, dev in enumerate((y_dev, x_dev)):
                self.a[i].wait_recv()
                cut = self.halves[i]
                ref = self.buf.at[y, :, :, :, cut] if i == 0 else self.buf.at[:, x, :, :, cut]
                self.b.append(go_copy(ref, ref, dev))

        def done(self):
            for cp in self.b:
                cp.wait_recv()

        def end(self):
            @pl.when(c != zh)
            def _():
                self.s0.wait_send()

            @pl.when(c == zh)
            def _():
                self.s1.wait_send()


    pieces = [pl.ds(i * (TOK // PIECES), TOK // PIECES) for i in range(PIECES)]

    class Share:
        def __init__(self, buf):
            self.buf = buf
            self.to_pair = [
                go_copy(buf.at[zp, c, cut], buf.at[zp, c, cut], pair_dev) for cut in pieces
            ]
            self.to_core = go_copy(buf.at[zp, c], buf.at[zp, c], core_dev)

        def forward(self):
            self.fwd = []
            for cp, cut in zip(self.to_pair, pieces):
                cp.wait_recv()
                ref = self.buf.at[1 - zp, c, cut]
                self.fwd.append(go_copy(ref, ref, core_dev))

        def core(self):
            self.to_core.wait_recv()

        def done(self):
            for cp in self.fwd:
                cp.wait_recv()

    class Reduce:
        def __init__(self, i):
            self.i = i

        def far_terms(self):
            i = self.i
            self.mine_far = go_copy(ps.at[i, 1 - zp, 1 - c], ps_in.at[i, 1 - zp], core_dev)

        def near_terms(self):
            i = self.i
            self.mine_near = go_copy(ps.at[i, zp, 1 - c], ps_in.at[i, zp], core_dev)

        def cross(self):
            i = self.i
            self.mine_far.wait_recv()
            self.far = []
            for cut in pieces:
                ps_far[i, cut] = (
                    ps[i, 1 - zp, c, cut].astype(F32) + ps_in[i, 1 - zp, cut].astype(F32)
                ).astype(BF)
                self.far.append(go_copy(ps_far.at[i, cut], ps_back.at[i, cut], pair_dev))

        def total(self):
            i = self.i
            self.mine_near.wait_recv()
            near = ps[i, zp, c].astype(F32) + ps_in[i, zp].astype(F32)
            for cp in self.far:
                cp.wait_recv()
            return near + ps_back[i].astype(F32)


    def add_into(target, extra):
        target[...] = (target[...].astype(F32) + extra[...].astype(F32)).astype(BF)

    def add_all(mine, got):
        n = got.shape[0]
        if n == 1:
            add_into(mine.at[0], got.at[0])
            return

        def body(j, carry):
            add_into(mine.at[j], got.at[j])
            return carry

        lax.fori_loop(0, n, body, 0)

    class Scatter:
        def __init__(self, buf, cols, r1, r2, r3, base=0):
            self.buf, self.r1, self.r2, self.r3 = buf, r1, r2, r3
            self.halves = (pl.ds(base, cols // 2), pl.ds(base + cols // 2, cols // 2))
            self.cols = pl.ds(base, cols)
            self.per_half = buf.shape[0] // 2
            self.rest = (slice(None),) * (len(buf.shape) - 4)
            self.c1, self.c2 = {}, {}

        def of(self, which):
            return pl.ds(self.per_half * which, self.per_half)

        def line(self, i, which, other):
            if i == 0:
                at = (1 - y if other else y, slice(None))
            else:
                at = (slice(None), 1 - x if other else x)
            return self.buf.at[(self.of(which),) + at + self.rest + (self.halves[i],)]

        def spot(self, i, which, other):
            Y, X = (y, x) if not other else ((y, 1 - x) if i == 0 else (1 - y, x))
            return self.buf.at[(self.of(which), Y, X) + self.rest + (self.halves[i],)]

        def first(self, far):
            which = 1 - zh if far else zh
            self.c1[far] = [
                go_copy(self.line(i, which, True), self.r1.at[i, far], dev)
                for i, dev in enumerate((y_dev, x_dev))
            ]

        def second(self, far):
            which = 1 - zh if far else zh
            self.c2[far] = []
            for i, dev in enumerate((x_dev, y_dev)):
                self.c1[far][i].wait_recv()
                add_all(self.line(i, which, False), self.r1.at[i, far])
                self.c2[far].append(go_copy(self.spot(i, which, True), self.r2.at[i, far], dev))

        def third(self, far):
            which = 1 - zh if far else zh
            for i in range(2):
                self.c2[far][i].wait_recv()
                add_all(self.spot(i, which, False), self.r2.at[i, far])
            if far:
                src = self.buf.at[(self.of(which), y, x) + self.rest + (self.cols,)]
                self.c3 = go_copy(src, self.r3, half_dev)

    class ScatterRows(Scatter):
        def fourth(self, out):
            self.c3.wait_recv()
            cols = self.cols
            add_all(self.buf.at[self.of(zh), y, x, :, :, cols], self.r3)
            self.c4 = []
            for dev, _, (there, core) in others:
                src = self.buf.at[there, y, x, core, :, cols]
                self.c4.append(go_copy(src, out.at[role, :, cols], dev))
            out[role, :, cols] = self.buf[z, y, x, c, :, cols]

        def done(self):
            for cp in self.c4:
                cp.wait_recv()

    class ScatterDown(Scatter):
        def fourth(self, out):
            self.c3.wait_recv()
            out[...] = self.buf[zh, y, x].astype(F32) + self.r3[0].astype(F32)

    class ScatterOut:
        def __init__(self, buf, cols, r1, r2, r3):
            self.buf, self.r1, self.r2, self.r3 = buf, r1, r2, r3
            self.halves = (pl.ds(0, cols // 2), pl.ds(cols // 2, cols // 2))

        def line(self, i, other):
            cut = self.halves[i]
            if i == 0:
                return self.buf.at[1 - y if other else y, :, :, :, cut]
            return self.buf.at[:, 1 - x if other else x, :, :, cut]

        def spot(self, i, other):
            Y, X = (y, x) if not other else ((y, 1 - x) if i == 0 else (1 - y, x))
            return self.buf.at[Y, X, :, :, self.halves[i]]

        def first(self):
            self.c1 = [
                go_copy(self.line(i, True), self.r1.at[i], dev)
                for i, dev in enumerate((y_dev, x_dev))
            ]

        def second(self):
            self.c2 = []
            for i, dev in enumerate((x_dev, y_dev)):
                self.c1[i].wait_recv()
                add_all(self.line(i, False), self.r1.at[i])
                self.c2.append(go_copy(self.spot(i, True), self.r2.at[i], dev))

        def third(self):
            for i in range(2):
                self.c2[i].wait_recv()
                add_all(self.spot(i, False), self.r2.at[i])
            self.c3 = copy_to(self.buf.at[y, x], self.r3, half_dev, keep=False)

            @pl.when(c != zh)
            def _():
                self.c3.start()

        def fourth(self, out):
            self.c4 = copy_to(self.r3.at[1 - c], out, core_dev, keep=False)

            @pl.when(c == zh)
            def _():
                self.c3.wait_recv()
                add_all(self.r3, self.buf.at[y, x])
                self.c4.start()
                out[...] = self.r3[c]

        def done(self):
            @pl.when(c != zh)
            def _():
                self.c4.wait_recv()
                self.c3.wait_send()

            @pl.when(c == zh)
            def _():
                self.c4.wait_send()

    qkv_rows = 3 * WIDTH // TOK
    lines[0 : 32 * qkv_rows] = wq_flat[...].astype(F32)
    gain = column(gain1_in)
    for j in range(qkv_rows):
        part, cut = divmod(j, 8)
        r = (cut // 2 + cut // 4) % 2 * 2 + cut // 4
        w = lines[pl.ds(j, 32, stride=qkv_rows), :] * gain
        wq_in[r, :, pl.ds(part * 256 + cut % 2 * 128, 128)] = w.astype(BF)
    wq[z, y, x, c] = wq_in[role]
    g_q, g_d = Gather(wq, QKV), Gather(wd, WIDTH)
    g_i, g_j = Gather(wi, HID), Gather(wi, HID, HID)
    g_o = GatherOut(wo, WIDTH)


    r_d = ScatterDown(gd, WIDTH, rd1, rd2, rd3)
    r_i = ScatterRows(gi, HID, ri1.at[0], ri2.at[0], ri3.at[0])
    r_j = ScatterRows(gi, HID, ri1.at[1], ri2.at[1], ri3.at[1], HID)
    r_q = ScatterRows(gq, QKV, rq1, rq2, rq3)
    r_o = ScatterOut(go, WIDTH, ro1, ro2, ro3)
    on = {}
    red = [Reduce(i) for i in range(4)]
    lanes = lax.broadcasted_iota(jnp.int32, (1, 128), 1)
    low_half = lax.rem(lanes, 64) < 32
    first_head = lanes < 64

    def qkv_step(s, carry):
        rows = n1[s].reshape(256, WIDTH)
        for part, dst in enumerate((q_buf, k_buf, v_buf)):
            for j in range(2):
                at = part * 256 + j * 128
                w = wq[:, :, :, :, :, pl.ds(at, 128)].reshape(WIDTH, 128)
                u = dot_nn(rows, w)
                if part < 2:
                    u = u * cos_ref[...] + turned(u, low_half) * sin_ref[...]
                dst[s, j] = u.astype(BF)
        return carry

    def only(head, u):
        return jnp.where(first_head if head == 0 else ~first_head, u, jnp.zeros_like(u))

    def attend(i, carry):
        s, j = i // 2, lax.rem(i, 2)
        q, k, v = q_buf[s, j], k_buf[s, j], v_buf[s, j]
        seg_row = jnp.concatenate([seg_buf[s, 0, 0:1], seg_buf[s, 1, 0:1]], axis=1)
        seg_col = jnp.broadcast_to(seg_row, (128, 256)).T[:, 0:1]
        same = seg_col == seg_row
        heads = []
        for h in range(2):
            scores = matmul_nt(only(h, q), k) * 0.125
            scores = jnp.where(same, scores, -1e30)
            weights = jnp.exp(scores - jnp.max(scores, axis=-1, keepdims=True))
            p = weights * (1.0 / jnp.sum(weights, axis=-1, keepdims=True))
            probs[i, h] = p
            heads.append(dot_nn(p.astype(BF), v))
        att[s, j] = jnp.where(first_head, heads[0], heads[1]).astype(BF)
        return carry

    def att_rows(s):
        return jnp.concatenate([att[s, 0], att[s, 1]], axis=1)

    def branch(s, carry):
        w = wo[...].reshape(256, WIDTH)
        ps[0, s] = dot_nn(att_rows(s), w).astype(BF).reshape(2, TOK, WIDTH)
        return carry

    def upper_for(s):
        def upper(j, carry):
            at = pl.multiple_of(j * 256, 256)
            rows = n2[s].reshape(256, WIDTH)
            inner = dot_nn(rows, wi[:, :, :, :, :, pl.ds(at, 256)].reshape(WIDTH, 256))
            gate = dot_nn(
                rows,
                wi[:, :, :, :, :, pl.ds(pl.multiple_of(HID + at, 256), 256)].reshape(WIDTH, 256),
            )
            cdf = 0.5 * (1.0 + lax.erf(inner * math.sqrt(0.5)))
            slope = cdf + inner * jnp.exp(-0.5 * inner * inner) * (1.0 / math.sqrt(2 * math.pi))
            bent = inner * cdf
            up_a[s, :, pl.ds(at, 256)] = gate * slope
            up_b[s, :, pl.ds(at, 256)] = bent
            hidden[s, :, pl.ds(at, 256)] = (bent * gate).astype(BF)
            return carry

        lax.fori_loop(0, HID // 256, upper, 0)

    def down_grad(i, carry):
        lhs = hidden[:, :, pl.ds(pl.multiple_of(i * 384, 384), 384)].reshape(512, 384)
        for j in range(2):
            rhs = cot[:, :, :, pl.ds(j * 512, 512)].reshape(512, 512)
            gd[i, :, :, :, pl.ds(j * 512, 512)] = (
                matmul_tn(lhs, rhs).astype(BF).reshape(2, 2, PAD, 512)
            )
        return carry

    def hidden_grad_for(s):
        def hidden_grad(i, carry):
            w = wd[i].reshape(384, WIDTH)
            at = pl.multiple_of(i * 384, 384)
            dh = matmul_nt(cot[s].reshape(256, WIDTH), w)
            d_up[s, :, pl.ds(at, 384)] = (dh * up_a[s, :, pl.ds(at, 384)]).astype(BF)
            d_up[s, :, pl.ds(pl.multiple_of(HID + at, 384), 384)] = (
                dh * up_b[s, :, pl.ds(at, 384)]
            ).astype(BF)
            return carry

        lax.fori_loop(0, 2, hidden_grad, 0)

    def normed_two_grad_for(s):
        def normed_two_grad(i, carry):
            w = wi[i].reshape(256, 2 * HID)
            at = pl.multiple_of(i * 256, 256)
            ps[1, s, :, :, pl.ds(at, 256)] = matmul_nt(d_up[s], w).astype(BF).reshape(2, TOK, 256)
            return carry

        lax.fori_loop(0, 4, normed_two_grad, 0)

    def in_grad_for(base, first):
        def in_grad(i, carry):
            lhs = n2[:, :, :, pl.ds(pl.multiple_of(i * 256, 256), 256)].reshape(512, 256)
            for j in range(HID // 256):
                at = base + j * 256
                rhs = d_up[:, :, pl.ds(at, 256)].reshape(512, 256)
                gi[i, :, :, :, :, pl.ds(at, 256)] = (
                    matmul_tn(lhs, rhs).astype(BF).reshape(2, 2, 2, 32, 256)
                )
            return carry

        lax.fori_loop(first, first + 2, in_grad, 0)

    def down(i, carry):
        w = wd[...].reshape(HID, WIDTH)
        ps[2, i] = dot_nn(hidden[i], w).astype(BF).reshape(2, TOK, WIDTH)
        return carry

    def attended_grad(s, carry):
        rows = db[s].reshape(256, WIDTH)
        da = matmul_nt(rows, wo[...].reshape(256, WIDTH)).astype(BF)
        datt[s, 0] = da[:, 0:128]
        datt[s, 1] = da[:, 128:256]
        return carry

    def attend_back(i, carry):
        s, j = i // 2, lax.rem(i, 2)
        q, k, v, da = q_buf[s, j], k_buf[s, j], v_buf[s, j], datt[s, j]
        dq, dk, dv = [], [], []
        for h in range(2):
            p = probs[i, h]
            dprob = matmul_nt(only(h, da), v)
            delta = jnp.sum(p * dprob, axis=-1, keepdims=True)
            ds = (p * (dprob - delta)).astype(BF)
            dq.append(dot_nn(ds, k))
            dk.append(matmul_tn(ds, q))
            dv.append(matmul_tn(p.astype(BF), da))
        for part, pieces in enumerate((dq, dk, dv)):
            u = jnp.where(first_head, pieces[0], pieces[1])
            if part < 2:
                u = u * 0.125
                u = u * cos_ref[...] - turned(u, low_half) * sin_ref[...]
            dqkv[part, j, s] = u.astype(BF)
        return carry

    def first_grads_for(s):
        rows = jnp.concatenate([dqkv[p, j, s] for p in range(3) for j in range(2)], axis=1)

        def first_grads(i, carry):
            w = wq[i].reshape(256, QKV)
            at = pl.multiple_of(i * 256, 256)
            ps[3, s, :, :, pl.ds(at, 256)] = matmul_nt(rows, w).astype(BF).reshape(2, TOK, 256)
            return carry

        lax.fori_loop(0, 4, first_grads, 0)

    def qkv_grad(i, carry):
        lhs = n1[:, :, :, pl.ds(pl.multiple_of(i * 256, 256), 256)].reshape(512, 256)
        for p in range(3):
            for j in range(2):
                rhs = dqkv[p, j].reshape(512, 128)
                gq[i, :, :, :, :, pl.ds(p * 256 + j * 128, 128)] = (
                    matmul_tn(lhs, rhs).astype(BF).reshape(2, 2, 2, 32, 128)
                )
        return carry

    pl.semaphore_wait(barrier, 6)
    on["s_q"] = spread(wq_in, wq)
    wide[0:256] = wo_flat[...].astype(F32)
    for j in range(8):
        wo_in[:, pl.ds(j * 128, 128)] = wide[pl.ds(j, 32, stride=8), :].astype(BF)
    g_o.start()
    wide[0 : 8 * PART] = wd_flat[...].astype(F32)
    wide[8 * PART : 8 * PAD] = jnp.zeros((8 * (PAD - PART), TOK), F32)
    for j in range(8):
        wd[zh, y, x, :, pl.ds(j * 128, 128)] = wide[pl.ds(j, PAD, stride=8), :].astype(BF)
    g_d.own_first()
    in_rows = 2 * FF // TOK
    lines[...] = wi_flat[...].astype(F32)
    gain = column(gain2_in)
    for j in range(in_rows):
        wide[pl.ds(j * 32, 32), :] = lines[pl.ds(j, 32, stride=in_rows), :] * gain
    for r in range(4):
        for u in range(2 * HID // TOK):
            tile = moved(in_moves(r, u), lambda t: wide[pl.ds(t * 32, 32), :])
            wi_in[r, :, pl.ds(u * 128, 128)] = tile.astype(BF)
    wi[z, y, x, c] = wi_in[role]
    tokens = x_ref[...].astype(F32)
    centred = tokens - jnp.mean(tokens, axis=-1, keepdims=True)
    inv = lax.rsqrt(jnp.mean(centred * centred, axis=-1, keepdims=True) + EPSILON)
    unit = centred * inv
    unit1[...] = unit
    inv1[...] = jnp.broadcast_to(inv, (TOK, 128))
    n1[zp, c] = unit.astype(BF)
    seg_buf[zp, c] = jnp.broadcast_to(seg_in[...].astype(F32), (8, TOK))
    cot[zp, c] = cot_in[...]
    for cp in on["s_q"]:
        cp.wait_recv()
    g_q.own_first()
    g_o.across()
    on["s_i"] = spread(wi_in, wi)
    g_o.first()
    g_q.across()
    on["n1"] = Share(n1)
    g_d.own_second()
    g_q.own_second()
    on["seg"] = [go_copy(seg_buf.at[zp, c], seg_buf.at[zp, c], dev) for dev, _, _ in others]
    g_q.far_first()
    g_o.second()
    for cp in on["s_i"]:
        cp.wait_recv()
    g_i.across()
    g_q.far_second()
    g_i.own_first()
    on["cot"] = Share(cot)
    g_j.across()
    on["n1"].forward()
    on["n1"].core()
    g_j.own_first()
    g_q.done()
    on["n1"].done()
    g_i.far_first()
    for cp in on["seg"]:
        cp.wait_recv()
    lax.fori_loop(1 - zp, 2 - zp, qkv_step, 0)
    lax.fori_loop(2 * (1 - zp), 2 * (1 - zp) + 2, attend, 0)
    g_o.done()
    lax.fori_loop(zp, zp + 1, qkv_step, 0)
    lax.fori_loop(1 - zp, 2 - zp, branch, 0)
    red[0].far_terms()
    g_i.own_second()
    red[0].cross()
    g_j.far_first()
    g_i.far_second()
    g_d.across()
    lax.fori_loop(2 * zp, 2 * zp + 2, attend, 0)
    g_j.own_second()
    lax.fori_loop(zp, zp + 1, branch, 0)
    red[0].near_terms()
    g_d.far_first()
    on["cot"].forward()
    g_i.done()
    mid = x_ref[...].astype(F32) + red[0].total()
    middle[...] = mid
    centred = mid - jnp.mean(mid, axis=-1, keepdims=True)
    inv = lax.rsqrt(jnp.mean(centred * centred, axis=-1, keepdims=True) + EPSILON)
    unit = centred * inv
    unit2[...] = unit
    inv2[...] = jnp.broadcast_to(inv, (TOK, 128))
    n2[zp, c] = unit.astype(BF)
    on["n2"] = Share(n2)
    g_j.far_second()
    g_d.far_second()
    on["n2"].core()
    on["cot"].core()
    on["n2"].forward()
    g_j.done()
    on["cot"].done()
    on["mark"] = len(sent)
    upper_for(zp)
    on["n2"].done()
    upper_for(1 - zp)
    lax.fori_loop(0, 2, down_grad, 0)
    r_d.first(1)
    g_d.done()
    hidden_grad_for(1 - zp)
    hidden_grad_for(zp)
    in_grad_for(HID, 2 * (1 - zh))
    r_j.first(1)
    normed_two_grad_for(1 - zp)
    red[1].far_terms()
    red[1].cross()
    r_d.second(1)
    in_grad_for(0, 2 * (1 - zh))
    r_i.first(1)
    lax.fori_loop(1 - zp, 2 - zp, down, 0)
    red[2].far_terms()
    normed_two_grad_for(zp)
    red[1].near_terms()
    r_j.second(1)
    in_grad_for(HID, 2 * zh)
    settle(on["mark"])
    e = red[1].total()
    n = unit2[...]
    d_middle = cot_in[...].astype(F32) + inv2[:, 0:1] * (
        e
        - jnp.mean(e, axis=-1, keepdims=True)
        - n * jnp.mean(e * n, axis=-1, keepdims=True)
    )
    dmid[...] = d_middle
    db[zp, c] = d_middle.astype(BF)
    on["db"] = Share(db)
    red[2].cross()
    lax.fori_loop(zp, zp + 1, down, 0)
    red[2].near_terms()
    r_d.third(1)
    in_grad_for(0, 2 * zh)
    on["db"].core()
    r_i.first(0)
    r_i.second(1)
    r_j.first(0)
    r_j.third(1)
    lax.fori_loop(zp, zp + 1, attended_grad, 0)
    r_d.first(0)
    lax.fori_loop(2 * zp, 2 * zp + 2, attend_back, 0)
    on["db"].forward()
    on["db"].done()
    lax.fori_loop(1 - zp, 2 - zp, attended_grad, 0)
    lax.fori_loop(2 * (1 - zp), 2 * (1 - zp) + 2, attend_back, 0)
    lax.fori_loop(2 * (1 - zh), 2 * (1 - zh) + 2, qkv_grad, 0)
    first_grads_for(zp)
    red[3].near_terms()
    first_grads_for(1 - zp)
    red[3].far_terms()
    r_j.second(0)
    lhs = att
    for j in range(2):
        for half in range(2):
            rhs = db[:, :, :, pl.ds(half * 512, 512)].reshape(512, 512)
            go[j, :, :, :, pl.ds(half * 512, 512)] = (
                matmul_tn(lhs[:, j].reshape(512, 128), rhs).astype(BF).reshape(2, 2, 32, 512)
            )
    red[3].cross()
    r_i.third(1)
    r_q.first(1)
    r_i.second(0)
    r_j.third(0)
    lax.fori_loop(2 * zh, 2 * zh + 2, qkv_grad, 0)
    r_q.second(1)
    r_o.first()
    r_q.first(0)
    r_q.third(1)
    r_i.third(0)
    r_o.second()
    e = red[3].total()
    n = unit1[...]
    ig_vm[...] = dmid[...] + inv1[:, 0:1] * (
        e
        - jnp.mean(e, axis=-1, keepdims=True)
        - n * jnp.mean(e * n, axis=-1, keepdims=True)
    )
    emit(1, ig_vm, ig_ref)
    r_i.fourth(gi_vm)
    r_j.fourth(gi_vm)
    r_q.second(0)
    out_vm[...] = (middle[...] + red[2].total()).astype(BF)
    emit(0, out_vm, out_ref)
    r_o.third()
    r_i.done()
    r_d.second(0)
    r_q.third(0)
    r_q.fourth(gq_vm)
    r_j.done()
    in_rows = 2 * FF // TOK
    lines[...] = wi_flat[...].astype(F32)
    gain = column(gain2_in)
    total = jnp.zeros((32, 128), F32)
    for j in range(in_rows):
        g = moved(out_moves(j), lambda t: gi_vm[t[0], :, pl.ds(t[1] * 128, 128)].astype(F32))
        total = total + g * lines[pl.ds(j, 32, stride=in_rows), :]
        gi_own[pl.ds(j, 32, stride=in_rows), :] = g * gain
    sums[...] = total
    emit(3, gi_own, gi_ref)
    emit(6, sums, sums_ref)
    r_o.fourth(go_vm)
    r_d.third(0)
    r_d.fourth(gd_vm)
    emit(2, gd_vm, gd_ref)
    r_q.done()
    emit(5, gq_vm, gq_ref)
    r_o.done()
    emit(4, go_vm, go_ref)
    g_o.end()
    assert n_sems[0] == N_COPIES
    settle(len(sent))
    for cp in local:
        cp.wait()


def block_device(inputs, segments, cotangent, ln1_gain, w_qkv, w_attn_out, ln2_gain, w_in, w_mlp_out):
    places = np.arange(2 * TOK, dtype=np.float32)
    freqs = (1.0 / ROPE_BASE ** (np.arange(0, HD, 2, dtype=np.float64) / HD)).astype(np.float32)
    angles = np.tile(places[:, None] * freqs[None, :], (1, 4))
    signs = np.where(np.arange(2 * HD) % HD < HD // 2, -1.0, 1.0).astype(np.float32)
    cosines = jnp.asarray(np.cos(angles))
    sines = jnp.asarray(np.sin(angles) * signs)
    gain_one, gain_two = ln1_gain[None], ln2_gain[None]
    wq_flat, wo_flat = w_qkv.reshape(-1, TOK), w_attn_out.reshape(-1, TOK)
    wi_flat, wd_flat = w_in.reshape(-1, TOK), w_mlp_out.reshape(-1, TOK)

    vm = pltpu.VMEM
    group = (2, 2, TOK, WIDTH)
    rows = (4, 2, 2, 2, 32)
    outs = pl.pallas_call(
        layer_kernel,
        out_shape=(
            jax.ShapeDtypeStruct((TOK, WIDTH), BF),
            jax.ShapeDtypeStruct((TOK, WIDTH), F32),
            jax.ShapeDtypeStruct((4, 32, QKV), BF),
            jax.ShapeDtypeStruct((32, WIDTH), BF),
            jax.ShapeDtypeStruct(wi_flat.shape, F32),
            jax.ShapeDtypeStruct((PAD, WIDTH), F32),
            jax.ShapeDtypeStruct((32, TOK), F32),
        ),
        in_specs=[pl.BlockSpec(memory_space=vm)] * 11,
        out_specs=(pl.BlockSpec(memory_space=pl.ANY),) * 7,
        scratch_shapes=[
            vm((2, 2, 8, TOK), F32),
            vm(group, BF),
            vm(group, BF),
            vm(group, BF),
            vm(group, BF),
            vm(rows + (QKV,), BF),
            vm((2, 2, 2, 32, WIDTH), BF),
            vm(rows + (2 * HID,), BF),
            vm((2, 2, 2, PAD, WIDTH), BF),
            vm((TOK, WIDTH), F32),
            vm((TOK, 128), F32),
            vm((TOK, WIDTH), F32),
            vm((TOK, 128), F32),
            vm((TOK, WIDTH), F32),
            vm((TOK, WIDTH), F32),
            vm((2, 2, 256, 128), BF),
            vm((2, 2, 256, 128), BF),
            vm((2, 2, 256, 128), BF),
            vm((4, 2, 256, 256), F32),
            vm((2, 2, 256, 128), BF),
            vm((2, 2, 256, 128), BF),
            vm((2, 256, HID), F32),
            vm((2, 256, HID), F32),
            vm((2, 256, HID), BF),
            vm((2, 256, 2 * HID), BF),
            vm((3, 2, 2, 256, 128), BF),
            vm((4,) + group, BF),
            vm((4, 2, TOK, WIDTH), BF),
            vm((4, TOK, WIDTH), BF),
            vm((4, TOK, WIDTH), BF),
            vm(rows + (QKV,), BF),
            vm((2, 2, 2, 32, WIDTH), BF),
            vm(rows + (2 * HID,), BF),
            vm((2, 2, 2, PAD, WIDTH), BF),
            vm((2, 2, 2, 2, 2, 32, QKV // 2), BF),
            vm((2, 2, 2, 2, 32, QKV // 2), BF),
            vm((2, 2, 32, QKV), BF),
            vm((2, 2, 2, 32, WIDTH // 2), BF),
            vm((2, 2, 32, WIDTH // 2), BF),
            vm((2, 32, WIDTH), BF),
            vm((2, 2, 2, 2, 2, 2, 32, HID // 2), BF),
            vm((2, 2, 2, 2, 2, 32, HID // 2), BF),
            vm((2, 2, 2, 32, HID), BF),
            vm((2, 2, 1, 2, PAD, WIDTH // 2), BF),
            vm((2, 2, 1, PAD, WIDTH // 2), BF),
            vm((1, PAD, WIDTH), BF),
            vm((4, 32, QKV), BF),
            vm((32, WIDTH), BF),
            vm((4, 32, 2 * HID), BF),
            vm((64 * FF // TOK, TOK), F32),
            vm((64 * FF // TOK, TOK), F32),
            vm((TOK, WIDTH), BF),
            vm((TOK, WIDTH), F32),
            vm((4, 32, QKV), BF),
            vm((32, WIDTH), BF),
            vm((4, 32, 2 * HID), BF),
            vm((PAD, WIDTH), F32),
            vm(wi_flat.shape, F32),
            vm((32, TOK), F32),
            pltpu.SemaphoreType.DMA((N_SENDS,)),
            pltpu.SemaphoreType.DMA((N_COPIES,)),
            pltpu.SemaphoreType.DMA((7,)),
        ],
        compiler_params=pltpu.CompilerParams(
            collective_id=0, has_side_effects=True, vmem_limit_bytes=60 * 2**20
        ),
    )(
        inputs[0],
        cotangent[0],
        segments,
        cosines,
        sines,
        gain_one,
        gain_two,
        wq_flat,
        wo_flat,
        wi_flat,
        wd_flat,
    )
    output, input_grad, gq, go, gi, gd, sums = outs
    final = pl.pallas_call(
        finish_kernel,
        out_shape=(
            jax.ShapeDtypeStruct((TOK, WIDTH), BF),
            jax.ShapeDtypeStruct((TOK, WIDTH), F32),
            jax.ShapeDtypeStruct((1, 32), F32),
            jax.ShapeDtypeStruct(wq_flat.shape, F32),
            jax.ShapeDtypeStruct(wo_flat.shape, F32),
            jax.ShapeDtypeStruct((1, 32), F32),
            jax.ShapeDtypeStruct(wi_flat.shape, F32),
            jax.ShapeDtypeStruct(wd_flat.shape, F32),
        ),
        in_specs=[pl.BlockSpec(memory_space=pl.ANY)] * 6
        + [pl.BlockSpec(memory_space=vm)] * 2
        + [pl.BlockSpec(memory_space=pl.ANY)],
        out_specs=tuple(
            pl.BlockSpec(memory_space=vm if i in (2, 5) else pl.ANY) for i in range(8)
        ),
        scratch_shapes=[
            vm(wq_flat.shape, F32),
            vm((4, 32, QKV), BF),
            vm((32, WIDTH), BF),
            vm(wi_flat.shape, F32),
            vm((PAD, WIDTH), F32),
            vm(wq_flat.shape, BF),
            vm(wq_flat.shape, F32),
            vm(wo_flat.shape, F32),
            vm(wd_flat.shape, F32),
            vm((TOK, WIDTH), F32),
            vm((TOK, WIDTH), BF),
            pltpu.SemaphoreType.DMA((14,)),
        ],
        compiler_params=pltpu.CompilerParams(vmem_limit_bytes=60 * 2**20),
    )(gq, go, gi, gd, output, input_grad, gain_one, sums, wq_flat)
    return (final[0][None], final[1][None]) + tuple(f.reshape(-1) for f in final[2:])


N_COPIES = 142
N_SENDS = 89
PIECES = 2


def solution(mesh):
    block = dict(mesh.shape) == {"dp": 16, "seq": 2}
    placed = (
        P("dp", "seq", None),
        P("dp", "seq"),
        P("dp", "seq", None),
        P(("dp", "seq")),
        P(("dp", "seq")),
        P(("dp", "seq")),
        P(("dp", "seq")),
        P(("dp", "seq")),
        P(("dp", "seq")),
    )
    return jax.shard_map(
        block_device if block else general_device,
        mesh=mesh,
        in_specs=placed,
        out_specs=(
            P("dp", "seq", None),
            P("dp", "seq", None),
            P(("dp", "seq")),
            P(("dp", "seq")),
            P(("dp", "seq")),
            P(("dp", "seq")),
            P(("dp", "seq")),
            P(("dp", "seq")),
        ),
        check_vma=False,
    )
```
